32 devices in a mesh: seq: 8 (over z, y), fsdp: 4 (over x, core).
Axes of the slice: x: 2, y: 2, z: 4, core: 2. Of those that a mesh axis runs over, the one named last changes fastest.
Arguments:
- tokens_in: bfloat16 [2, 2048, 2048], P(None, 'seq', 'fsdp'), may hold values from -6 to 6
- cotangent: bfloat16 [2, 2048, 2048], P(None, 'seq', 'fsdp'), may hold values from -6 to 6
- gain_attn: bfloat16 [2048], P('seq'), may hold values from 0.099609375 to 1.8984375
- query_weight: bfloat16 [2048, 2048], P('seq', 'fsdp'), may hold values from -0.0625 to 0.0625
- key_weight: bfloat16 [2048, 2048], P('seq', 'fsdp'), may hold values from -0.0625 to 0.0625
- value_weight: bfloat16 [2048, 2048], P('seq', 'fsdp'), may hold values from -0.125 to 0.125
- output_weight: bfloat16 [2048, 2048], P('seq', 'fsdp'), may hold values from -0.75 to 0.75
- bias_table: bfloat16 [32, 32], P('seq', 'fsdp'), may hold values from -6 to 6
- gain_ffn: bfloat16 [2048], P('seq'), may hold values from 0.099609375 to 1.8984375
- gate_weight: bfloat16 [2048, 5120], P('seq', 'fsdp'), may hold values from -0.125 to 0.125
- up_weight: bfloat16 [2048, 5120], P('seq', 'fsdp'), may hold values from -0.125 to 0.125
- down_weight: bfloat16 [2048, 5120], P('seq', 'fsdp'), may hold values from -0.078125 to 0.078125
- lengths: int32 [2], replicated, may hold values from 256 to 2048, as said below
- buckets: int32 [4095], replicated, may hold values from 0 to 31
Outputs:
- layer_out: bfloat16 [2, 2048, 2048], P(None, 'seq', 'fsdp')
- grad_tokens: float32 [2, 2048, 2048], P(None, 'seq', 'fsdp')
- grad_gain_attn: float32 [2048], P('seq')
- grad_query: float32 [2048, 2048], P('seq', 'fsdp')
- grad_key: float32 [2048, 2048], P('seq', 'fsdp')
- grad_value: float32 [2048, 2048], P('seq', 'fsdp')
- grad_output: float32 [2048, 2048], P('seq', 'fsdp')
- grad_table: float32 [32, 32], P('seq', 'fsdp')
- grad_gain_ffn: float32 [2048], P('seq')
- grad_gate: float32 [2048, 5120], P('seq', 'fsdp')
- grad_up: float32 [2048, 5120], P('seq', 'fsdp')
- grad_down: float32 [2048, 5120], P('seq', 'fsdp')
The draws below stay inside these ranges and needn't reach their ends.
Inputs may be any that keep to these rules, and one draw needn't show every extreme that they name: `lengths`: exactly one of the 2 sequences is valid over all 2048 slots; the others end at least 256 slots earlier.
All inputs are finite; a program needn't handle non-finite values.
Results may differ from the reference program's by a relative error of at most 0.014.
The reference program's roundings to bfloat16 on the way count: a program that leaves them out, or rounds other values in their place, can miss the bound.
Values may be sent and summed in bfloat16 or wider, within the bound.
A program may use at most 384 MiB of HBM per device.

```python
import jax
import jax.numpy as jnp
from jax import lax

D = 2048
H = 32
DH = 64
FF = 5120
NB = 32
SEQS = 2
LENGTH = 2048
SLOTS = 256


def draw_lengths(key, part):
    key = jax.random.fold_in(key, 41)
    pick_key = jax.random.fold_in(key, 5)
    length_key = jax.random.fold_in(key, 9)
    lowest = LENGTH // 8
    highest_len = LENGTH - SLOTS
    raw_bits = jax.random.bits(length_key, (SEQS,))
    spread_count = highest_len - lowest + 1
    others = lowest + (raw_bits % spread_count).astype(jnp.int32)
    chosen = jax.random.randint(pick_key, (), 0, SEQS)
    return jnp.where(jnp.arange(SEQS) == chosen, LENGTH, others).astype(jnp.int32)


def plant(array, rng, smallest, high):
    longest = array.shape.index(max(array.shape))
    spots = []
    for shift in (0, 1):
        where = [jax.random.randint(jax.random.fold_in(rng, axis), (), 0, length) for axis, length in enumerate(array.shape)]
        where[longest] = (where[longest] + shift) % array.shape[longest]
        spots.append(tuple(where))
    return array.at[spots[0]].set(smallest).at[spots[1]].set(high)


def block_levels(key, dims, shards, low, largest):
    def one(dim, shards_of):
        draws = jax.random.uniform(jax.random.fold_in(jax.random.fold_in(key, 6), dim), (shards_of,), jnp.float32, low / len(shards), largest / len(shards))
        return jnp.repeat(jnp.exp(draws), dims[dim] // shards_of).reshape((-1,) + (1,) * (len(dims) - dim - 1))

    level = one(*shards[0])
    for cut in shards[1:]:
        level = level * one(*cut)
    return level


def normal_values(stream_key, shape, deviation, limit, shards=(), held_as=jnp.bfloat16):
    level = block_levels(stream_key, shape, shards, -0.22, 0.18) if shards else 1.0
    array = jax.random.normal(stream_key, shape, jnp.float32) * deviation * level
    return jnp.minimum(jnp.maximum(array, -limit), limit).astype(held_as)


def setup_inputs(seed: int = 0) -> dict:
    streams_of = jax.random.split(jax.random.key(seed), 15)
    return {
        "tokens_in": normal_values(streams_of[0], (SEQS, LENGTH, D), 1.0, 6.0, ((1, 8), (2, 4))),
        "cotangent": normal_values(streams_of[1], (SEQS, LENGTH, D), 1.0, 6.0, ((1, 8), (2, 4))),
        "gain_attn": jnp.clip(1.0 + 0.18 * jax.random.normal(streams_of[2], (D,), jnp.float32), 0.099609375, 1.8984375).astype(jnp.bfloat16),
        "query_weight": normal_values(streams_of[3], (D, H * DH), (4 * D) ** -0.5, 0.0625, ((0, 8), (1, 4))),
        "key_weight": normal_values(streams_of[4], (D, H * DH), (4 * D) ** -0.5, 0.0625, ((0, 8), (1, 4))),
        "value_weight": normal_values(streams_of[5], (D, H * DH), D ** -0.5, 0.125, ((0, 8), (1, 4))),
        "output_weight": normal_values(streams_of[6], (D, H * DH), (H * DH // 32) ** -0.5, 0.75, ((0, 8), (1, 4))),
        "bias_table": normal_values(streams_of[7], (NB, H), 1.0, 6.0, ((0, 8), (1, 4))),
        "gain_ffn": jnp.clip(1.0 + 0.18 * jax.random.normal(streams_of[8], (D,), jnp.float32), 0.099609375, 1.8984375).astype(jnp.bfloat16),
        "gate_weight": normal_values(streams_of[9], (D, FF), D ** -0.5, 0.125, ((0, 8), (1, 4))),
        "up_weight": normal_values(streams_of[10], (D, FF), D ** -0.5, 0.125, ((0, 8), (1, 4))),
        "down_weight": normal_values(streams_of[11], (D, FF), FF ** -0.5, 0.078125, ((0, 8), (1, 4))),
        "lengths": draw_lengths(jax.random.fold_in(streams_of[14], 71), 0),
        "buckets": plant(jax.random.randint(streams_of[13], (2 * LENGTH - 1,), 0, NB), jax.random.fold_in(streams_of[13], 1), 0, NB - 1).astype(jnp.int32),
    }


@jax.custom_vjp
def low(v):
    return lax.optimization_barrier(v.astype(jnp.bfloat16)).astype(jnp.float32)

@jax.custom_vjp
def low_back(v):
    return v

def low_keep(v):
    return (low(v), None)

def low_pass(kept, grad):
    return (grad,)

def back_keep(v):
    return (v, None)

def back_low(kept, grad):
    return (low(grad),)
low.defvjp(low_keep, low_pass)
low_back.defvjp(back_keep, back_low)
epsilon = 1e-06
highest = lax.Precision.HIGHEST

def plain_product(left, right):
    return jnp.dot(left, right, precision=highest, preferred_element_type=jnp.float32)

def rms_scale(rows, gain):
    return rows * lax.rsqrt(lax.optimization_barrier(jnp.mean(rows * rows, axis=-1, keepdims=True)) + epsilon) * gain

def reference(tokens_in, cotangent, gain_attn, query_weight, key_weight, value_weight, output_weight, bias_table, gain_ffn, gate_weight, up_weight, down_weight, lengths, buckets):
    positions = jnp.arange(LENGTH)
    key_valid = positions[None, :] < lengths[:, None]
    offset_index = positions[None, :] - positions[:, None] + (LENGTH - 1)
    bucket_hot = (buckets[:, None] == jnp.arange(NB)[None, :]).astype(jnp.float32)

    def attend_head(inputs):
        query_tile_rows, key_tile_rows, value_tile_rows, bias_line = inputs
        scores = jnp.einsum('sid,sjd->sij', query_tile_rows, key_tile_rows, precision=highest) + bias_line[offset_index][None]
        scores = low_back(scores)
        scores = jnp.where(key_valid[:, None, :], scores, -1e+30)
        weights_reduced_precision = low(jax.nn.softmax(scores, axis=-1))
        return low_back(low(jnp.einsum('sij,sjd->sid', weights_reduced_precision, value_tile_rows, precision=highest)))

    def forward(tokens, gain_one, query_w, key_w, value_w, output_w, table, gain_two, gate_w, upward_w, down_w):
        rows = tokens.reshape(SEQS * LENGTH, D)
        normed = low(rms_scale(rows, gain_one))

        def heads_of(weight):
            return low_back(low(plain_product(normed, weight))).reshape(SEQS, LENGTH, H, DH).transpose(2, 0, 1, 3)
        offsets = plain_product(bucket_hot, table).T
        context = lax.map(jax.checkpoint(attend_head), (heads_of(query_w), heads_of(key_w), heads_of(value_w), offsets))
        context = context.transpose(1, 2, 0, 3).reshape(SEQS * LENGTH, H * DH)
        attended = low_back(plain_product(context, output_w.T))
        residual = rows + attended
        normed_ffn = low(rms_scale(residual, gain_two))
        gate = low_back(plain_product(normed_ffn, gate_w))
        upward = low_back(plain_product(normed_ffn, upward_w))
        hidden = low(jax.nn.gelu(gate) * upward)
        return (residual + plain_product(hidden, down_w.T)).reshape(SEQS, LENGTH, D)
    floats = [item.astype(jnp.float32) for item in (tokens_in, gain_attn, query_weight, key_weight, value_weight, output_weight, bias_table, gain_ffn, gate_weight, up_weight, down_weight)]
    layer, backward = jax.vjp(forward, *floats)
    row_valid = key_valid.astype(jnp.float32)[:, :, None]
    grads = backward(cotangent.astype(jnp.float32) * row_valid)
    return (layer.astype(jnp.bfloat16), grads[0], grads[1], grads[2], grads[3], grads[4], grads[5], grads[6], grads[7], grads[8], grads[9], grads[10])
```

```python
from functools import partial

import jax
import jax.numpy as jnp
from jax import lax
from jax.experimental import pallas as pl
from jax.experimental.pallas import tpu as pltpu
from jax.sharding import PartitionSpec as P

DH = 64


epsilon = 1e-06
highest = lax.Precision.HIGHEST
masked_score = -1e30


def plain_product(left, right):
    return jnp.dot(left, right, preferred_element_type=jnp.float32)


def right_transposed(left, right):
    return lax.dot_general(
        left, right, (((1,), (1,)), ((), ())), preferred_element_type=jnp.float32
    )


def left_transposed(left, right):
    return lax.dot_general(
        left, right, (((0,), (0,)), ((), ())), preferred_element_type=jnp.float32
    )


def normalize(rows, gain):
    row_scale = lax.rsqrt(jnp.mean(rows * rows, axis=-1, keepdims=True) + epsilon)
    unit_rows = rows * row_scale
    return (unit_rows, row_scale, (unit_rows * gain.astype(jnp.float32)).astype(jnp.bfloat16))


def norm_back(grad_normed, unit_rows, row_scale, gain):
    weighted = grad_normed * gain.astype(jnp.float32)
    return row_scale * (
        weighted - unit_rows * jnp.mean(weighted * unit_rows, axis=-1, keepdims=True)
    )


def to_heads(rows, batch_count, head_size):
    slot_count = rows.shape[0] // batch_count
    number_of_heads = rows.shape[1] // head_size
    return rows.reshape(batch_count, slot_count, number_of_heads, head_size).transpose(2, 0, 1, 3)


def from_heads(blocks):
    number_of_heads, batch_count, slot_count, head_size = blocks.shape
    return blocks.transpose(1, 2, 0, 3).reshape(
        batch_count * slot_count, number_of_heads * head_size
    )


def bias_rows(bias_line, first_query, slot_count, length):
    span = slot_count + length - 1
    segment = lax.dynamic_slice_in_dim(bias_line, length - first_query - slot_count, span)
    flat = jnp.tile(segment, slot_count)
    skewed = flat[slot_count - 1 : slot_count - 1 + slot_count * (span - 1)].reshape(
        slot_count, span - 1
    )
    return skewed[:, :length]


def bias_rows_back(block_grad, first_query, slot_count, length, line_length):
    span = slot_count + length - 1
    widened = jnp.pad(block_grad, ((0, 0), (0, span - 1 - length)))
    flat = jnp.pad(widened.reshape(-1), (slot_count - 1, 1))
    segment_grad = jnp.sum(flat.reshape(slot_count, span), axis=0)
    return lax.dynamic_update_slice_in_dim(
        jnp.zeros((line_length,), jnp.float32), segment_grad, length - first_query - slot_count, 0
    )


def full_features(block):
    gathered = lax.all_gather(block, "fsdp", axis=2, tiled=True)
    return gathered.reshape(gathered.shape[0] * gathered.shape[1], gathered.shape[2])


def feature_total(partial_rows):
    return lax.psum(partial_rows, "fsdp")


def shards(
    tokens_in,
    cotangent,
    gain_attn,
    query_weight,
    key_weight,
    value_weight,
    output_weight,
    bias_table,
    gain_ffn,
    gate_weight,
    up_weight,
    down_weight,
    lengths,
    buckets,
):
    batch_count, slot_count, part_width = tokens_in.shape
    head_size = DH
    seq_index = lax.axis_index("seq")
    fsdp_index = lax.axis_index("fsdp")
    length = slot_count * lax.axis_size("seq")
    line_length = buckets.shape[0]
    first_query = seq_index * slot_count
    positions = jnp.arange(length, dtype=jnp.int32)
    query_positions = first_query + jnp.arange(slot_count, dtype=jnp.int32)
    key_valid = positions[None, :] < lengths[:, None]
    own_valid = query_positions[None, :] < lengths[:, None]
    gain_one, query_full, key_full, value_full, output_full, table_full = (
        lax.all_gather(gain_attn, "seq", axis=0, tiled=True),
        lax.all_gather(query_weight, "seq", axis=0, tiled=True),
        lax.all_gather(key_weight, "seq", axis=0, tiled=True),
        lax.all_gather(value_weight, "seq", axis=0, tiled=True),
        lax.all_gather(output_weight, "seq", axis=0, tiled=True),
        lax.all_gather(bias_table, "seq", axis=0, tiled=True),
    )
    token_rows = full_features(tokens_in).astype(jnp.float32)
    unit_one, scale_one, normed_one = normalize(token_rows, gain_one)
    query_heads = to_heads(
        plain_product(normed_one, query_full).astype(jnp.bfloat16), batch_count, head_size
    )
    key_heads = to_heads(
        plain_product(normed_one, key_full).astype(jnp.bfloat16), batch_count, head_size
    )
    value_heads = to_heads(
        plain_product(normed_one, value_full).astype(jnp.bfloat16), batch_count, head_size
    )
    number_of_heads = query_heads.shape[0]
    flat_shape = (number_of_heads, batch_count, slot_count * head_size)
    gathered_keys, gathered_values = (
        lax.all_gather(key_heads.reshape(flat_shape), "seq", axis=2, tiled=True),
        lax.all_gather(value_heads.reshape(flat_shape), "seq", axis=2, tiled=True),
    )
    all_keys = gathered_keys.reshape(number_of_heads, batch_count, length, head_size)
    all_values = gathered_values.reshape(number_of_heads, batch_count, length, head_size)
    bucket_hot = (
        buckets[:, None] == jnp.arange(table_full.shape[0], dtype=jnp.int32)[None, :]
    ).astype(jnp.float32)
    offset_bias = lax.dot_general(
        table_full.astype(jnp.float32), bucket_hot, (((0,), (1,)), ((), ())), precision=highest
    )

    def masked_scores(query_tile_rows, key_tile_rows, bias_block):
        raw = (
            jnp.einsum(
                "jht,jxt->jhx", query_tile_rows, key_tile_rows, preferred_element_type=jnp.float32
            )
            + bias_block[None]
        )
        return jnp.where(key_valid[:, None, :], raw, masked_score)

    def attend(inputs):
        query_tile_rows, key_tile_rows, value_tile_rows, bias_line = inputs
        scores = masked_scores(
            query_tile_rows, key_tile_rows, bias_rows(bias_line, first_query, slot_count, length)
        )
        row_peak = jnp.max(scores, axis=-1, keepdims=True)
        raised = jnp.exp(scores - row_peak)
        denominator = jnp.sum(raised, axis=-1, keepdims=True)
        weights_reduced_precision = (raised / denominator).astype(jnp.bfloat16)
        context = jnp.einsum(
            "wot,wtf->wof",
            weights_reduced_precision,
            value_tile_rows,
            preferred_element_type=jnp.float32,
        ).astype(jnp.bfloat16)
        return (context, (row_peak + jnp.log(denominator))[..., 0])

    context_heads, log_totals = lax.map(attend, (query_heads, all_keys, all_values, offset_bias))
    context_rows = from_heads(context_heads)
    residual = token_rows + feature_total(right_transposed(context_rows, output_full))
    gain_two, gate_full, up_full, down_full = (
        lax.all_gather(gain_ffn, "seq", axis=0, tiled=True),
        lax.all_gather(gate_weight, "seq", axis=0, tiled=True),
        lax.all_gather(up_weight, "seq", axis=0, tiled=True),
        lax.all_gather(down_weight, "seq", axis=0, tiled=True),
    )
    unit_two, scale_two, normed_two = normalize(residual, gain_two)
    gate_pre = plain_product(normed_two, gate_full)
    up_pre = plain_product(normed_two, up_full)
    activated, gelu_back = jax.vjp(jax.nn.gelu, gate_pre)
    hidden = (activated * up_pre).astype(jnp.bfloat16)
    ffn_share = lax.psum_scatter(
        right_transposed(hidden, down_full), "fsdp", scatter_dimension=1, tiled=True
    )
    residual_share = lax.dynamic_slice_in_dim(residual, fsdp_index * part_width, part_width, 1)
    layer_out = (
        (residual_share + ffn_share)
        .astype(jnp.bfloat16)
        .reshape(batch_count, slot_count, part_width)
    )
    masked_cot = jnp.where(own_valid[:, :, None], cotangent, jnp.zeros_like(cotangent))
    grad_rows = full_features(masked_cot)
    grad_down = left_transposed(grad_rows, hidden)
    grad_hidden = plain_product(grad_rows, down_full)
    grad_gate_pre = gelu_back(grad_hidden * up_pre)[0].astype(jnp.bfloat16)
    grad_up_pre = (grad_hidden * activated).astype(jnp.bfloat16)
    grad_gate = left_transposed(normed_two, grad_gate_pre)
    grad_up = left_transposed(normed_two, grad_up_pre)
    normed_two_grad = right_transposed(grad_gate_pre, gate_full) + right_transposed(
        grad_up_pre, up_full
    )
    second_gain_piece = jnp.sum(normed_two_grad * unit_two, axis=0)
    ffn_grads = (
        lax.psum_scatter(second_gain_piece, "seq", scatter_dimension=0, tiled=True),
        lax.psum_scatter(grad_gate, "seq", scatter_dimension=0, tiled=True),
        lax.psum_scatter(grad_up, "seq", scatter_dimension=0, tiled=True),
        lax.psum_scatter(grad_down, "seq", scatter_dimension=0, tiled=True),
    )
    residual_grad = grad_rows.astype(jnp.float32) + norm_back(
        feature_total(normed_two_grad), unit_two, scale_two, gain_two
    )
    residual_low = residual_grad.astype(jnp.bfloat16)
    grad_output = left_transposed(residual_low, context_rows)
    context_grad = to_heads(
        plain_product(residual_low, output_full).astype(jnp.bfloat16), batch_count, head_size
    )

    def query_side(inputs, with_keys):
        query_tile_rows, key_tile_rows, value_tile_rows, bias_line, log_total, context_tile_rows = (
            inputs
        )
        scores = masked_scores(
            query_tile_rows, key_tile_rows, bias_rows(bias_line, first_query, slot_count, length)
        )
        probs = jnp.exp(scores - log_total[..., None])
        prob_grad = jnp.einsum(
            "jht,jxt->jhx", context_tile_rows, value_tile_rows, preferred_element_type=jnp.float32
        )
        delta = jnp.sum(probs * prob_grad, axis=-1)
        score_gradient = (probs * (prob_grad - delta[..., None])).astype(jnp.bfloat16)
        query_grad = jnp.einsum(
            "wot,wtf->wof", score_gradient, key_tile_rows, preferred_element_type=jnp.float32
        )
        bias_grad = bias_rows_back(
            jnp.sum(score_gradient.astype(jnp.float32), axis=0),
            first_query,
            slot_count,
            length,
            line_length,
        )
        key_term = jnp.einsum(
            "xic,xil->xcl", score_gradient, query_tile_rows, preferred_element_type=jnp.float32
        )
        value_term = jnp.einsum(
            "xic,xil->xcl",
            probs.astype(jnp.bfloat16),
            context_tile_rows,
            preferred_element_type=jnp.float32,
        )
        return (query_grad, bias_grad, delta, key_term, value_term)

    side_inputs = (query_heads, all_keys, all_values, offset_bias, log_totals, context_grad)
    query_grad, bias_grad, delta, key_terms, value_terms = lax.map(
        partial(query_side, with_keys=True), side_inputs
    )
    wide_shape = (number_of_heads, batch_count, length * head_size)
    key_sums, value_sums = (
        lax.psum_scatter(key_terms.reshape(wide_shape), "seq", scatter_dimension=2, tiled=True),
        lax.psum_scatter(value_terms.reshape(wide_shape), "seq", scatter_dimension=2, tiled=True),
    )
    own_shape = (number_of_heads, batch_count, slot_count, head_size)
    query_low = from_heads(query_grad.astype(jnp.bfloat16))
    key_low = from_heads(key_sums.reshape(own_shape).astype(jnp.bfloat16))
    value_low = from_heads(value_sums.reshape(own_shape).astype(jnp.bfloat16))
    grad_query = left_transposed(normed_one, query_low)
    grad_key = left_transposed(normed_one, key_low)
    grad_value = left_transposed(normed_one, value_low)
    grad_table = lax.dot_general(bucket_hot, bias_grad, (((0,), (1,)), ((), ())), precision=highest)
    normed_one_grad = (
        right_transposed(query_low, query_full)
        + right_transposed(key_low, key_full)
        + right_transposed(value_low, value_full)
    )
    gain_one_part = jnp.sum(normed_one_grad * unit_one, axis=0)
    attn_grads = (
        lax.psum_scatter(gain_one_part, "seq", scatter_dimension=0, tiled=True),
        lax.psum_scatter(grad_query, "seq", scatter_dimension=0, tiled=True),
        lax.psum_scatter(grad_key, "seq", scatter_dimension=0, tiled=True),
        lax.psum_scatter(grad_value, "seq", scatter_dimension=0, tiled=True),
        lax.psum_scatter(grad_output, "seq", scatter_dimension=0, tiled=True),
        lax.psum_scatter(grad_table, "seq", scatter_dimension=0, tiled=True),
    )
    token_grad = residual_grad + norm_back(
        feature_total(normed_one_grad), unit_one, scale_one, gain_one
    )
    token_share = lax.dynamic_slice_in_dim(
        token_grad, fsdp_index * part_width, part_width, 1
    ).reshape(batch_count, slot_count, part_width)
    gain_one_sum, gain_two_sum = lax.psum((attn_grads[0], ffn_grads[0]), "fsdp")
    return (
        layer_out,
        token_share,
        gain_one_sum,
        attn_grads[1],
        attn_grads[2],
        attn_grads[3],
        attn_grads[4],
        attn_grads[5],
        gain_two_sum,
        ffn_grads[1],
        ffn_grads[2],
        ffn_grads[3],
    )


BLOCK = 128
BOTH = ("seq", "fsdp")


def move(value, target):
    pairs = []
    for z in range(4):
        for y in range(2):
            for x in range(2):
                for c in range(2):
                    zt, yt, xt, ct = target(z, y, x, c)
                    pairs.append(((2 * z + y) * 4 + 2 * x + c, (2 * zt + yt) * 4 + 2 * xt + ct))
    return lax.ppermute(value, BOTH, pairs)


def spread_slot(k):
    return lambda z, y, x, c: (2 * c + (k ^ (z & 1)), y, x, z >> 1)


def spread_plane(dy, dx):
    return lambda z, y, x, c: (z, y ^ dy, c ^ dx, x)


def join_plane(dy, dx):
    return lambda z, y, x, c: (z, y ^ dy, c, x ^ dx)


def along_z(d):
    return lambda z, y, x, c: (z ^ d, y, x, c)


def other_core(z, y, x, c):
    return (z, y, x, c ^ 1)


def across(dx, dy):
    return lambda z, y, x, c: (z, y ^ dy, x ^ dx, c)


def across_fsdp(d):
    return lambda z, y, x, c: (z, y, x ^ (d >> 1), c ^ (d & 1))


def in_place(relative, me):
    current, bit = list(relative), 1
    while bit < len(current):
        swap = (me & bit) != 0
        current = [jnp.where(swap, current[i ^ bit], current[i]) for i in range(len(current))]
        bit *= 2
    return current


def share_rows(rows):
    mine = jnp.concatenate([rows] + [move(rows, along_z(d)) for d in (1, 2, 3)], axis=0)
    return jnp.concatenate([mine, move(mine, other_core)], axis=0)


def sum_rows(mine, other):
    mine = mine + move(other, other_core).astype(jnp.float32)
    count = mine.shape[0] // 4
    total = mine[:count]
    for d in (1, 2, 3):
        part = mine[d * count : (d + 1) * count].astype(jnp.bfloat16)
        total = total + move(part, along_z(d)).astype(jnp.float32)
    return total


def assemble_kernel(widths, *refs):
    pieces, outs, sem = refs[:8], refs[8:-1], refs[-1]
    z, y = lax.axis_index("seq") // 2, lax.axis_index("seq") % 2
    x = lax.axis_index("fsdp") // 2
    mask = 4 * x + 2 * (z % 2) + y
    copies = []
    for i, piece in enumerate(pieces):
        rows = piece.shape[0]
        first = pl.multiple_of(jnp.bitwise_xor(mask, i) * rows, rows)
        start = 0
        for n, (out, width) in enumerate(zip(outs, widths)):
            copies.append(
                pltpu.make_async_copy(
                    piece.at[:, pl.ds(start, width)], out.at[pl.ds(first, rows), :], sem.at[i, n]
                )
            )
            start += width
    for copy in copies:
        copy.start()
    for copy in copies:
        copy.wait()


def assemble(pieces, widths):
    rows = pieces[0].shape[0] * 8
    return pl.pallas_call(
        partial(assemble_kernel, widths),
        name="assemble",
        out_shape=[jax.ShapeDtypeStruct((rows, w), jnp.bfloat16) for w in widths],
        in_specs=[pl.BlockSpec(memory_space=pl.ANY)] * 8,
        out_specs=[pl.BlockSpec(memory_space=pltpu.VMEM)] * len(widths),
        scratch_shapes=[pltpu.SemaphoreType.DMA((8, len(widths)))],
        compiler_params=pltpu.CompilerParams(vmem_limit_bytes=24 << 20),
    )(*pieces)


def gather_weights(slots, widths):
    pieces = [None] * 8
    for k in range(2):
        held = move(slots[k], spread_slot(k))
        for dx in range(2):
            for dy in range(2):
                pieces[4 * dx + 2 * k + dy] = move(held, spread_plane(dy, dx))
    return assemble(pieces, widths)


def scatter_grads(grads, mask, count):
    out = []
    for k in range(2):
        total = 0.0
        for dx in range(2):
            for dy in range(2):
                first = ((4 * dx + 2 * k + dy) ^ mask) * count
                part = jnp.concatenate(
                    [lax.dynamic_slice_in_dim(g, first, count, 0) for g in grads], axis=1
                )
                total = total + move(part, join_plane(dy, dx)).astype(jnp.float32)
        out.append(move(total.astype(jnp.bfloat16), spread_slot(k)).astype(jnp.float32))
    return out


KEYS = 256
QUERIES = 256
OFFSET = 1920


def skew_table(rev_ref, table):
    width = rev_ref.shape[1]
    line = jnp.broadcast_to(rev_ref[...], (8, width))
    for first in range(0, BLOCK, 8):
        table[first : first + 8, :] = pltpu.roll(
            line, (width - (BLOCK - 1) + first) % width, axis=1, stride=1, stride_axis=0
        )


def place_of(piece, part, z, y, x, c):
    c_rel, d = part // 4, part % 4
    b = jnp.bitwise_xor(x, piece // 2)
    block = (
        4 * jnp.bitwise_xor(z, d)
        + 2 * jnp.bitwise_xor(y, piece % 2)
        + jnp.bitwise_xor(c, c_rel)
    )
    return b, block


def part_of(b, block, z, y, x, c):
    piece = 2 * jnp.bitwise_xor(b, x) + jnp.bitwise_xor((block // 2) % 2, y)
    part = 4 * jnp.bitwise_xor(block % 2, c) + jnp.bitwise_xor(block // 4, z)
    return piece, part


def lanes(first, count):
    return pl.ds(pl.multiple_of(first, BLOCK), count)


def attend_kernel(sc, p0, p1, p2, p3, rev_ref, ctx_ref, ctx_wide, lse_ref, qkv, keys, table):
    z, y, x, c = sc[2], sc[3], sc[4], sc[5]
    for piece, ref in enumerate((p0, p1, p2, p3)):
        for part in range(8):
            b, block = place_of(piece, part, z, y, x, c)
            data = ref[:, :, part * BLOCK : (part + 1) * BLOCK]
            qkv[b, :, :, lanes(block * BLOCK, BLOCK)] = data
            keys[b, lanes(block * BLOCK, BLOCK), :] = data[1].T
    skew_table(rev_ref, table)
    length = qkv.shape[-1]
    for b in range(2):
        valid = sc[b]
        full = valid // KEYS

        @pl.loop(0, length // QUERIES)
        def _(i):
            first_query = i * QUERIES
            query = qkv[b, 0, :, lanes(first_query, QUERIES)]

            def tile(j, carry, masked):
                peak, total, acc = carry
                first_key = j * KEYS
                score = jnp.dot(
                    keys[b, lanes(first_key, KEYS), :], query, preferred_element_type=jnp.float32
                )
                score = score + jnp.concatenate(
                    [
                        table[:, lanes(first_query - first_key + OFFSET - t, QUERIES)]
                        for t in range(0, KEYS, BLOCK)
                    ],
                    axis=0,
                )
                if masked:
                    position = first_key + lax.broadcasted_iota(jnp.int32, (KEYS, QUERIES), 0)
                    score = jnp.where(position < valid, score, masked_score)
                now = jnp.maximum(peak, jnp.max(score, axis=0, keepdims=True))
                scale = jnp.exp(peak - now)
                prob = jnp.exp(score - now)
                total = total * scale + jnp.sum(prob, axis=0, keepdims=True)
                acc = acc * scale + jnp.dot(
                    qkv[b, 2, :, lanes(first_key, KEYS)],
                    prob.astype(jnp.bfloat16),
                    preferred_element_type=jnp.float32,
                )
                return now, total, acc

            carry = (
                jnp.full((1, QUERIES), masked_score, jnp.float32),
                jnp.zeros((1, QUERIES), jnp.float32),
                jnp.zeros((DH, QUERIES), jnp.float32),
            )
            carry = lax.fori_loop(0, full, lambda j, s: tile(j, s, False), carry)
            peak, total, acc = lax.cond(
                valid > full * KEYS, lambda s: tile(full, s, True), lambda s: s, carry
            )
            context = acc / total
            ctx_wide[b, :, lanes(first_query, QUERIES)] = context
            lse_ref[b, :, lanes(first_query, QUERIES)] = peak + jnp.log(total)
            low = context.astype(jnp.bfloat16)
            for t in range(QUERIES // BLOCK):
                piece, part = part_of(b, i * (QUERIES // BLOCK) + t, z, y, x, c)
                ctx_ref[piece, :, lanes(part * BLOCK, BLOCK)] = low[:, t * BLOCK : (t + 1) * BLOCK]


def attend(scalars, pieces, rev_line):
    _, head_size, tokens = pieces[0].shape
    length = tokens * 2
    smem, vmem = pl.BlockSpec(memory_space=pltpu.SMEM), pl.BlockSpec(memory_space=pltpu.VMEM)
    return pl.pallas_call(
        attend_kernel,
        name="attend",
        out_shape=[
            jax.ShapeDtypeStruct((4, head_size, tokens), jnp.bfloat16),
            jax.ShapeDtypeStruct((2, head_size, length), jnp.float32),
            jax.ShapeDtypeStruct((2, 1, length), jnp.float32),
            jax.ShapeDtypeStruct((2, 3, head_size, length), jnp.bfloat16),
        ],
        in_specs=[smem] + [vmem] * 5,
        out_specs=[vmem] * 4,
        scratch_shapes=[
            pltpu.VMEM((2, length, head_size), jnp.bfloat16),
            pltpu.VMEM((BLOCK, rev_line.shape[1]), jnp.float32),
        ],
        compiler_params=pltpu.CompilerParams(vmem_limit_bytes=48 << 20),
    )(scalars, *pieces, rev_line)


def attend_back_kernel(
    sc, p0, p1, p2, p3, rev_ref, ctx_wide, lse_ref, qkv,
    out_ref, line_ref,
    queries, keys, values, grads, grads_t, delta, query_sum, key_sum, value_sum, table, table_sum,
):
    z, y, x, c = sc[2], sc[3], sc[4], sc[5]
    length = qkv.shape[-1]
    for piece, ref in enumerate((p0, p1, p2, p3)):
        for part in range(8):
            b, block = place_of(piece, part, z, y, x, c)
            data = ref[:, part * BLOCK : (part + 1) * BLOCK]
            grads_t[b, :, lanes(block * BLOCK, BLOCK)] = data
            grads[b, lanes(block * BLOCK, BLOCK), :] = data.T
    for b in range(2):
        for first in range(0, length, BLOCK):
            here = slice(first, first + BLOCK)
            queries[b, here, :] = qkv[b, 0, :, here].T
            keys[b, here, :] = qkv[b, 1, :, here].T
            values[b, here, :] = qkv[b, 2, :, here].T
        delta[b] = jnp.sum(
            ctx_wide[b] * grads_t[b].astype(jnp.float32), axis=0, keepdims=True
        )
    skew_table(rev_ref, table)
    table_sum[...] = jnp.zeros_like(table_sum)
    query_sum[...] = jnp.zeros_like(query_sum)
    out_ref[...] = jnp.zeros_like(out_ref)
    for b in range(2):
        valid = sc[b]
        full = valid // KEYS
        count = (valid + KEYS - 1) // KEYS

        def key_step(j, masked):
            first_key = j * KEYS
            key, value = keys[b, lanes(first_key, KEYS), :], values[b, lanes(first_key, KEYS), :]
            key_t = qkv[b, 1, :, lanes(first_key, KEYS)]
            key_sum[...] = jnp.zeros_like(key_sum)
            value_sum[...] = jnp.zeros_like(value_sum)

            @pl.loop(0, count)
            def _(i):
                first_query = i * QUERIES
                here = lanes(first_query, QUERIES)
                score = jnp.dot(key, qkv[b, 0, :, here], preferred_element_type=jnp.float32)
                score = score + jnp.concatenate(
                    [
                        table[:, lanes(first_query - first_key + OFFSET - t, QUERIES)]
                        for t in range(0, KEYS, BLOCK)
                    ],
                    axis=0,
                )
                if masked:
                    position = first_key + lax.broadcasted_iota(jnp.int32, (KEYS, QUERIES), 0)
                    score = jnp.where(position < valid, score, masked_score)
                prob = jnp.exp(score - lse_ref[b, :, here])
                prob_grad = jnp.dot(value, grads_t[b, :, here], preferred_element_type=jnp.float32)
                score_grad = (prob * (prob_grad - delta[b, :, here])).astype(jnp.bfloat16)
                value_sum[...] += jnp.dot(
                    prob.astype(jnp.bfloat16), grads[b, here, :], preferred_element_type=jnp.float32
                )
                key_sum[...] += jnp.dot(
                    score_grad, queries[b, here, :], preferred_element_type=jnp.float32
                )
                query_sum[b, :, here] += jnp.dot(
                    key_t, score_grad, preferred_element_type=jnp.float32
                )
                for t in range(0, KEYS, BLOCK):
                    table_sum[:, lanes(first_query - first_key + OFFSET - t, QUERIES)] += score_grad[
                        t : t + BLOCK
                    ].astype(jnp.float32)

            for t in range(KEYS // BLOCK):
                piece, part = part_of(b, j * (KEYS // BLOCK) + t, z, y, x, c)
                rows = slice(t * BLOCK, (t + 1) * BLOCK)
                at = lanes(part * BLOCK, BLOCK)
                out_ref[piece, 1, :, at] = key_sum[rows, :].T.astype(jnp.bfloat16)
                out_ref[piece, 2, :, at] = value_sum[rows, :].T.astype(jnp.bfloat16)

        pl.loop(0, full)(lambda j: key_step(j, False))
        pl.when(valid > full * KEYS)(lambda: key_step(full, True))
        for block in range(length // BLOCK):
            piece, part = part_of(b, block, z, y, x, c)
            out_ref[piece, 0, :, lanes(part * BLOCK, BLOCK)] = query_sum[
                b, :, block * BLOCK : (block + 1) * BLOCK
            ].astype(jnp.bfloat16)
    width = table_sum.shape[1]
    line = jnp.zeros((8, width), jnp.float32)
    for first in range(0, BLOCK, 8):
        line = line + pltpu.roll(table_sum[first : first + 8, :], BLOCK - 8 - first, axis=1)
    ahead = 7 - lax.broadcasted_iota(jnp.int32, (8, width), 0)
    for bit in (1, 2, 4):
        line = jnp.where((ahead & bit) != 0, pltpu.roll(line, bit, axis=1), line)
    line_ref[...] = jnp.sum(line, axis=0, keepdims=True)


def attend_back(scalars, pieces, rev_line, ctx_wide, lse, qkv):
    head_size, tokens = pieces[0].shape
    length = tokens * 2
    smem, vmem = pl.BlockSpec(memory_space=pltpu.SMEM), pl.BlockSpec(memory_space=pltpu.VMEM)
    low = pltpu.VMEM((2, length, head_size), jnp.bfloat16)
    return pl.pallas_call(
        attend_back_kernel,
        name="attend_back",
        out_shape=[
            jax.ShapeDtypeStruct((4, 3, head_size, tokens), jnp.bfloat16),
            jax.ShapeDtypeStruct(rev_line.shape, jnp.float32),
        ],
        in_specs=[smem] + [vmem] * 8,
        out_specs=[vmem] * 2,
        scratch_shapes=[
            low, low, low, low,
            pltpu.VMEM((2, head_size, length), jnp.bfloat16),
            pltpu.VMEM((2, 1, length), jnp.float32),
            pltpu.VMEM((2, head_size, length), jnp.float32),
            pltpu.VMEM((KEYS, head_size), jnp.float32),
            pltpu.VMEM((KEYS, head_size), jnp.float32),
            pltpu.VMEM((BLOCK, rev_line.shape[1]), jnp.float32),
            pltpu.VMEM((BLOCK, rev_line.shape[1]), jnp.float32),
        ],
        compiler_params=pltpu.CompilerParams(vmem_limit_bytes=48 << 20),
    )(scalars, *pieces, rev_line, ctx_wide, lse, qkv)


def fast_shards(
    tokens_in,
    cotangent,
    gain_attn,
    query_weight,
    key_weight,
    value_weight,
    output_weight,
    bias_table,
    gain_ffn,
    gate_weight,
    up_weight,
    down_weight,
    lengths,
    buckets,
):
    seq_index, fsdp_index = lax.axis_index("seq"), lax.axis_index("fsdp")
    z, y, x, c = seq_index // 2, seq_index % 2, fsdp_index // 2, fsdp_index % 2
    z_low, z_high = z % 2, z // 2
    batch_count, slot_count, part_width = tokens_in.shape
    width = part_width * 4
    row_count = query_weight.shape[0]
    heads = query_weight.shape[1] // DH
    group_heads = heads // 2
    group_width = group_heads * DH
    hidden_width = gate_weight.shape[1] // 2
    scalars = jnp.concatenate(
        [lengths, jnp.stack([z, y, x, c]).astype(jnp.int32), jnp.zeros((2,), jnp.int32)]
    )
    mask = 4 * x + 2 * z_low + y

    def halves(weights):
        slots = []
        for k in range(2):
            half = k ^ z_low
            slots.append(
                jnp.concatenate(
                    [
                        lax.dynamic_slice_in_dim(w, half * (w.shape[1] // 2), w.shape[1] // 2, 1)
                        for w in weights
                    ],
                    axis=1,
                )
            )
        return slots

    small = jnp.concatenate([gain_attn, gain_ffn, bias_table.reshape(-1)])[None]
    for d in range(3):
        small = jnp.concatenate(
            [small, move(small, (across(0, 1), along_z(1), along_z(2))[d])], axis=0
        )
    small = jnp.stack(in_place([small[i] for i in range(8)], seq_index))
    gain_one = small[:, :row_count].reshape(-1)
    gain_two = small[:, row_count : 2 * row_count].reshape(-1)
    tables = small[:, 2 * row_count :][None]
    for d in range(2):
        tables = jnp.concatenate([tables, move(tables, across_fsdp(1 << d))], axis=0)
    tables = jnp.stack(in_place([tables[i] for i in range(4)], fsdp_index))
    tables = tables.reshape(4, 8, -1, heads).transpose(1, 2, 0, 3).reshape(-1, 4 * heads)
    own_head = (2 * c + z_high) * heads + z_low * group_heads + 2 * x + y
    table_column = lax.dynamic_slice_in_dim(tables, own_head, 1, 1)[:, 0].astype(jnp.float32)
    line_length = buckets.shape[0]
    rev_buckets = jnp.concatenate([buckets[::-1], jnp.full((1,), -1, jnp.int32)])
    bucket_hot = rev_buckets[:, None] == jnp.arange(table_column.shape[0], dtype=jnp.int32)[None, :]
    rev_line = jnp.sum(jnp.where(bucket_hot, table_column[None, :], 0.0), axis=1)[None, :]

    def own_rows(block):
        parts = block.reshape(4, slot_count // 2, part_width)
        got = [lax.dynamic_index_in_dim(parts, fsdp_index, 0, False)]
        for d in (1, 2, 3):
            piece = lax.dynamic_index_in_dim(parts, fsdp_index ^ d, 0, False)
            got.append(move(piece, across_fsdp(d)))
        return jnp.concatenate(in_place(got, fsdp_index), axis=1)

    def home_rows(rows):
        got = []
        for d in range(4):
            piece = lax.dynamic_slice_in_dim(rows, (fsdp_index ^ d) * part_width, part_width, 1)
            got.append(piece if d == 0 else move(piece, across_fsdp(d)))
        return jnp.stack(in_place(got, fsdp_index)).reshape(batch_count, slot_count, part_width)

    first_slot = seq_index * slot_count + c * (slot_count // 2)
    own_slots = first_slot + jnp.arange(slot_count // 2, dtype=jnp.int32)
    own_valid = own_slots < lax.dynamic_index_in_dim(lengths, x, 0, False)
    token_rows = own_rows(tokens_in).astype(jnp.float32)
    (qkv_weight,) = gather_weights(
        halves([query_weight, key_weight, value_weight]), [3 * group_width]
    )
    unit_one, scale_one, normed_own = normalize(token_rows, gain_one)
    normed_one = share_rows(normed_own)
    qkv = lax.dot_general(
        qkv_weight, normed_one, (((0,), (1,)), ((), ())), preferred_element_type=jnp.float32
    ).astype(jnp.bfloat16)
    tokens = qkv.shape[1]
    qkv = qkv.reshape(3, group_heads, DH, tokens)
    own = 2 * x + y

    def to_heads_owner(parts, axis):
        got = []
        for d in range(4):
            piece = lax.dynamic_index_in_dim(parts, own ^ d, axis, False)
            got.append(piece if d == 0 else move(piece, across(d // 2, d % 2)))
        return got

    pieces = to_heads_owner(qkv, 1)
    context_pieces, context_wide, lse, qkv_all = attend(scalars, pieces, rev_line)

    output_full, gate_up, down_full = gather_weights(
        halves([output_weight, gate_weight, up_weight, down_weight]),
        [group_width, 2 * hidden_width, hidden_width],
    )
    grad_own = jnp.where(own_valid[:, None], own_rows(cotangent), jnp.zeros((), jnp.bfloat16))
    grad_rows = share_rows(grad_own)

    def from_heads_owner(parts):
        got = [parts[0]] + [move(parts[d], across(d // 2, d % 2)) for d in (1, 2, 3)]
        return in_place(got, own)

    context = jnp.concatenate(from_heads_owner(context_pieces), axis=0)
    half_rows = tokens // 2

    def product_rows(left, right, dims):
        axis = 1 - dims[0]
        first, second = (
            lax.slice_in_dim(left, 0, half_rows, axis=axis),
            lax.slice_in_dim(left, half_rows, tokens, axis=axis),
        )
        run = lambda part: lax.dot_general(
            part, right, (((dims[0],), (dims[1],)), ((), ())), preferred_element_type=jnp.float32
        )
        return run(first), run(second).astype(jnp.bfloat16)

    residual = token_rows + sum_rows(*product_rows(context, output_full, (0, 1)))
    unit_two, scale_two, normed_two_own = normalize(residual, gain_two)
    normed_two = share_rows(normed_two_own)
    gate_up_pre = plain_product(normed_two, gate_up)
    gate_pre, up_pre = gate_up_pre[:, :hidden_width], gate_up_pre[:, hidden_width:]
    activated, gelu_back = jax.vjp(jax.nn.gelu, gate_pre)
    hidden = (activated * up_pre).astype(jnp.bfloat16)
    grad_hidden = plain_product(grad_rows, down_full)
    grad_pre = jnp.concatenate(
        [
            gelu_back(grad_hidden * up_pre)[0].astype(jnp.bfloat16),
            (grad_hidden * activated).astype(jnp.bfloat16),
        ],
        axis=1,
    )
    normed_two_grad = sum_rows(*product_rows(grad_pre, gate_up, (1, 1)))
    residual_grad = grad_own.astype(jnp.float32) + norm_back(
        normed_two_grad, unit_two, scale_two, gain_two
    )
    residual_low = share_rows(residual_grad.astype(jnp.bfloat16))
    context_grad = lax.dot_general(
        output_full, residual_low, (((0,), (1,)), ((), ())), preferred_element_type=jnp.float32
    ).astype(jnp.bfloat16)
    grad_pieces = to_heads_owner(context_grad.reshape(group_heads, DH, tokens), 0)
    qkv_grad_pieces, line_grad = attend_back(
        scalars, grad_pieces, rev_line, context_wide, lse, qkv_all
    )

    grad_gate_up = left_transposed(normed_two, grad_pre).astype(jnp.bfloat16)
    grad_down = left_transposed(grad_rows, hidden).astype(jnp.bfloat16)
    grad_output = lax.dot_general(
        residual_low, context, (((0,), (1,)), ((), ())), preferred_element_type=jnp.float32
    ).astype(jnp.bfloat16)
    ffn_share = sum_rows(*product_rows(hidden, down_full, (1, 1)))
    layer_out = home_rows((residual + ffn_share).astype(jnp.bfloat16))

    def own_columns(slots, first, size):
        cut = [s[:, first : first + size] for s in slots]
        return jnp.concatenate(
            [jnp.where(z_low == 0, cut[0], cut[1]), jnp.where(z_low == 0, cut[1], cut[0])], axis=1
        )

    ffn_sums = scatter_grads([grad_output, grad_gate_up, grad_down], mask, row_count)
    output_sum = own_columns(ffn_sums, 0, group_width)
    gate_sum = own_columns(ffn_sums, group_width, hidden_width)
    up_sum = own_columns(ffn_sums, group_width + hidden_width, hidden_width)
    down_sum = own_columns(ffn_sums, group_width + 2 * hidden_width, hidden_width)

    qkv_grad = jnp.stack(from_heads_owner(qkv_grad_pieces), axis=1).reshape(3 * group_width, tokens)
    grad_qkv = lax.dot_general(
        normed_one, qkv_grad, (((0,), (1,)), ((), ())), preferred_element_type=jnp.float32
    ).astype(jnp.bfloat16)
    normed_one_grad = sum_rows(*product_rows(qkv_grad, qkv_weight, (0, 1)))
    qkv_sums = scatter_grads([grad_qkv], mask, row_count)
    query_sum = own_columns(qkv_sums, 0, group_width)
    key_sum = own_columns(qkv_sums, group_width, group_width)
    value_sum = own_columns(qkv_sums, 2 * group_width, group_width)
    token_grad = residual_grad + norm_back(normed_one_grad, unit_one, scale_one, gain_one)
    token_share = home_rows(token_grad)

    table_grad = jnp.sum(jnp.where(bucket_hot, line_grad[0][:, None], 0.0), axis=0)
    head_hot = (jnp.arange(4 * heads) == own_head).astype(jnp.float32)
    packed = jnp.concatenate(
        [
            jnp.sum(normed_one_grad * unit_one, axis=0).reshape(8, row_count),
            jnp.sum(normed_two_grad * unit_two, axis=0).reshape(8, row_count),
            (table_grad[:, None] * head_hot[None, :]).reshape(8, -1),
        ],
        axis=1,
    )
    for index, size, way in ((z_high, 4, along_z(2)), (z_low, 2, along_z(1)), (y, 1, across(0, 1))):
        kept = lax.dynamic_slice_in_dim(packed, index * size, size, 0)
        sent = lax.dynamic_slice_in_dim(packed, (1 - index) * size, size, 0)
        packed = kept + move(sent, way)
    for d in range(2):
        packed = packed + move(packed, across_fsdp(1 << d))
    packed = packed[0]
    table_sum = lax.dynamic_slice_in_dim(
        packed[2 * row_count :].reshape(-1, 4 * heads), fsdp_index * heads, heads, 1
    )
    return (
        layer_out,
        token_share,
        packed[:row_count],
        query_sum,
        key_sum,
        value_sum,
        output_sum,
        table_sum,
        packed[row_count : 2 * row_count],
        gate_sum,
        up_sum,
        down_sum,
    )


def solution(mesh):
    placed = (
        P(None, "seq", "fsdp"),
        P(None, "seq", "fsdp"),
        P("seq"),
        P("seq", "fsdp"),
        P("seq", "fsdp"),
        P("seq", "fsdp"),
        P("seq", "fsdp"),
        P("seq", "fsdp"),
        P("seq"),
        P("seq", "fsdp"),
        P("seq", "fsdp"),
        P("seq", "fsdp"),
        P(),
        P(),
    )
    return jax.shard_map(
        fast_shards if (mesh.shape["seq"], mesh.shape["fsdp"]) == (8, 4) else shards,
        mesh=mesh,
        in_specs=placed,
        out_specs=(
            P(None, "seq", "fsdp"),
            P(None, "seq", "fsdp"),
            P("seq"),
            P("seq", "fsdp"),
            P("seq", "fsdp"),
            P("seq", "fsdp"),
            P("seq", "fsdp"),
            P("seq", "fsdp"),
            P("seq"),
            P("seq", "fsdp"),
            P("seq", "fsdp"),
            P("seq", "fsdp"),
        ),
        check_vma=False,
    )
```

```python
from functools import partial

import jax
import jax.numpy as jnp
from jax import lax
from jax.experimental import pallas as pl
from jax.experimental.pallas import tpu as pltpu
from jax.sharding import PartitionSpec as P

DH = 64


epsilon = 1e-06
highest = lax.Precision.HIGHEST
masked_score = -1e30


def plain_product(left, right):
    return jnp.dot(left, right, preferred_element_type=jnp.float32)


def right_transposed(left, right):
    return lax.dot_general(
        left, right, (((1,), (1,)), ((), ())), preferred_element_type=jnp.float32
    )


def left_transposed(left, right):
    return lax.dot_general(
        left, right, (((0,), (0,)), ((), ())), preferred_element_type=jnp.float32
    )


def normalize(rows, gain):
    row_scale = lax.rsqrt(jnp.mean(rows * rows, axis=-1, keepdims=True) + epsilon)
    unit_rows = rows * row_scale
    return (unit_rows, row_scale, (unit_rows * gain.astype(jnp.float32)).astype(jnp.bfloat16))


def norm_back(grad_normed, unit_rows, row_scale, gain):
    weighted = grad_normed * gain.astype(jnp.float32)
    return row_scale * (
        weighted - unit_rows * jnp.mean(weighted * unit_rows, axis=-1, keepdims=True)
    )


def to_heads(rows, batch_count, head_size):
    slot_count = rows.shape[0] // batch_count
    number_of_heads = rows.shape[1] // head_size
    return rows.reshape(batch_count, slot_count, number_of_heads, head_size).transpose(2, 0, 1, 3)


def from_heads(blocks):
    number_of_heads, batch_count, slot_count, head_size = blocks.shape
    return blocks.transpose(1, 2, 0, 3).reshape(
        batch_count * slot_count, number_of_heads * head_size
    )


def bias_rows(bias_line, first_query, slot_count, length):
    span = slot_count + length - 1
    segment = lax.dynamic_slice_in_dim(bias_line, length - first_query - slot_count, span)
    flat = jnp.tile(segment, slot_count)
    skewed = flat[slot_count - 1 : slot_count - 1 + slot_count * (span - 1)].reshape(
        slot_count, span - 1
    )
    return skewed[:, :length]


def bias_rows_back(block_grad, first_query, slot_count, length, line_length):
    span = slot_count + length - 1
    widened = jnp.pad(block_grad, ((0, 0), (0, span - 1 - length)))
    flat = jnp.pad(widened.reshape(-1), (slot_count - 1, 1))
    segment_grad = jnp.sum(flat.reshape(slot_count, span), axis=0)
    return lax.dynamic_update_slice_in_dim(
        jnp.zeros((line_length,), jnp.float32), segment_grad, length - first_query - slot_count, 0
    )


def full_features(block):
    gathered = lax.all_gather(block, "fsdp", axis=2, tiled=True)
    return gathered.reshape(gathered.shape[0] * gathered.shape[1], gathered.shape[2])


def feature_total(partial_rows):
    return lax.psum(partial_rows, "fsdp")


def shards(
    tokens_in,
    cotangent,
    gain_attn,
    query_weight,
    key_weight,
    value_weight,
    output_weight,
    bias_table,
    gain_ffn,
    gate_weight,
    up_weight,
    down_weight,
    lengths,
    buckets,
):
    batch_count, slot_count, part_width = tokens_in.shape
    head_size = DH
    seq_index = lax.axis_index("seq")
    fsdp_index = lax.axis_index("fsdp")
    length = slot_count * lax.axis_size("seq")
    line_length = buckets.shape[0]
    first_query = seq_index * slot_count
    positions = jnp.arange(length, dtype=jnp.int32)
    query_positions = first_query + jnp.arange(slot_count, dtype=jnp.int32)
    key_valid = positions[None, :] < lengths[:, None]
    own_valid = query_positions[None, :] < lengths[:, None]
    gain_one, query_full, key_full, value_full, output_full, table_full = (
        lax.all_gather(gain_attn, "seq", axis=0, tiled=True),
        lax.all_gather(query_weight, "seq", axis=0, tiled=True),
        lax.all_gather(key_weight, "seq", axis=0, tiled=True),
        lax.all_gather(value_weight, "seq", axis=0, tiled=True),
        lax.all_gather(output_weight, "seq", axis=0, tiled=True),
        lax.all_gather(bias_table, "seq", axis=0, tiled=True),
    )
    token_rows = full_features(tokens_in).astype(jnp.float32)
    unit_one, scale_one, normed_one = normalize(token_rows, gain_one)
    query_heads = to_heads(
        plain_product(normed_one, query_full).astype(jnp.bfloat16), batch_count, head_size
    )
    key_heads = to_heads(
        plain_product(normed_one, key_full).astype(jnp.bfloat16), batch_count, head_size
    )
    value_heads = to_heads(
        plain_product(normed_one, value_full).astype(jnp.bfloat16), batch_count, head_size
    )
    number_of_heads = query_heads.shape[0]
    flat_shape = (number_of_heads, batch_count, slot_count * head_size)
    gathered_keys, gathered_values = (
        lax.all_gather(key_heads.reshape(flat_shape), "seq", axis=2, tiled=True),
        lax.all_gather(value_heads.reshape(flat_shape), "seq", axis=2, tiled=True),
    )
    all_keys = gathered_keys.reshape(number_of_heads, batch_count, length, head_size)
    all_values = gathered_values.reshape(number_of_heads, batch_count, length, head_size)
    bucket_hot = (
        buckets[:, None] == jnp.arange(table_full.shape[0], dtype=jnp.int32)[None, :]
    ).astype(jnp.float32)
    offset_bias = lax.dot_general(
        table_full.astype(jnp.float32), bucket_hot, (((0,), (1,)), ((), ())), precision=highest
    )

    def masked_scores(query_tile_rows, key_tile_rows, bias_block):
        raw = (
            jnp.einsum(
                "jht,jxt->jhx", query_tile_rows, key_tile_rows, preferred_element_type=jnp.float32
            )
            + bias_block[None]
        )
        return jnp.where(key_valid[:, None, :], raw, masked_score)

    def attend(inputs):
        query_tile_rows, key_tile_rows, value_tile_rows, bias_line = inputs
        scores = masked_scores(
            query_tile_rows, key_tile_rows, bias_rows(bias_line, first_query, slot_count, length)
        )
        row_peak = jnp.max(scores, axis=-1, keepdims=True)
        raised = jnp.exp(scores - row_peak)
        denominator = jnp.sum(raised, axis=-1, keepdims=True)
        weights_reduced_precision = (raised / denominator).astype(jnp.bfloat16)
        context = jnp.einsum(
            "wot,wtf->wof",
            weights_reduced_precision,
            value_tile_rows,
            preferred_element_type=jnp.float32,
        ).astype(jnp.bfloat16)
        return (context, (row_peak + jnp.log(denominator))[..., 0])

    context_heads, log_totals = lax.map(attend, (query_heads, all_keys, all_values, offset_bias))
    context_rows = from_heads(context_heads)
    residual = token_rows + feature_total(right_transposed(context_rows, output_full))
    gain_two, gate_full, up_full, down_full = (
        lax.all_gather(gain_ffn, "seq", axis=0, tiled=True),
        lax.all_gather(gate_weight, "seq", axis=0, tiled=True),
        lax.all_gather(up_weight, "seq", axis=0, tiled=True),
        lax.all_gather(down_weight, "seq", axis=0, tiled=True),
    )
    unit_two, scale_two, normed_two = normalize(residual, gain_two)
    gate_pre = plain_product(normed_two, gate_full)
    up_pre = plain_product(normed_two, up_full)
    activated, gelu_back = jax.vjp(jax.nn.gelu, gate_pre)
    hidden = (activated * up_pre).astype(jnp.bfloat16)
    ffn_share = lax.psum_scatter(
        right_transposed(hidden, down_full), "fsdp", scatter_dimension=1, tiled=True
    )
    residual_share = lax.dynamic_slice_in_dim(residual, fsdp_index * part_width, part_width, 1)
    layer_out = (
        (residual_share + ffn_share)
        .astype(jnp.bfloat16)
        .reshape(batch_count, slot_count, part_width)
    )
    masked_cot = jnp.where(own_valid[:, :, None], cotangent, jnp.zeros_like(cotangent))
    grad_rows = full_features(masked_cot)
    grad_down = left_transposed(grad_rows, hidden)
    grad_hidden = plain_product(grad_rows, down_full)
    grad_gate_pre = gelu_back(grad_hidden * up_pre)[0].astype(jnp.bfloat16)
    grad_up_pre = (grad_hidden * activated).astype(jnp.bfloat16)
    grad_gate = left_transposed(normed_two, grad_gate_pre)
    grad_up = left_transposed(normed_two, grad_up_pre)
    normed_two_grad = right_transposed(grad_gate_pre, gate_full) + right_transposed(
        grad_up_pre, up_full
    )
    second_gain_piece = jnp.sum(normed_two_grad * unit_two, axis=0)
    ffn_grads = (
        lax.psum_scatter(second_gain_piece, "seq", scatter_dimension=0, tiled=True),
        lax.psum_scatter(grad_gate, "seq", scatter_dimension=0, tiled=True),
        lax.psum_scatter(grad_up, "seq", scatter_dimension=0, tiled=True),
        lax.psum_scatter(grad_down, "seq", scatter_dimension=0, tiled=True),
    )
    residual_grad = grad_rows.astype(jnp.float32) + norm_back(
        feature_total(normed_two_grad), unit_two, scale_two, gain_two
    )
    residual_low = residual_grad.astype(jnp.bfloat16)
    grad_output = left_transposed(residual_low, context_rows)
    context_grad = to_heads(
        plain_product(residual_low, output_full).astype(jnp.bfloat16), batch_count, head_size
    )

    def query_side(inputs, with_keys):
        query_tile_rows, key_tile_rows, value_tile_rows, bias_line, log_total, context_tile_rows = (
            inputs
        )
        scores = masked_scores(
            query_tile_rows, key_tile_rows, bias_rows(bias_line, first_query, slot_count, length)
        )
        probs = jnp.exp(scores - log_total[..., None])
        prob_grad = jnp.einsum(
            "jht,jxt->jhx", context_tile_rows, value_tile_rows, preferred_element_type=jnp.float32
        )
        delta = jnp.sum(probs * prob_grad, axis=-1)
        score_gradient = (probs * (prob_grad - delta[..., None])).astype(jnp.bfloat16)
        query_grad = jnp.einsum(
            "wot,wtf->wof", score_gradient, key_tile_rows, preferred_element_type=jnp.float32
        )
        bias_grad = bias_rows_back(
            jnp.sum(score_gradient.astype(jnp.float32), axis=0),
            first_query,
            slot_count,
            length,
            line_length,
        )
        key_term = jnp.einsum(
            "xic,xil->xcl", score_gradient, query_tile_rows, preferred_element_type=jnp.float32
        )
        value_term = jnp.einsum(
            "xic,xil->xcl",
            probs.astype(jnp.bfloat16),
            context_tile_rows,
            preferred_element_type=jnp.float32,
        )
        return (query_grad, bias_grad, delta, key_term, value_term)

    side_inputs = (query_heads, all_keys, all_values, offset_bias, log_totals, context_grad)
    query_grad, bias_grad, delta, key_terms, value_terms = lax.map(
        partial(query_side, with_keys=True), side_inputs
    )
    wide_shape = (number_of_heads, batch_count, length * head_size)
    key_sums, value_sums = (
        lax.psum_scatter(key_terms.reshape(wide_shape), "seq", scatter_dimension=2, tiled=True),
        lax.psum_scatter(value_terms.reshape(wide_shape), "seq", scatter_dimension=2, tiled=True),
    )
    own_shape = (number_of_heads, batch_count, slot_count, head_size)
    query_low = from_heads(query_grad.astype(jnp.bfloat16))
    key_low = from_heads(key_sums.reshape(own_shape).astype(jnp.bfloat16))
    value_low = from_heads(value_sums.reshape(own_shape).astype(jnp.bfloat16))
    grad_query = left_transposed(normed_one, query_low)
    grad_key = left_transposed(normed_one, key_low)
    grad_value = left_transposed(normed_one, value_low)
    grad_table = lax.dot_general(bucket_hot, bias_grad, (((0,), (1,)), ((), ())), precision=highest)
    normed_one_grad = (
        right_transposed(query_low, query_full)
        + right_transposed(key_low, key_full)
        + right_transposed(value_low, value_full)
    )
    gain_one_part = jnp.sum(normed_one_grad * unit_one, axis=0)
    attn_grads = (
        lax.psum_scatter(gain_one_part, "seq", scatter_dimension=0, tiled=True),
        lax.psum_scatter(grad_query, "seq", scatter_dimension=0, tiled=True),
        lax.psum_scatter(grad_key, "seq", scatter_dimension=0, tiled=True),
        lax.psum_scatter(grad_value, "seq", scatter_dimension=0, tiled=True),
        lax.psum_scatter(grad_output, "seq", scatter_dimension=0, tiled=True),
        lax.psum_scatter(grad_table, "seq", scatter_dimension=0, tiled=True),
    )
    token_grad = residual_grad + norm_back(
        feature_total(normed_one_grad), unit_one, scale_one, gain_one
    )
    token_share = lax.dynamic_slice_in_dim(
        token_grad, fsdp_index * part_width, part_width, 1
    ).reshape(batch_count, slot_count, part_width)
    gain_one_sum, gain_two_sum = lax.psum((attn_grads[0], ffn_grads[0]), "fsdp")
    return (
        layer_out,
        token_share,
        gain_one_sum,
        attn_grads[1],
        attn_grads[2],
        attn_grads[3],
        attn_grads[4],
        attn_grads[5],
        gain_two_sum,
        ffn_grads[1],
        ffn_grads[2],
        ffn_grads[3],
    )


BLOCK = 128
BOTH = ("seq", "fsdp")


def move(value, target):
    pairs = []
    for z in range(4):
        for y in range(2):
            for x in range(2):
                for c in range(2):
                    zt, yt, xt, ct = target(z, y, x, c)
                    pairs.append(((2 * z + y) * 4 + 2 * x + c, (2 * zt + yt) * 4 + 2 * xt + ct))
    return lax.ppermute(value, BOTH, pairs)


def spread_slot(k):
    return lambda z, y, x, c: (2 * c + (k ^ (z & 1)), y, x, z >> 1)


def spread_plane(dy, dx):
    return lambda z, y, x, c: (z, y ^ dy, c ^ dx, x)


def join_plane(dy, dx):
    return lambda z, y, x, c: (z, y ^ dy, c, x ^ dx)


def along_z(d):
    return lambda z, y, x, c: (z ^ d, y, x, c)


def other_core(z, y, x, c):
    return (z, y, x, c ^ 1)


def across(dx, dy):
    return lambda z, y, x, c: (z, y ^ dy, x ^ dx, c)


def across_fsdp(d):
    return lambda z, y, x, c: (z, y, x ^ (d >> 1), c ^ (d & 1))


def in_place(relative, me):
    current, bit = list(relative), 1
    while bit < len(current):
        swap = (me & bit) != 0
        current = [jnp.where(swap, current[i ^ bit], current[i]) for i in range(len(current))]
        bit *= 2
    return current


def sum_rows(mine, other):
    mine = mine + move(other, other_core).astype(jnp.float32)
    count = mine.shape[0] // 4
    total = mine[:count]
    for d in (1, 2, 3):
        part = mine[d * count : (d + 1) * count].astype(jnp.bfloat16)
        total = total + move(part, along_z(d)).astype(jnp.float32)
    return total


KEYS = 256
QUERIES = 256
OFFSET = 1920


def skew_table(rev_ref, table):
    width = rev_ref.shape[1]
    line = jnp.broadcast_to(rev_ref[...], (8, width))
    for first in range(0, BLOCK, 8):
        table[first : first + 8, :] = pltpu.roll(
            line, (width - (BLOCK - 1) + first) % width, axis=1, stride=1, stride_axis=0
        )


def place_of(piece, part, z, y, x, c):
    c_rel, d = part // 4, part % 4
    b = jnp.bitwise_xor(x, piece // 2)
    block = (
        4 * jnp.bitwise_xor(z, d)
        + 2 * jnp.bitwise_xor(y, piece % 2)
        + jnp.bitwise_xor(c, c_rel)
    )
    return b, block


def part_of(b, block, z, y, x, c):
    piece = 2 * jnp.bitwise_xor(b, x) + jnp.bitwise_xor((block // 2) % 2, y)
    part = 4 * jnp.bitwise_xor(block % 2, c) + jnp.bitwise_xor(block // 4, z)
    return piece, part


def lanes(first, count):
    return pl.ds(pl.multiple_of(first, BLOCK), count)


def attend_kernel(sc, pieces, rev_ref, ctx_ref, ctx_wide, lse_ref, qkv, keys, table):
    z, y, x, c = sc[2], sc[3], sc[4], sc[5]
    for piece in range(4):
        for part in range(8):
            b, block = place_of(piece, part, z, y, x, c)
            data = pieces[piece, :, :, part * BLOCK : (part + 1) * BLOCK]
            qkv[b, :, :, lanes(block * BLOCK, BLOCK)] = data
            keys[b, lanes(block * BLOCK, BLOCK), :] = data[1].T
    skew_table(rev_ref, table)
    length = qkv.shape[-1]
    for b in range(2):
        valid = sc[b]
        full = valid // KEYS

        @pl.loop(0, length // QUERIES)
        def _(i):
            first_query = i * QUERIES
            query = qkv[b, 0, :, lanes(first_query, QUERIES)]

            def tile(j, carry, masked):
                peak, total, acc = carry
                first_key = j * KEYS
                score = jnp.dot(
                    keys[b, lanes(first_key, KEYS), :], query, preferred_element_type=jnp.float32
                )
                score = score + jnp.concatenate(
                    [
                        table[:, lanes(first_query - first_key + OFFSET - t, QUERIES)]
                        for t in range(0, KEYS, BLOCK)
                    ],
                    axis=0,
                )
                if masked:
                    position = first_key + lax.broadcasted_iota(jnp.int32, (KEYS, QUERIES), 0)
                    score = jnp.where(position < valid, score, masked_score)
                now = jnp.maximum(peak, jnp.max(score, axis=0, keepdims=True))
                scale = jnp.exp(peak - now)
                prob = jnp.exp(score - now)
                total = total * scale + jnp.sum(prob, axis=0, keepdims=True)
                acc = acc * scale + jnp.dot(
                    qkv[b, 2, :, lanes(first_key, KEYS)],
                    prob.astype(jnp.bfloat16),
                    preferred_element_type=jnp.float32,
                )
                return now, total, acc

            carry = (
                jnp.full((1, QUERIES), masked_score, jnp.float32),
                jnp.zeros((1, QUERIES), jnp.float32),
                jnp.zeros((DH, QUERIES), jnp.float32),
            )
            carry = lax.fori_loop(0, full, lambda j, s: tile(j, s, False), carry)
            peak, total, acc = lax.cond(
                valid > full * KEYS, lambda s: tile(full, s, True), lambda s: s, carry
            )
            context = acc / total
            ctx_wide[b, :, lanes(first_query, QUERIES)] = context
            lse_ref[b, :, lanes(first_query, QUERIES)] = peak + jnp.log(total)
            low = context.astype(jnp.bfloat16)
            for t in range(QUERIES // BLOCK):
                piece, part = part_of(b, i * (QUERIES // BLOCK) + t, z, y, x, c)
                ctx_ref[piece, :, lanes(part * BLOCK, BLOCK)] = low[:, t * BLOCK : (t + 1) * BLOCK]


def attend(scalars, pieces, rev_line):
    _, _, head_size, tokens = pieces.shape
    length = tokens * 2
    smem, vmem = pl.BlockSpec(memory_space=pltpu.SMEM), pl.BlockSpec(memory_space=pltpu.VMEM)
    return pl.pallas_call(
        attend_kernel,
        name="attend",
        out_shape=[
            jax.ShapeDtypeStruct((4, head_size, tokens), jnp.bfloat16),
            jax.ShapeDtypeStruct((2, head_size, length), jnp.float32),
            jax.ShapeDtypeStruct((2, 1, length), jnp.float32),
            jax.ShapeDtypeStruct((2, 3, head_size, length), jnp.bfloat16),
        ],
        in_specs=[smem] + [vmem] * 2,
        out_specs=[vmem] * 4,
        scratch_shapes=[
            pltpu.VMEM((2, length, head_size), jnp.bfloat16),
            pltpu.VMEM((BLOCK, rev_line.shape[1]), jnp.float32),
        ],
        cost_estimate=pl.CostEstimate(
            flops=46_000_000_000, bytes_accessed=4 << 20, transcendentals=0
        ),
        compiler_params=pltpu.CompilerParams(vmem_limit_bytes=48 << 20),
    )(scalars, pieces, rev_line)


def attend_back_kernel(
    sc, pieces, rev_ref, ctx_wide, lse_ref, qkv,
    out_ref, line_ref,
    queries, keys, values, grads, grads_t, delta, query_sum, key_sum, value_sum, table, table_sum,
):
    z, y, x, c = sc[2], sc[3], sc[4], sc[5]
    length = qkv.shape[-1]
    for piece in range(4):
        for part in range(8):
            b, block = place_of(piece, part, z, y, x, c)
            data = pieces[piece, :, part * BLOCK : (part + 1) * BLOCK]
            grads_t[b, :, lanes(block * BLOCK, BLOCK)] = data
            grads[b, lanes(block * BLOCK, BLOCK), :] = data.T
    for b in range(2):
        for first in range(0, length, BLOCK):
            here = slice(first, first + BLOCK)
            queries[b, here, :] = qkv[b, 0, :, here].T
            keys[b, here, :] = qkv[b, 1, :, here].T
            values[b, here, :] = qkv[b, 2, :, here].T
        delta[b] = jnp.sum(
            ctx_wide[b] * grads_t[b].astype(jnp.float32), axis=0, keepdims=True
        )
    skew_table(rev_ref, table)
    table_sum[...] = jnp.zeros_like(table_sum)
    query_sum[...] = jnp.zeros_like(query_sum)
    out_ref[...] = jnp.zeros_like(out_ref)
    for b in range(2):
        valid = sc[b]
        full = valid // KEYS
        count = (valid + KEYS - 1) // KEYS

        def key_step(j, masked):
            first_key = j * KEYS
            key, value = keys[b, lanes(first_key, KEYS), :], values[b, lanes(first_key, KEYS), :]
            key_t = qkv[b, 1, :, lanes(first_key, KEYS)]
            key_sum[...] = jnp.zeros_like(key_sum)
            value_sum[...] = jnp.zeros_like(value_sum)

            @pl.loop(0, count)
            def _(i):
                first_query = i * QUERIES
                here = lanes(first_query, QUERIES)
                score = jnp.dot(key, qkv[b, 0, :, here], preferred_element_type=jnp.float32)
                score = score + jnp.concatenate(
                    [
                        table[:, lanes(first_query - first_key + OFFSET - t, QUERIES)]
                        for t in range(0, KEYS, BLOCK)
                    ],
                    axis=0,
                )
                if masked:
                    position = first_key + lax.broadcasted_iota(jnp.int32, (KEYS, QUERIES), 0)
                    score = jnp.where(position < valid, score, masked_score)
                prob = jnp.exp(score - lse_ref[b, :, here])
                prob_grad = jnp.dot(value, grads_t[b, :, here], preferred_element_type=jnp.float32)
                score_grad = (prob * (prob_grad - delta[b, :, here])).astype(jnp.bfloat16)
                value_sum[...] += jnp.dot(
                    prob.astype(jnp.bfloat16), grads[b, here, :], preferred_element_type=jnp.float32
                )
                key_sum[...] += jnp.dot(
                    score_grad, queries[b, here, :], preferred_element_type=jnp.float32
                )
                query_sum[b, :, here] += jnp.dot(
                    key_t, score_grad, preferred_element_type=jnp.float32
                )
                for t in range(0, KEYS, BLOCK):
                    table_sum[:, lanes(first_query - first_key + OFFSET - t, QUERIES)] += score_grad[
                        t : t + BLOCK
                    ].astype(jnp.float32)

            for t in range(KEYS // BLOCK):
                piece, part = part_of(b, j * (KEYS // BLOCK) + t, z, y, x, c)
                rows = slice(t * BLOCK, (t + 1) * BLOCK)
                at = lanes(part * BLOCK, BLOCK)
                out_ref[piece, 1, :, at] = key_sum[rows, :].T.astype(jnp.bfloat16)
                out_ref[piece, 2, :, at] = value_sum[rows, :].T.astype(jnp.bfloat16)

        pl.loop(0, full)(lambda j: key_step(j, False))
        pl.when(valid > full * KEYS)(lambda: key_step(full, True))
        for block in range(length // BLOCK):
            piece, part = part_of(b, block, z, y, x, c)
            out_ref[piece, 0, :, lanes(part * BLOCK, BLOCK)] = query_sum[
                b, :, block * BLOCK : (block + 1) * BLOCK
            ].astype(jnp.bfloat16)
    width = table_sum.shape[1]
    line = jnp.zeros((8, width), jnp.float32)
    for first in range(0, BLOCK, 8):
        line = line + pltpu.roll(table_sum[first : first + 8, :], BLOCK - 8 - first, axis=1)
    ahead = 7 - lax.broadcasted_iota(jnp.int32, (8, width), 0)
    for bit in (1, 2, 4):
        line = jnp.where((ahead & bit) != 0, pltpu.roll(line, bit, axis=1), line)
    line_ref[...] = jnp.sum(line, axis=0, keepdims=True)


def attend_back(scalars, pieces, rev_line, ctx_wide, lse, qkv):
    _, head_size, tokens = pieces.shape
    length = tokens * 2
    smem, vmem = pl.BlockSpec(memory_space=pltpu.SMEM), pl.BlockSpec(memory_space=pltpu.VMEM)
    low = pltpu.VMEM((2, length, head_size), jnp.bfloat16)
    return pl.pallas_call(
        attend_back_kernel,
        name="attend_back",
        out_shape=[
            jax.ShapeDtypeStruct((4, 3, head_size, tokens), jnp.bfloat16),
            jax.ShapeDtypeStruct(rev_line.shape, jnp.float32),
        ],
        in_specs=[smem] + [vmem] * 5,
        out_specs=[vmem] * 2,
        scratch_shapes=[
            low, low, low, low,
            pltpu.VMEM((2, head_size, length), jnp.bfloat16),
            pltpu.VMEM((2, 1, length), jnp.float32),
            pltpu.VMEM((2, head_size, length), jnp.float32),
            pltpu.VMEM((KEYS, head_size), jnp.float32),
            pltpu.VMEM((KEYS, head_size), jnp.float32),
            pltpu.VMEM((BLOCK, rev_line.shape[1]), jnp.float32),
            pltpu.VMEM((BLOCK, rev_line.shape[1]), jnp.float32),
        ],
        cost_estimate=pl.CostEstimate(
            flops=46_000_000_000, bytes_accessed=4 << 20, transcendentals=0
        ),
        compiler_params=pltpu.CompilerParams(vmem_limit_bytes=48 << 20),
    )(scalars, pieces, rev_line, ctx_wide, lse, qkv)


CHUNKS = 2
MESH_ID = pl.DeviceIdType.MESH
IN_VMEM = pl.BlockSpec(memory_space=pltpu.VMEM)
IN_PLACE = pl.BlockSpec(memory_space=pl.ANY)
COPIES = pltpu.SemaphoreType.DMA


def flip(a, b):
    return a + b - 2 * a * b


def flip_pair(a, b):
    return 2 * flip(a // 2, b // 2) + flip(a % 2, b % 2)


def position():
    s, f = lax.axis_index("seq"), lax.axis_index("fsdp")
    return s // 2, s % 2, f // 2, f % 2


def device(z, y, x, c):
    return (2 * z + y, 2 * x + c)


def ring_of(z):
    high, low = z // 2, z % 2
    following = 2 * low + 1 - high
    return following, (2 * (1 - low) + high, 2 * (1 - high) + 1 - low, following)


def greet(z, y, x, c):
    peers = []
    for d in range(1, 8):
        peers.append(device(z, flip(y, d // 4), flip(x, (d // 2) % 2), flip(c, d % 2)))
        if d > 1:
            peers.append(device(flip_pair(z, d // 2), y, x, flip(c, d % 2)))
    barrier = pltpu.get_barrier_semaphore()
    for peer in peers:
        pl.semaphore_signal(barrier, inc=1, device_id=peer, device_id_type=MESH_ID)
    pl.semaphore_wait(barrier, len(peers))


def remote(source, target, send, recv, to):
    return pltpu.make_async_remote_copy(
        src_ref=source,
        dst_ref=target,
        send_sem=send,
        recv_sem=recv,
        device_id=to,
        device_id_type=MESH_ID,
    )


class Links:
    def __init__(self, send, recv):
        self.send, self.recv, self.used, self.sent = send, recv, 0, []

    def go(self, source, target, to):
        i = self.used
        self.used += 1
        made = remote(source, target, self.send.at[i], self.recv.at[i], to)
        made.start()
        self.sent.append(made)
        return made

    def go_unless(self, own, source, target, to, send=None, recv=None):
        if send is None:
            send, recv = self.send.at[self.used], self.recv.at[self.used]
            self.used += 1
        made = remote(source, target, send, recv, to)
        if own is None:
            made.start()
            self.sent.append(made)
            return made
        local = pltpu.make_async_copy(source, target, recv)
        pl.when(own)(lambda: local.start())
        pl.when(jnp.logical_not(own))(lambda: made.start())
        self.sent.append((own, made))
        return made

    def finish(self):
        for made in self.sent:
            if isinstance(made, tuple):
                pl.when(jnp.logical_not(made[0]))(lambda made=made: made[1].wait_send())
            else:
                made.wait_send()


def share_start(links, rows_all, me):
    z, y, x, c = me
    following, _ = ring_of(z)
    rows = rows_all.shape[1] // CHUNKS
    ring = []
    for h in range(CHUNKS):
        here = pl.ds(h * rows, rows)
        target = rows_all.at[flip_pair(following, z), here]
        ring.append(links.go(rows_all.at[0, here], target, device(following, y, x, c)))
    core = [links.go(rows_all.at[0], rows_all.at[4], device(z, y, x, 1 - c))]
    return [ring], core


def share_step(links, rows_all, me, state, step):
    z, y, x, c = me
    following, back = ring_of(z)
    rows = rows_all.shape[1] // CHUNKS
    ring, core = state
    slot = flip_pair(z, back[step - 1])
    sent = []
    for h in range(CHUNKS):
        here = pl.ds(h * rows, rows)
        ring[-1][h].wait_recv()
        source = rows_all.at[slot, here]
        if step < 3:
            target = rows_all.at[flip_pair(following, back[step - 1]), here]
            sent.append(links.go(source, target, device(following, y, x, c)))
        core.append(links.go(source, rows_all.at[4 + slot, here], device(z, y, x, 1 - c)))
    ring.append(sent)


def share_end(state):
    for made in state[1]:
        made.wait_recv()


def sum_order(z):
    _, back = ring_of(z)
    return [flip_pair(z, b) for b in back] + [0]


def reduce_start(links, me, product, mine, core_out, core_in):
    z, y, x, c = me
    core = []
    for i, d in enumerate(sum_order(z)):
        core_out[i] = product(4 + d).astype(jnp.bfloat16)
        core.append(links.go(core_out.at[i], core_in.at[i], device(z, y, x, 1 - c)))
        mine[i] = product(d)
    return core, []


def reduce_step(links, me, state, i, mine, core_in, ring_out, ring_in):
    core, ring = state
    z, y, x, c = me
    following, _ = ring_of(z)
    rows = mine.shape[1] // CHUNKS
    core[i].wait_recv()
    sent, last = [], []
    for h in range(CHUNKS):
        here = pl.ds(h * rows, rows)
        value = mine[i, here, :] + core_in[i, here, :].astype(jnp.float32)
        if i:
            ring[-1][h].wait_recv()
            value = value + ring_in[i - 1, here, :].astype(jnp.float32)
        if i < 3:
            ring_out[i, here, :] = value.astype(jnp.bfloat16)
            target = ring_in.at[i, here]
            sent.append(links.go(ring_out.at[i, here], target, device(following, y, x, c)))
        else:
            last.append(value)
    ring.append(sent)
    return last


def column_go(links, me, k, source, target):
    z, y, x, c = me
    own = z // 2 == c if k == 0 else None
    to = device(2 * c + flip(k, z % 2), y, x, z // 2)
    return links.go_unless(own, source, target, to)


def spread_go(links, me, k, source, full, send, recv):
    z, y, x, c = me
    rows = source.shape[0]
    first = pl.multiple_of((4 * c + 2 * flip(k, z % 2) + y) * rows, rows)
    target = full.at[pl.ds(first, rows), :]
    for dy in range(2):
        for dx in range(2):
            own = None if dy + dx else c == x
            to = device(z, flip(y, dy), flip(x, dx), x)
            links.go_unless(own, source, target, to, send.at[k, dy, dx], recv.at[k, dy, c])


def spread_wait(full, recv):
    rows = full.shape[0] // 8
    for k in range(2):
        for dy in range(2):
            for r in range(2):
                here = full.at[pl.ds(0, rows), :]
                pltpu.make_async_copy(here, here, recv.at[k, dy, r]).wait()


def join_go(links, me, k, grads, into, send, recv):
    z, y, x, c = me
    rows = into.shape[3]
    for dy in range(2):
        for r in range(2):
            block = 4 * r + 2 * flip(k, z % 2) + flip(y, dy)
            source = grads.at[pl.ds(pl.multiple_of(block * rows, rows), rows), :]
            own = None if dy else jnp.logical_and(c == x, c == r)
            to = device(z, flip(y, dy), c, r)
            links.go_unless(
                own, source, into.at[k, dy, x], to, send.at[k, dy, r], recv.at[k, dy, x]
            )


def join_sum(k, into, recv):
    total = 0.0
    for dy in range(2):
        for other in range(2):
            here = into.at[k, dy, other]
            pltpu.make_async_copy(here, here, recv.at[k, dy, other]).wait()
            total = total + into[k, dy, other].astype(jnp.float32)
    return total.astype(jnp.bfloat16)


def rms(rows):
    return lax.rsqrt(jnp.mean(rows * rows, axis=-1, keepdims=True) + epsilon)


def entry_kernel(
    tok_ref, cot_ref, valid_ref, gain_ref, w0_ref, w1_ref,
    rows_ref, normed, grads, pieces, weight,
    tok_in, cot_in, held, qkv, send, recv, plane_send, plane_recv,
):
    me = z, y, x, c = position()
    greet(*me)
    links = Links(send, recv)
    f, part, half = 2 * x + c, tok_in.shape[2], tok_in.shape[1]

    def gather_rows(ref, into):
        got = []
        for d in (1, 2, 3):
            xd, cd = flip(x, d // 2), flip(c, d % 2)
            source = ref.at[xd, pl.ds(pl.multiple_of(cd * half, half), half)]
            got.append(links.go(source, into.at[f], device(z, y, xd, cd)))
        into[f] = ref[x, pl.ds(pl.multiple_of(c * half, half), half), :]
        return got

    tok_got = gather_rows(tok_ref, tok_in)
    way = [column_go(links, me, k, (w0_ref, w1_ref)[k], held.at[k]) for k in range(2)]
    cot_got = gather_rows(cot_ref, cot_in)
    for made in tok_got:
        made.wait_recv()
    wide = [tok_in[i].astype(jnp.float32) for i in range(4)]
    mean = sum(jnp.sum(w * w, axis=-1, keepdims=True) for w in wide) / (4 * part)
    scale = lax.rsqrt(mean + epsilon)
    for i in range(4):
        here = slice(i * part, (i + 1) * part)
        rows_ref[:, here] = tok_in[i]
        gain = gain_ref[:, here].astype(jnp.float32)
        normed[0, :, here] = (wide[i] * scale * gain).astype(jnp.bfloat16)
    first = share_start(links, normed, me)
    for made in cot_got:
        made.wait_recv()
    for i in range(4):
        grads[0, :, i * part : (i + 1) * part] = cot_in[i] * valid_ref[...]
    for k in range(2):
        way[k].wait_recv()
        spread_go(links, me, k, held.at[k], weight, plane_send, plane_recv)
    for step in (1, 2, 3):
        share_step(links, normed, me, first, step)
    second = share_start(links, grads, me)
    share_end(first)
    spread_wait(weight, plane_recv)
    count = 2 * normed.shape[1]
    group = qkv.shape[1]

    @pl.loop(0, 4)
    def _(i):
        left = normed[pl.ds(2 * i, 2)].reshape(count, 4 * part)
        out = jnp.dot(left, weight[...], preferred_element_type=jnp.float32)
        out = out.astype(jnp.bfloat16).T
        qkv[:, :, :, lanes(i * count, count)] = out.reshape(3, group, DH, count)

    own = 2 * x + y
    heads = []
    for d in (1, 2, 3):
        xd, yd = flip(x, d // 2), flip(y, d % 2)
        heads.append(
            links.go(qkv.at[:, 2 * xd + yd], pieces.at[d], device(z, yd, xd, c))
        )
    pieces[0] = qkv[:, own]
    for step in (1, 2, 3):
        share_step(links, grads, me, second, step)
    share_end(second)
    for made in heads:
        made.wait_recv()
    links.finish()


def low_array(*shape):
    return jax.ShapeDtypeStruct(shape, jnp.bfloat16)


def wide_array(*shape):
    return jax.ShapeDtypeStruct(shape, jnp.float32)


def low_space(*shape):
    return pltpu.VMEM(shape, jnp.bfloat16)


def entry(tokens_in, cotangent, valid, gain, slots):
    _, slot_count, part = tokens_in.shape
    rows, width = slot_count // 2, 4 * part
    depth, wide = slots[0].shape
    group = wide // (3 * DH)
    return pl.pallas_call(
        entry_kernel,
        name="entry",
        out_shape=[
            low_array(rows, width),
            low_array(8, rows, width),
            low_array(8, rows, width),
            low_array(4, 3, DH, 8 * rows),
            low_array(8 * depth, wide),
        ],
        in_specs=[IN_VMEM] * 6,
        out_specs=[IN_VMEM] * 5,
        scratch_shapes=[
            low_space(4, rows, part),
            low_space(4, rows, part),
            low_space(2, depth, wide),
            low_space(3, group, DH, 8 * rows),
            COPIES((48,)),
            COPIES((48,)),
            COPIES((2, 2, 2)),
            COPIES((2, 2, 2)),
        ],
        compiler_params=pltpu.CompilerParams(
            collective_id=1, has_side_effects=True, vmem_limit_bytes=48 << 20
        ),
    )(tokens_in, cotangent, valid, gain, *slots)


def middle_kernel(
    ctx_ref, rows_ref, gain_ref, o0, o1, g0, g1, d0, d1,
    normed, residual_ref, context, out_weight, gate_up, down,
    ctx_all, mine, core_out, core_in, ring_out, ring_in, send, recv, plane_send, plane_recv,
):
    me = z, y, x, c = position()
    greet(*me)
    links = Links(send, recv)
    own = 2 * x + y
    heads = []
    for d in (1, 2, 3):
        xd, yd = flip(x, d // 2), flip(y, d % 2)
        heads.append(links.go(ctx_ref.at[d], ctx_all.at[own], device(z, yd, xd, c)))
    for n, (slots, full) in enumerate(
        (((o0, o1), out_weight), ((g0, g1), gate_up), ((d0, d1), down))
    ):
        for k in range(2):
            spread_go(links, me, k, slots[k], full, plane_send.at[n], plane_recv.at[n])
    ctx_all[own] = ctx_ref[0]
    for made in heads:
        made.wait_recv()
    group, size, tokens = ctx_all.shape
    context[...] = ctx_all[...].reshape(group * size, tokens).T
    spread_wait(out_weight, plane_recv.at[0])
    rows = tokens // 8

    def product(block):
        return right_transposed(
            context[pl.ds(pl.multiple_of(block * rows, rows), rows), :], out_weight[...]
        )

    state = reduce_start(links, me, product, mine, core_out, core_in)
    for i in range(4):
        last = reduce_step(links, me, state, i, mine, core_in, ring_out, ring_in)
    residual = rows_ref[...].astype(jnp.float32) + jnp.concatenate(last, axis=0)
    residual_ref[...] = residual
    gain = gain_ref[...].astype(jnp.float32)
    normed[0] = (residual * rms(residual) * gain).astype(jnp.bfloat16)
    shared = share_start(links, normed, me)
    for step in (1, 2, 3):
        share_step(links, normed, me, shared, step)
    share_end(shared)
    spread_wait(gate_up, plane_recv.at[1])
    spread_wait(down, plane_recv.at[2])
    links.finish()


def reduce_space(rows, width):
    return [
        pltpu.VMEM((4, rows, width), jnp.float32),
        low_space(4, rows, width),
        low_space(4, rows, width),
        low_space(3, rows, width),
        low_space(3, rows, width),
    ]


def middle(ctx_pieces, token_rows, gain, slots):
    _, size, tokens = ctx_pieces.shape
    rows, width = token_rows.shape
    depth = slots[0].shape[0]
    return pl.pallas_call(
        middle_kernel,
        name="middle",
        out_shape=[
            low_array(8, rows, width),
            wide_array(rows, width),
            low_array(tokens, 4 * size),
            low_array(8 * depth, slots[0].shape[1]),
            low_array(8 * depth, slots[2].shape[1]),
            low_array(8 * depth, slots[4].shape[1]),
        ],
        in_specs=[IN_VMEM] * 3 + [IN_PLACE] * 6,
        out_specs=[IN_VMEM] * 4 + [IN_PLACE] * 2,
        scratch_shapes=[
            low_space(4, size, tokens),
            *reduce_space(rows, width),
            COPIES((48,)),
            COPIES((48,)),
            COPIES((3, 2, 2, 2)),
            COPIES((3, 2, 2, 2)),
        ],
        compiler_params=pltpu.CompilerParams(
            collective_id=2, has_side_effects=True, vmem_limit_bytes=48 << 20
        ),
    )(ctx_pieces, token_rows, gain, *slots)


def back_kernel(
    pre_ref, weight_ref, residual_ref, own_ref, gain_ref, out_weight, grad_gu, grad_d,
    low_ref, wide_ref, part_ref, pieces, sum_gu, sum_d,
    heads_out, in_gu, in_d, mine, core_out, core_in, ring_out, ring_in, send, recv, plane_send, plane_recv,
):
    me = z, y, x, c = position()
    greet(*me)
    links = Links(send, recv)
    rows = mine.shape[1]

    def product(block):
        return right_transposed(
            pre_ref[pl.ds(pl.multiple_of(block * rows, rows), rows), :], weight_ref[...]
        )

    for k in range(2):
        join_go(links, me, k, grad_gu, in_gu, plane_send.at[0], plane_recv.at[0])
        join_go(links, me, k, grad_d, in_d, plane_send.at[1], plane_recv.at[1])
    state = reduce_start(links, me, product, mine, core_out, core_in)
    for i in range(4):
        last = reduce_step(links, me, state, i, mine, core_in, ring_out, ring_in)
    normed_grad = jnp.concatenate(last, axis=0)
    residual = residual_ref[...]
    scale = rms(residual)
    unit = residual * scale
    part_ref[...] = jnp.sum(normed_grad * unit, axis=0, keepdims=True)
    out = own_ref[...].astype(jnp.float32) + norm_back(normed_grad, unit, scale, gain_ref[...])
    wide_ref[...] = out
    low_ref[0] = out.astype(jnp.bfloat16)
    shared = share_start(links, low_ref, me)
    for step in (1, 2, 3):
        share_step(links, low_ref, me, shared, step)
    share_end(shared)
    group, size, tokens = heads_out.shape
    count = 2 * rows
    for i in range(4):
        left = low_ref[2 * i : 2 * i + 2].reshape(count, low_ref.shape[2])
        out = jnp.dot(left, out_weight[...], preferred_element_type=jnp.float32)
        out = out.astype(jnp.bfloat16).T
        heads_out[:, :, i * count : (i + 1) * count] = out.reshape(group, size, count)
    heads = []
    for d in (1, 2, 3):
        xd, yd = flip(x, d // 2), flip(y, d % 2)
        heads.append(links.go(heads_out.at[2 * xd + yd], pieces.at[d], device(z, yd, xd, c)))
    pieces[0] = heads_out[2 * x + y]
    for made in heads:
        made.wait_recv()
    for k in range(2):
        sum_gu[k] = join_sum(k, in_gu, plane_recv.at[0])
        sum_d[k] = join_sum(k, in_d, plane_recv.at[1])
    links.finish()


def back(grad_pre, gate_up, residual, grad_own, gain, out_weight, grad_gate_up, grad_down):
    rows, width = residual.shape
    group = out_weight.shape[1] // DH
    depth = gate_up.shape[0] // 8
    return pl.pallas_call(
        back_kernel,
        name="back",
        out_shape=[
            low_array(8, rows, width),
            wide_array(rows, width),
            wide_array(1, width),
            low_array(group, DH, 8 * rows),
            low_array(2, depth, grad_gate_up.shape[1]),
            low_array(2, depth, grad_down.shape[1]),
        ],
        in_specs=[IN_VMEM] * 6 + [IN_PLACE] * 2,
        out_specs=[IN_VMEM] * 6,
        scratch_shapes=[
            low_space(group, DH, 8 * rows),
            low_space(2, 2, 2, depth, grad_gate_up.shape[1]),
            low_space(2, 2, 2, depth, grad_down.shape[1]),
            *reduce_space(rows, width),
            COPIES((48,)),
            COPIES((48,)),
            COPIES((2, 2, 2, 2)),
            COPIES((2, 2, 2, 2)),
        ],
        compiler_params=pltpu.CompilerParams(
            collective_id=3, has_side_effects=True, vmem_limit_bytes=56 << 20
        ),
    )(grad_pre, gate_up, residual, grad_own, gain, out_weight, grad_gate_up, grad_down)


def exit_kernel(
    piece_ref, normed_ref, weight_ref, token_ref, wide_ref, gain_ref, out_grad,
    slots_ref, home_ref, part_ref,
    heads_in, rows_low, grad_qkv, in_qkv, in_out, held, token_out,
    mine, core_out, core_in, ring_out, ring_in, send, recv, plane_send, plane_recv,
):
    me = z, y, x, c = position()
    greet(*me)
    links = Links(send, recv)
    own, f = 2 * x + y, 2 * x + c
    heads = []
    for d in (1, 2, 3):
        xd, yd = flip(x, d // 2), flip(y, d % 2)
        heads.append(links.go(piece_ref.at[d], heads_in.at[own], device(z, yd, xd, c)))
    heads_in[own] = piece_ref[0]
    for k in range(2):
        join_go(links, me, k, out_grad, in_out, plane_send.at[1], plane_recv.at[1])
    for made in heads:
        made.wait_recv()
    group, three, size, tokens = heads_in.shape
    for part in range(three):
        here = slice(part * group * size, (part + 1) * group * size)
        rows_low[:, here] = heads_in[:, part].reshape(group * size, tokens).T
    rows = tokens // 8

    def product(block):
        return right_transposed(
            rows_low[pl.ds(pl.multiple_of(block * rows, rows), rows), :], weight_ref[...]
        )

    state = reduce_start(links, me, product, mine, core_out, core_in)
    reduce_step(links, me, state, 0, mine, core_in, ring_out, ring_in)
    depth = grad_qkv.shape[0] // 8
    width = normed_ref.shape[2]
    for k in range(2):
        for part in range(4):
            block = 4 * (part // 2) + 2 * flip(k, z % 2) + part % 2
            here = pl.ds(pl.multiple_of(block * depth, depth), depth)
            left = normed_ref[:, :, here].reshape(tokens, depth)
            grad_qkv[here, :] = left_transposed(left, rows_low[...]).astype(jnp.bfloat16)
        join_go(links, me, k, grad_qkv, in_qkv, plane_send.at[0], plane_recv.at[0])
        reduce_step(links, me, state, 1 + k, mine, core_in, ring_out, ring_in)
    last = reduce_step(links, me, state, 3, mine, core_in, ring_out, ring_in)
    normed_grad = jnp.concatenate(last, axis=0)
    tokens_wide = token_ref[...].astype(jnp.float32)
    scale = rms(tokens_wide)
    unit = tokens_wide * scale
    part_ref[...] = jnp.sum(normed_grad * unit, axis=0, keepdims=True)
    token_grad = wide_ref[...] + norm_back(normed_grad, unit, scale, gain_ref[...])
    part = width // 4
    for i in range(4):
        token_out[i] = token_grad[:, i * part : (i + 1) * part].astype(jnp.bfloat16)
    home = []
    for d in (1, 2, 3):
        xd, cd = flip(x, d // 2), flip(c, d % 2)
        home.append(links.go(token_out.at[2 * xd + cd], home_ref.at[f], device(z, y, xd, cd)))
    home_ref[f] = token_out[f]
    wide_qkv = in_qkv.shape[-1]
    way = []
    for k in range(2):
        held[k, :, :wide_qkv] = join_sum(k, in_qkv, plane_recv.at[0])
        held[k, :, wide_qkv:] = join_sum(k, in_out, plane_recv.at[1])
        way.append(column_go(links, me, k, held.at[k], slots_ref.at[k]))
    for made in way + home:
        made.wait_recv()
    links.finish()


def leave(pieces, normed, weight, token_rows, wide_grad, gain, out_grad):
    _, _, size, tokens = pieces.shape
    rows, width = token_rows.shape
    depth, wide = weight.shape[0] // 8, weight.shape[1]
    both = wide + out_grad.shape[1]
    return pl.pallas_call(
        exit_kernel,
        name="leave",
        out_shape=[
            low_array(2, depth, both),
            low_array(4, rows, width // 4),
            wide_array(1, width),
        ],
        in_specs=[IN_VMEM] * 6 + [IN_PLACE],
        out_specs=[IN_VMEM] * 3,
        scratch_shapes=[
            low_space(4, 3, size, tokens),
            low_space(tokens, wide),
            low_space(8 * depth, wide),
            low_space(2, 2, 2, depth, wide),
            low_space(2, 2, 2, depth, out_grad.shape[1]),
            low_space(2, depth, both),
            low_space(4, rows, width // 4),
            *reduce_space(rows, width),
            COPIES((48,)),
            COPIES((48,)),
            COPIES((2, 2, 2, 2)),
            COPIES((2, 2, 2, 2)),
        ],
        compiler_params=pltpu.CompilerParams(
            collective_id=4, has_side_effects=True, vmem_limit_bytes=56 << 20
        ),
    )(pieces, normed, weight, token_rows, wide_grad, gain, out_grad)


def fast_shards(
    tokens_in,
    cotangent,
    gain_attn,
    query_weight,
    key_weight,
    value_weight,
    output_weight,
    bias_table,
    gain_ffn,
    gate_weight,
    up_weight,
    down_weight,
    lengths,
    buckets,
):
    seq_index, fsdp_index = lax.axis_index("seq"), lax.axis_index("fsdp")
    z, y, x, c = seq_index // 2, seq_index % 2, fsdp_index // 2, fsdp_index % 2
    z_low, z_high = z % 2, z // 2
    batch_count, slot_count, part_width = tokens_in.shape
    width = part_width * 4
    row_count = query_weight.shape[0]
    heads = query_weight.shape[1] // DH
    group_heads = heads // 2
    group_width = group_heads * DH
    hidden_width = gate_weight.shape[1] // 2
    scalars = jnp.concatenate(
        [lengths, jnp.stack([z, y, x, c]).astype(jnp.int32), jnp.zeros((2,), jnp.int32)]
    )

    def halves(weights):
        slots = []
        for k in range(2):
            half = k ^ z_low
            slots.append(
                jnp.concatenate(
                    [
                        lax.dynamic_slice_in_dim(w, half * (w.shape[1] // 2), w.shape[1] // 2, 1)
                        for w in weights
                    ],
                    axis=1,
                )
            )
        return slots

    small = jnp.concatenate([gain_attn, gain_ffn, bias_table.reshape(-1)])[None]
    for d in range(3):
        small = jnp.concatenate(
            [small, move(small, (across(0, 1), along_z(1), along_z(2))[d])], axis=0
        )
    small = jnp.stack(in_place([small[i] for i in range(8)], seq_index))
    gain_one = small[:, :row_count].reshape(-1)
    gain_two = small[:, row_count : 2 * row_count].reshape(-1)
    tables = small[:, 2 * row_count :][None]
    for d in range(2):
        tables = jnp.concatenate([tables, move(tables, across_fsdp(1 << d))], axis=0)
    tables = jnp.stack(in_place([tables[i] for i in range(4)], fsdp_index))
    tables = tables.reshape(4, 8, -1, heads).transpose(1, 2, 0, 3).reshape(-1, 4 * heads)
    own_head = (2 * c + z_high) * heads + z_low * group_heads + 2 * x + y
    table_column = lax.dynamic_slice_in_dim(tables, own_head, 1, 1)[:, 0].astype(jnp.float32)
    line_length = buckets.shape[0]
    rev_buckets = jnp.concatenate([buckets[::-1], jnp.full((1,), -1, jnp.int32)])
    bucket_hot = rev_buckets[:, None] == jnp.arange(table_column.shape[0], dtype=jnp.int32)[None, :]
    rev_line = jnp.sum(jnp.where(bucket_hot, table_column[None, :], 0.0), axis=1)[None, :]

    def home_rows(rows):
        got = []
        for d in range(4):
            piece = lax.dynamic_slice_in_dim(rows, (fsdp_index ^ d) * part_width, part_width, 1)
            got.append(piece if d == 0 else move(piece, across_fsdp(d)))
        return jnp.stack(in_place(got, fsdp_index)).reshape(batch_count, slot_count, part_width)

    first_slot = seq_index * slot_count + c * (slot_count // 2)
    own_slots = first_slot + jnp.arange(slot_count // 2, dtype=jnp.int32)
    own_valid = own_slots < lax.dynamic_index_in_dim(lengths, x, 0, False)
    token_low, normed_one, grad_rows, pieces, qkv_weight = entry(
        tokens_in,
        cotangent,
        own_valid[:, None].astype(jnp.bfloat16),
        gain_one[None],
        halves([query_weight, key_weight, value_weight]),
    )
    tokens = 4 * slot_count
    grad_own = grad_rows[0]
    later = halves([output_weight]) + halves([gate_weight, up_weight]) + halves([down_weight])
    pieces, *later = lax.optimization_barrier((pieces, *later))
    held = [move(w, spread_slot(i % 2)) for i, w in enumerate(later)]
    context_pieces, context_wide, lse, qkv_all = attend(scalars, pieces, rev_line)
    normed_two, residual, context, output_full, gate_up, down_full = middle(
        context_pieces, token_low, gain_two[None], held
    )
    normed_two = normed_two.reshape(tokens, width)
    grad_rows = grad_rows.reshape(tokens, width)
    gate_up_pre = plain_product(normed_two, gate_up)
    gate_pre, up_pre = gate_up_pre[:, :hidden_width], gate_up_pre[:, hidden_width:]
    activated, gelu_back = jax.vjp(jax.nn.gelu, gate_pre)
    hidden = (activated * up_pre).astype(jnp.bfloat16)
    grad_hidden = plain_product(grad_rows, down_full)
    grad_pre = jnp.concatenate(
        [
            gelu_back(grad_hidden * up_pre)[0].astype(jnp.bfloat16),
            (grad_hidden * activated).astype(jnp.bfloat16),
        ],
        axis=1,
    )
    grad_gate_up = left_transposed(normed_two, grad_pre).astype(jnp.bfloat16)
    grad_down = left_transposed(grad_rows, hidden).astype(jnp.bfloat16)
    residual_low, residual_grad, gain_two_part, grad_pieces, sum_gate_up, sum_down = back(
        grad_pre, gate_up, residual, grad_own, gain_two[None], output_full, grad_gate_up, grad_down
    )
    gate_up_slots = [move(sum_gate_up[k], spread_slot(k)) for k in range(2)]
    down_slots = [move(sum_down[k], spread_slot(k)) for k in range(2)]
    half_rows = tokens // 2
    ffn_share = sum_rows(
        right_transposed(hidden[:half_rows], down_full),
        right_transposed(hidden[half_rows:], down_full).astype(jnp.bfloat16),
    )
    layer_out = home_rows((residual + ffn_share).astype(jnp.bfloat16))
    qkv_grad_pieces, line_grad = attend_back(
        scalars, grad_pieces, rev_line, context_wide, lse, qkv_all
    )
    grad_output = left_transposed(residual_low.reshape(tokens, width), context).astype(jnp.bfloat16)
    slots, home, gain_one_part = leave(
        qkv_grad_pieces, normed_one, qkv_weight, token_low, residual_grad, gain_one[None], grad_output
    )
    token_share = home.astype(jnp.float32).reshape(batch_count, slot_count, part_width)

    def own_columns(slots, first, size):
        cut = [s[:, first : first + size].astype(jnp.float32) for s in slots]
        return jnp.concatenate(
            [jnp.where(z_low == 0, cut[0], cut[1]), jnp.where(z_low == 0, cut[1], cut[0])], axis=1
        )

    query_sum, key_sum, value_sum, output_sum = (
        own_columns([slots[0], slots[1]], i * group_width, group_width) for i in range(4)
    )
    gate_sum = own_columns(gate_up_slots, 0, hidden_width)
    up_sum = own_columns(gate_up_slots, hidden_width, hidden_width)
    down_sum = own_columns(down_slots, 0, hidden_width)

    table_grad = jnp.sum(jnp.where(bucket_hot, line_grad[0][:, None], 0.0), axis=0)
    head_hot = (jnp.arange(4 * heads) == own_head).astype(jnp.float32)
    packed = jnp.concatenate(
        [
            gain_one_part.reshape(8, row_count),
            gain_two_part.reshape(8, row_count),
            (table_grad[:, None] * head_hot[None, :]).reshape(8, -1),
        ],
        axis=1,
    )
    for index, size, way in ((z_high, 4, along_z(2)), (z_low, 2, along_z(1)), (y, 1, across(0, 1))):
        kept = lax.dynamic_slice_in_dim(packed, index * size, size, 0)
        sent = lax.dynamic_slice_in_dim(packed, (1 - index) * size, size, 0)
        packed = kept + move(sent, way)
    for d in range(2):
        packed = packed + move(packed, across_fsdp(1 << d))
    packed = packed[0]
    table_sum = lax.dynamic_slice_in_dim(
        packed[2 * row_count :].reshape(-1, 4 * heads), fsdp_index * heads, heads, 1
    )
    return (
        layer_out,
        token_share,
        packed[:row_count],
        query_sum,
        key_sum,
        value_sum,
        output_sum,
        table_sum,
        packed[row_count : 2 * row_count],
        gate_sum,
        up_sum,
        down_sum,
    )


def solution(mesh):
    placed = (
        P(None, "seq", "fsdp"),
        P(None, "seq", "fsdp"),
        P("seq"),
        P("seq", "fsdp"),
        P("seq", "fsdp"),
        P("seq", "fsdp"),
        P("seq", "fsdp"),
        P("seq", "fsdp"),
        P("seq"),
        P("seq", "fsdp"),
        P("seq", "fsdp"),
        P("seq", "fsdp"),
        P(),
        P(),
    )
    return jax.shard_map(
        fast_shards if (mesh.shape["seq"], mesh.shape["fsdp"]) == (8, 4) else shards,
        mesh=mesh,
        in_specs=placed,
        out_specs=(
            P(None, "seq", "fsdp"),
            P(None, "seq", "fsdp"),
            P("seq"),
            P("seq", "fsdp"),
            P("seq", "fsdp"),
            P("seq", "fsdp"),
            P("seq", "fsdp"),
            P("seq", "fsdp"),
            P("seq"),
            P("seq", "fsdp"),
            P("seq", "fsdp"),
            P("seq", "fsdp"),
        ),
        check_vma=False,
    )
```

```python
from functools import partial

import jax
import jax.numpy as jnp
from jax import lax
from jax.experimental import pallas as pl
from jax.experimental.pallas import tpu as pltpu
from jax.sharding import PartitionSpec as P

DH = 64


epsilon = 1e-06
highest = lax.Precision.HIGHEST
masked_score = -1e30


def plain_product(left, right):
    return jnp.dot(left, right, preferred_element_type=jnp.float32)


def right_transposed(left, right):
    return lax.dot_general(
        left, right, (((1,), (1,)), ((), ())), preferred_element_type=jnp.float32
    )


def left_transposed(left, right):
    return lax.dot_general(
        left, right, (((0,), (0,)), ((), ())), preferred_element_type=jnp.float32
    )


def normalize(rows, gain):
    row_scale = lax.rsqrt(jnp.mean(rows * rows, axis=-1, keepdims=True) + epsilon)
    unit_rows = rows * row_scale
    return (unit_rows, row_scale, (unit_rows * gain.astype(jnp.float32)).astype(jnp.bfloat16))


def norm_back(grad_normed, unit_rows, row_scale, gain):
    weighted = grad_normed * gain.astype(jnp.float32)
    return row_scale * (
        weighted - unit_rows * jnp.mean(weighted * unit_rows, axis=-1, keepdims=True)
    )


def to_heads(rows, batch_count, head_size):
    slot_count = rows.shape[0] // batch_count
    number_of_heads = rows.shape[1] // head_size
    return rows.reshape(batch_count, slot_count, number_of_heads, head_size).transpose(2, 0, 1, 3)


def from_heads(blocks):
    number_of_heads, batch_count, slot_count, head_size = blocks.shape
    return blocks.transpose(1, 2, 0, 3).reshape(
        batch_count * slot_count, number_of_heads * head_size
    )


def bias_rows(bias_line, first_query, slot_count, length):
    span = slot_count + length - 1
    segment = lax.dynamic_slice_in_dim(bias_line, length - first_query - slot_count, span)
    flat = jnp.tile(segment, slot_count)
    skewed = flat[slot_count - 1 : slot_count - 1 + slot_count * (span - 1)].reshape(
        slot_count, span - 1
    )
    return skewed[:, :length]


def bias_rows_back(block_grad, first_query, slot_count, length, line_length):
    span = slot_count + length - 1
    widened = jnp.pad(block_grad, ((0, 0), (0, span - 1 - length)))
    flat = jnp.pad(widened.reshape(-1), (slot_count - 1, 1))
    segment_grad = jnp.sum(flat.reshape(slot_count, span), axis=0)
    return lax.dynamic_update_slice_in_dim(
        jnp.zeros((line_length,), jnp.float32), segment_grad, length - first_query - slot_count, 0
    )


def full_features(block):
    gathered = lax.all_gather(block, "fsdp", axis=2, tiled=True)
    return gathered.reshape(gathered.shape[0] * gathered.shape[1], gathered.shape[2])


def feature_total(partial_rows):
    return lax.psum(partial_rows, "fsdp")


def shards(
    tokens_in,
    cotangent,
    gain_attn,
    query_weight,
    key_weight,
    value_weight,
    output_weight,
    bias_table,
    gain_ffn,
    gate_weight,
    up_weight,
    down_weight,
    lengths,
    buckets,
):
    batch_count, slot_count, part_width = tokens_in.shape
    head_size = DH
    seq_index = lax.axis_index("seq")
    fsdp_index = lax.axis_index("fsdp")
    length = slot_count * lax.axis_size("seq")
    line_length = buckets.shape[0]
    first_query = seq_index * slot_count
    positions = jnp.arange(length, dtype=jnp.int32)
    query_positions = first_query + jnp.arange(slot_count, dtype=jnp.int32)
    key_valid = positions[None, :] < lengths[:, None]
    own_valid = query_positions[None, :] < lengths[:, None]
    gain_one, query_full, key_full, value_full, output_full, table_full = (
        lax.all_gather(gain_attn, "seq", axis=0, tiled=True),
        lax.all_gather(query_weight, "seq", axis=0, tiled=True),
        lax.all_gather(key_weight, "seq", axis=0, tiled=True),
        lax.all_gather(value_weight, "seq", axis=0, tiled=True),
        lax.all_gather(output_weight, "seq", axis=0, tiled=True),
        lax.all_gather(bias_table, "seq", axis=0, tiled=True),
    )
    token_rows = full_features(tokens_in).astype(jnp.float32)
    unit_one, scale_one, normed_one = normalize(token_rows, gain_one)
    query_heads = to_heads(
        plain_product(normed_one, query_full).astype(jnp.bfloat16), batch_count, head_size
    )
    key_heads = to_heads(
        plain_product(normed_one, key_full).astype(jnp.bfloat16), batch_count, head_size
    )
    value_heads = to_heads(
        plain_product(normed_one, value_full).astype(jnp.bfloat16), batch_count, head_size
    )
    number_of_heads = query_heads.shape[0]
    flat_shape = (number_of_heads, batch_count, slot_count * head_size)
    gathered_keys, gathered_values = (
        lax.all_gather(key_heads.reshape(flat_shape), "seq", axis=2, tiled=True),
        lax.all_gather(value_heads.reshape(flat_shape), "seq", axis=2, tiled=True),
    )
    all_keys = gathered_keys.reshape(number_of_heads, batch_count, length, head_size)
    all_values = gathered_values.reshape(number_of_heads, batch_count, length, head_size)
    bucket_hot = (
        buckets[:, None] == jnp.arange(table_full.shape[0], dtype=jnp.int32)[None, :]
    ).astype(jnp.float32)
    offset_bias = lax.dot_general(
        table_full.astype(jnp.float32), bucket_hot, (((0,), (1,)), ((), ())), precision=highest
    )

    def masked_scores(query_tile_rows, key_tile_rows, bias_block):
        raw = (
            jnp.einsum(
                "jht,jxt->jhx", query_tile_rows, key_tile_rows, preferred_element_type=jnp.float32
            )
            + bias_block[None]
        )
        return jnp.where(key_valid[:, None, :], raw, masked_score)

    def attend(inputs):
        query_tile_rows, key_tile_rows, value_tile_rows, bias_line = inputs
        scores = masked_scores(
            query_tile_rows, key_tile_rows, bias_rows(bias_line, first_query, slot_count, length)
        )
        row_peak = jnp.max(scores, axis=-1, keepdims=True)
        raised = jnp.exp(scores - row_peak)
        denominator = jnp.sum(raised, axis=-1, keepdims=True)
        weights_reduced_precision = (raised / denominator).astype(jnp.bfloat16)
        context = jnp.einsum(
            "wot,wtf->wof",
            weights_reduced_precision,
            value_tile_rows,
            preferred_element_type=jnp.float32,
        ).astype(jnp.bfloat16)
        return (context, (row_peak + jnp.log(denominator))[..., 0])

    context_heads, log_totals = lax.map(attend, (query_heads, all_keys, all_values, offset_bias))
    context_rows = from_heads(context_heads)
    residual = token_rows + feature_total(right_transposed(context_rows, output_full))
    gain_two, gate_full, up_full, down_full = (
        lax.all_gather(gain_ffn, "seq", axis=0, tiled=True),
        lax.all_gather(gate_weight, "seq", axis=0, tiled=True),
        lax.all_gather(up_weight, "seq", axis=0, tiled=True),
        lax.all_gather(down_weight, "seq", axis=0, tiled=True),
    )
    unit_two, scale_two, normed_two = normalize(residual, gain_two)
    gate_pre = plain_product(normed_two, gate_full)
    up_pre = plain_product(normed_two, up_full)
    activated, gelu_back = jax.vjp(jax.nn.gelu, gate_pre)
    hidden = (activated * up_pre).astype(jnp.bfloat16)
    ffn_share = lax.psum_scatter(
        right_transposed(hidden, down_full), "fsdp", scatter_dimension=1, tiled=True
    )
    residual_share = lax.dynamic_slice_in_dim(residual, fsdp_index * part_width, part_width, 1)
    layer_out = (
        (residual_share + ffn_share)
        .astype(jnp.bfloat16)
        .reshape(batch_count, slot_count, part_width)
    )
    masked_cot = jnp.where(own_valid[:, :, None], cotangent, jnp.zeros_like(cotangent))
    grad_rows = full_features(masked_cot)
    grad_down = left_transposed(grad_rows, hidden)
    grad_hidden = plain_product(grad_rows, down_full)
    grad_gate_pre = gelu_back(grad_hidden * up_pre)[0].astype(jnp.bfloat16)
    grad_up_pre = (grad_hidden * activated).astype(jnp.bfloat16)
    grad_gate = left_transposed(normed_two, grad_gate_pre)
    grad_up = left_transposed(normed_two, grad_up_pre)
    normed_two_grad = right_transposed(grad_gate_pre, gate_full) + right_transposed(
        grad_up_pre, up_full
    )
    second_gain_piece = jnp.sum(normed_two_grad * unit_two, axis=0)
    ffn_grads = (
        lax.psum_scatter(second_gain_piece, "seq", scatter_dimension=0, tiled=True),
        lax.psum_scatter(grad_gate, "seq", scatter_dimension=0, tiled=True),
        lax.psum_scatter(grad_up, "seq", scatter_dimension=0, tiled=True),
        lax.psum_scatter(grad_down, "seq", scatter_dimension=0, tiled=True),
    )
    residual_grad = grad_rows.astype(jnp.float32) + norm_back(
        feature_total(normed_two_grad), unit_two, scale_two, gain_two
    )
    residual_low = residual_grad.astype(jnp.bfloat16)
    grad_output = left_transposed(residual_low, context_rows)
    context_grad = to_heads(
        plain_product(residual_low, output_full).astype(jnp.bfloat16), batch_count, head_size
    )

    def query_side(inputs, with_keys):
        query_tile_rows, key_tile_rows, value_tile_rows, bias_line, log_total, context_tile_rows = (
            inputs
        )
        scores = masked_scores(
            query_tile_rows, key_tile_rows, bias_rows(bias_line, first_query, slot_count, length)
        )
        probs = jnp.exp(scores - log_total[..., None])
        prob_grad = jnp.einsum(
            "jht,jxt->jhx", context_tile_rows, value_tile_rows, preferred_element_type=jnp.float32
        )
        delta = jnp.sum(probs * prob_grad, axis=-1)
        score_gradient = (probs * (prob_grad - delta[..., None])).astype(jnp.bfloat16)
        query_grad = jnp.einsum(
            "wot,wtf->wof", score_gradient, key_tile_rows, preferred_element_type=jnp.float32
        )
        bias_grad = bias_rows_back(
            jnp.sum(score_gradient.astype(jnp.float32), axis=0),
            first_query,
            slot_count,
            length,
            line_length,
        )
        key_term = jnp.einsum(
            "xic,xil->xcl", score_gradient, query_tile_rows, preferred_element_type=jnp.float32
        )
        value_term = jnp.einsum(
            "xic,xil->xcl",
            probs.astype(jnp.bfloat16),
            context_tile_rows,
            preferred_element_type=jnp.float32,
        )
        return (query_grad, bias_grad, delta, key_term, value_term)

    side_inputs = (query_heads, all_keys, all_values, offset_bias, log_totals, context_grad)
    query_grad, bias_grad, delta, key_terms, value_terms = lax.map(
        partial(query_side, with_keys=True), side_inputs
    )
    wide_shape = (number_of_heads, batch_count, length * head_size)
    key_sums, value_sums = (
        lax.psum_scatter(key_terms.reshape(wide_shape), "seq", scatter_dimension=2, tiled=True),
        lax.psum_scatter(value_terms.reshape(wide_shape), "seq", scatter_dimension=2, tiled=True),
    )
    own_shape = (number_of_heads, batch_count, slot_count, head_size)
    query_low = from_heads(query_grad.astype(jnp.bfloat16))
    key_low = from_heads(key_sums.reshape(own_shape).astype(jnp.bfloat16))
    value_low = from_heads(value_sums.reshape(own_shape).astype(jnp.bfloat16))
    grad_query = left_transposed(normed_one, query_low)
    grad_key = left_transposed(normed_one, key_low)
    grad_value = left_transposed(normed_one, value_low)
    grad_table = lax.dot_general(bucket_hot, bias_grad, (((0,), (1,)), ((), ())), precision=highest)
    normed_one_grad = (
        right_transposed(query_low, query_full)
        + right_transposed(key_low, key_full)
        + right_transposed(value_low, value_full)
    )
    gain_one_part = jnp.sum(normed_one_grad * unit_one, axis=0)
    attn_grads = (
        lax.psum_scatter(gain_one_part, "seq", scatter_dimension=0, tiled=True),
        lax.psum_scatter(grad_query, "seq", scatter_dimension=0, tiled=True),
        lax.psum_scatter(grad_key, "seq", scatter_dimension=0, tiled=True),
        lax.psum_scatter(grad_value, "seq", scatter_dimension=0, tiled=True),
        lax.psum_scatter(grad_output, "seq", scatter_dimension=0, tiled=True),
        lax.psum_scatter(grad_table, "seq", scatter_dimension=0, tiled=True),
    )
    token_grad = residual_grad + norm_back(
        feature_total(normed_one_grad), unit_one, scale_one, gain_one
    )
    token_share = lax.dynamic_slice_in_dim(
        token_grad, fsdp_index * part_width, part_width, 1
    ).reshape(batch_count, slot_count, part_width)
    gain_one_sum, gain_two_sum = lax.psum((attn_grads[0], ffn_grads[0]), "fsdp")
    return (
        layer_out,
        token_share,
        gain_one_sum,
        attn_grads[1],
        attn_grads[2],
        attn_grads[3],
        attn_grads[4],
        attn_grads[5],
        gain_two_sum,
        ffn_grads[1],
        ffn_grads[2],
        ffn_grads[3],
    )


BLOCK = 128
BOTH = ("seq", "fsdp")


def move(value, target):
    pairs = []
    for z in range(4):
        for y in range(2):
            for x in range(2):
                for c in range(2):
                    zt, yt, xt, ct = target(z, y, x, c)
                    pairs.append(((2 * z + y) * 4 + 2 * x + c, (2 * zt + yt) * 4 + 2 * xt + ct))
    return lax.ppermute(value, BOTH, pairs)


def spread_slot(k):
    return lambda z, y, x, c: (2 * c + (k ^ (z & 1)), y, x, z >> 1)


def spread_plane(dy, dx):
    return lambda z, y, x, c: (z, y ^ dy, c ^ dx, x)


def join_plane(dy, dx):
    return lambda z, y, x, c: (z, y ^ dy, c, x ^ dx)


def along_z(d):
    return lambda z, y, x, c: (z ^ d, y, x, c)


def other_core(z, y, x, c):
    return (z, y, x, c ^ 1)


def across(dx, dy):
    return lambda z, y, x, c: (z, y ^ dy, x ^ dx, c)


def across_fsdp(d):
    return lambda z, y, x, c: (z, y, x ^ (d >> 1), c ^ (d & 1))


def in_place(relative, me):
    current, bit = list(relative), 1
    while bit < len(current):
        swap = (me & bit) != 0
        current = [jnp.where(swap, current[i ^ bit], current[i]) for i in range(len(current))]
        bit *= 2
    return current


def sum_rows(mine, other):
    mine = mine + move(other, other_core).astype(jnp.float32)
    count = mine.shape[0] // 4
    total = mine[:count]
    for d in (1, 2, 3):
        part = mine[d * count : (d + 1) * count].astype(jnp.bfloat16)
        total = total + move(part, along_z(d)).astype(jnp.float32)
    return total


KEYS = 256
QUERIES = 256
OFFSET = 1920


def skew_table(rev_ref, table):
    width = rev_ref.shape[1]
    line = jnp.broadcast_to(rev_ref[...], (8, width))
    for first in range(0, BLOCK, 8):
        table[first : first + 8, :] = pltpu.roll(
            line, (width - (BLOCK - 1) + first) % width, axis=1, stride=1, stride_axis=0
        )


def place_of(piece, part, z, y, x, c):
    c_rel, d = part // 4, part % 4
    b = jnp.bitwise_xor(x, piece // 2)
    block = (
        4 * jnp.bitwise_xor(z, d)
        + 2 * jnp.bitwise_xor(y, piece % 2)
        + jnp.bitwise_xor(c, c_rel)
    )
    return b, block


def part_of(b, block, z, y, x, c):
    piece = 2 * jnp.bitwise_xor(b, x) + jnp.bitwise_xor((block // 2) % 2, y)
    part = 4 * jnp.bitwise_xor(block % 2, c) + jnp.bitwise_xor(block // 4, z)
    return piece, part


def lanes(first, count):
    return pl.ds(pl.multiple_of(first, BLOCK), count)


def attend_kernel(sc, pieces, rev_ref, ctx_ref, ctx_wide, lse_ref, qkv, keys, table):
    z, y, x, c = position()
    for piece in range(4):
        for part in range(8):
            b, block = place_of(piece, part, z, y, x, c)
            data = pieces[piece, :, :, part * BLOCK : (part + 1) * BLOCK]
            qkv[b, :, :, lanes(block * BLOCK, BLOCK)] = data
            keys[b, lanes(block * BLOCK, BLOCK), :] = data[1].T
    skew_table(rev_ref, table)
    length = qkv.shape[-1]
    for b in range(2):
        valid = sc[b]
        full = valid // KEYS

        @pl.loop(0, length // QUERIES)
        def _(i):
            first_query = i * QUERIES
            query = qkv[b, 0, :, lanes(first_query, QUERIES)]

            def tile(j, carry, masked):
                peak, total, acc = carry
                first_key = j * KEYS
                score = jnp.dot(
                    keys[b, lanes(first_key, KEYS), :], query, preferred_element_type=jnp.float32
                )
                score = score + jnp.concatenate(
                    [
                        table[:, lanes(first_query - first_key + OFFSET - t, QUERIES)]
                        for t in range(0, KEYS, BLOCK)
                    ],
                    axis=0,
                )
                if masked:
                    position = first_key + lax.broadcasted_iota(jnp.int32, (KEYS, QUERIES), 0)
                    score = jnp.where(position < valid, score, masked_score)
                now = jnp.maximum(peak, jnp.max(score, axis=0, keepdims=True))
                scale = jnp.exp(peak - now)
                prob = jnp.exp(score - now)
                total = total * scale + jnp.sum(prob, axis=0, keepdims=True)
                acc = acc * scale + jnp.dot(
                    qkv[b, 2, :, lanes(first_key, KEYS)],
                    prob.astype(jnp.bfloat16),
                    preferred_element_type=jnp.float32,
                )
                return now, total, acc

            carry = (
                jnp.full((1, QUERIES), masked_score, jnp.float32),
                jnp.zeros((1, QUERIES), jnp.float32),
                jnp.zeros((DH, QUERIES), jnp.float32),
            )
            carry = lax.fori_loop(0, full, lambda j, s: tile(j, s, False), carry)
            peak, total, acc = lax.cond(
                valid > full * KEYS, lambda s: tile(full, s, True), lambda s: s, carry
            )
            context = acc / total
            ctx_wide[b, :, lanes(first_query, QUERIES)] = context
            lse_ref[b, :, lanes(first_query, QUERIES)] = peak + jnp.log(total)
            low = context.astype(jnp.bfloat16)
            for t in range(QUERIES // BLOCK):
                piece, part = part_of(b, i * (QUERIES // BLOCK) + t, z, y, x, c)
                ctx_ref[piece, :, lanes(part * BLOCK, BLOCK)] = low[:, t * BLOCK : (t + 1) * BLOCK]


def attend(scalars, pieces, rev_line):
    _, _, head_size, tokens = pieces.shape
    length = tokens * 2
    smem, vmem = pl.BlockSpec(memory_space=pltpu.SMEM), pl.BlockSpec(memory_space=pltpu.VMEM)
    return pl.pallas_call(
        attend_kernel,
        name="attend",
        out_shape=[
            jax.ShapeDtypeStruct((4, head_size, tokens), jnp.bfloat16),
            jax.ShapeDtypeStruct((2, head_size, length), jnp.float32),
            jax.ShapeDtypeStruct((2, 1, length), jnp.float32),
            jax.ShapeDtypeStruct((2, 3, head_size, length), jnp.bfloat16),
        ],
        in_specs=[smem] + [vmem] * 2,
        out_specs=[vmem] * 4,
        scratch_shapes=[
            pltpu.VMEM((2, length, head_size), jnp.bfloat16),
            pltpu.VMEM((BLOCK, rev_line.shape[1]), jnp.float32),
        ],
        cost_estimate=pl.CostEstimate(
            flops=46_000_000_000, bytes_accessed=4 << 20, transcendentals=0
        ),
        compiler_params=pltpu.CompilerParams(vmem_limit_bytes=48 << 20),
    )(scalars, pieces, rev_line)


def attend_back_kernel(
    sc, pieces, rev_ref, ctx_wide, lse_ref, qkv,
    out_ref, line_ref,
    queries, keys, values, grads, grads_t, delta, query_sum, key_sum, value_sum, table, table_sum,
):
    z, y, x, c = position()
    length = qkv.shape[-1]
    for piece in range(4):
        for part in range(8):
            b, block = place_of(piece, part, z, y, x, c)
            data = pieces[piece, :, part * BLOCK : (part + 1) * BLOCK]
            grads_t[b, :, lanes(block * BLOCK, BLOCK)] = data
            grads[b, lanes(block * BLOCK, BLOCK), :] = data.T
    for b in range(2):
        for first in range(0, length, BLOCK):
            here = slice(first, first + BLOCK)
            queries[b, here, :] = qkv[b, 0, :, here].T
            keys[b, here, :] = qkv[b, 1, :, here].T
            values[b, here, :] = qkv[b, 2, :, here].T
        delta[b] = jnp.sum(
            ctx_wide[b] * grads_t[b].astype(jnp.float32), axis=0, keepdims=True
        )
    skew_table(rev_ref, table)
    table_sum[...] = jnp.zeros_like(table_sum)
    query_sum[...] = jnp.zeros_like(query_sum)
    out_ref[...] = jnp.zeros_like(out_ref)
    for b in range(2):
        valid = sc[b]
        full = valid // KEYS
        count = (valid + KEYS - 1) // KEYS

        def key_step(j, masked):
            first_key = j * KEYS
            key, value = keys[b, lanes(first_key, KEYS), :], values[b, lanes(first_key, KEYS), :]
            key_t = qkv[b, 1, :, lanes(first_key, KEYS)]
            key_sum[...] = jnp.zeros_like(key_sum)
            value_sum[...] = jnp.zeros_like(value_sum)

            @pl.loop(0, count)
            def _(i):
                first_query = i * QUERIES
                here = lanes(first_query, QUERIES)
                score = jnp.dot(key, qkv[b, 0, :, here], preferred_element_type=jnp.float32)
                score = score + jnp.concatenate(
                    [
                        table[:, lanes(first_query - first_key + OFFSET - t, QUERIES)]
                        for t in range(0, KEYS, BLOCK)
                    ],
                    axis=0,
                )
                if masked:
                    position = first_key + lax.broadcasted_iota(jnp.int32, (KEYS, QUERIES), 0)
                    score = jnp.where(position < valid, score, masked_score)
                prob = jnp.exp(score - lse_ref[b, :, here])
                prob_grad = jnp.dot(value, grads_t[b, :, here], preferred_element_type=jnp.float32)
                score_grad = (prob * (prob_grad - delta[b, :, here])).astype(jnp.bfloat16)
                value_sum[...] += jnp.dot(
                    prob.astype(jnp.bfloat16), grads[b, here, :], preferred_element_type=jnp.float32
                )
                key_sum[...] += jnp.dot(
                    score_grad, queries[b, here, :], preferred_element_type=jnp.float32
                )
                query_sum[b, :, here] += jnp.dot(
                    key_t, score_grad, preferred_element_type=jnp.float32
                )
                for t in range(0, KEYS, BLOCK):
                    table_sum[:, lanes(first_query - first_key + OFFSET - t, QUERIES)] += score_grad[
                        t : t + BLOCK
                    ].astype(jnp.float32)

            for t in range(KEYS // BLOCK):
                piece, part = part_of(b, j * (KEYS // BLOCK) + t, z, y, x, c)
                rows = slice(t * BLOCK, (t + 1) * BLOCK)
                at = lanes(part * BLOCK, BLOCK)
                out_ref[piece, 1, :, at] = key_sum[rows, :].T.astype(jnp.bfloat16)
                out_ref[piece, 2, :, at] = value_sum[rows, :].T.astype(jnp.bfloat16)

        pl.loop(0, full)(lambda j: key_step(j, False))
        pl.when(valid > full * KEYS)(lambda: key_step(full, True))
        for block in range(length // BLOCK):
            piece, part = part_of(b, block, z, y, x, c)
            out_ref[piece, 0, :, lanes(part * BLOCK, BLOCK)] = query_sum[
                b, :, block * BLOCK : (block + 1) * BLOCK
            ].astype(jnp.bfloat16)
    width = table_sum.shape[1]
    line = jnp.zeros((8, width), jnp.float32)
    for first in range(0, BLOCK, 8):
        line = line + pltpu.roll(table_sum[first : first + 8, :], BLOCK - 8 - first, axis=1)
    ahead = 7 - lax.broadcasted_iota(jnp.int32, (8, width), 0)
    for bit in (1, 2, 4):
        line = jnp.where((ahead & bit) != 0, pltpu.roll(line, bit, axis=1), line)
    line_ref[...] = jnp.sum(line, axis=0, keepdims=True)


def attend_back(scalars, pieces, rev_line, ctx_wide, lse, qkv):
    _, head_size, tokens = pieces.shape
    length = tokens * 2
    smem, vmem = pl.BlockSpec(memory_space=pltpu.SMEM), pl.BlockSpec(memory_space=pltpu.VMEM)
    low = pltpu.VMEM((2, length, head_size), jnp.bfloat16)
    return pl.pallas_call(
        attend_back_kernel,
        name="attend_back",
        out_shape=[
            jax.ShapeDtypeStruct((4, 3, head_size, tokens), jnp.bfloat16),
            jax.ShapeDtypeStruct(rev_line.shape, jnp.float32),
        ],
        in_specs=[smem] + [vmem] * 5,
        out_specs=[vmem] * 2,
        scratch_shapes=[
            low, low, low, low,
            pltpu.VMEM((2, head_size, length), jnp.bfloat16),
            pltpu.VMEM((2, 1, length), jnp.float32),
            pltpu.VMEM((2, head_size, length), jnp.float32),
            pltpu.VMEM((KEYS, head_size), jnp.float32),
            pltpu.VMEM((KEYS, head_size), jnp.float32),
            pltpu.VMEM((BLOCK, rev_line.shape[1]), jnp.float32),
            pltpu.VMEM((BLOCK, rev_line.shape[1]), jnp.float32),
        ],
        cost_estimate=pl.CostEstimate(
            flops=46_000_000_000, bytes_accessed=4 << 20, transcendentals=0
        ),
        compiler_params=pltpu.CompilerParams(vmem_limit_bytes=48 << 20),
    )(scalars, pieces, rev_line, ctx_wide, lse, qkv)


CHUNKS = 2
MESH_ID = pl.DeviceIdType.MESH
IN_VMEM = pl.BlockSpec(memory_space=pltpu.VMEM)
IN_PLACE = pl.BlockSpec(memory_space=pl.ANY)
COPIES = pltpu.SemaphoreType.DMA


def flip(a, b):
    return a + b - 2 * a * b


def flip_pair(a, b):
    return 2 * flip(a // 2, b // 2) + flip(a % 2, b % 2)


def position():
    s, f = lax.axis_index("seq"), lax.axis_index("fsdp")
    return s // 2, s % 2, f // 2, f % 2


def device(z, y, x, c):
    return (2 * z + y, 2 * x + c)


def ring_of(z):
    high, low = z // 2, z % 2
    following = 2 * low + 1 - high
    return following, (2 * (1 - low) + high, 2 * (1 - high) + 1 - low, following)


def greet(z, y, x, c):
    peers = []
    for d in range(1, 8):
        peers.append(device(z, flip(y, d // 4), flip(x, (d // 2) % 2), flip(c, d % 2)))
        if d > 1:
            peers.append(device(flip_pair(z, d // 2), y, x, flip(c, d % 2)))
    barrier = pltpu.get_barrier_semaphore()
    for peer in peers:
        pl.semaphore_signal(barrier, inc=1, device_id=peer, device_id_type=MESH_ID)
    pl.semaphore_wait(barrier, len(peers))


def remote(source, target, send, recv, to):
    return pltpu.make_async_remote_copy(
        src_ref=source,
        dst_ref=target,
        send_sem=send,
        recv_sem=recv,
        device_id=to,
        device_id_type=MESH_ID,
    )


class Links:
    def __init__(self, send, recv):
        self.send, self.recv, self.used, self.sent = send, recv, 0, []

    def go(self, source, target, to):
        i = self.used
        self.used += 1
        made = remote(source, target, self.send.at[i], self.recv.at[i], to)
        made.start()
        self.sent.append(made)
        return made

    def go_unless(self, own, source, target, to, send=None, recv=None):
        if send is None:
            send, recv = self.send.at[self.used], self.recv.at[self.used]
            self.used += 1
        made = remote(source, target, send, recv, to)
        if own is None:
            made.start()
            self.sent.append(made)
            return made
        local = pltpu.make_async_copy(source, target, recv)
        pl.when(own)(lambda: local.start())
        pl.when(jnp.logical_not(own))(lambda: made.start())
        self.sent.append((own, made))
        return made

    def done(self, made):
        made.wait_send()
        self.sent = [m for m in self.sent if m is not made]

    def finish(self):
        for made in self.sent:
            if isinstance(made, tuple):
                pl.when(jnp.logical_not(made[0]))(lambda made=made: made[1].wait_send())
            else:
                made.wait_send()


def share_start(links, rows_all, me):
    z, y, x, c = me
    following, _ = ring_of(z)
    rows = rows_all.shape[1] // CHUNKS
    ring = []
    for h in range(CHUNKS):
        here = pl.ds(h * rows, rows)
        target = rows_all.at[flip_pair(following, z), here]
        ring.append(links.go(rows_all.at[0, here], target, device(following, y, x, c)))
    core = [links.go(rows_all.at[0], rows_all.at[4], device(z, y, x, 1 - c))]
    return [ring], core


def share_step(links, rows_all, me, state, step):
    z, y, x, c = me
    following, back = ring_of(z)
    rows = rows_all.shape[1] // CHUNKS
    ring, core = state
    slot = flip_pair(z, back[step - 1])
    sent = []
    for h in range(CHUNKS):
        here = pl.ds(h * rows, rows)
        ring[-1][h].wait_recv()
        source = rows_all.at[slot, here]
        if step < 3:
            target = rows_all.at[flip_pair(following, back[step - 1]), here]
            sent.append(links.go(source, target, device(following, y, x, c)))
        core.append(links.go(source, rows_all.at[4 + slot, here], device(z, y, x, 1 - c)))
    ring.append(sent)


def share_end(state):
    for made in state[1]:
        made.wait_recv()


def sum_order(z):
    _, back = ring_of(z)
    return [flip_pair(z, b) for b in back] + [0]


def reduce_start(links, me, product, core_out, core_in):
    z, y, x, c = me
    core = []
    for i, d in enumerate(sum_order(z)):
        core_out[i] = product(4 + d).astype(jnp.bfloat16)
        core.append(links.go(core_out.at[i], core_in.at[i], device(z, y, x, 1 - c)))
    return core, []


def reduce_step(links, me, state, i, product, core_in, ring_out, ring_in):
    core, ring = state
    z, y, x, c = me
    following, _ = ring_of(z)
    mine = product(sum_order(z)[i])
    rows = mine.shape[0] // CHUNKS
    core[i].wait_recv()
    sent, last = [], []
    for h in range(CHUNKS):
        cut = slice(h * rows, (h + 1) * rows)
        here = pl.ds(h * rows, rows)
        value = mine[cut] + core_in[i, here, :].astype(jnp.float32)
        if i:
            ring[-1][h].wait_recv()
            value = value + ring_in[i - 1, here, :].astype(jnp.float32)
        if i < 3:
            ring_out[i, here, :] = value.astype(jnp.bfloat16)
            target = ring_in.at[i, here]
            sent.append(links.go(ring_out.at[i, here], target, device(following, y, x, c)))
        else:
            last.append(value)
    ring.append(sent)
    return last


def column_go(links, me, k, source, target):
    z, y, x, c = me
    own = z // 2 == c if k == 0 else None
    to = device(2 * c + flip(k, z % 2), y, x, z // 2)
    return links.go_unless(own, source, target, to)


def spread_go(links, me, k, source, full, send, recv):
    z, y, x, c = me
    rows = source.shape[0]
    first = pl.multiple_of((4 * c + 2 * flip(k, z % 2) + y) * rows, rows)
    target = full.at[pl.ds(first, rows), :]
    for dy in range(2):
        for dx in range(2):
            own = None if dy + dx else c == x
            to = device(z, flip(y, dy), flip(x, dx), x)
            links.go_unless(own, source, target, to, send.at[k, dy, dx], recv.at[k, dy, c])


def spread_wait(full, recv):
    rows = full.shape[0] // 8
    for k in range(2):
        for dy in range(2):
            for r in range(2):
                here = full.at[pl.ds(0, rows), :]
                pltpu.make_async_copy(here, here, recv.at[k, dy, r]).wait()


def join_go(links, me, k, grads, into, send, recv):
    z, y, x, c = me
    rows = into.shape[3]
    for dy in range(2):
        for r in range(2):
            block = 4 * r + 2 * flip(k, z % 2) + flip(y, dy)
            source = grads.at[pl.ds(pl.multiple_of(block * rows, rows), rows), :]
            own = None if dy else jnp.logical_and(c == x, c == r)
            to = device(z, flip(y, dy), c, r)
            links.go_unless(
                own, source, into.at[k, dy, x], to, send.at[k, dy, r], recv.at[k, dy, x]
            )


def join_sum(k, into, recv):
    total = 0.0
    for dy in range(2):
        for other in range(2):
            here = into.at[k, dy, other]
            pltpu.make_async_copy(here, here, recv.at[k, dy, other]).wait()
            total = total + into[k, dy, other].astype(jnp.float32)
    return total.astype(jnp.bfloat16)


def rms(rows):
    return lax.rsqrt(jnp.mean(rows * rows, axis=-1, keepdims=True) + epsilon)


def lane_sum(values):
    return jnp.sum(values, axis=-1, keepdims=True)


def head_of(z, y, x, c, heads):
    return 2 * c + z // 2, (z % 2) * (heads // 2) + 2 * x + y


def entry_kernel(
    lengths, tok_ref, cot_ref, small_ref, bucket_ref, wq_ref, wk_ref, wv_ref,
    rows_ref, normed, grads, pieces, weight, gain_one, gain_two, rev_ref,
    tok_in, cot_in, held, qkv, small, send, recv, plane_send, plane_recv,
):
    me = z, y, x, c = position()
    greet(*me)
    links = Links(send, recv)
    f, part, half = 2 * x + c, tok_in.shape[2], tok_in.shape[1]

    def gather_rows(ref, into):
        got = []
        for d in (1, 2, 3):
            xd, cd = flip(x, d // 2), flip(c, d % 2)
            source = ref.at[xd, pl.ds(pl.multiple_of(cd * half, half), half)]
            got.append(links.go(source, into.at[f], device(z, y, xd, cd)))
        into[f] = ref[x, pl.ds(pl.multiple_of(c * half, half), half), :]
        return got

    tok_got = gather_rows(tok_ref, tok_in)
    small[f, z, y] = small_ref[...]
    small_got = []
    for d in (1, 2, 3):
        here = small.at[f, z, y]
        small_got.append(links.go(here, here, device(flip_pair(z, d), y, x, c)))
    group_width = wq_ref.shape[1] // 2
    way = []
    for k in range(2):
        cut = pl.ds(pl.multiple_of(flip(k, z % 2) * group_width, group_width), group_width)
        for n, ref in enumerate((wq_ref, wk_ref, wv_ref)):
            target = held.at[k, :, n * group_width : (n + 1) * group_width]
            way.append(column_go(links, me, k, ref.at[:, cut], target))
    cot_got = gather_rows(cot_ref, cot_in)
    for made in small_got:
        made.wait_recv()
    here = small.at[f, :, y]
    links.go(here, here, device(z, 1 - y, x, c)).wait_recv()
    tables = []
    for d in (1, 2, 3):
        here = small.at[f]
        tables.append(links.go(here, here, device(z, y, flip(x, d // 2), flip(c, d % 2))))
    for i in range(4 * part // BLOCK):
        here = slice(i * BLOCK, (i + 1) * BLOCK)
        block = (i // 2) // 2, (i // 2) % 2
        gain_one[:, here] = small[f, block[0], block[1], i % 2 : i % 2 + 1, :]
        gain_two[:, here] = small[f, block[0], block[1], 2 + i % 2 : 3 + i % 2, :]
    for made in tok_got:
        made.wait_recv()
    wide = [tok_in[i].astype(jnp.float32) for i in range(4)]
    mean = sum(lane_sum(w * w) for w in wide) / (4 * part)
    scale = lax.rsqrt(mean + epsilon)
    for i in range(4):
        here = slice(i * part, (i + 1) * part)
        rows_ref[:, here] = tok_in[i]
        normed[0, :, here] = (wide[i] * scale * gain_one[:, here]).astype(jnp.bfloat16)
    first = share_start(links, normed, me)
    for made in cot_got:
        made.wait_recv()
    slot = (4 * z + 2 * y + c) * half + lax.broadcasted_iota(jnp.int32, (half, part), 0)
    valid = slot < jnp.where(x == 0, lengths[0], lengths[1])
    for i in range(4):
        grads[0, :, i * part : (i + 1) * part] = jnp.where(valid, cot_in[i], jnp.zeros_like(cot_in[i]))
    for k in range(2):
        for made in way[3 * k : 3 * k + 3]:
            made.wait_recv()
        spread_go(links, me, k, held.at[k], weight, plane_send, plane_recv)
    for step in (1, 2, 3):
        share_step(links, normed, me, first, step)
    second = share_start(links, grads, me)
    for made in tables:
        made.wait_recv()
    group = qkv.shape[1]
    heads = 2 * group
    source, place = head_of(z, y, x, c, heads)
    lane = lax.broadcasted_iota(jnp.int32, (1, BLOCK), 1)
    line = jnp.zeros(bucket_ref.shape, jnp.float32)
    per_block = 4
    for n in range(8 * per_block):
        block = n // per_block
        row = small[source, block // 2, block % 2, 4:5, :]
        value = lane_sum(jnp.where(lane == (n % per_block) * heads + place, row, 0.0))
        line = jnp.where(bucket_ref[...] == n, value, line)
    rev_ref[...] = line
    share_end(first)
    spread_wait(weight, plane_recv)
    count = 2 * normed.shape[1]

    @pl.loop(0, 4)
    def _(i):
        left = normed[pl.ds(2 * i, 2)].reshape(count, 4 * part)
        out = jnp.dot(left, weight[...], preferred_element_type=jnp.float32)
        out = out.astype(jnp.bfloat16).T
        qkv[:, :, :, lanes(i * count, count)] = out.reshape(3, group, DH, count)

    sent = []
    for d in (1, 2, 3):
        xd, yd = flip(x, d // 2), flip(y, d % 2)
        sent.append(links.go(qkv.at[:, 2 * xd + yd], pieces.at[d], device(z, yd, xd, c)))
    pieces[0] = qkv[:, 2 * x + y]
    for step in (1, 2, 3):
        share_step(links, grads, me, second, step)
    share_end(second)
    for made in sent:
        made.wait_recv()
    links.finish()


def low_array(*shape):
    return jax.ShapeDtypeStruct(shape, jnp.bfloat16)


def wide_array(*shape):
    return jax.ShapeDtypeStruct(shape, jnp.float32)


def low_space(*shape):
    return pltpu.VMEM(shape, jnp.bfloat16)


def entry(lengths, tokens_in, cotangent, small, rev_buckets, weights):
    _, slot_count, part = tokens_in.shape
    rows, width = slot_count // 2, 4 * part
    depth, cols = weights[0].shape
    group = cols // (2 * DH)
    wide = 3 * cols // 2
    return pl.pallas_call(
        entry_kernel,
        name="entry",
        out_shape=[
            low_array(rows, width),
            low_array(8, rows, width),
            low_array(8, rows, width),
            low_array(4, 3, DH, 8 * rows),
            low_array(8 * depth, wide),
            wide_array(1, width),
            wide_array(1, width),
            wide_array(*rev_buckets.shape),
        ],
        in_specs=[pl.BlockSpec(memory_space=pltpu.SMEM)] + [IN_VMEM] * 7,
        out_specs=[IN_VMEM] * 8,
        scratch_shapes=[
            low_space(4, rows, part),
            low_space(4, rows, part),
            low_space(2, depth, wide),
            low_space(3, group, DH, 8 * rows),
            pltpu.VMEM((4, 4, 2, 8, BLOCK), jnp.float32),
            COPIES((64,)),
            COPIES((64,)),
            COPIES((2, 2, 2)),
            COPIES((2, 2, 2)),
        ],
        compiler_params=pltpu.CompilerParams(
            collective_id=1, has_side_effects=True, vmem_limit_bytes=48 << 20
        ),
    )(lengths, tokens_in, cotangent, small, rev_buckets, *weights)


def middle_kernel(
    ctx_ref, rows_ref, gain_ref, slot0, slot1,
    normed, residual_ref, context, out_weight, gate_up, down,
    ctx_all, core_out, core_in, ring_out, ring_in, send, recv, plane_send, plane_recv,
):
    me = z, y, x, c = position()
    greet(*me)
    links = Links(send, recv)
    own = 2 * x + y
    heads = []
    for d in (1, 2, 3):
        xd, yd = flip(x, d // 2), flip(y, d % 2)
        heads.append(links.go(ctx_ref.at[d], ctx_all.at[own], device(z, yd, xd, c)))
    start = 0
    for n, full in enumerate((out_weight, gate_up, down)):
        cut = slice(start, start + full.shape[1])
        start = start + full.shape[1]
        for k, slot in enumerate((slot0, slot1)):
            spread_go(links, me, k, slot.at[:, cut], full, plane_send.at[n], plane_recv.at[n])
    ctx_all[own] = ctx_ref[0]
    for made in heads:
        made.wait_recv()
    group, size, tokens = ctx_all.shape
    context[...] = ctx_all[...].reshape(group * size, tokens).T
    spread_wait(out_weight, plane_recv.at[0])
    rows = tokens // 8

    def product(block):
        return right_transposed(
            context[pl.ds(pl.multiple_of(block * rows, rows), rows), :], out_weight[...]
        )

    state = reduce_start(links, me, product, core_out, core_in)
    for i in range(4):
        last = reduce_step(links, me, state, i, product, core_in, ring_out, ring_in)
    residual = rows_ref[...].astype(jnp.float32) + jnp.concatenate(last, axis=0)
    residual_ref[...] = residual
    gain = gain_ref[...].astype(jnp.float32)
    normed[0] = (residual * rms(residual) * gain).astype(jnp.bfloat16)
    shared = share_start(links, normed, me)
    for step in (1, 2, 3):
        share_step(links, normed, me, shared, step)
    share_end(shared)
    spread_wait(gate_up, plane_recv.at[1])
    spread_wait(down, plane_recv.at[2])
    links.finish()


def reduce_space(rows, width):
    return [
        low_space(4, rows, width),
        low_space(4, rows, width),
        low_space(3, rows, width),
        low_space(3, rows, width),
    ]


def middle(ctx_pieces, token_rows, gain, slots, widths):
    _, size, tokens = ctx_pieces.shape
    rows, width = token_rows.shape
    depth = slots[0].shape[0]
    return pl.pallas_call(
        middle_kernel,
        name="middle",
        out_shape=[
            low_array(8, rows, width),
            wide_array(rows, width),
            low_array(tokens, 4 * size),
            *(low_array(8 * depth, w) for w in widths),
        ],
        in_specs=[IN_VMEM] * 5,
        out_specs=[IN_VMEM] * 4 + [IN_PLACE] * 2,
        scratch_shapes=[
            low_space(4, size, tokens),
            *reduce_space(rows, width),
            COPIES((48,)),
            COPIES((48,)),
            COPIES((3, 2, 2, 2)),
            COPIES((3, 2, 2, 2)),
        ],
        compiler_params=pltpu.CompilerParams(
            collective_id=2, has_side_effects=True, vmem_limit_bytes=48 << 20
        ),
    )(ctx_pieces, token_rows, gain, *slots)


def back_kernel(
    pre_ref, weight_ref, residual_ref, own_ref, gain_ref, out_weight, grad_gu, grad_d,
    low_ref, wide_ref, part_ref, pieces, sum0, sum1,
    heads_out, in_gu, in_d, core_out, core_in, ring_out, ring_in, send, recv, plane_send, plane_recv,
):
    me = z, y, x, c = position()
    greet(*me)
    links = Links(send, recv)
    rows = residual_ref.shape[0]

    def product(block):
        return right_transposed(
            pre_ref[pl.ds(pl.multiple_of(block * rows, rows), rows), :], weight_ref[...]
        )

    for k in range(2):
        join_go(links, me, k, grad_gu, in_gu, plane_send.at[0], plane_recv.at[0])
        join_go(links, me, k, grad_d, in_d, plane_send.at[1], plane_recv.at[1])
    state = reduce_start(links, me, product, core_out, core_in)
    for i in range(4):
        last = reduce_step(links, me, state, i, product, core_in, ring_out, ring_in)
    normed_grad = jnp.concatenate(last, axis=0)
    residual = residual_ref[...]
    scale = rms(residual)
    unit = residual * scale
    part_ref[...] = jnp.sum(normed_grad * unit, axis=0, keepdims=True)
    out = own_ref[...].astype(jnp.float32) + norm_back(normed_grad, unit, scale, gain_ref[...])
    wide_ref[...] = out
    low_ref[0] = out.astype(jnp.bfloat16)
    shared = share_start(links, low_ref, me)
    for step in (1, 2, 3):
        share_step(links, low_ref, me, shared, step)
    share_end(shared)
    group, size, tokens = heads_out.shape
    count = 2 * rows
    for i in range(4):
        left = low_ref[2 * i : 2 * i + 2].reshape(count, low_ref.shape[2])
        out = jnp.dot(left, out_weight[...], preferred_element_type=jnp.float32)
        out = out.astype(jnp.bfloat16).T
        heads_out[:, :, i * count : (i + 1) * count] = out.reshape(group, size, count)
    heads = []
    for d in (1, 2, 3):
        xd, yd = flip(x, d // 2), flip(y, d % 2)
        heads.append(links.go(heads_out.at[2 * xd + yd], pieces.at[d], device(z, yd, xd, c)))
    pieces[0] = heads_out[2 * x + y]
    for made in heads:
        made.wait_recv()
    for k in range(2):
        wide = in_gu.shape[-1]
        (sum0, sum1)[k][:, :wide] = join_sum(k, in_gu, plane_recv.at[0])
        (sum0, sum1)[k][:, wide:] = join_sum(k, in_d, plane_recv.at[1])
    links.finish()


def back(grad_pre, gate_up, residual, grad_own, gain, out_weight, grad_gate_up, grad_down):
    rows, width = residual.shape
    group = out_weight.shape[1] // DH
    depth = gate_up.shape[0] // 8
    return pl.pallas_call(
        back_kernel,
        name="back",
        out_shape=[
            low_array(8, rows, width),
            wide_array(rows, width),
            wide_array(1, width),
            low_array(group, DH, 8 * rows),
            low_array(depth, grad_gate_up.shape[1] + grad_down.shape[1]),
            low_array(depth, grad_gate_up.shape[1] + grad_down.shape[1]),
        ],
        in_specs=[IN_VMEM] * 6 + [IN_PLACE] * 2,
        out_specs=[IN_VMEM] * 6,
        scratch_shapes=[
            low_space(group, DH, 8 * rows),
            low_space(2, 2, 2, depth, grad_gate_up.shape[1]),
            low_space(2, 2, 2, depth, grad_down.shape[1]),
            *reduce_space(rows, width),
            COPIES((48,)),
            COPIES((48,)),
            COPIES((2, 2, 2, 2)),
            COPIES((2, 2, 2, 2)),
        ],
        compiler_params=pltpu.CompilerParams(
            collective_id=3, has_side_effects=True, vmem_limit_bytes=56 << 20
        ),
    )(grad_pre, gate_up, residual, grad_own, gain, out_weight, grad_gate_up, grad_down)


def exit_kernel(
    piece_ref, normed_ref, weight_ref, token_ref, wide_ref, gain_ref, low_ref, context_ref,
    hidden_ref, down_ref, residual_ref, gain_two_ref, line_ref, bucket_ref,
    query_out, key_out, value_out, output_out, home_ref, layer_ref, small_ref,
    heads_in, rows_low, grad_qkv, grad_out, in_qkv, in_out, held, token_out, layer_own,
    packed, in_f, in_y, in_z,
    core_out, core_in, ring_out, ring_in, core_out2, core_in2, ring_out2, ring_in2,
    send, recv, plane_send, plane_recv,
):
    me = z, y, x, c = position()
    greet(*me)
    links = Links(send, recv)
    own, f = 2 * x + y, 2 * x + c
    group, three, size, tokens = heads_in.shape
    rows = tokens // 8
    depth = grad_qkv.shape[0] // 8
    width = normed_ref.shape[2]
    part = width // 4
    heads = []
    for d in (1, 2, 3):
        xd, yd = flip(x, d // 2), flip(y, d % 2)
        heads.append(links.go(piece_ref.at[d], heads_in.at[own], device(z, yd, xd, c)))
    heads_in[own] = piece_ref[0]

    def block_rows(ref, block):
        return ref[pl.ds(pl.multiple_of(block * rows, rows), rows), :]

    def ffn_product(block):
        return right_transposed(block_rows(hidden_ref, block), down_ref[...])

    def product(block):
        return right_transposed(block_rows(rows_low, block), weight_ref[...])

    def to_home(source, into):
        got = []
        for d in (1, 2, 3):
            xd, cd = flip(x, d // 2), flip(c, d % 2)
            got.append(links.go(source.at[2 * xd + cd], into.at[f], device(z, y, xd, cd)))
        into[f] = source[f]
        return got

    def ffn_step(i):
        return reduce_step(links, me, ffn, i, ffn_product, core_in2, ring_out2, ring_in2)

    def step(i):
        return reduce_step(links, me, state, i, product, core_in, ring_out, ring_in)

    ffn = reduce_start(links, me, ffn_product, core_out2, core_in2)
    ffn_step(0)
    for k in range(2):
        for n in range(4):
            block = 4 * (n // 2) + 2 * flip(k, z % 2) + n % 2
            here = pl.ds(pl.multiple_of(block * depth, depth), depth)
            left = low_ref[:, :, here].reshape(tokens, depth)
            grad_out[here, :] = left_transposed(left, context_ref[...]).astype(jnp.bfloat16)
        join_go(links, me, k, grad_out, in_out, plane_send.at[1], plane_recv.at[1])
    for made in heads:
        made.wait_recv()
    for n in range(three):
        here = slice(n * group * size, (n + 1) * group * size)
        rows_low[:, here] = heads_in[:, n].reshape(group * size, tokens).T
    state = reduce_start(links, me, product, core_out, core_in)
    step(0)
    ffn_step(1)
    for k in range(2):
        for n in range(4):
            block = 4 * (n // 2) + 2 * flip(k, z % 2) + n % 2
            here = pl.ds(pl.multiple_of(block * depth, depth), depth)
            left = normed_ref[:, :, here].reshape(tokens, depth)
            grad_qkv[here, :] = left_transposed(left, rows_low[...]).astype(jnp.bfloat16)
        join_go(links, me, k, grad_qkv, in_qkv, plane_send.at[0], plane_recv.at[0])
        step(1 + k)
        last = ffn_step(2 + k)
    layer = (residual_ref[...] + jnp.concatenate(last, axis=0)).astype(jnp.bfloat16)
    for i in range(4):
        layer_own[i] = layer[:, i * part : (i + 1) * part]
    home = to_home(layer_own, layer_ref)

    packed[...] = jnp.zeros_like(packed)
    per_block = 4
    all_heads = BLOCK // per_block
    source, place = head_of(z, y, x, c, all_heads // 4)
    lane = lax.broadcasted_iota(jnp.int32, (1, BLOCK), 1)
    for block in range(8):
        row = jnp.zeros((1, BLOCK), jnp.float32)
        for n in range(per_block):
            hot = bucket_ref[...] == block * per_block + n
            value = lane_sum(jnp.where(hot, line_ref[...], 0.0))
            row = jnp.where(lane == n * all_heads + source * (all_heads // 4) + place, value, row)
        packed[block // 2, block % 2, 4:5, :] = row
    last = step(3)
    normed_grad = jnp.concatenate(last, axis=0)
    tokens_wide = token_ref[...].astype(jnp.float32)
    scale = rms(tokens_wide)
    unit = tokens_wide * scale
    token_grad = wide_ref[...] + norm_back(normed_grad, unit, scale, gain_ref[...])
    for i in range(4):
        token_out[i] = token_grad[:, i * part : (i + 1) * part].astype(jnp.bfloat16)
    home += to_home(token_out, home_ref)
    gain_part = jnp.sum(normed_grad * unit, axis=0, keepdims=True)
    for i in range(width // BLOCK):
        here = slice(i * BLOCK, (i + 1) * BLOCK)
        block = (i // 2) // 2, (i // 2) % 2
        packed[block[0], block[1], i % 2 : i % 2 + 1, :] = gain_part[:, here]
        packed[block[0], block[1], 2 + i % 2 : 3 + i % 2, :] = gain_two_ref[:, here]
    got = []
    for d in (1, 2, 3):
        to = device(z, y, flip(x, d // 2), flip(c, d % 2))
        got.append(links.go(packed, in_f.at[d - 1], to))
    wide_qkv = in_qkv.shape[-1]
    group_width = wide_qkv // 3
    cut = pl.ds(pl.multiple_of((z % 2) * group_width, group_width), group_width)
    way = []
    for k in range(2):
        held[k, :, :wide_qkv] = join_sum(k, in_qkv, plane_recv.at[0])
        held[k, :, wide_qkv:] = join_sum(k, in_out, plane_recv.at[1])
        for n, ref in enumerate((query_out, key_out, value_out, output_out)):
            sent = held.at[k, :, n * group_width : (n + 1) * group_width]
            way.append(column_go(links, me, k, sent, ref.at[:, cut]))
    for made in got:
        made.wait_recv()
    for made in got:
        links.done(made)
    packed[...] = packed[...] + in_f[0] + in_f[1] + in_f[2]
    made = links.go(packed.at[:, 1 - y], in_y, device(z, 1 - y, x, c))
    made.wait_recv()
    in_y[...] = in_y[...] + packed[:, y]
    got = []
    for d in (1, 2, 3):
        other = flip_pair(z, d)
        got.append(links.go(in_y.at[other], in_z.at[d - 1], device(other, y, x, c)))
    for made in got:
        made.wait_recv()
    small_ref[...] = in_y[z] + in_z[0] + in_z[1] + in_z[2]
    for made in way + home:
        made.wait_recv()
    links.finish()


def leave(pieces, normed, weight, token_rows, wide_grad, gain, low, context, hidden, down, residual,
          gain_two_part, line_grad, rev_buckets):
    _, _, size, tokens = pieces.shape
    rows, width = token_rows.shape
    depth, wide = weight.shape[0] // 8, weight.shape[1]
    out_wide = context.shape[1]
    cols = 2 * wide // 3
    tile = (8, BLOCK)
    return pl.pallas_call(
        exit_kernel,
        name="leave",
        out_shape=[
            *(low_array(depth, cols) for _ in range(4)),
            low_array(4, rows, width // 4),
            low_array(4, rows, width // 4),
            wide_array(*tile),
        ],
        in_specs=[IN_VMEM] * 14,
        out_specs=[IN_VMEM] * 7,
        scratch_shapes=[
            low_space(4, 3, size, tokens),
            low_space(tokens, wide),
            low_space(8 * depth, wide),
            low_space(8 * depth, out_wide),
            low_space(2, 2, 2, depth, wide),
            low_space(2, 2, 2, depth, out_wide),
            low_space(2, depth, wide + out_wide),
            low_space(4, rows, width // 4),
            low_space(4, rows, width // 4),
            pltpu.VMEM((4, 2, *tile), jnp.float32),
            pltpu.VMEM((3, 4, 2, *tile), jnp.float32),
            pltpu.VMEM((4, *tile), jnp.float32),
            pltpu.VMEM((3, *tile), jnp.float32),
            *reduce_space(rows, width),
            *reduce_space(rows, width),
            COPIES((64,)),
            COPIES((64,)),
            COPIES((2, 2, 2, 2)),
            COPIES((2, 2, 2, 2)),
        ],
        compiler_params=pltpu.CompilerParams(
            collective_id=4, has_side_effects=True, vmem_limit_bytes=60 << 20
        ),
    )(pieces, normed, weight, token_rows, wide_grad, gain, low, context, hidden, down, residual,
      gain_two_part, line_grad, rev_buckets)


def fast_shards(
    tokens_in,
    cotangent,
    gain_attn,
    query_weight,
    key_weight,
    value_weight,
    output_weight,
    bias_table,
    gain_ffn,
    gate_weight,
    up_weight,
    down_weight,
    lengths,
    buckets,
):
    seq_index, fsdp_index = lax.axis_index("seq"), lax.axis_index("fsdp")
    z, y, x, c = seq_index // 2, seq_index % 2, fsdp_index // 2, fsdp_index % 2
    z_low, z_high = z % 2, z // 2
    batch_count, slot_count, part_width = tokens_in.shape
    width = part_width * 4
    row_count = query_weight.shape[0]
    heads = query_weight.shape[1] // DH
    group_heads = heads // 2
    group_width = group_heads * DH
    hidden_width = gate_weight.shape[1] // 2
    def halves(weights):
        slots = []
        for k in range(2):
            half = k ^ z_low
            slots.append(
                jnp.concatenate(
                    [
                        lax.dynamic_slice_in_dim(w, half * (w.shape[1] // 2), w.shape[1] // 2, 1)
                        for w in weights
                    ],
                    axis=1,
                )
            )
        return slots

    small = jnp.concatenate(
        [gain_attn, gain_ffn, bias_table.reshape(-1), jnp.zeros((2 * row_count - bias_table.size,), jnp.bfloat16)]
    )
    small = small.astype(jnp.float32).reshape(8, BLOCK)
    rev_buckets = jnp.concatenate([buckets[::-1], jnp.full((1,), -1, jnp.int32)])[None, :]
    token_low, normed_one, grad_rows, pieces, qkv_weight, gain_one, gain_two, rev_line = entry(
        lengths,
        tokens_in,
        cotangent,
        small,
        rev_buckets,
        (query_weight, key_weight, value_weight),
    )
    tokens = 4 * slot_count
    grad_own = grad_rows[0]
    later = halves([output_weight, gate_weight, up_weight, down_weight])
    pieces, *later = lax.optimization_barrier((pieces, *later))
    held = [move(later[k], spread_slot(k)) for k in range(2)]
    context_pieces, context_wide, lse, qkv_all = attend(lengths, pieces, rev_line)
    normed_two, residual, context, output_full, gate_up, down_full = middle(
        context_pieces, token_low, gain_two, held, (group_width, 2 * hidden_width, hidden_width)
    )
    normed_two = normed_two.reshape(tokens, width)
    grad_rows = grad_rows.reshape(tokens, width)
    gate_up_pre = plain_product(normed_two, gate_up)
    gate_pre, up_pre = gate_up_pre[:, :hidden_width], gate_up_pre[:, hidden_width:]
    activated, gelu_back = jax.vjp(jax.nn.gelu, gate_pre)
    hidden = (activated * up_pre).astype(jnp.bfloat16)
    grad_hidden = plain_product(grad_rows, down_full)
    grad_pre = jnp.concatenate(
        [
            gelu_back(grad_hidden * up_pre)[0].astype(jnp.bfloat16),
            (grad_hidden * activated).astype(jnp.bfloat16),
        ],
        axis=1,
    )
    grad_gate_up = left_transposed(normed_two, grad_pre).astype(jnp.bfloat16)
    grad_down = left_transposed(grad_rows, hidden).astype(jnp.bfloat16)
    residual_low, residual_grad, gain_two_part, grad_pieces, *sums = back(
        grad_pre, gate_up, residual, grad_own, gain_two, output_full, grad_gate_up, grad_down
    )
    ffn_slots = [move(sums[k], spread_slot(k)) for k in range(2)]
    qkv_grad_pieces, line_grad = attend_back(
        lengths, grad_pieces, rev_line, context_wide, lse, qkv_all
    )
    qkv_grad_pieces, *ffn_slots = lax.optimization_barrier((qkv_grad_pieces, *ffn_slots))
    *attn_sums, home, layer, small = leave(
        qkv_grad_pieces,
        normed_one,
        qkv_weight,
        token_low,
        residual_grad,
        gain_one,
        residual_low,
        context,
        hidden,
        down_full,
        residual,
        gain_two_part,
        line_grad,
        rev_buckets,
    )
    token_share = home.astype(jnp.float32).reshape(batch_count, slot_count, part_width)
    layer_out = layer.reshape(batch_count, slot_count, part_width)

    def own_columns(first, size):
        cut = [s[:, first : first + size].astype(jnp.float32) for s in ffn_slots]
        return jnp.concatenate(
            [jnp.where(z_low == 0, cut[0], cut[1]), jnp.where(z_low == 0, cut[1], cut[0])], axis=1
        )

    query_sum, key_sum, value_sum, output_sum = (s.astype(jnp.float32) for s in attn_sums)
    gate_sum, up_sum, down_sum = (own_columns(i * hidden_width, hidden_width) for i in range(3))
    table_sum = lax.dynamic_slice_in_dim(
        small[4].reshape(-1, 4 * heads), fsdp_index * heads, heads, 1
    )
    return (
        layer_out,
        token_share,
        small[:2].reshape(-1),
        query_sum,
        key_sum,
        value_sum,
        output_sum,
        table_sum,
        small[2:4].reshape(-1),
        gate_sum,
        up_sum,
        down_sum,
    )


def solution(mesh):
    placed = (
        P(None, "seq", "fsdp"),
        P(None, "seq", "fsdp"),
        P("seq"),
        P("seq", "fsdp"),
        P("seq", "fsdp"),
        P("seq", "fsdp"),
        P("seq", "fsdp"),
        P("seq", "fsdp"),
        P("seq"),
        P("seq", "fsdp"),
        P("seq", "fsdp"),
        P("seq", "fsdp"),
        P(),
        P(),
    )
    return jax.shard_map(
        fast_shards if (mesh.shape["seq"], mesh.shape["fsdp"]) == (8, 4) else shards,
        mesh=mesh,
        in_specs=placed,
        out_specs=(
            P(None, "seq", "fsdp"),
            P(None, "seq", "fsdp"),
            P("seq"),
            P("seq", "fsdp"),
            P("seq", "fsdp"),
            P("seq", "fsdp"),
            P("seq", "fsdp"),
            P("seq", "fsdp"),
            P("seq"),
            P("seq", "fsdp"),
            P("seq", "fsdp"),
            P("seq", "fsdp"),
        ),
        check_vma=False,
    )
```

```python
from functools import partial

import jax
import jax.numpy as jnp
from jax import lax
from jax.experimental import pallas as pl
from jax.experimental.pallas import tpu as pltpu
from jax.sharding import PartitionSpec as P

DH = 64


epsilon = 1e-06
highest = lax.Precision.HIGHEST
masked_score = -1e30
root_two_over_pi = 0.7978845608028654


def plain_product(left, right):
    return jnp.dot(left, right, preferred_element_type=jnp.float32)


def right_transposed(left, right):
    return lax.dot_general(
        left, right, (((1,), (1,)), ((), ())), preferred_element_type=jnp.float32
    )


def left_transposed(left, right):
    return lax.dot_general(
        left, right, (((0,), (0,)), ((), ())), preferred_element_type=jnp.float32
    )


def normalize(rows, gain):
    row_scale = lax.rsqrt(jnp.mean(rows * rows, axis=-1, keepdims=True) + epsilon)
    unit_rows = rows * row_scale
    return (unit_rows, row_scale, (unit_rows * gain.astype(jnp.float32)).astype(jnp.bfloat16))


def norm_back(grad_normed, unit_rows, row_scale, gain):
    weighted = grad_normed * gain.astype(jnp.float32)
    return row_scale * (
        weighted - unit_rows * jnp.mean(weighted * unit_rows, axis=-1, keepdims=True)
    )


def to_heads(rows, batch_count, head_size):
    slot_count = rows.shape[0] // batch_count
    number_of_heads = rows.shape[1] // head_size
    return rows.reshape(batch_count, slot_count, number_of_heads, head_size).transpose(2, 0, 1, 3)


def from_heads(blocks):
    number_of_heads, batch_count, slot_count, head_size = blocks.shape
    return blocks.transpose(1, 2, 0, 3).reshape(
        batch_count * slot_count, number_of_heads * head_size
    )


def bias_rows(bias_line, first_query, slot_count, length):
    span = slot_count + length - 1
    segment = lax.dynamic_slice_in_dim(bias_line, length - first_query - slot_count, span)
    flat = jnp.tile(segment, slot_count)
    skewed = flat[slot_count - 1 : slot_count - 1 + slot_count * (span - 1)].reshape(
        slot_count, span - 1
    )
    return skewed[:, :length]


def bias_rows_back(block_grad, first_query, slot_count, length, line_length):
    span = slot_count + length - 1
    widened = jnp.pad(block_grad, ((0, 0), (0, span - 1 - length)))
    flat = jnp.pad(widened.reshape(-1), (slot_count - 1, 1))
    segment_grad = jnp.sum(flat.reshape(slot_count, span), axis=0)
    return lax.dynamic_update_slice_in_dim(
        jnp.zeros((line_length,), jnp.float32), segment_grad, length - first_query - slot_count, 0
    )


def full_features(block):
    gathered = lax.all_gather(block, "fsdp", axis=2, tiled=True)
    return gathered.reshape(gathered.shape[0] * gathered.shape[1], gathered.shape[2])


def feature_total(partial_rows):
    return lax.psum(partial_rows, "fsdp")


def shards(
    tokens_in,
    cotangent,
    gain_attn,
    query_weight,
    key_weight,
    value_weight,
    output_weight,
    bias_table,
    gain_ffn,
    gate_weight,
    up_weight,
    down_weight,
    lengths,
    buckets,
):
    batch_count, slot_count, part_width = tokens_in.shape
    head_size = DH
    seq_index = lax.axis_index("seq")
    fsdp_index = lax.axis_index("fsdp")
    length = slot_count * lax.axis_size("seq")
    line_length = buckets.shape[0]
    first_query = seq_index * slot_count
    positions = jnp.arange(length, dtype=jnp.int32)
    query_positions = first_query + jnp.arange(slot_count, dtype=jnp.int32)
    key_valid = positions[None, :] < lengths[:, None]
    own_valid = query_positions[None, :] < lengths[:, None]
    gain_one, query_full, key_full, value_full, output_full, table_full = (
        lax.all_gather(gain_attn, "seq", axis=0, tiled=True),
        lax.all_gather(query_weight, "seq", axis=0, tiled=True),
        lax.all_gather(key_weight, "seq", axis=0, tiled=True),
        lax.all_gather(value_weight, "seq", axis=0, tiled=True),
        lax.all_gather(output_weight, "seq", axis=0, tiled=True),
        lax.all_gather(bias_table, "seq", axis=0, tiled=True),
    )
    token_rows = full_features(tokens_in).astype(jnp.float32)
    unit_one, scale_one, normed_one = normalize(token_rows, gain_one)
    query_heads = to_heads(
        plain_product(normed_one, query_full).astype(jnp.bfloat16), batch_count, head_size
    )
    key_heads = to_heads(
        plain_product(normed_one, key_full).astype(jnp.bfloat16), batch_count, head_size
    )
    value_heads = to_heads(
        plain_product(normed_one, value_full).astype(jnp.bfloat16), batch_count, head_size
    )
    number_of_heads = query_heads.shape[0]
    flat_shape = (number_of_heads, batch_count, slot_count * head_size)
    gathered_keys, gathered_values = (
        lax.all_gather(key_heads.reshape(flat_shape), "seq", axis=2, tiled=True),
        lax.all_gather(value_heads.reshape(flat_shape), "seq", axis=2, tiled=True),
    )
    all_keys = gathered_keys.reshape(number_of_heads, batch_count, length, head_size)
    all_values = gathered_values.reshape(number_of_heads, batch_count, length, head_size)
    bucket_hot = (
        buckets[:, None] == jnp.arange(table_full.shape[0], dtype=jnp.int32)[None, :]
    ).astype(jnp.float32)
    offset_bias = lax.dot_general(
        table_full.astype(jnp.float32), bucket_hot, (((0,), (1,)), ((), ())), precision=highest
    )

    def masked_scores(query_tile_rows, key_tile_rows, bias_block):
        raw = (
            jnp.einsum(
                "jht,jxt->jhx", query_tile_rows, key_tile_rows, preferred_element_type=jnp.float32
            )
            + bias_block[None]
        )
        return jnp.where(key_valid[:, None, :], raw, masked_score)

    def attend(inputs):
        query_tile_rows, key_tile_rows, value_tile_rows, bias_line = inputs
        scores = masked_scores(
            query_tile_rows, key_tile_rows, bias_rows(bias_line, first_query, slot_count, length)
        )
        row_peak = jnp.max(scores, axis=-1, keepdims=True)
        raised = jnp.exp(scores - row_peak)
        denominator = jnp.sum(raised, axis=-1, keepdims=True)
        weights_reduced_precision = (raised / denominator).astype(jnp.bfloat16)
        context = jnp.einsum(
            "wot,wtf->wof",
            weights_reduced_precision,
            value_tile_rows,
            preferred_element_type=jnp.float32,
        ).astype(jnp.bfloat16)
        return (context, (row_peak + jnp.log(denominator))[..., 0])

    context_heads, log_totals = lax.map(attend, (query_heads, all_keys, all_values, offset_bias))
    context_rows = from_heads(context_heads)
    residual = token_rows + feature_total(right_transposed(context_rows, output_full))
    gain_two, gate_full, up_full, down_full = (
        lax.all_gather(gain_ffn, "seq", axis=0, tiled=True),
        lax.all_gather(gate_weight, "seq", axis=0, tiled=True),
        lax.all_gather(up_weight, "seq", axis=0, tiled=True),
        lax.all_gather(down_weight, "seq", axis=0, tiled=True),
    )
    unit_two, scale_two, normed_two = normalize(residual, gain_two)
    gate_pre = plain_product(normed_two, gate_full)
    up_pre = plain_product(normed_two, up_full)
    activated, gelu_back = jax.vjp(jax.nn.gelu, gate_pre)
    hidden = (activated * up_pre).astype(jnp.bfloat16)
    ffn_share = lax.psum_scatter(
        right_transposed(hidden, down_full), "fsdp", scatter_dimension=1, tiled=True
    )
    residual_share = lax.dynamic_slice_in_dim(residual, fsdp_index * part_width, part_width, 1)
    layer_out = (
        (residual_share + ffn_share)
        .astype(jnp.bfloat16)
        .reshape(batch_count, slot_count, part_width)
    )
    masked_cot = jnp.where(own_valid[:, :, None], cotangent, jnp.zeros_like(cotangent))
    grad_rows = full_features(masked_cot)
    grad_down = left_transposed(grad_rows, hidden)
    grad_hidden = plain_product(grad_rows, down_full)
    grad_gate_pre = gelu_back(grad_hidden * up_pre)[0].astype(jnp.bfloat16)
    grad_up_pre = (grad_hidden * activated).astype(jnp.bfloat16)
    grad_gate = left_transposed(normed_two, grad_gate_pre)
    grad_up = left_transposed(normed_two, grad_up_pre)
    normed_two_grad = right_transposed(grad_gate_pre, gate_full) + right_transposed(
        grad_up_pre, up_full
    )
    second_gain_piece = jnp.sum(normed_two_grad * unit_two, axis=0)
    ffn_grads = (
        lax.psum_scatter(second_gain_piece, "seq", scatter_dimension=0, tiled=True),
        lax.psum_scatter(grad_gate, "seq", scatter_dimension=0, tiled=True),
        lax.psum_scatter(grad_up, "seq", scatter_dimension=0, tiled=True),
        lax.psum_scatter(grad_down, "seq", scatter_dimension=0, tiled=True),
    )
    residual_grad = grad_rows.astype(jnp.float32) + norm_back(
        feature_total(normed_two_grad), unit_two, scale_two, gain_two
    )
    residual_low = residual_grad.astype(jnp.bfloat16)
    grad_output = left_transposed(residual_low, context_rows)
    context_grad = to_heads(
        plain_product(residual_low, output_full).astype(jnp.bfloat16), batch_count, head_size
    )

    def query_side(inputs, with_keys):
        query_tile_rows, key_tile_rows, value_tile_rows, bias_line, log_total, context_tile_rows = (
            inputs
        )
        scores = masked_scores(
            query_tile_rows, key_tile_rows, bias_rows(bias_line, first_query, slot_count, length)
        )
        probs = jnp.exp(scores - log_total[..., None])
        prob_grad = jnp.einsum(
            "jht,jxt->jhx", context_tile_rows, value_tile_rows, preferred_element_type=jnp.float32
        )
        delta = jnp.sum(probs * prob_grad, axis=-1)
        score_gradient = (probs * (prob_grad - delta[..., None])).astype(jnp.bfloat16)
        query_grad = jnp.einsum(
            "wot,wtf->wof", score_gradient, key_tile_rows, preferred_element_type=jnp.float32
        )
        bias_grad = bias_rows_back(
            jnp.sum(score_gradient.astype(jnp.float32), axis=0),
            first_query,
            slot_count,
            length,
            line_length,
        )
        key_term = jnp.einsum(
            "xic,xil->xcl", score_gradient, query_tile_rows, preferred_element_type=jnp.float32
        )
        value_term = jnp.einsum(
            "xic,xil->xcl",
            probs.astype(jnp.bfloat16),
            context_tile_rows,
            preferred_element_type=jnp.float32,
        )
        return (query_grad, bias_grad, delta, key_term, value_term)

    side_inputs = (query_heads, all_keys, all_values, offset_bias, log_totals, context_grad)
    query_grad, bias_grad, delta, key_terms, value_terms = lax.map(
        partial(query_side, with_keys=True), side_inputs
    )
    wide_shape = (number_of_heads, batch_count, length * head_size)
    key_sums, value_sums = (
        lax.psum_scatter(key_terms.reshape(wide_shape), "seq", scatter_dimension=2, tiled=True),
        lax.psum_scatter(value_terms.reshape(wide_shape), "seq", scatter_dimension=2, tiled=True),
    )
    own_shape = (number_of_heads, batch_count, slot_count, head_size)
    query_low = from_heads(query_grad.astype(jnp.bfloat16))
    key_low = from_heads(key_sums.reshape(own_shape).astype(jnp.bfloat16))
    value_low = from_heads(value_sums.reshape(own_shape).astype(jnp.bfloat16))
    grad_query = left_transposed(normed_one, query_low)
    grad_key = left_transposed(normed_one, key_low)
    grad_value = left_transposed(normed_one, value_low)
    grad_table = lax.dot_general(bucket_hot, bias_grad, (((0,), (1,)), ((), ())), precision=highest)
    normed_one_grad = (
        right_transposed(query_low, query_full)
        + right_transposed(key_low, key_full)
        + right_transposed(value_low, value_full)
    )
    gain_one_part = jnp.sum(normed_one_grad * unit_one, axis=0)
    attn_grads = (
        lax.psum_scatter(gain_one_part, "seq", scatter_dimension=0, tiled=True),
        lax.psum_scatter(grad_query, "seq", scatter_dimension=0, tiled=True),
        lax.psum_scatter(grad_key, "seq", scatter_dimension=0, tiled=True),
        lax.psum_scatter(grad_value, "seq", scatter_dimension=0, tiled=True),
        lax.psum_scatter(grad_output, "seq", scatter_dimension=0, tiled=True),
        lax.psum_scatter(grad_table, "seq", scatter_dimension=0, tiled=True),
    )
    token_grad = residual_grad + norm_back(
        feature_total(normed_one_grad), unit_one, scale_one, gain_one
    )
    token_share = lax.dynamic_slice_in_dim(
        token_grad, fsdp_index * part_width, part_width, 1
    ).reshape(batch_count, slot_count, part_width)
    gain_one_sum, gain_two_sum = lax.psum((attn_grads[0], ffn_grads[0]), "fsdp")
    return (
        layer_out,
        token_share,
        gain_one_sum,
        attn_grads[1],
        attn_grads[2],
        attn_grads[3],
        attn_grads[4],
        attn_grads[5],
        gain_two_sum,
        ffn_grads[1],
        ffn_grads[2],
        ffn_grads[3],
    )


BLOCK = 128
BOTH = ("seq", "fsdp")


def move(value, target):
    pairs = []
    for z in range(4):
        for y in range(2):
            for x in range(2):
                for c in range(2):
                    zt, yt, xt, ct = target(z, y, x, c)
                    pairs.append(((2 * z + y) * 4 + 2 * x + c, (2 * zt + yt) * 4 + 2 * xt + ct))
    return lax.ppermute(value, BOTH, pairs)


def spread_slot(k):
    return lambda z, y, x, c: (2 * c + (k ^ (z & 1)), y, x, z >> 1)


KEYS = 512
QUERIES = 512
WIDE_QUERIES = 1024
OFFSET = 1920


def skew_table(rev_ref, table):
    width = rev_ref.shape[1]
    line = jnp.broadcast_to(rev_ref[...], (8, width))
    for first in range(0, BLOCK, 8):
        table[first : first + 8, :] = pltpu.roll(
            line, (width - (BLOCK - 1) + first) % width, axis=1, stride=1, stride_axis=0
        )


def place_of(piece, part, z, y, x, c):
    c_rel, d = part // 4, part % 4
    b = jnp.bitwise_xor(x, piece // 2)
    block = (
        4 * jnp.bitwise_xor(z, d)
        + 2 * jnp.bitwise_xor(y, piece % 2)
        + jnp.bitwise_xor(c, c_rel)
    )
    return b, block


def part_of(b, block, z, y, x, c):
    piece = 2 * jnp.bitwise_xor(b, x) + jnp.bitwise_xor((block // 2) % 2, y)
    part = 4 * jnp.bitwise_xor(block % 2, c) + jnp.bitwise_xor(block // 4, z)
    return piece, part


def lanes(first, count):
    return pl.ds(pl.multiple_of(first, BLOCK), count)


def attend_kernel(sc, pieces, rev_ref, ctx_ref, ctx_wide, lse_ref, qkv, keys, table):
    z, y, x, c = position()
    for piece in range(4):
        for part in range(8):
            b, block = place_of(piece, part, z, y, x, c)
            data = pieces[piece, :, :, part * BLOCK : (part + 1) * BLOCK]
            qkv[b, :, :, lanes(block * BLOCK, BLOCK)] = data
            keys[b, lanes(block * BLOCK, BLOCK), :] = data[1].T
    skew_table(rev_ref, table)
    length = qkv.shape[-1]
    for b in range(2):
        valid = sc[b]
        full = valid // KEYS

        @pl.loop(0, length // WIDE_QUERIES)
        def _(i):
            first_query = i * WIDE_QUERIES
            query = qkv[b, 0, :, lanes(first_query, WIDE_QUERIES)]

            def tile(j, carry, masked):
                peak, total, acc = carry
                first_key = j * KEYS
                score = jnp.dot(
                    keys[b, lanes(first_key, KEYS), :], query, preferred_element_type=jnp.float32
                )
                score = score + jnp.concatenate(
                    [
                        table[:, lanes(first_query - first_key + OFFSET - t, WIDE_QUERIES)]
                        for t in range(0, KEYS, BLOCK)
                    ],
                    axis=0,
                )
                if masked:
                    position = first_key + lax.broadcasted_iota(jnp.int32, (KEYS, WIDE_QUERIES), 0)
                    score = jnp.where(position < valid, score, masked_score)
                now = jnp.maximum(peak, jnp.max(score, axis=0, keepdims=True))
                scale = jnp.exp(peak - now)
                prob = jnp.exp(score - now)
                total = total * scale + jnp.sum(prob, axis=0, keepdims=True)
                acc = acc * scale + jnp.dot(
                    qkv[b, 2, :, lanes(first_key, KEYS)],
                    prob.astype(jnp.bfloat16),
                    preferred_element_type=jnp.float32,
                )
                return now, total, acc

            carry = (
                jnp.full((1, WIDE_QUERIES), masked_score, jnp.float32),
                jnp.zeros((1, WIDE_QUERIES), jnp.float32),
                jnp.zeros((DH, WIDE_QUERIES), jnp.float32),
            )
            carry = lax.fori_loop(0, full, lambda j, s: tile(j, s, False), carry)
            peak, total, acc = lax.cond(
                valid > full * KEYS, lambda s: tile(full, s, True), lambda s: s, carry
            )
            context = acc / total
            ctx_wide[b, :, lanes(first_query, WIDE_QUERIES)] = context
            lse_ref[b, :, lanes(first_query, WIDE_QUERIES)] = peak + jnp.log(total)
            low = context.astype(jnp.bfloat16)
            for t in range(WIDE_QUERIES // BLOCK):
                piece, part = part_of(b, i * (WIDE_QUERIES // BLOCK) + t, z, y, x, c)
                ctx_ref[piece, :, lanes(part * BLOCK, BLOCK)] = low[:, t * BLOCK : (t + 1) * BLOCK]


def attend(scalars, pieces, rev_line):
    _, _, head_size, tokens = pieces.shape
    length = tokens * 2
    smem, vmem = pl.BlockSpec(memory_space=pltpu.SMEM), pl.BlockSpec(memory_space=pltpu.VMEM)
    return pl.pallas_call(
        attend_kernel,
        name="attend",
        out_shape=[
            jax.ShapeDtypeStruct((4, head_size, tokens), jnp.bfloat16),
            jax.ShapeDtypeStruct((2, head_size, length), jnp.float32),
            jax.ShapeDtypeStruct((2, 1, length), jnp.float32),
            jax.ShapeDtypeStruct((2, 3, head_size, length), jnp.bfloat16),
        ],
        in_specs=[smem] + [vmem] * 2,
        out_specs=[vmem] * 4,
        scratch_shapes=[
            pltpu.VMEM((2, length, head_size), jnp.bfloat16),
            pltpu.VMEM((BLOCK, rev_line.shape[1]), jnp.float32),
        ],
        cost_estimate=pl.CostEstimate(
            flops=46_000_000_000, bytes_accessed=4 << 20, transcendentals=0
        ),
        compiler_params=pltpu.CompilerParams(vmem_limit_bytes=48 << 20),
    )(scalars, pieces, rev_line)


def attend_back_kernel(
    sc, pieces, rev_ref, ctx_wide, lse_ref, qkv,
    out_ref, line_ref,
    queries, keys, values, grads, grads_t, delta, query_sum, key_sum, value_sum, table, table_sum,
):
    z, y, x, c = position()
    length = qkv.shape[-1]
    for piece in range(4):
        for part in range(8):
            b, block = place_of(piece, part, z, y, x, c)
            data = pieces[piece, :, part * BLOCK : (part + 1) * BLOCK]
            grads_t[b, :, lanes(block * BLOCK, BLOCK)] = data
            grads[b, lanes(block * BLOCK, BLOCK), :] = data.T
    for b in range(2):
        for first in range(0, length, BLOCK):
            here = slice(first, first + BLOCK)
            queries[b, here, :] = qkv[b, 0, :, here].T
            keys[b, here, :] = qkv[b, 1, :, here].T
            values[b, here, :] = qkv[b, 2, :, here].T
        delta[b] = jnp.sum(
            ctx_wide[b] * grads_t[b].astype(jnp.float32), axis=0, keepdims=True
        )
    skew_table(rev_ref, table)
    table_sum[...] = jnp.zeros_like(table_sum)
    query_sum[...] = jnp.zeros_like(query_sum)
    out_ref[...] = jnp.zeros_like(out_ref)
    for b in range(2):
        valid = sc[b]
        full = valid // KEYS
        count = (valid + QUERIES - 1) // QUERIES

        def key_step(j, masked):
            first_key = j * KEYS
            key, value = keys[b, lanes(first_key, KEYS), :], values[b, lanes(first_key, KEYS), :]
            key_t = qkv[b, 1, :, lanes(first_key, KEYS)]
            key_sum[...] = jnp.zeros_like(key_sum)
            value_sum[...] = jnp.zeros_like(value_sum)

            @pl.loop(0, count)
            def _(i):
                first_query = i * QUERIES
                here = lanes(first_query, QUERIES)
                score = jnp.dot(key, qkv[b, 0, :, here], preferred_element_type=jnp.float32)
                score = score + jnp.concatenate(
                    [
                        table[:, lanes(first_query - first_key + OFFSET - t, QUERIES)]
                        for t in range(0, KEYS, BLOCK)
                    ],
                    axis=0,
                )
                if masked:
                    position = first_key + lax.broadcasted_iota(jnp.int32, (KEYS, QUERIES), 0)
                    score = jnp.where(position < valid, score, masked_score)
                prob = jnp.exp(score - lse_ref[b, :, here])
                prob_grad = jnp.dot(value, grads_t[b, :, here], preferred_element_type=jnp.float32)
                score_grad = (prob * (prob_grad - delta[b, :, here])).astype(jnp.bfloat16)
                value_sum[...] += jnp.dot(
                    prob.astype(jnp.bfloat16), grads[b, here, :], preferred_element_type=jnp.float32
                )
                key_sum[...] += jnp.dot(
                    score_grad, queries[b, here, :], preferred_element_type=jnp.float32
                )
                query_sum[b, :, here] += jnp.dot(
                    key_t, score_grad, preferred_element_type=jnp.float32
                )
                for t in range(0, KEYS, BLOCK):
                    table_sum[:, lanes(first_query - first_key + OFFSET - t, QUERIES)] += score_grad[
                        t : t + BLOCK
                    ].astype(jnp.float32)

            for t in range(KEYS // BLOCK):
                piece, part = part_of(b, j * (KEYS // BLOCK) + t, z, y, x, c)
                rows = slice(t * BLOCK, (t + 1) * BLOCK)
                at = lanes(part * BLOCK, BLOCK)
                out_ref[piece, 1, :, at] = key_sum[rows, :].T.astype(jnp.bfloat16)
                out_ref[piece, 2, :, at] = value_sum[rows, :].T.astype(jnp.bfloat16)

        pl.loop(0, full)(lambda j: key_step(j, False))
        pl.when(valid > full * KEYS)(lambda: key_step(full, True))
        for block in range(length // BLOCK):
            piece, part = part_of(b, block, z, y, x, c)
            out_ref[piece, 0, :, lanes(part * BLOCK, BLOCK)] = query_sum[
                b, :, block * BLOCK : (block + 1) * BLOCK
            ].astype(jnp.bfloat16)
    width = table_sum.shape[1]
    line = jnp.zeros((8, width), jnp.float32)
    for first in range(0, BLOCK, 8):
        line = line + pltpu.roll(table_sum[first : first + 8, :], BLOCK - 8 - first, axis=1)
    ahead = 7 - lax.broadcasted_iota(jnp.int32, (8, width), 0)
    for bit in (1, 2, 4):
        line = jnp.where((ahead & bit) != 0, pltpu.roll(line, bit, axis=1), line)
    line_ref[...] = jnp.sum(line, axis=0, keepdims=True)


def attend_back(scalars, pieces, rev_line, ctx_wide, lse, qkv):
    _, head_size, tokens = pieces.shape
    length = tokens * 2
    smem, vmem = pl.BlockSpec(memory_space=pltpu.SMEM), pl.BlockSpec(memory_space=pltpu.VMEM)
    low = pltpu.VMEM((2, length, head_size), jnp.bfloat16)
    return pl.pallas_call(
        attend_back_kernel,
        name="attend_back",
        out_shape=[
            jax.ShapeDtypeStruct((4, 3, head_size, tokens), jnp.bfloat16),
            jax.ShapeDtypeStruct(rev_line.shape, jnp.float32),
        ],
        in_specs=[smem] + [vmem] * 5,
        out_specs=[vmem] * 2,
        scratch_shapes=[
            low, low, low, low,
            pltpu.VMEM((2, head_size, length), jnp.bfloat16),
            pltpu.VMEM((2, 1, length), jnp.float32),
            pltpu.VMEM((2, head_size, length), jnp.float32),
            pltpu.VMEM((KEYS, head_size), jnp.float32),
            pltpu.VMEM((KEYS, head_size), jnp.float32),
            pltpu.VMEM((BLOCK, rev_line.shape[1]), jnp.float32),
            pltpu.VMEM((BLOCK, rev_line.shape[1]), jnp.float32),
        ],
        cost_estimate=pl.CostEstimate(
            flops=46_000_000_000, bytes_accessed=4 << 20, transcendentals=0
        ),
        compiler_params=pltpu.CompilerParams(vmem_limit_bytes=48 << 20),
    )(scalars, pieces, rev_line, ctx_wide, lse, qkv)


CHUNKS = 2
MESH_ID = pl.DeviceIdType.MESH
IN_VMEM = pl.BlockSpec(memory_space=pltpu.VMEM)
IN_PLACE = pl.BlockSpec(memory_space=pl.ANY)
COPIES = pltpu.SemaphoreType.DMA


def flip(a, b):
    return a + b - 2 * a * b


def flip_pair(a, b):
    return 2 * flip(a // 2, b // 2) + flip(a % 2, b % 2)


def position():
    s, f = lax.axis_index("seq"), lax.axis_index("fsdp")
    return s // 2, s % 2, f // 2, f % 2


def device(z, y, x, c):
    return (2 * z + y, 2 * x + c)


def ring_of(z):
    high, low = z // 2, z % 2
    following = 2 * low + 1 - high
    return following, (2 * (1 - low) + high, 2 * (1 - high) + 1 - low, following)


def greet(z, y, x, c):
    peers = []
    for d in range(1, 8):
        peers.append(device(z, flip(y, d // 4), flip(x, (d // 2) % 2), flip(c, d % 2)))
        if d > 1:
            peers.append(device(flip_pair(z, d // 2), y, x, flip(c, d % 2)))
    barrier = pltpu.get_barrier_semaphore()
    for peer in peers:
        pl.semaphore_signal(barrier, inc=1, device_id=peer, device_id_type=MESH_ID)
    pl.semaphore_wait(barrier, len(peers))


def remote(source, target, send, recv, to):
    return pltpu.make_async_remote_copy(
        src_ref=source,
        dst_ref=target,
        send_sem=send,
        recv_sem=recv,
        device_id=to,
        device_id_type=MESH_ID,
    )


class Links:
    def __init__(self, send, recv):
        self.send, self.recv, self.used, self.sent = send, recv, 0, []

    def go(self, source, target, to):
        i = self.used
        self.used += 1
        made = remote(source, target, self.send.at[i], self.recv.at[i], to)
        made.start()
        self.sent.append(made)
        return made

    def go_unless(self, own, source, target, to, send=None, recv=None):
        if send is None:
            send, recv = self.send.at[self.used], self.recv.at[self.used]
            self.used += 1
        made = remote(source, target, send, recv, to)
        if own is None:
            made.start()
            self.sent.append(made)
            return made
        local = pltpu.make_async_copy(source, target, recv)
        pl.when(own)(lambda: local.start())
        pl.when(jnp.logical_not(own))(lambda: made.start())
        self.sent.append((own, made))
        return made

    def go_if(self, there, here, source, target, send, recv, to):
        made = remote(source, target, send, recv, to)
        pl.when(there)(lambda: made.start())
        if here is not None:
            local = pltpu.make_async_copy(source, target, recv)
            pl.when(here)(lambda: local.start())
        self.sent.append((jnp.logical_not(there), made))

    def done(self, made):
        made.wait_send()
        self.sent = [m for m in self.sent if m is not made]

    def finish(self):
        for made in self.sent:
            if isinstance(made, tuple):
                pl.when(jnp.logical_not(made[0]))(lambda made=made: made[1].wait_send())
            else:
                made.wait_send()


def share_start(links, rows_all, me):
    z, y, x, c = me
    following, _ = ring_of(z)
    rows = rows_all.shape[1] // CHUNKS
    ring = []
    for h in range(CHUNKS):
        here = pl.ds(h * rows, rows)
        target = rows_all.at[flip_pair(following, z), here]
        ring.append(links.go(rows_all.at[0, here], target, device(following, y, x, c)))
    core = [links.go(rows_all.at[0], rows_all.at[4], device(z, y, x, 1 - c))]
    return [ring], core


def share_step(links, rows_all, me, state, step):
    z, y, x, c = me
    following, back = ring_of(z)
    rows = rows_all.shape[1] // CHUNKS
    ring, core = state
    slot = flip_pair(z, back[step - 1])
    sent = []
    for h in range(CHUNKS):
        here = pl.ds(h * rows, rows)
        ring[-1][h].wait_recv()
        source = rows_all.at[slot, here]
        if step < 3:
            target = rows_all.at[flip_pair(following, back[step - 1]), here]
            sent.append(links.go(source, target, device(following, y, x, c)))
        core.append(links.go(source, rows_all.at[4 + slot, here], device(z, y, x, 1 - c)))
    ring.append(sent)


def share_end(state):
    for made in state[1]:
        made.wait_recv()


def sum_order(z):
    _, back = ring_of(z)
    return [flip_pair(z, b) for b in back] + [0]


def column_go(links, me, k, source, target):
    z, y, x, c = me
    own = z // 2 == c if k == 0 else None
    to = device(2 * c + flip(k, z % 2), y, x, z // 2)
    return links.go_unless(own, source, target, to)


def arrived(place, sem):
    pltpu.make_async_copy(place, place, sem).wait()


def spread_go(links, me, k, source, full, send, recv):
    z, y, x, c = me
    rows = source.shape[0]
    first = pl.multiple_of((4 * c + 2 * flip(k, z % 2) + y) * rows, rows)
    target = full.at[pl.ds(first, rows), :]
    for dy, dx in ((0, 1), (1, 0), (0, 0)):
        own = None if dy + dx else c == x
        to = device(z, flip(y, dy), flip(x, dx), x)
        links.go_unless(own, source, target, to, send.at[k, dy, dx], recv.at[k, dy, c])


def spread_relay(links, me, full, send, recv):
    z, y, x, c = me
    odd = flip(c, x)
    k, step = 1 - odd, 1 - odd
    rows = full.shape[0] // 8
    to = device(z, flip(y, odd), flip(x, 1 - odd), c)
    for r in range(2):
        first = pl.multiple_of((4 * r + 2 * flip(k, z % 2) + flip(y, step)) * rows, rows)
        here = full.at[pl.ds(first, rows), :]
        arrived(here, recv.at[k, step, r])
        made = remote(here, here, send.at[r, 1, 1], recv.at[k, 1, r], to)
        made.start()
        links.sent.append(made)


def spread_wait(me, full, recv):
    z, y, x, c = me
    odd = flip(c, x)
    here = full.at[pl.ds(0, full.shape[0] // 8), :]
    for k, step in ((1 - odd, odd), (odd, 0), (odd, 1)):
        for r in range(2):
            arrived(here, recv.at[k, step, r])


def join_go(links, me, k, grads, into, relay, send, recv, relay_recv):
    z, y, x, c = me
    odd = flip(c, x) == 1
    even = jnp.logical_not(odd)
    rows = into.shape[2]
    for r in range(2):

        def block(step):
            index = 4 * r + 2 * flip(k, z % 2) + flip(y, step)
            return grads.at[pl.ds(pl.multiple_of(index * rows, rows), rows), :]

        same, other = device(z, y, c, r), device(z, 1 - y, c, r)
        mine = jnp.logical_and(even, c == r)
        partner = jnp.logical_and(even, c != r)
        links.go_if(
            partner, mine, block(0), into.at[k, 0], send.at[k, 0, r], recv.at[k, 0], same
        )
        if k == 0:
            links.go_if(even, None, block(1), into.at[0, 1], send.at[0, 1, r], recv.at[0, 1], other)
            to = device(z, 1 - y, x, c)
        else:
            links.go_if(odd, None, block(0), into.at[1, 1], send.at[1, 1, r], recv.at[1, 1], same)
            to = device(z, y, c, c)
        links.go_if(odd, None, block(1), relay.at[r], send.at[k, 2, r], relay_recv.at[r], to)


def join_relay(links, me, grads, into, relay, send, recv, relay_recv):
    z, y, x, c = me
    odd = flip(c, x)
    k, step = 1 - odd, 1 - odd
    rows = into.shape[2]
    for r in range(2):
        arrived(relay.at[r], relay_recv.at[r])
        index = 4 * r + 2 * flip(k, z % 2) + flip(y, step)
        own = grads[pl.ds(pl.multiple_of(index * rows, rows), rows), :]
        total = relay[r].astype(jnp.float32) + own.astype(jnp.float32)
        relay[r] = total.astype(jnp.bfloat16)
        to = device(z, flip(y, step), c, r)
        made = remote(relay.at[r], into.at[k, 2], send.at[0, 3, r], recv.at[k, 2], to)
        made.start()
        links.sent.append(made)


def join_sum(k, into, recv):
    total = 0.0
    for j in range(3):
        arrived(into.at[k, j], recv.at[k, j])
        total = total + into[k, j].astype(jnp.float32)
    return total.astype(jnp.bfloat16)


def rms(rows):
    return lax.rsqrt(jnp.mean(rows * rows, axis=-1, keepdims=True) + epsilon)


def lane_sum(values):
    return jnp.sum(values, axis=-1, keepdims=True)


def head_of(z, y, x, c, heads):
    return 2 * c + z // 2, (z % 2) * (heads // 2) + 2 * x + y


def entry_kernel(
    lengths, tok_ref, cot_ref, small_ref, bucket_ref, wq_ref, wk_ref, wv_ref, wo_ref, wg_ref,
    rows_ref, normed, grads, pieces, weight, gain_one, gain_two, rev_ref, slots_o, slots_g,
    tok_in, cot_in, held, qkv, small, send, recv, plane_send, plane_recv, local,
):
    me = z, y, x, c = position()
    greet(*me)
    links = Links(send, recv)
    f, part, half = 2 * x + c, tok_in.shape[2], tok_in.shape[1]

    def gather_rows(n, ref, into):
        def source(xd, cd):
            return ref.at[xd, pl.ds(pl.multiple_of(cd * half, half), half)]

        own = pltpu.make_async_copy(source(x, c), into.at[f], local.at[n])
        own.start()
        got = []
        for d in (1, 2, 3):
            xd, cd = flip(x, d // 2), flip(c, d % 2)
            got.append(links.go(source(xd, cd), into.at[f], device(z, y, xd, cd)))
        return own, got

    tok_own, tok_got = gather_rows(0, tok_ref, tok_in)
    small[f, z, y] = small_ref[...]
    small_got = []
    for d in (1, 2, 3):
        here = small.at[f, z, y]
        small_got.append(links.go(here, here, device(flip_pair(z, d), y, x, c)))
    group_width = wq_ref.shape[1] // 2
    way = []
    for k in range(2):
        cut = pl.ds(pl.multiple_of(flip(k, z % 2) * group_width, group_width), group_width)
        for n, ref in enumerate((wq_ref, wk_ref, wv_ref)):
            target = held.at[k, :, n * group_width : (n + 1) * group_width]
            way.append(column_go(links, me, k, ref.at[:, cut], target))
    cot_own, cot_got = gather_rows(1, cot_ref, cot_in)
    for made in small_got:
        made.wait_recv()
    here = small.at[f, :, y]
    links.go(here, here, device(z, 1 - y, x, c)).wait_recv()
    tables = []
    for d in (1, 2, 3):
        here = small.at[f]
        tables.append(links.go(here, here, device(z, y, flip(x, d // 2), flip(c, d % 2))))
    for i in range(4 * part // BLOCK):
        here = slice(i * BLOCK, (i + 1) * BLOCK)
        block = (i // 2) // 2, (i // 2) % 2
        gain_one[:, here] = small[f, block[0], block[1], i % 2 : i % 2 + 1, :]
        gain_two[:, here] = small[f, block[0], block[1], 2 + i % 2 : 3 + i % 2, :]
    tok_own.wait()
    for made in tok_got:
        made.wait_recv()
    wide = [tok_in[i].astype(jnp.float32) for i in range(4)]
    mean = sum(lane_sum(w * w) for w in wide) / (4 * part)
    scale = lax.rsqrt(mean + epsilon)
    for i in range(4):
        here = slice(i * part, (i + 1) * part)
        rows_ref[:, here] = tok_in[i]
        normed[0, :, here] = (wide[i] * scale * gain_one[:, here]).astype(jnp.bfloat16)
    first = share_start(links, normed, me)
    cot_own.wait()
    for made in cot_got:
        made.wait_recv()
    slot = (4 * z + 2 * y + c) * half + lax.broadcasted_iota(jnp.int32, (half, part), 0)
    valid = slot < jnp.where(x == 0, lengths[0], lengths[1])
    for i in range(4):
        grads[:, i * part : (i + 1) * part] = jnp.where(valid, cot_in[i], jnp.zeros_like(cot_in[i]))
    for k in range(2):
        for made in way[3 * k : 3 * k + 3]:
            made.wait_recv()
        spread_go(links, me, k, held.at[k], weight, plane_send, plane_recv)
    share_step(links, normed, me, first, 1)
    share_step(links, normed, me, first, 2)
    later = []
    half_ffn = wg_ref.shape[1] // 2
    for k in range(2):
        side = flip(k, z % 2)
        cut = pl.ds(pl.multiple_of(side * group_width, group_width), group_width)
        later.append(column_go(links, me, k, wo_ref.at[:, cut], slots_o.at[k]))
        cut = pl.ds(pl.multiple_of(side * half_ffn, half_ffn), half_ffn)
        later.append(column_go(links, me, k, wg_ref.at[:, cut], slots_g.at[k]))
    spread_relay(links, me, weight, plane_send, plane_recv)
    for made in tables:
        made.wait_recv()
    group = qkv.shape[1]
    heads = 2 * group
    source, place = head_of(z, y, x, c, heads)
    lane = lax.broadcasted_iota(jnp.int32, (1, BLOCK), 1)
    line = jnp.zeros(bucket_ref.shape, jnp.float32)
    per_block = 4
    for n in range(8 * per_block):
        block = n // per_block
        row = small[source, block // 2, block % 2, 4:5, :]
        value = lane_sum(jnp.where(lane == (n % per_block) * heads + place, row, 0.0))
        line = jnp.where(bucket_ref[...] == n, value, line)
    rev_ref[...] = line
    spread_wait(me, weight, plane_recv)
    rows = normed.shape[1]
    sent = []

    def project(d):
        out = jnp.dot(pair_of(normed, d), weight[...], preferred_element_type=jnp.float32)
        out = out.astype(jnp.bfloat16).T
        for side, slot in enumerate((d, 4 + d)):
            here = lanes(slot * rows, rows)
            cut = out[:, side * rows : (side + 1) * rows]
            qkv[:, :, :, here] = cut.reshape(3, group, DH, rows)
            pieces[0, :, :, here] = qkv[:, 2 * x + y, :, here]
            for e in (1, 2, 3):
                xd, yd = flip(x, e // 2), flip(y, e % 2)
                source = qkv.at[:, 2 * xd + yd, :, here]
                sent.append(links.go(source, pieces.at[e, :, :, here], device(z, yd, xd, c)))

    order = sum_order(z)
    first[1][0].wait_recv()
    project(0)
    for step in (1, 2, 3):
        if step == 3:
            share_step(links, normed, me, first, 3)
        for made in first[1][1 + CHUNKS * (step - 1) : 1 + CHUNKS * step]:
            made.wait_recv()
        project(order[step - 1])
    for made in sent + later:
        made.wait_recv()
    links.finish()


def low_array(*shape):
    return jax.ShapeDtypeStruct(shape, jnp.bfloat16)


def wide_array(*shape):
    return jax.ShapeDtypeStruct(shape, jnp.float32)


def low_space(*shape):
    return pltpu.VMEM(shape, jnp.bfloat16)


def entry(lengths, tokens_in, cotangent, small, rev_buckets, weights):
    _, slot_count, part = tokens_in.shape
    rows, width = slot_count // 2, 4 * part
    depth, cols = weights[0].shape
    group = cols // (2 * DH)
    wide = 3 * cols // 2
    return pl.pallas_call(
        entry_kernel,
        name="entry",
        out_shape=[
            low_array(rows, width),
            low_array(8, rows, width),
            low_array(rows, width),
            low_array(4, 3, DH, 8 * rows),
            low_array(8 * depth, wide),
            wide_array(1, width),
            wide_array(1, width),
            wide_array(*rev_buckets.shape),
            low_array(2, depth, cols // 2),
            low_array(2, depth, weights[4].shape[1] // 2),
        ],
        in_specs=[pl.BlockSpec(memory_space=pltpu.SMEM)]
        + [IN_PLACE] * 2
        + [IN_VMEM] * 2
        + [IN_PLACE] * 5,
        out_specs=[IN_VMEM] * 10,
        scratch_shapes=[
            low_space(4, rows, part),
            low_space(4, rows, part),
            low_space(2, depth, wide),
            low_space(3, group, DH, 8 * rows),
            pltpu.VMEM((4, 4, 2, 8, BLOCK), jnp.float32),
            COPIES((64,)),
            COPIES((64,)),
            COPIES((2, 2, 2)),
            COPIES((2, 2, 2)),
            COPIES((2,)),
        ],
        compiler_params=pltpu.CompilerParams(
            collective_id=1, has_side_effects=True, vmem_limit_bytes=48 << 20
        ),
    )(lengths, tokens_in, cotangent, small, rev_buckets, *weights)


def gelu_pair(t):
    inner = jnp.tanh(root_two_over_pi * (t + 0.044715 * (t * t * t)))
    half = 0.5 * (1.0 + inner)
    slope = half + 0.5 * t * (1.0 - inner * inner) * root_two_over_pi * (1.0 + 0.134145 * (t * t))
    return t * half, slope


def pair_of(ref, slot):
    return jnp.concatenate([ref[slot], ref[4 + slot]], axis=0)


def pair_go(links, me, core, i, terms, core_out, core_in):
    z, y, x, c = me
    size = terms.shape[0] // 2
    core_out[i] = terms[size:].astype(jnp.bfloat16)
    core.append(links.go(core_out.at[i], core_in.at[i], device(z, y, x, 1 - c)))
    return terms[:size]


def sum_step(links, me, core, ring, i, mine, core_in, ring_out, ring_in):
    z, y, x, c = me
    following, _ = ring_of(z)
    rows = mine.shape[0] // CHUNKS
    core.wait_recv()
    sent, last = [], []
    for h in range(CHUNKS):
        cut = slice(h * rows, (h + 1) * rows)
        here = pl.ds(h * rows, rows)
        value = mine[cut] + core_in[i, here, :].astype(jnp.float32)
        if i:
            ring[-1][h].wait_recv()
            value = value + ring_in[i - 1, here, :].astype(jnp.float32)
        if i < 3:
            ring_out[i, here, :] = value.astype(jnp.bfloat16)
            target = ring_in.at[i, here]
            sent.append(links.go(ring_out.at[i, here], target, device(following, y, x, c)))
        else:
            last.append(value)
    ring.append(sent)
    return last


def reduce_pair(links, me, state, i, terms, core_out, core_in, ring_out, ring_in):
    mine = pair_go(links, me, state[0], i, terms, core_out, core_in)
    return sum_step(links, me, state[0][i], state[1], i, mine, core_in, ring_out, ring_in)


def core_kernel(
    ctx_ref, rows_ref, gain_ref, own_ref, slots_o, slots_g, slot_ud0, slot_ud1,
    residual_ref, context, down, hidden, low, wide_ref, part_ref, pieces, in_gu, in_d,
    out_weight, gate_up, normed, grads, pre, ctx_all, heads_out, grad_gu, grad_d,
    mine, core_out, core_in, ring_out, ring_in, ring_out2, ring_in2,
    relay_gu, relay_d, send, recv, plane_send, plane_recv, join_send, join_recv, relay_recv,
):
    me = z, y, x, c = position()
    greet(*me)
    links = Links(send, recv)
    own = 2 * x + y
    heads = []
    for d in (1, 2, 3):
        xd, yd = flip(x, d // 2), flip(y, d % 2)
        heads.append(links.go(ctx_ref.at[d], ctx_all.at[own], device(z, yd, xd, c)))
    grads[0] = own_ref[...]
    second = share_start(links, grads, me)

    ffn = down.shape[1]
    fulls = out_weight, gate_up.at[:, :ffn], gate_up.at[:, ffn:], down

    def weight_go(n):
        slots = (
            (slots_o.at[0], slots_o.at[1]),
            (slots_g.at[0], slots_g.at[1]),
            (slot_ud0.at[:, :ffn], slot_ud1.at[:, :ffn]),
            (slot_ud0.at[:, ffn:], slot_ud1.at[:, ffn:]),
        )[n]
        for k in range(2):
            spread_go(links, me, k, slots[k], fulls[n], plane_send.at[n], plane_recv.at[n])

    def weight_relay(n):
        spread_relay(links, me, fulls[n], plane_send.at[n], plane_recv.at[n])

    def weight_wait(n):
        spread_wait(me, fulls[n], plane_recv.at[n])

    weight_go(0)
    ctx_all[own] = ctx_ref[0]
    for made in heads:
        made.wait_recv()
    group, size, tokens = ctx_all.shape
    rows, width = residual_ref.shape
    depth = gate_up.shape[0] // 8
    half_tokens = tokens // 2
    context[...] = ctx_all[...].reshape(group * size, tokens).T
    weight_relay(0)
    weight_go(1)
    weight_go(2)
    weight_wait(0)
    order = sum_order(z)

    def first_row(block):
        return pl.multiple_of(block * rows, rows)

    def pair_rows(ref, d):
        return jnp.concatenate(
            [ref[pl.ds(first_row(d), rows), :], ref[pl.ds(first_row(4 + d), rows), :]], axis=0
        )

    state = [], []
    for i in range(4):
        terms = right_transposed(pair_rows(context, order[i]), out_weight[...])
        last = reduce_pair(links, me, state, i, terms, core_out, core_in, ring_out, ring_in)
        if i < 3:
            share_step(links, grads, me, second, i + 1)
        if i == 1:
            weight_go(3)
        if i == 2:
            weight_relay(1)
            weight_relay(2)
    residual = rows_ref[...].astype(jnp.float32) + jnp.concatenate(last, axis=0)
    residual_ref[...] = residual
    gain = gain_ref[...]
    normed[0] = (residual * rms(residual) * gain).astype(jnp.bfloat16)
    shared = share_start(links, normed, me)
    weight_relay(3)
    share_end(second)
    for made in state[0]:
        links.done(made)
    ring, terms_go = [], []

    def take_in(i):
        share_step(links, normed, me, shared, i + 1)

    def feed(i):
        d = order[i]
        for made in shared[1][:1] if i == 3 else shared[1][1 + CHUNKS * i : 1 + CHUNKS * (i + 1)]:
            made.wait_recv()
        gate_up_pre = jnp.dot(
            pair_of(normed, d), gate_up[...], preferred_element_type=jnp.float32
        )
        activated, slope = gelu_pair(gate_up_pre[:, :ffn])
        up_pre = gate_up_pre[:, ffn:]
        made = (activated * up_pre).astype(jnp.bfloat16)
        hidden[pl.ds(first_row(d), rows), :] = made[:rows]
        hidden[pl.ds(first_row(4 + d), rows), :] = made[rows:]
        if i == 0:
            weight_wait(3)
        grad_hidden = jnp.dot(pair_of(grads, d), down[...], preferred_element_type=jnp.float32)
        grad_pre = jnp.concatenate(
            [
                (grad_hidden * up_pre * slope).astype(jnp.bfloat16),
                (grad_hidden * activated).astype(jnp.bfloat16),
            ],
            axis=1,
        )
        pre[pl.ds(first_row(d), rows), :] = grad_pre[:rows]
        pre[pl.ds(first_row(4 + d), rows), :] = grad_pre[rows:]
        terms = right_transposed(grad_pre, gate_up[...])
        kept = []
        mine[i] = pair_go(links, me, kept, i, terms, core_out, core_in)
        return kept[0]

    def pass_on(i, core):
        return sum_step(links, me, core, ring, i, mine[i], core_in, ring_out2, ring_in2)

    joins = (grad_gu, in_gu, relay_gu), (grad_d, in_d, relay_d)

    def weight_grads(k):
        for n in range(4):
            block = 4 * (n // 2) + 2 * flip(k, z % 2) + n % 2
            here = pl.ds(pl.multiple_of(block * depth, depth), depth)
            left = normed[:, :, here].reshape(tokens, depth)
            grad_gu[here, :] = left_transposed(left, pre[...]).astype(jnp.bfloat16)
            left = grads[:, :, here].reshape(tokens, depth)
            grad_d[here, :] = left_transposed(left, hidden[...]).astype(jnp.bfloat16)
        for n, (grad, into, relay) in enumerate(joins):
            sems = join_send.at[n], join_recv.at[n], relay_recv.at[n]
            join_go(links, me, k, grad, into, relay, *sems)

    take_in(0)
    weight_wait(1)
    weight_wait(2)
    first = feed(0)
    pass_on(0, first)
    take_in(1)
    following = feed(1)
    take_in(2)
    final = feed(3)
    pass_on(1, following)
    third = feed(2)
    weight_grads(0)
    pass_on(2, third)
    weight_grads(1)
    last = pass_on(3, final)
    normed_grad = jnp.concatenate(last, axis=0)
    residual = residual_ref[...]
    scale = rms(residual)
    unit = residual * scale
    part_ref[...] = jnp.sum(normed_grad * unit, axis=0, keepdims=True)
    out = own_ref[...].astype(jnp.float32) + norm_back(normed_grad, unit, scale, gain)
    wide_ref[...] = out
    low[0] = out.astype(jnp.bfloat16)
    shared = share_start(links, low, me)
    sent = []

    def context_back(d):
        made = jnp.dot(pair_of(low, d), out_weight[...], preferred_element_type=jnp.float32)
        made = made.astype(jnp.bfloat16).T
        for half, slot in enumerate((d, 4 + d)):
            here = lanes(slot * rows, rows)
            cut = made[:, half * rows : (half + 1) * rows]
            heads_out[:, :, here] = cut.reshape(group, size, rows)
            pieces[0, :, here] = heads_out[own, :, here]
            for e in (1, 2, 3):
                xd, yd = flip(x, e // 2), flip(y, e % 2)
                source = heads_out.at[2 * xd + yd, :, here]
                sent.append(links.go(source, pieces.at[e, :, here], device(z, yd, xd, c)))

    shared[1][0].wait_recv()
    context_back(0)
    for step in (1, 2, 3):
        share_step(links, low, me, shared, step)
        if step == 2:
            for n, (grad, into, relay) in enumerate(joins):
                sems = join_send.at[n], join_recv.at[n], relay_recv.at[n]
                join_relay(links, me, grad, into, relay, *sems)
        for made in shared[1][1 + CHUNKS * (step - 1) : 1 + CHUNKS * step]:
            made.wait_recv()
        context_back(order[step - 1])
    for made in sent:
        made.wait_recv()
    for n, (_, into, _) in enumerate(joins):
        for k in range(2):
            for j in range(3):
                arrived(into.at[k, j], join_recv.at[n, k, j])
    links.finish()


def reduce_space(rows, width):
    return [
        low_space(4, rows, width),
        low_space(4, rows, width),
        low_space(3, rows, width),
        low_space(3, rows, width),
    ]


def core(ctx_pieces, token_rows, gain, grad_own, slots_o, slots_g, slots_ud):
    _, size, tokens = ctx_pieces.shape
    rows, width = token_rows.shape
    _, depth, ffn = slots_g.shape
    group = slots_o.shape[2] // DH
    return pl.pallas_call(
        core_kernel,
        name="core",
        out_shape=[
            wide_array(rows, width),
            low_array(tokens, 4 * size),
            low_array(8 * depth, ffn),
            low_array(tokens, ffn),
            low_array(8, rows, width),
            wide_array(rows, width),
            wide_array(1, width),
            low_array(4, size, tokens),
            low_array(2, 3, depth, 2 * ffn),
            low_array(2, 3, depth, ffn),
        ],
        in_specs=[IN_VMEM] * 4 + [IN_PLACE] * 4,
        out_specs=[IN_VMEM] * 8 + [IN_PLACE] * 2,
        scratch_shapes=[
            low_space(8 * depth, group * size),
            low_space(8 * depth, 2 * ffn),
            low_space(8, rows, width),
            low_space(8, rows, width),
            low_space(tokens, 2 * ffn),
            low_space(4, size, tokens),
            low_space(group, size, tokens),
            low_space(8 * depth, 2 * ffn),
            low_space(8 * depth, ffn),
            pltpu.VMEM((4, rows, width), jnp.float32),
            *reduce_space(rows, width),
            low_space(3, rows, width),
            low_space(3, rows, width),
            low_space(2, depth, 2 * ffn),
            low_space(2, depth, ffn),
            COPIES((112,)),
            COPIES((112,)),
            COPIES((4, 2, 2, 2)),
            COPIES((4, 2, 2, 2)),
            COPIES((2, 2, 4, 2)),
            COPIES((2, 2, 3)),
            COPIES((2, 2)),
        ],
        compiler_params=pltpu.CompilerParams(
            collective_id=2, has_side_effects=True, vmem_limit_bytes=63 << 20
        ),
    )(ctx_pieces, token_rows, gain, grad_own, slots_o, slots_g, *slots_ud)


def exit_kernel(
    piece_ref, normed_ref, weight_ref, token_ref, wide_ref, gain_ref, low_ref, context_ref,
    hidden_ref, down_ref, residual_ref, gain_two_ref, line_ref, bucket_ref,
    query_out, key_out, value_out, output_out, home_ref, layer_ref, small_ref,
    heads_in, rows_low, grad_qkv, grad_out, in_qkv, in_out, held, token_out, layer_own,
    packed, in_f, in_y, in_z,
    core_out, core_in, ring_out, ring_in, core_out2, core_in2, ring_out2, ring_in2,
    relay_qkv, relay_out, send, recv, plane_send, plane_recv, relay_recv,
):
    me = z, y, x, c = position()
    greet(*me)
    links = Links(send, recv)
    own, f = 2 * x + y, 2 * x + c
    group, three, size, tokens = heads_in.shape
    rows = tokens // 8
    depth = grad_qkv.shape[0] // 8
    width = normed_ref.shape[2]
    part = width // 4
    heads = []
    for d in (1, 2, 3):
        xd, yd = flip(x, d // 2), flip(y, d % 2)
        heads.append(links.go(piece_ref.at[d], heads_in.at[own], device(z, yd, xd, c)))
    heads_in[own] = piece_ref[0]

    order = sum_order(z)

    def pair_rows(ref, d):
        return jnp.concatenate(
            [ref[lanes(block * rows, rows), :] for block in (d, 4 + d)], axis=0
        )

    def to_home(source, into):
        got = []
        for d in (1, 2, 3):
            xd, cd = flip(x, d // 2), flip(c, d % 2)
            got.append(links.go(source.at[2 * xd + cd], into.at[f], device(z, y, xd, cd)))
        into[f] = source[f]
        return got

    ffn, state = ([], []), ([], [])
    joins = (grad_qkv, in_qkv, relay_qkv), (grad_out, in_out, relay_out)

    def sems(n):
        return plane_send.at[n], plane_recv.at[n], relay_recv.at[n]

    def ffn_step(i):
        terms = right_transposed(pair_rows(hidden_ref, order[i]), down_ref[...])
        return reduce_pair(links, me, ffn, i, terms, core_out2, core_in2, ring_out2, ring_in2)

    def step(i):
        terms = right_transposed(pair_rows(rows_low, order[i]), weight_ref[...])
        return reduce_pair(links, me, state, i, terms, core_out, core_in, ring_out, ring_in)

    def weight_grads(k, ref, right, join, n):
        for part_of_rows in range(4):
            block = 4 * (part_of_rows // 2) + 2 * flip(k, z % 2) + part_of_rows % 2
            here = pl.ds(pl.multiple_of(block * depth, depth), depth)
            left = ref[:, :, here].reshape(tokens, depth)
            join[0][here, :] = left_transposed(left, right[...]).astype(jnp.bfloat16)
        join_go(links, me, k, *join, *sems(n))

    ffn_step(0)
    for k in range(2):
        weight_grads(k, low_ref, context_ref, joins[1], 1)
    for made in heads:
        made.wait_recv()
    for n in range(three):
        here = slice(n * group * size, (n + 1) * group * size)
        rows_low[:, here] = heads_in[:, n].reshape(group * size, tokens).T
    step(0)
    ffn_step(1)
    for k in range(2):
        weight_grads(k, normed_ref, rows_low, joins[0], 0)
    join_relay(links, me, *joins[1], *sems(1))
    step(1)
    ffn_step(2)
    join_relay(links, me, *joins[0], *sems(0))
    step(2)
    last = ffn_step(3)
    layer = (residual_ref[...] + jnp.concatenate(last, axis=0)).astype(jnp.bfloat16)
    for i in range(4):
        layer_own[i] = layer[:, i * part : (i + 1) * part]
    home = to_home(layer_own, layer_ref)
    wide_qkv = in_qkv.shape[-1]
    group_width = wide_qkv // 3
    cut = pl.ds(pl.multiple_of((z % 2) * group_width, group_width), group_width)
    way = []
    for k in range(2):
        held[k, :, :wide_qkv] = join_sum(k, in_qkv, plane_recv.at[0])
        held[k, :, wide_qkv:] = join_sum(k, in_out, plane_recv.at[1])
        for n, ref in enumerate((query_out, key_out, value_out, output_out)):
            sent = held.at[k, :, n * group_width : (n + 1) * group_width]
            way.append(column_go(links, me, k, sent, ref.at[:, cut]))

    packed[...] = jnp.zeros_like(packed)
    per_block = 4
    all_heads = BLOCK // per_block
    source, place = head_of(z, y, x, c, all_heads // 4)
    lane = lax.broadcasted_iota(jnp.int32, (1, BLOCK), 1)
    for block in range(8):
        row = jnp.zeros((1, BLOCK), jnp.float32)
        for n in range(per_block):
            hot = bucket_ref[...] == block * per_block + n
            value = lane_sum(jnp.where(hot, line_ref[...], 0.0))
            row = jnp.where(lane == n * all_heads + source * (all_heads // 4) + place, value, row)
        packed[block // 2, block % 2, 4:5, :] = row
    last = step(3)
    normed_grad = jnp.concatenate(last, axis=0)
    tokens_wide = token_ref[...].astype(jnp.float32)
    scale = rms(tokens_wide)
    unit = tokens_wide * scale
    token_grad = wide_ref[...] + norm_back(normed_grad, unit, scale, gain_ref[...])
    for i in range(4):
        token_out[i] = token_grad[:, i * part : (i + 1) * part].astype(jnp.bfloat16)
    home += to_home(token_out, home_ref)
    gain_part = jnp.sum(normed_grad * unit, axis=0, keepdims=True)
    for i in range(width // BLOCK):
        here = slice(i * BLOCK, (i + 1) * BLOCK)
        block = (i // 2) // 2, (i // 2) % 2
        packed[block[0], block[1], i % 2 : i % 2 + 1, :] = gain_part[:, here]
        packed[block[0], block[1], 2 + i % 2 : 3 + i % 2, :] = gain_two_ref[:, here]
    got = []
    for d in (1, 2, 3):
        to = device(z, y, flip(x, d // 2), flip(c, d % 2))
        got.append(links.go(packed, in_f.at[d - 1], to))
    for made in got:
        made.wait_recv()
    for made in got:
        links.done(made)
    packed[...] = packed[...] + in_f[0] + in_f[1] + in_f[2]
    made = links.go(packed.at[:, 1 - y], in_y, device(z, 1 - y, x, c))
    made.wait_recv()
    in_y[...] = in_y[...] + packed[:, y]
    got = []
    for d in (1, 2, 3):
        other = flip_pair(z, d)
        got.append(links.go(in_y.at[other], in_z.at[d - 1], device(other, y, x, c)))
    for made in got:
        made.wait_recv()
    small_ref[...] = in_y[z] + in_z[0] + in_z[1] + in_z[2]
    for made in way + home:
        made.wait_recv()
    links.finish()


def leave(pieces, normed, weight, token_rows, wide_grad, gain, low, context, hidden, down, residual,
          gain_two_part, line_grad, rev_buckets):
    _, _, size, tokens = pieces.shape
    rows, width = token_rows.shape
    depth, wide = weight.shape[0] // 8, weight.shape[1]
    out_wide = context.shape[1]
    cols = 2 * wide // 3
    tile = (8, BLOCK)
    return pl.pallas_call(
        exit_kernel,
        name="leave",
        out_shape=[
            *(low_array(depth, cols) for _ in range(4)),
            low_array(4, rows, width // 4),
            low_array(4, rows, width // 4),
            wide_array(*tile),
        ],
        in_specs=[IN_VMEM] * 14,
        out_specs=[IN_VMEM] * 7,
        scratch_shapes=[
            low_space(4, 3, size, tokens),
            low_space(tokens, wide),
            low_space(8 * depth, wide),
            low_space(8 * depth, out_wide),
            low_space(2, 3, depth, wide),
            low_space(2, 3, depth, out_wide),
            low_space(2, depth, wide + out_wide),
            low_space(4, rows, width // 4),
            low_space(4, rows, width // 4),
            pltpu.VMEM((4, 2, *tile), jnp.float32),
            pltpu.VMEM((3, 4, 2, *tile), jnp.float32),
            pltpu.VMEM((4, *tile), jnp.float32),
            pltpu.VMEM((3, *tile), jnp.float32),
            *reduce_space(rows, width),
            *reduce_space(rows, width),
            low_space(2, depth, wide),
            low_space(2, depth, out_wide),
            COPIES((64,)),
            COPIES((64,)),
            COPIES((2, 2, 4, 2)),
            COPIES((2, 2, 3)),
            COPIES((2, 2)),
        ],
        compiler_params=pltpu.CompilerParams(
            collective_id=4, has_side_effects=True, vmem_limit_bytes=60 << 20
        ),
    )(pieces, normed, weight, token_rows, wide_grad, gain, low, context, hidden, down, residual,
      gain_two_part, line_grad, rev_buckets)


def widen_kernel(*refs):
    attn, slots, home, outs = refs[:4], refs[4:6], refs[6], refs[7:]
    z_low = (lax.axis_index("seq") // 2) % 2
    for ref, out in zip(attn, outs[:4]):
        out[...] = ref[...].astype(jnp.float32)
    size = slots[0].shape[1] // 3
    for k in range(2):
        cut = lanes((k + z_low - 2 * k * z_low) * size, size)
        for n, out in enumerate(outs[4:7]):
            out[:, cut] = slots[k][:, n * size : (n + 1) * size].astype(jnp.float32)
    outs[7][...] = home[...].astype(jnp.float32)


def widen(attn, slots, home):
    depth, cols = attn[0].shape
    size = 2 * slots[0].shape[1] // 3
    return pl.pallas_call(
        widen_kernel,
        name="widen",
        out_shape=[wide_array(depth, cols)] * 4
        + [wide_array(depth, size)] * 3
        + [wide_array(*home.shape)],
        in_specs=[IN_VMEM] * 7,
        out_specs=[IN_VMEM] * 8,
        compiler_params=pltpu.CompilerParams(vmem_limit_bytes=32 << 20),
    )(*attn, *slots, home)


def fast_shards(
    tokens_in,
    cotangent,
    gain_attn,
    query_weight,
    key_weight,
    value_weight,
    output_weight,
    bias_table,
    gain_ffn,
    gate_weight,
    up_weight,
    down_weight,
    lengths,
    buckets,
):
    seq_index, fsdp_index = lax.axis_index("seq"), lax.axis_index("fsdp")
    z, y, x, c = seq_index // 2, seq_index % 2, fsdp_index // 2, fsdp_index % 2
    z_low, z_high = z % 2, z // 2
    batch_count, slot_count, part_width = tokens_in.shape
    width = part_width * 4
    row_count = query_weight.shape[0]
    heads = query_weight.shape[1] // DH
    group_heads = heads // 2
    group_width = group_heads * DH
    hidden_width = gate_weight.shape[1] // 2
    def halves(weights):
        slots = []
        for k in range(2):
            half = k ^ z_low
            slots.append(
                jnp.concatenate(
                    [
                        lax.dynamic_slice_in_dim(w, half * (w.shape[1] // 2), w.shape[1] // 2, 1)
                        for w in weights
                    ],
                    axis=1,
                )
            )
        return slots

    small = jnp.concatenate(
        [gain_attn, gain_ffn, bias_table.reshape(-1), jnp.zeros((2 * row_count - bias_table.size,), jnp.bfloat16)]
    )
    small = small.astype(jnp.float32).reshape(8, BLOCK)
    rev_buckets = jnp.concatenate([buckets[::-1], jnp.full((1,), -1, jnp.int32)])[None, :]
    (
        token_low,
        normed_one,
        grad_own,
        pieces,
        qkv_weight,
        gain_one,
        gain_two,
        rev_line,
        slots_o,
        slots_g,
    ) = entry(
        lengths,
        tokens_in,
        cotangent,
        small,
        rev_buckets,
        (query_weight, key_weight, value_weight, output_weight, gate_weight),
    )
    pieces, *later = lax.optimization_barrier((pieces, *halves([up_weight, down_weight])))
    slots_ud = [move(later[k], spread_slot(k)) for k in range(2)]
    context_pieces, context_wide, lse, qkv_all = attend(lengths, pieces, rev_line)
    (
        residual,
        context,
        down_full,
        hidden,
        residual_low,
        residual_grad,
        gain_two_part,
        grad_pieces,
        terms_gate_up,
        terms_down,
    ) = core(context_pieces, token_low, gain_two, grad_own, slots_o, slots_g, slots_ud)

    def slot_sum(k):
        sums = [
            jnp.sum(t[k].astype(jnp.float32), axis=0).astype(jnp.bfloat16)
            for t in (terms_gate_up, terms_down)
        ]
        return jnp.concatenate(sums, axis=1)

    ffn_slots = [move(slot_sum(k), spread_slot(k)) for k in range(2)]
    qkv_grad_pieces, line_grad = attend_back(
        lengths, grad_pieces, rev_line, context_wide, lse, qkv_all
    )
    qkv_grad_pieces, *ffn_slots = lax.optimization_barrier((qkv_grad_pieces, *ffn_slots))
    *attn_sums, home, layer, small = leave(
        qkv_grad_pieces,
        normed_one,
        qkv_weight,
        token_low,
        residual_grad,
        gain_one,
        residual_low,
        context,
        hidden,
        down_full,
        residual,
        gain_two_part,
        line_grad,
        rev_buckets,
    )
    query_sum, key_sum, value_sum, output_sum, gate_sum, up_sum, down_sum, home = widen(
        attn_sums, ffn_slots, home
    )
    token_share = home.reshape(batch_count, slot_count, part_width)
    layer_out = layer.reshape(batch_count, slot_count, part_width)
    table_sum = lax.dynamic_slice_in_dim(
        small[4].reshape(-1, 4 * heads), fsdp_index * heads, heads, 1
    )
    return (
        layer_out,
        token_share,
        small[:2].reshape(-1),
        query_sum,
        key_sum,
        value_sum,
        output_sum,
        table_sum,
        small[2:4].reshape(-1),
        gate_sum,
        up_sum,
        down_sum,
    )


def solution(mesh):
    placed = (
        P(None, "seq", "fsdp"),
        P(None, "seq", "fsdp"),
        P("seq"),
        P("seq", "fsdp"),
        P("seq", "fsdp"),
        P("seq", "fsdp"),
        P("seq", "fsdp"),
        P("seq", "fsdp"),
        P("seq"),
        P("seq", "fsdp"),
        P("seq", "fsdp"),
        P("seq", "fsdp"),
        P(),
        P(),
    )
    return jax.shard_map(
        fast_shards if (mesh.shape["seq"], mesh.shape["fsdp"]) == (8, 4) else shards,
        mesh=mesh,
        in_specs=placed,
        out_specs=(
            P(None, "seq", "fsdp"),
            P(None, "seq", "fsdp"),
            P("seq"),
            P("seq", "fsdp"),
            P("seq", "fsdp"),
            P("seq", "fsdp"),
            P("seq", "fsdp"),
            P("seq", "fsdp"),
            P("seq"),
            P("seq", "fsdp"),
            P("seq", "fsdp"),
            P("seq", "fsdp"),
        ),
        check_vma=False,
    )
```

```python
from functools import partial

import jax
import jax.numpy as jnp
from jax import lax
from jax.experimental import pallas as pl
from jax.experimental.pallas import tpu as pltpu
from jax.sharding import PartitionSpec as P

DH = 64


epsilon = 1e-06
highest = lax.Precision.HIGHEST
masked_score = -1e30
root_two_over_pi = 0.7978845608028654


def plain_product(left, right):
    return jnp.dot(left, right, preferred_element_type=jnp.float32)


def right_transposed(left, right):
    return lax.dot_general(
        left, right, (((1,), (1,)), ((), ())), preferred_element_type=jnp.float32
    )


def left_transposed(left, right):
    return lax.dot_general(
        left, right, (((0,), (0,)), ((), ())), preferred_element_type=jnp.float32
    )


def normalize(rows, gain):
    row_scale = lax.rsqrt(jnp.mean(rows * rows, axis=-1, keepdims=True) + epsilon)
    unit_rows = rows * row_scale
    return (unit_rows, row_scale, (unit_rows * gain.astype(jnp.float32)).astype(jnp.bfloat16))


def norm_back(grad_normed, unit_rows, row_scale, gain):
    weighted = grad_normed * gain.astype(jnp.float32)
    return row_scale * (
        weighted - unit_rows * jnp.mean(weighted * unit_rows, axis=-1, keepdims=True)
    )


def to_heads(rows, batch_count, head_size):
    slot_count = rows.shape[0] // batch_count
    number_of_heads = rows.shape[1] // head_size
    return rows.reshape(batch_count, slot_count, number_of_heads, head_size).transpose(2, 0, 1, 3)


def from_heads(blocks):
    number_of_heads, batch_count, slot_count, head_size = blocks.shape
    return blocks.transpose(1, 2, 0, 3).reshape(
        batch_count * slot_count, number_of_heads * head_size
    )


def bias_rows(bias_line, first_query, slot_count, length):
    span = slot_count + length - 1
    segment = lax.dynamic_slice_in_dim(bias_line, length - first_query - slot_count, span)
    flat = jnp.tile(segment, slot_count)
    skewed = flat[slot_count - 1 : slot_count - 1 + slot_count * (span - 1)].reshape(
        slot_count, span - 1
    )
    return skewed[:, :length]


def bias_rows_back(block_grad, first_query, slot_count, length, line_length):
    span = slot_count + length - 1
    widened = jnp.pad(block_grad, ((0, 0), (0, span - 1 - length)))
    flat = jnp.pad(widened.reshape(-1), (slot_count - 1, 1))
    segment_grad = jnp.sum(flat.reshape(slot_count, span), axis=0)
    return lax.dynamic_update_slice_in_dim(
        jnp.zeros((line_length,), jnp.float32), segment_grad, length - first_query - slot_count, 0
    )


def full_features(block):
    gathered = lax.all_gather(block, "fsdp", axis=2, tiled=True)
    return gathered.reshape(gathered.shape[0] * gathered.shape[1], gathered.shape[2])


def feature_total(partial_rows):
    return lax.psum(partial_rows, "fsdp")


def shards(
    tokens_in,
    cotangent,
    gain_attn,
    query_weight,
    key_weight,
    value_weight,
    output_weight,
    bias_table,
    gain_ffn,
    gate_weight,
    up_weight,
    down_weight,
    lengths,
    buckets,
):
    batch_count, slot_count, part_width = tokens_in.shape
    head_size = DH
    seq_index = lax.axis_index("seq")
    fsdp_index = lax.axis_index("fsdp")
    length = slot_count * lax.axis_size("seq")
    line_length = buckets.shape[0]
    first_query = seq_index * slot_count
    positions = jnp.arange(length, dtype=jnp.int32)
    query_positions = first_query + jnp.arange(slot_count, dtype=jnp.int32)
    key_valid = positions[None, :] < lengths[:, None]
    own_valid = query_positions[None, :] < lengths[:, None]
    gain_one, query_full, key_full, value_full, output_full, table_full = (
        lax.all_gather(gain_attn, "seq", axis=0, tiled=True),
        lax.all_gather(query_weight, "seq", axis=0, tiled=True),
        lax.all_gather(key_weight, "seq", axis=0, tiled=True),
        lax.all_gather(value_weight, "seq", axis=0, tiled=True),
        lax.all_gather(output_weight, "seq", axis=0, tiled=True),
        lax.all_gather(bias_table, "seq", axis=0, tiled=True),
    )
    token_rows = full_features(tokens_in).astype(jnp.float32)
    unit_one, scale_one, normed_one = normalize(token_rows, gain_one)
    query_heads = to_heads(
        plain_product(normed_one, query_full).astype(jnp.bfloat16), batch_count, head_size
    )
    key_heads = to_heads(
        plain_product(normed_one, key_full).astype(jnp.bfloat16), batch_count, head_size
    )
    value_heads = to_heads(
        plain_product(normed_one, value_full).astype(jnp.bfloat16), batch_count, head_size
    )
    number_of_heads = query_heads.shape[0]
    flat_shape = (number_of_heads, batch_count, slot_count * head_size)
    gathered_keys, gathered_values = (
        lax.all_gather(key_heads.reshape(flat_shape), "seq", axis=2, tiled=True),
        lax.all_gather(value_heads.reshape(flat_shape), "seq", axis=2, tiled=True),
    )
    all_keys = gathered_keys.reshape(number_of_heads, batch_count, length, head_size)
    all_values = gathered_values.reshape(number_of_heads, batch_count, length, head_size)
    bucket_hot = (
        buckets[:, None] == jnp.arange(table_full.shape[0], dtype=jnp.int32)[None, :]
    ).astype(jnp.float32)
    offset_bias = lax.dot_general(
        table_full.astype(jnp.float32), bucket_hot, (((0,), (1,)), ((), ())), precision=highest
    )

    def masked_scores(query_tile_rows, key_tile_rows, bias_block):
        raw = (
            jnp.einsum(
                "jht,jxt->jhx", query_tile_rows, key_tile_rows, preferred_element_type=jnp.float32
            )
            + bias_block[None]
        )
        return jnp.where(key_valid[:, None, :], raw, masked_score)

    def attend(inputs):
        query_tile_rows, key_tile_rows, value_tile_rows, bias_line = inputs
        scores = masked_scores(
            query_tile_rows, key_tile_rows, bias_rows(bias_line, first_query, slot_count, length)
        )
        row_peak = jnp.max(scores, axis=-1, keepdims=True)
        raised = jnp.exp(scores - row_peak)
        denominator = jnp.sum(raised, axis=-1, keepdims=True)
        weights_reduced_precision = (raised / denominator).astype(jnp.bfloat16)
        context = jnp.einsum(
            "wot,wtf->wof",
            weights_reduced_precision,
            value_tile_rows,
            preferred_element_type=jnp.float32,
        ).astype(jnp.bfloat16)
        return (context, (row_peak + jnp.log(denominator))[..., 0])

    context_heads, log_totals = lax.map(attend, (query_heads, all_keys, all_values, offset_bias))
    context_rows = from_heads(context_heads)
    residual = token_rows + feature_total(right_transposed(context_rows, output_full))
    gain_two, gate_full, up_full, down_full = (
        lax.all_gather(gain_ffn, "seq", axis=0, tiled=True),
        lax.all_gather(gate_weight, "seq", axis=0, tiled=True),
        lax.all_gather(up_weight, "seq", axis=0, tiled=True),
        lax.all_gather(down_weight, "seq", axis=0, tiled=True),
    )
    unit_two, scale_two, normed_two = normalize(residual, gain_two)
    gate_pre = plain_product(normed_two, gate_full)
    up_pre = plain_product(normed_two, up_full)
    activated, gelu_back = jax.vjp(jax.nn.gelu, gate_pre)
    hidden = (activated * up_pre).astype(jnp.bfloat16)
    ffn_share = lax.psum_scatter(
        right_transposed(hidden, down_full), "fsdp", scatter_dimension=1, tiled=True
    )
    residual_share = lax.dynamic_slice_in_dim(residual, fsdp_index * part_width, part_width, 1)
    layer_out = (
        (residual_share + ffn_share)
        .astype(jnp.bfloat16)
        .reshape(batch_count, slot_count, part_width)
    )
    masked_cot = jnp.where(own_valid[:, :, None], cotangent, jnp.zeros_like(cotangent))
    grad_rows = full_features(masked_cot)
    grad_down = left_transposed(grad_rows, hidden)
    grad_hidden = plain_product(grad_rows, down_full)
    grad_gate_pre = gelu_back(grad_hidden * up_pre)[0].astype(jnp.bfloat16)
    grad_up_pre = (grad_hidden * activated).astype(jnp.bfloat16)
    grad_gate = left_transposed(normed_two, grad_gate_pre)
    grad_up = left_transposed(normed_two, grad_up_pre)
    normed_two_grad = right_transposed(grad_gate_pre, gate_full) + right_transposed(
        grad_up_pre, up_full
    )
    second_gain_piece = jnp.sum(normed_two_grad * unit_two, axis=0)
    ffn_grads = (
        lax.psum_scatter(second_gain_piece, "seq", scatter_dimension=0, tiled=True),
        lax.psum_scatter(grad_gate, "seq", scatter_dimension=0, tiled=True),
        lax.psum_scatter(grad_up, "seq", scatter_dimension=0, tiled=True),
        lax.psum_scatter(grad_down, "seq", scatter_dimension=0, tiled=True),
    )
    residual_grad = grad_rows.astype(jnp.float32) + norm_back(
        feature_total(normed_two_grad), unit_two, scale_two, gain_two
    )
    residual_low = residual_grad.astype(jnp.bfloat16)
    grad_output = left_transposed(residual_low, context_rows)
    context_grad = to_heads(
        plain_product(residual_low, output_full).astype(jnp.bfloat16), batch_count, head_size
    )

    def query_side(inputs, with_keys):
        query_tile_rows, key_tile_rows, value_tile_rows, bias_line, log_total, context_tile_rows = (
            inputs
        )
        scores = masked_scores(
            query_tile_rows, key_tile_rows, bias_rows(bias_line, first_query, slot_count, length)
        )
        probs = jnp.exp(scores - log_total[..., None])
        prob_grad = jnp.einsum(
            "jht,jxt->jhx", context_tile_rows, value_tile_rows, preferred_element_type=jnp.float32
        )
        delta = jnp.sum(probs * prob_grad, axis=-1)
        score_gradient = (probs * (prob_grad - delta[..., None])).astype(jnp.bfloat16)
        query_grad = jnp.einsum(
            "wot,wtf->wof", score_gradient, key_tile_rows, preferred_element_type=jnp.float32
        )
        bias_grad = bias_rows_back(
            jnp.sum(score_gradient.astype(jnp.float32), axis=0),
            first_query,
            slot_count,
            length,
            line_length,
        )
        key_term = jnp.einsum(
            "xic,xil->xcl", score_gradient, query_tile_rows, preferred_element_type=jnp.float32
        )
        value_term = jnp.einsum(
            "xic,xil->xcl",
            probs.astype(jnp.bfloat16),
            context_tile_rows,
            preferred_element_type=jnp.float32,
        )
        return (query_grad, bias_grad, delta, key_term, value_term)

    side_inputs = (query_heads, all_keys, all_values, offset_bias, log_totals, context_grad)
    query_grad, bias_grad, delta, key_terms, value_terms = lax.map(
        partial(query_side, with_keys=True), side_inputs
    )
    wide_shape = (number_of_heads, batch_count, length * head_size)
    key_sums, value_sums = (
        lax.psum_scatter(key_terms.reshape(wide_shape), "seq", scatter_dimension=2, tiled=True),
        lax.psum_scatter(value_terms.reshape(wide_shape), "seq", scatter_dimension=2, tiled=True),
    )
    own_shape = (number_of_heads, batch_count, slot_count, head_size)
    query_low = from_heads(query_grad.astype(jnp.bfloat16))
    key_low = from_heads(key_sums.reshape(own_shape).astype(jnp.bfloat16))
    value_low = from_heads(value_sums.reshape(own_shape).astype(jnp.bfloat16))
    grad_query = left_transposed(normed_one, query_low)
    grad_key = left_transposed(normed_one, key_low)
    grad_value = left_transposed(normed_one, value_low)
    grad_table = lax.dot_general(bucket_hot, bias_grad, (((0,), (1,)), ((), ())), precision=highest)
    normed_one_grad = (
        right_transposed(query_low, query_full)
        + right_transposed(key_low, key_full)
        + right_transposed(value_low, value_full)
    )
    gain_one_part = jnp.sum(normed_one_grad * unit_one, axis=0)
    attn_grads = (
        lax.psum_scatter(gain_one_part, "seq", scatter_dimension=0, tiled=True),
        lax.psum_scatter(grad_query, "seq", scatter_dimension=0, tiled=True),
        lax.psum_scatter(grad_key, "seq", scatter_dimension=0, tiled=True),
        lax.psum_scatter(grad_value, "seq", scatter_dimension=0, tiled=True),
        lax.psum_scatter(grad_output, "seq", scatter_dimension=0, tiled=True),
        lax.psum_scatter(grad_table, "seq", scatter_dimension=0, tiled=True),
    )
    token_grad = residual_grad + norm_back(
        feature_total(normed_one_grad), unit_one, scale_one, gain_one
    )
    token_share = lax.dynamic_slice_in_dim(
        token_grad, fsdp_index * part_width, part_width, 1
    ).reshape(batch_count, slot_count, part_width)
    gain_one_sum, gain_two_sum = lax.psum((attn_grads[0], ffn_grads[0]), "fsdp")
    return (
        layer_out,
        token_share,
        gain_one_sum,
        attn_grads[1],
        attn_grads[2],
        attn_grads[3],
        attn_grads[4],
        attn_grads[5],
        gain_two_sum,
        ffn_grads[1],
        ffn_grads[2],
        ffn_grads[3],
    )


BLOCK = 128
BOTH = ("seq", "fsdp")


def move(value, target):
    pairs = []
    for z in range(4):
        for y in range(2):
            for x in range(2):
                for c in range(2):
                    zt, yt, xt, ct = target(z, y, x, c)
                    pairs.append(((2 * z + y) * 4 + 2 * x + c, (2 * zt + yt) * 4 + 2 * xt + ct))
    return lax.ppermute(value, BOTH, pairs)


def spread_slot(k):
    return lambda z, y, x, c: (2 * c + (k ^ (z & 1)), y, x, z >> 1)


KEYS = 512
QUERIES = 512
WIDE_QUERIES = 1024
OFFSET = 1920


def skew_table(rev_ref, table):
    width = rev_ref.shape[1]
    line = jnp.broadcast_to(rev_ref[...], (8, width))
    for first in range(0, BLOCK, 8):
        table[first : first + 8, :] = pltpu.roll(
            line, (width - (BLOCK - 1) + first) % width, axis=1, stride=1, stride_axis=0
        )


def place_of(piece, part, z, y, x, c):
    c_rel, d = part // 4, part % 4
    b = jnp.bitwise_xor(x, piece // 2)
    block = (
        4 * jnp.bitwise_xor(z, d)
        + 2 * jnp.bitwise_xor(y, piece % 2)
        + jnp.bitwise_xor(c, c_rel)
    )
    return b, block


def part_of(b, block, z, y, x, c):
    piece = 2 * jnp.bitwise_xor(b, x) + jnp.bitwise_xor((block // 2) % 2, y)
    part = 4 * jnp.bitwise_xor(block % 2, c) + jnp.bitwise_xor(block // 4, z)
    return piece, part


def lanes(first, count):
    return pl.ds(pl.multiple_of(first, BLOCK), count)


def attend_kernel(sc, pieces, rev_ref, ctx_ref, ctx_wide, lse_ref, qkv, keys, table):
    z, y, x, c = position()
    for piece in range(4):
        for part in range(8):
            b, block = place_of(piece, part, z, y, x, c)
            data = pieces[piece, :, :, part * BLOCK : (part + 1) * BLOCK]
            qkv[b, :, :, lanes(block * BLOCK, BLOCK)] = data
            keys[b, lanes(block * BLOCK, BLOCK), :] = data[1].T
    skew_table(rev_ref, table)
    length = qkv.shape[-1]
    for b in range(2):
        valid = sc[b]
        full = valid // KEYS

        @pl.loop(0, length // WIDE_QUERIES)
        def _(i):
            first_query = i * WIDE_QUERIES
            query = qkv[b, 0, :, lanes(first_query, WIDE_QUERIES)]

            def tile(j, carry, masked):
                peak, total, acc = carry
                first_key = j * KEYS
                score = jnp.dot(
                    keys[b, lanes(first_key, KEYS), :], query, preferred_element_type=jnp.float32
                )
                score = score + jnp.concatenate(
                    [
                        table[:, lanes(first_query - first_key + OFFSET - t, WIDE_QUERIES)]
                        for t in range(0, KEYS, BLOCK)
                    ],
                    axis=0,
                )
                if masked:
                    position = first_key + lax.broadcasted_iota(jnp.int32, (KEYS, WIDE_QUERIES), 0)
                    score = jnp.where(position < valid, score, masked_score)
                now = jnp.maximum(peak, jnp.max(score, axis=0, keepdims=True))
                scale = jnp.exp(peak - now)
                prob = jnp.exp(score - now)
                total = total * scale + jnp.sum(prob, axis=0, keepdims=True)
                acc = acc * scale + jnp.dot(
                    qkv[b, 2, :, lanes(first_key, KEYS)],
                    prob.astype(jnp.bfloat16),
                    preferred_element_type=jnp.float32,
                )
                return now, total, acc

            carry = (
                jnp.full((1, WIDE_QUERIES), masked_score, jnp.float32),
                jnp.zeros((1, WIDE_QUERIES), jnp.float32),
                jnp.zeros((DH, WIDE_QUERIES), jnp.float32),
            )
            carry = lax.fori_loop(0, full, lambda j, s: tile(j, s, False), carry)
            peak, total, acc = lax.cond(
                valid > full * KEYS, lambda s: tile(full, s, True), lambda s: s, carry
            )
            context = acc / total
            ctx_wide[b, :, lanes(first_query, WIDE_QUERIES)] = context
            lse_ref[b, :, lanes(first_query, WIDE_QUERIES)] = peak + jnp.log(total)
            low = context.astype(jnp.bfloat16)
            for t in range(WIDE_QUERIES // BLOCK):
                piece, part = part_of(b, i * (WIDE_QUERIES // BLOCK) + t, z, y, x, c)
                ctx_ref[piece, :, lanes(part * BLOCK, BLOCK)] = low[:, t * BLOCK : (t + 1) * BLOCK]


def attend(scalars, pieces, rev_line):
    _, _, head_size, tokens = pieces.shape
    length = tokens * 2
    smem, vmem = pl.BlockSpec(memory_space=pltpu.SMEM), pl.BlockSpec(memory_space=pltpu.VMEM)
    return pl.pallas_call(
        attend_kernel,
        name="attend",
        out_shape=[
            jax.ShapeDtypeStruct((4, head_size, tokens), jnp.bfloat16),
            jax.ShapeDtypeStruct((2, head_size, length), jnp.float32),
            jax.ShapeDtypeStruct((2, 1, length), jnp.float32),
            jax.ShapeDtypeStruct((2, 3, head_size, length), jnp.bfloat16),
        ],
        in_specs=[smem] + [vmem] * 2,
        out_specs=[vmem] * 4,
        scratch_shapes=[
            pltpu.VMEM((2, length, head_size), jnp.bfloat16),
            pltpu.VMEM((BLOCK, rev_line.shape[1]), jnp.float32),
        ],
        cost_estimate=pl.CostEstimate(
            flops=46_000_000_000, bytes_accessed=4 << 20, transcendentals=0
        ),
        compiler_params=pltpu.CompilerParams(vmem_limit_bytes=48 << 20),
    )(scalars, pieces, rev_line)


def attend_back_kernel(
    sc, pieces, rev_ref, ctx_wide, lse_ref, qkv,
    out_ref, line_ref,
    queries, keys, values, grads, grads_t, delta, query_sum, key_sum, value_sum, table, table_sum,
):
    z, y, x, c = position()
    length = qkv.shape[-1]
    for piece in range(4):
        for part in range(8):
            b, block = place_of(piece, part, z, y, x, c)
            data = pieces[piece, :, part * BLOCK : (part + 1) * BLOCK]
            grads_t[b, :, lanes(block * BLOCK, BLOCK)] = data
            grads[b, lanes(block * BLOCK, BLOCK), :] = data.T
    for b in range(2):
        for first in range(0, length, BLOCK):
            here = slice(first, first + BLOCK)
            queries[b, here, :] = qkv[b, 0, :, here].T
            keys[b, here, :] = qkv[b, 1, :, here].T
            values[b, here, :] = qkv[b, 2, :, here].T
        delta[b] = jnp.sum(
            ctx_wide[b] * grads_t[b].astype(jnp.float32), axis=0, keepdims=True
        )
    skew_table(rev_ref, table)
    table_sum[...] = jnp.zeros_like(table_sum)
    query_sum[...] = jnp.zeros_like(query_sum)
    out_ref[...] = jnp.zeros_like(out_ref)
    for b in range(2):
        valid = sc[b]
        full = valid // KEYS
        count = (valid + QUERIES - 1) // QUERIES

        def key_step(j, masked):
            first_key = j * KEYS
            key, value = keys[b, lanes(first_key, KEYS), :], values[b, lanes(first_key, KEYS), :]
            key_t = qkv[b, 1, :, lanes(first_key, KEYS)]
            key_sum[...] = jnp.zeros_like(key_sum)
            value_sum[...] = jnp.zeros_like(value_sum)

            @pl.loop(0, count)
            def _(i):
                first_query = i * QUERIES
                here = lanes(first_query, QUERIES)
                score = jnp.dot(key, qkv[b, 0, :, here], preferred_element_type=jnp.float32)
                score = score + jnp.concatenate(
                    [
                        table[:, lanes(first_query - first_key + OFFSET - t, QUERIES)]
                        for t in range(0, KEYS, BLOCK)
                    ],
                    axis=0,
                )
                if masked:
                    position = first_key + lax.broadcasted_iota(jnp.int32, (KEYS, QUERIES), 0)
                    score = jnp.where(position < valid, score, masked_score)
                prob = jnp.exp(score - lse_ref[b, :, here])
                prob_grad = jnp.dot(value, grads_t[b, :, here], preferred_element_type=jnp.float32)
                score_grad = (prob * (prob_grad - delta[b, :, here])).astype(jnp.bfloat16)
                value_sum[...] += jnp.dot(
                    prob.astype(jnp.bfloat16), grads[b, here, :], preferred_element_type=jnp.float32
                )
                key_sum[...] += jnp.dot(
                    score_grad, queries[b, here, :], preferred_element_type=jnp.float32
                )
                query_sum[b, :, here] += jnp.dot(
                    key_t, score_grad, preferred_element_type=jnp.float32
                )
                for t in range(0, KEYS, BLOCK):
                    table_sum[:, lanes(first_query - first_key + OFFSET - t, QUERIES)] += score_grad[
                        t : t + BLOCK
                    ].astype(jnp.float32)

            for t in range(KEYS // BLOCK):
                piece, part = part_of(b, j * (KEYS // BLOCK) + t, z, y, x, c)
                rows = slice(t * BLOCK, (t + 1) * BLOCK)
                at = lanes(part * BLOCK, BLOCK)
                out_ref[piece, 1, :, at] = key_sum[rows, :].T.astype(jnp.bfloat16)
                out_ref[piece, 2, :, at] = value_sum[rows, :].T.astype(jnp.bfloat16)

        pl.loop(0, full)(lambda j: key_step(j, False))
        pl.when(valid > full * KEYS)(lambda: key_step(full, True))
        for block in range(length // BLOCK):
            piece, part = part_of(b, block, z, y, x, c)
            out_ref[piece, 0, :, lanes(part * BLOCK, BLOCK)] = query_sum[
                b, :, block * BLOCK : (block + 1) * BLOCK
            ].astype(jnp.bfloat16)
    width = table_sum.shape[1]
    line = jnp.zeros((8, width), jnp.float32)
    for first in range(0, BLOCK, 8):
        line = line + pltpu.roll(table_sum[first : first + 8, :], BLOCK - 8 - first, axis=1)
    ahead = 7 - lax.broadcasted_iota(jnp.int32, (8, width), 0)
    for bit in (1, 2, 4):
        line = jnp.where((ahead & bit) != 0, pltpu.roll(line, bit, axis=1), line)
    line_ref[...] = jnp.sum(line, axis=0, keepdims=True)


def attend_back(scalars, pieces, rev_line, ctx_wide, lse, qkv):
    _, head_size, tokens = pieces.shape
    length = tokens * 2
    smem, vmem = pl.BlockSpec(memory_space=pltpu.SMEM), pl.BlockSpec(memory_space=pltpu.VMEM)
    low = pltpu.VMEM((2, length, head_size), jnp.bfloat16)
    return pl.pallas_call(
        attend_back_kernel,
        name="attend_back",
        out_shape=[
            jax.ShapeDtypeStruct((4, 3, head_size, tokens), jnp.bfloat16),
            jax.ShapeDtypeStruct(rev_line.shape, jnp.float32),
        ],
        in_specs=[smem] + [vmem] * 5,
        out_specs=[vmem] * 2,
        scratch_shapes=[
            low, low, low, low,
            pltpu.VMEM((2, head_size, length), jnp.bfloat16),
            pltpu.VMEM((2, 1, length), jnp.float32),
            pltpu.VMEM((2, head_size, length), jnp.float32),
            pltpu.VMEM((KEYS, head_size), jnp.float32),
            pltpu.VMEM((KEYS, head_size), jnp.float32),
            pltpu.VMEM((BLOCK, rev_line.shape[1]), jnp.float32),
            pltpu.VMEM((BLOCK, rev_line.shape[1]), jnp.float32),
        ],
        cost_estimate=pl.CostEstimate(
            flops=46_000_000_000, bytes_accessed=4 << 20, transcendentals=0
        ),
        compiler_params=pltpu.CompilerParams(vmem_limit_bytes=48 << 20),
    )(scalars, pieces, rev_line, ctx_wide, lse, qkv)


CHUNKS = 2
MESH_ID = pl.DeviceIdType.MESH
IN_VMEM = pl.BlockSpec(memory_space=pltpu.VMEM)
IN_PLACE = pl.BlockSpec(memory_space=pl.ANY)
COPIES = pltpu.SemaphoreType.DMA


def flip(a, b):
    return a + b - 2 * a * b


def flip_pair(a, b):
    return 2 * flip(a // 2, b // 2) + flip(a % 2, b % 2)


def position():
    s, f = lax.axis_index("seq"), lax.axis_index("fsdp")
    return s // 2, s % 2, f // 2, f % 2


def device(z, y, x, c):
    return (2 * z + y, 2 * x + c)


def ring_of(z):
    high, low = z // 2, z % 2
    following = 2 * low + 1 - high
    return following, (2 * (1 - low) + high, 2 * (1 - high) + 1 - low, following)


def greet(z, y, x, c):
    peers = []
    for d in range(1, 8):
        peers.append(device(z, flip(y, d // 4), flip(x, (d // 2) % 2), flip(c, d % 2)))
        if d > 1:
            peers.append(device(flip_pair(z, d // 2), y, x, flip(c, d % 2)))
    barrier = pltpu.get_barrier_semaphore()
    for peer in peers:
        pl.semaphore_signal(barrier, inc=1, device_id=peer, device_id_type=MESH_ID)
    pl.semaphore_wait(barrier, len(peers))


def remote(source, target, send, recv, to):
    return pltpu.make_async_remote_copy(
        src_ref=source,
        dst_ref=target,
        send_sem=send,
        recv_sem=recv,
        device_id=to,
        device_id_type=MESH_ID,
    )


class Links:
    def __init__(self, send, recv):
        self.send, self.recv, self.used, self.sent = send, recv, 0, []

    def go(self, source, target, to):
        i = self.used
        self.used += 1
        made = remote(source, target, self.send.at[i], self.recv.at[i], to)
        made.start()
        self.sent.append(made)
        return made

    def go_unless(self, own, source, target, to, send=None, recv=None):
        if send is None:
            send, recv = self.send.at[self.used], self.recv.at[self.used]
            self.used += 1
        made = remote(source, target, send, recv, to)
        if own is None:
            made.start()
            self.sent.append(made)
            return made
        local = pltpu.make_async_copy(source, target, recv)
        pl.when(own)(lambda: local.start())
        pl.when(jnp.logical_not(own))(lambda: made.start())
        self.sent.append((own, made))
        return made

    def go_if(self, there, here, source, target, send, recv, to):
        made = remote(source, target, send, recv, to)
        pl.when(there)(lambda: made.start())
        if here is not None:
            local = pltpu.make_async_copy(source, target, recv)
            pl.when(here)(lambda: local.start())
        self.sent.append((jnp.logical_not(there), made))

    def done(self, made):
        made.wait_send()
        self.sent = [m for m in self.sent if m is not made]

    def finish(self):
        for made in self.sent:
            if isinstance(made, tuple):
                pl.when(jnp.logical_not(made[0]))(lambda made=made: made[1].wait_send())
            else:
                made.wait_send()


def share_start(links, rows_all, me):
    z, y, x, c = me
    following, _ = ring_of(z)
    rows = rows_all.shape[1] // CHUNKS
    ring = []
    for h in range(CHUNKS):
        here = pl.ds(h * rows, rows)
        target = rows_all.at[flip_pair(following, z), here]
        ring.append(links.go(rows_all.at[0, here], target, device(following, y, x, c)))
    core = [links.go(rows_all.at[0], rows_all.at[4], device(z, y, x, 1 - c))]
    return [ring], core


def share_step(links, rows_all, me, state, step):
    z, y, x, c = me
    following, back = ring_of(z)
    rows = rows_all.shape[1] // CHUNKS
    ring, core = state
    slot = flip_pair(z, back[step - 1])
    sent = []
    for h in range(CHUNKS):
        here = pl.ds(h * rows, rows)
        ring[-1][h].wait_recv()
        source = rows_all.at[slot, here]
        if step < 3:
            target = rows_all.at[flip_pair(following, back[step - 1]), here]
            sent.append(links.go(source, target, device(following, y, x, c)))
        core.append(links.go(source, rows_all.at[4 + slot, here], device(z, y, x, 1 - c)))
    ring.append(sent)


def share_end(state):
    for made in state[1]:
        made.wait_recv()


def sum_order(z):
    _, back = ring_of(z)
    return [flip_pair(z, b) for b in back] + [0]


def column_go(links, me, k, source, target):
    z, y, x, c = me
    own = z // 2 == c if k == 0 else None
    to = device(2 * c + flip(k, z % 2), y, x, z // 2)
    return links.go_unless(own, source, target, to)


def arrived(place, sem):
    pltpu.make_async_copy(place, place, sem).wait()


def spread_go(links, me, k, source, full, send, recv):
    z, y, x, c = me
    rows = source.shape[0]
    first = pl.multiple_of((4 * c + 2 * flip(k, z % 2) + y) * rows, rows)
    target = full.at[pl.ds(first, rows), :]
    for dy, dx in ((0, 1), (1, 0), (0, 0)):
        own = None if dy + dx else c == x
        to = device(z, flip(y, dy), flip(x, dx), x)
        links.go_unless(own, source, target, to, send.at[k, dy, dx], recv.at[k, dy, c])


def spread_relay(links, me, full, send, recv):
    z, y, x, c = me
    odd = flip(c, x)
    k, step = 1 - odd, 1 - odd
    rows = full.shape[0] // 8
    to = device(z, flip(y, odd), flip(x, 1 - odd), c)
    for r in range(2):
        first = pl.multiple_of((4 * r + 2 * flip(k, z % 2) + flip(y, step)) * rows, rows)
        here = full.at[pl.ds(first, rows), :]
        arrived(here, recv.at[k, step, r])
        made = remote(here, here, send.at[r, 1, 1], recv.at[k, 1, r], to)
        made.start()
        links.sent.append(made)


def spread_wait(me, full, recv):
    z, y, x, c = me
    odd = flip(c, x)
    here = full.at[pl.ds(0, full.shape[0] // 8), :]
    for k, step in ((1 - odd, odd), (odd, 0), (odd, 1)):
        for r in range(2):
            arrived(here, recv.at[k, step, r])


def join_go(links, me, k, grads, into, relay, send, recv, relay_recv):
    z, y, x, c = me
    odd = flip(c, x) == 1
    even = jnp.logical_not(odd)
    rows = into.shape[2]
    for r in range(2):

        def block(step):
            index = 4 * r + 2 * flip(k, z % 2) + flip(y, step)
            return grads.at[pl.ds(pl.multiple_of(index * rows, rows), rows), :]

        same, other = device(z, y, c, r), device(z, 1 - y, c, r)
        mine = jnp.logical_and(even, c == r)
        partner = jnp.logical_and(even, c != r)
        links.go_if(
            partner, mine, block(0), into.at[k, 0], send.at[k, 0, r], recv.at[k, 0], same
        )
        if k == 0:
            links.go_if(even, None, block(1), into.at[0, 1], send.at[0, 1, r], recv.at[0, 1], other)
            to = device(z, 1 - y, x, c)
        else:
            links.go_if(odd, None, block(0), into.at[1, 1], send.at[1, 1, r], recv.at[1, 1], same)
            to = device(z, y, c, c)
        links.go_if(odd, None, block(1), relay.at[r], send.at[k, 2, r], relay_recv.at[r], to)


def join_relay(links, me, grads, into, relay, send, recv, relay_recv):
    z, y, x, c = me
    odd = flip(c, x)
    k, step = 1 - odd, 1 - odd
    rows = into.shape[2]
    for r in range(2):
        arrived(relay.at[r], relay_recv.at[r])
        index = 4 * r + 2 * flip(k, z % 2) + flip(y, step)
        own = grads[pl.ds(pl.multiple_of(index * rows, rows), rows), :]
        total = relay[r].astype(jnp.float32) + own.astype(jnp.float32)
        relay[r] = total.astype(jnp.bfloat16)
        to = device(z, flip(y, step), c, r)
        made = remote(relay.at[r], into.at[k, 2], send.at[0, 3, r], recv.at[k, 2], to)
        made.start()
        links.sent.append(made)


def join_sum(k, into, recv):
    total = 0.0
    for j in range(3):
        arrived(into.at[k, j], recv.at[k, j])
        total = total + into[k, j].astype(jnp.float32)
    return total.astype(jnp.bfloat16)


def rms(rows):
    return lax.rsqrt(jnp.mean(rows * rows, axis=-1, keepdims=True) + epsilon)


def lane_sum(values):
    return jnp.sum(values, axis=-1, keepdims=True)


def head_of(z, y, x, c, heads):
    return 2 * c + z // 2, (z % 2) * (heads // 2) + 2 * x + y


def entry_kernel(
    lengths, tok_ref, cot_ref, small_ref, bucket_ref, wq_ref, wk_ref, wv_ref, wo_ref, wg_ref,
    rows_ref, normed, grads, pieces, weight, gain_one, gain_two, rev_ref, slots_o, slots_g,
    tok_in, cot_in, held, qkv, small, send, recv, plane_send, plane_recv, local,
):
    me = z, y, x, c = position()
    greet(*me)
    links = Links(send, recv)
    f, part, half = 2 * x + c, tok_in.shape[2], tok_in.shape[1]

    def gather_rows(n, ref, into):
        def source(xd, cd):
            return ref.at[xd, pl.ds(pl.multiple_of(cd * half, half), half)]

        own = pltpu.make_async_copy(source(x, c), into.at[f], local.at[n])
        own.start()
        got = []
        for d in (1, 2, 3):
            xd, cd = flip(x, d // 2), flip(c, d % 2)
            got.append(links.go(source(xd, cd), into.at[f], device(z, y, xd, cd)))
        return own, got

    tok_own, tok_got = gather_rows(0, tok_ref, tok_in)
    small[f, z, y] = small_ref[...]
    small_got = []
    for d in (1, 2, 3):
        here = small.at[f, z, y]
        small_got.append(links.go(here, here, device(flip_pair(z, d), y, x, c)))
    group_width = wq_ref.shape[1] // 2
    way = []
    for k in range(2):
        cut = pl.ds(pl.multiple_of(flip(k, z % 2) * group_width, group_width), group_width)
        for n, ref in enumerate((wq_ref, wk_ref, wv_ref)):
            target = held.at[k, :, n * group_width : (n + 1) * group_width]
            way.append(column_go(links, me, k, ref.at[:, cut], target))
    for made in small_got:
        made.wait_recv()
    here = small.at[f, :, y]
    links.go(here, here, device(z, 1 - y, x, c)).wait_recv()
    tables = []
    for d in (1, 2, 3):
        here = small.at[f]
        tables.append(links.go(here, here, device(z, y, flip(x, d // 2), flip(c, d % 2))))
    for i in range(4 * part // BLOCK):
        here = slice(i * BLOCK, (i + 1) * BLOCK)
        block = (i // 2) // 2, (i // 2) % 2
        gain_one[:, here] = small[f, block[0], block[1], i % 2 : i % 2 + 1, :]
        gain_two[:, here] = small[f, block[0], block[1], 2 + i % 2 : 3 + i % 2, :]
    tok_own.wait()
    for made in tok_got:
        made.wait_recv()
    cot_own, cot_got = gather_rows(1, cot_ref, cot_in)
    wide = [tok_in[i].astype(jnp.float32) for i in range(4)]
    mean = sum(lane_sum(w * w) for w in wide) / (4 * part)
    scale = lax.rsqrt(mean + epsilon)
    for i in range(4):
        here = slice(i * part, (i + 1) * part)
        rows_ref[:, here] = tok_in[i]
        normed[0, :, here] = (wide[i] * scale * gain_one[:, here]).astype(jnp.bfloat16)
    first = share_start(links, normed, me)
    for k in range(2):
        for made in way[3 * k : 3 * k + 3]:
            made.wait_recv()
        spread_go(links, me, k, held.at[k], weight, plane_send, plane_recv)
    share_step(links, normed, me, first, 1)
    share_step(links, normed, me, first, 2)
    later = []
    half_ffn = wg_ref.shape[1] // 2
    for k in range(2):
        side = flip(k, z % 2)
        cut = pl.ds(pl.multiple_of(side * group_width, group_width), group_width)
        later.append(column_go(links, me, k, wo_ref.at[:, cut], slots_o.at[k]))
        cut = pl.ds(pl.multiple_of(side * half_ffn, half_ffn), half_ffn)
        later.append(column_go(links, me, k, wg_ref.at[:, cut], slots_g.at[k]))
    spread_relay(links, me, weight, plane_send, plane_recv)
    for made in tables:
        made.wait_recv()
    group = qkv.shape[1]
    heads = 2 * group
    source, place = head_of(z, y, x, c, heads)
    lane = lax.broadcasted_iota(jnp.int32, (1, BLOCK), 1)
    line = jnp.zeros(bucket_ref.shape, jnp.float32)
    per_block = 4
    for n in range(8 * per_block):
        block = n // per_block
        row = small[source, block // 2, block % 2, 4:5, :]
        value = lane_sum(jnp.where(lane == (n % per_block) * heads + place, row, 0.0))
        line = jnp.where(bucket_ref[...] == n, value, line)
    rev_ref[...] = line
    spread_wait(me, weight, plane_recv)
    rows = normed.shape[1]
    sent = []

    def project(d):
        out = jnp.dot(pair_of(normed, d), weight[...], preferred_element_type=jnp.float32)
        out = out.astype(jnp.bfloat16).T
        for side, slot in enumerate((d, 4 + d)):
            here = lanes(slot * rows, rows)
            cut = out[:, side * rows : (side + 1) * rows]
            qkv[:, :, :, here] = cut.reshape(3, group, DH, rows)
            pieces[0, :, :, here] = qkv[:, 2 * x + y, :, here]
            for e in (1, 2, 3):
                xd, yd = flip(x, e // 2), flip(y, e % 2)
                source = qkv.at[:, 2 * xd + yd, :, here]
                sent.append(links.go(source, pieces.at[e, :, :, here], device(z, yd, xd, c)))

    cot_own.wait()
    for made in cot_got:
        made.wait_recv()
    slot = (4 * z + 2 * y + c) * half + lax.broadcasted_iota(jnp.int32, (half, part), 0)
    valid = slot < jnp.where(x == 0, lengths[0], lengths[1])
    for i in range(4):
        grads[:, i * part : (i + 1) * part] = jnp.where(valid, cot_in[i], jnp.zeros_like(cot_in[i]))
    order = sum_order(z)
    first[1][0].wait_recv()
    project(0)
    for step in (1, 2, 3):
        if step == 3:
            share_step(links, normed, me, first, 3)
        for made in first[1][1 + CHUNKS * (step - 1) : 1 + CHUNKS * step]:
            made.wait_recv()
        project(order[step - 1])
    for made in sent + later:
        made.wait_recv()
    links.finish()


def low_array(*shape):
    return jax.ShapeDtypeStruct(shape, jnp.bfloat16)


def wide_array(*shape):
    return jax.ShapeDtypeStruct(shape, jnp.float32)


def low_space(*shape):
    return pltpu.VMEM(shape, jnp.bfloat16)


def entry(lengths, tokens_in, cotangent, small, rev_buckets, weights):
    _, slot_count, part = tokens_in.shape
    rows, width = slot_count // 2, 4 * part
    depth, cols = weights[0].shape
    group = cols // (2 * DH)
    wide = 3 * cols // 2
    return pl.pallas_call(
        entry_kernel,
        name="entry",
        out_shape=[
            low_array(rows, width),
            low_array(8, rows, width),
            low_array(rows, width),
            low_array(4, 3, DH, 8 * rows),
            low_array(8 * depth, wide),
            wide_array(1, width),
            wide_array(1, width),
            wide_array(*rev_buckets.shape),
            low_array(2, depth, cols // 2),
            low_array(2, depth, weights[4].shape[1] // 2),
        ],
        in_specs=[pl.BlockSpec(memory_space=pltpu.SMEM)]
        + [IN_PLACE] * 2
        + [IN_VMEM] * 2
        + [IN_PLACE] * 5,
        out_specs=[IN_VMEM] * 10,
        scratch_shapes=[
            low_space(4, rows, part),
            low_space(4, rows, part),
            low_space(2, depth, wide),
            low_space(3, group, DH, 8 * rows),
            pltpu.VMEM((4, 4, 2, 8, BLOCK), jnp.float32),
            COPIES((64,)),
            COPIES((64,)),
            COPIES((2, 2, 2)),
            COPIES((2, 2, 2)),
            COPIES((2,)),
        ],
        compiler_params=pltpu.CompilerParams(
            collective_id=1, has_side_effects=True, vmem_limit_bytes=48 << 20
        ),
    )(lengths, tokens_in, cotangent, small, rev_buckets, *weights)


def gelu_pair(t):
    inner = jnp.tanh(root_two_over_pi * (t + 0.044715 * (t * t * t)))
    half = 0.5 * (1.0 + inner)
    slope = half + 0.5 * t * (1.0 - inner * inner) * root_two_over_pi * (1.0 + 0.134145 * (t * t))
    return t * half, slope


def pair_of(ref, slot):
    return jnp.concatenate([ref[slot], ref[4 + slot]], axis=0)


def pair_go(links, me, core, i, terms, core_out, core_in):
    z, y, x, c = me
    size = terms.shape[0] // 2
    core_out[i] = terms[size:].astype(jnp.bfloat16)
    core.append(links.go(core_out.at[i], core_in.at[i], device(z, y, x, 1 - c)))
    return terms[:size]


def sum_step(links, me, core, ring, i, mine, core_in, ring_out, ring_in):
    z, y, x, c = me
    following, _ = ring_of(z)
    rows = mine.shape[0] // CHUNKS
    core.wait_recv()
    sent, last = [], []
    for h in range(CHUNKS):
        cut = slice(h * rows, (h + 1) * rows)
        here = pl.ds(h * rows, rows)
        value = mine[cut] + core_in[i, here, :].astype(jnp.float32)
        if i:
            ring[-1][h].wait_recv()
            value = value + ring_in[i - 1, here, :].astype(jnp.float32)
        if i < 3:
            ring_out[i, here, :] = value.astype(jnp.bfloat16)
            target = ring_in.at[i, here]
            sent.append(links.go(ring_out.at[i, here], target, device(following, y, x, c)))
        else:
            last.append(value)
    ring.append(sent)
    return last


def reduce_pair(links, me, state, i, terms, core_out, core_in, ring_out, ring_in):
    mine = pair_go(links, me, state[0], i, terms, core_out, core_in)
    return sum_step(links, me, state[0][i], state[1], i, mine, core_in, ring_out, ring_in)


def core_kernel(
    ctx_ref, rows_ref, gain_ref, own_ref, slots_o, slots_g, slot_ud0, slot_ud1,
    layer_ref, context, low, wide_ref, part_ref, pieces, in_gu, in_d,
    residual_ref, down, hidden, out_weight, gate_up, normed, grads, pre, ctx_all, heads_out, grad_gu, grad_d,
    mine, core_out, core_in, ring_out, ring_in, ring_out2, ring_in2,
    relay_gu, relay_d, send, recv, plane_send, plane_recv, join_send, join_recv, relay_recv,
):
    me = z, y, x, c = position()
    greet(*me)
    links = Links(send, recv)
    own = 2 * x + y
    heads = []
    for d in (1, 2, 3):
        xd, yd = flip(x, d // 2), flip(y, d % 2)
        heads.append(links.go(ctx_ref.at[d], ctx_all.at[own], device(z, yd, xd, c)))
    grads[0] = own_ref[...]
    second = share_start(links, grads, me)

    ffn = down.shape[1]
    fulls = out_weight, gate_up.at[:, :ffn], gate_up.at[:, ffn:], down

    def weight_go(n):
        slots = (
            (slots_o.at[0], slots_o.at[1]),
            (slots_g.at[0], slots_g.at[1]),
            (slot_ud0.at[:, :ffn], slot_ud1.at[:, :ffn]),
            (slot_ud0.at[:, ffn:], slot_ud1.at[:, ffn:]),
        )[n]
        for k in range(2):
            spread_go(links, me, k, slots[k], fulls[n], plane_send.at[n], plane_recv.at[n])

    def weight_relay(n):
        spread_relay(links, me, fulls[n], plane_send.at[n], plane_recv.at[n])

    def weight_wait(n):
        spread_wait(me, fulls[n], plane_recv.at[n])

    weight_go(0)
    ctx_all[own] = ctx_ref[0]
    for made in heads:
        made.wait_recv()
    group, size, tokens = ctx_all.shape
    rows, width = residual_ref.shape
    depth = gate_up.shape[0] // 8
    half_tokens = tokens // 2
    context[...] = ctx_all[...].reshape(group * size, tokens).T
    weight_relay(0)
    weight_go(1)
    weight_go(2)
    weight_wait(0)
    order = sum_order(z)

    def first_row(block):
        return pl.multiple_of(block * rows, rows)

    def pair_rows(ref, d):
        return jnp.concatenate(
            [ref[pl.ds(first_row(d), rows), :], ref[pl.ds(first_row(4 + d), rows), :]], axis=0
        )

    state = [], []
    for i in range(4):
        terms = right_transposed(pair_rows(context, order[i]), out_weight[...])
        last = reduce_pair(links, me, state, i, terms, core_out, core_in, ring_out, ring_in)
        if i < 3:
            share_step(links, grads, me, second, i + 1)
        if i == 1:
            weight_go(3)
        if i == 2:
            weight_relay(1)
            weight_relay(2)
    residual = rows_ref[...].astype(jnp.float32) + jnp.concatenate(last, axis=0)
    residual_ref[...] = residual
    gain = gain_ref[...]
    normed[0] = (residual * rms(residual) * gain).astype(jnp.bfloat16)
    shared = share_start(links, normed, me)
    weight_relay(3)
    share_end(second)
    for made in state[0] + sum(state[1], []):
        links.done(made)
    ring = []

    def take_in(i):
        share_step(links, normed, me, shared, i + 1)

    def feed(i):
        d = order[i]
        for made in shared[1][:1] if i == 3 else shared[1][1 + CHUNKS * i : 1 + CHUNKS * (i + 1)]:
            made.wait_recv()
        gate_up_pre = jnp.dot(
            pair_of(normed, d), gate_up[...], preferred_element_type=jnp.float32
        )
        activated, slope = gelu_pair(gate_up_pre[:, :ffn])
        up_pre = gate_up_pre[:, ffn:]
        made = (activated * up_pre).astype(jnp.bfloat16)
        hidden[pl.ds(first_row(d), rows), :] = made[:rows]
        hidden[pl.ds(first_row(4 + d), rows), :] = made[rows:]
        if i == 0:
            weight_wait(3)
        grad_hidden = jnp.dot(pair_of(grads, d), down[...], preferred_element_type=jnp.float32)
        grad_pre = jnp.concatenate(
            [
                (grad_hidden * up_pre * slope).astype(jnp.bfloat16),
                (grad_hidden * activated).astype(jnp.bfloat16),
            ],
            axis=1,
        )
        pre[pl.ds(first_row(d), rows), :] = grad_pre[:rows]
        pre[pl.ds(first_row(4 + d), rows), :] = grad_pre[rows:]
        terms = right_transposed(grad_pre, gate_up[...])
        kept = []
        mine[i] = pair_go(links, me, kept, i, terms, core_out, core_in)
        return kept[0]

    def pass_on(i, core):
        return sum_step(links, me, core, ring, i, mine[i], core_in, ring_out2, ring_in2)

    joins = (grad_gu, in_gu, relay_gu), (grad_d, in_d, relay_d)

    def weight_grads(k):
        for n in range(4):
            block = 4 * (n // 2) + 2 * flip(k, z % 2) + n % 2
            here = pl.ds(pl.multiple_of(block * depth, depth), depth)
            left = normed[:, :, here].reshape(tokens, depth)
            grad_gu[here, :] = left_transposed(left, pre[...]).astype(jnp.bfloat16)
            left = grads[:, :, here].reshape(tokens, depth)
            grad_d[here, :] = left_transposed(left, hidden[...]).astype(jnp.bfloat16)
        for n, (grad, into, relay) in enumerate(joins):
            sems = join_send.at[n], join_recv.at[n], relay_recv.at[n]
            join_go(links, me, k, grad, into, relay, *sems)

    take_in(0)
    weight_wait(1)
    weight_wait(2)
    first = feed(0)
    pass_on(0, first)
    take_in(1)
    following = feed(1)
    take_in(2)
    final = feed(3)
    pass_on(1, following)
    third = feed(2)
    weight_grads(0)
    pass_on(2, third)
    weight_grads(1)
    last = pass_on(3, final)
    normed_grad = jnp.concatenate(last, axis=0)
    residual = residual_ref[...]
    scale = rms(residual)
    unit = residual * scale
    part_ref[...] = jnp.sum(normed_grad * unit, axis=0, keepdims=True)
    out = own_ref[...].astype(jnp.float32) + norm_back(normed_grad, unit, scale, gain)
    wide_ref[...] = out
    low[0] = out.astype(jnp.bfloat16)
    shared = share_start(links, low, me)
    sent = []

    def context_back(d):
        made = jnp.dot(pair_of(low, d), out_weight[...], preferred_element_type=jnp.float32)
        made = made.astype(jnp.bfloat16).T
        for half, slot in enumerate((d, 4 + d)):
            here = lanes(slot * rows, rows)
            cut = made[:, half * rows : (half + 1) * rows]
            heads_out[:, :, here] = cut.reshape(group, size, rows)
            pieces[0, :, here] = heads_out[own, :, here]
            for e in (1, 2, 3):
                xd, yd = flip(x, e // 2), flip(y, e % 2)
                source = heads_out.at[2 * xd + yd, :, here]
                sent.append(links.go(source, pieces.at[e, :, here], device(z, yd, xd, c)))

    shared[1][0].wait_recv()
    context_back(0)
    for made in (first, following, third, final):
        links.done(made)
    layer_core, layer_ring = [], []
    for i in range(4):
        terms = right_transposed(pair_rows(hidden, order[i]), down[...])
        mine[i] = pair_go(links, me, layer_core, i, terms, core_out, core_in)

    def layer_step(i):
        made = layer_core[i]
        return sum_step(links, me, made, layer_ring, i, mine[i], core_in, ring_out, ring_in)

    for step in (1, 2, 3):
        share_step(links, low, me, shared, step)
        if step == 2:
            layer_step(0)
            for n, (grad, into, relay) in enumerate(joins):
                sems = join_send.at[n], join_recv.at[n], relay_recv.at[n]
                join_relay(links, me, grad, into, relay, *sems)
        for made in shared[1][1 + CHUNKS * (step - 1) : 1 + CHUNKS * step]:
            made.wait_recv()
        context_back(order[step - 1])
    layer_step(1)
    layer_step(2)
    last = layer_step(3)
    layer = (residual_ref[...] + jnp.concatenate(last, axis=0)).astype(jnp.bfloat16)
    part = width // 4
    for i in range(4):
        layer_ref[i] = layer[:, i * part : (i + 1) * part]
    for made in sent:
        made.wait_recv()
    for n, (_, into, _) in enumerate(joins):
        for k in range(2):
            for j in range(3):
                arrived(into.at[k, j], join_recv.at[n, k, j])
    links.finish()


def reduce_space(rows, width):
    return [
        low_space(4, rows, width),
        low_space(4, rows, width),
        low_space(3, rows, width),
        low_space(3, rows, width),
    ]


def core(ctx_pieces, token_rows, gain, grad_own, slots_o, slots_g, slots_ud):
    _, size, tokens = ctx_pieces.shape
    rows, width = token_rows.shape
    _, depth, ffn = slots_g.shape
    group = slots_o.shape[2] // DH
    return pl.pallas_call(
        core_kernel,
        name="core",
        out_shape=[
            low_array(4, rows, width // 4),
            low_array(tokens, 4 * size),
            low_array(8, rows, width),
            wide_array(rows, width),
            wide_array(1, width),
            low_array(4, size, tokens),
            low_array(2, 3, depth, 2 * ffn),
            low_array(2, 3, depth, ffn),
        ],
        in_specs=[IN_VMEM] * 4 + [IN_PLACE] * 4,
        out_specs=[IN_VMEM] * 6 + [IN_PLACE] * 2,
        scratch_shapes=[
            pltpu.VMEM((rows, width), jnp.float32),
            low_space(8 * depth, ffn),
            low_space(tokens, ffn),
            low_space(8 * depth, group * size),
            low_space(8 * depth, 2 * ffn),
            low_space(8, rows, width),
            low_space(8, rows, width),
            low_space(tokens, 2 * ffn),
            low_space(4, size, tokens),
            low_space(group, size, tokens),
            low_space(8 * depth, 2 * ffn),
            low_space(8 * depth, ffn),
            pltpu.VMEM((4, rows, width), jnp.float32),
            *reduce_space(rows, width),
            low_space(3, rows, width),
            low_space(3, rows, width),
            low_space(2, depth, 2 * ffn),
            low_space(2, depth, ffn),
            COPIES((112,)),
            COPIES((112,)),
            COPIES((4, 2, 2, 2)),
            COPIES((4, 2, 2, 2)),
            COPIES((2, 2, 4, 2)),
            COPIES((2, 2, 3)),
            COPIES((2, 2)),
        ],
        compiler_params=pltpu.CompilerParams(
            collective_id=2, has_side_effects=True, vmem_limit_bytes=63 << 20
        ),
    )(ctx_pieces, token_rows, gain, grad_own, slots_o, slots_g, *slots_ud)


def exit_kernel(
    piece_ref, normed_ref, weight_ref, token_ref, wide_ref, gain_ref, low_ref, context_ref,
    layer_own, gain_two_ref, line_ref, bucket_ref,
    query_out, key_out, value_out, output_out, home_ref, layer_ref, small_ref,
    heads_in, rows_low, weight_grad, weight_in, weight_relay, held, token_out,
    packed, in_f, in_y, in_z,
    core_out, core_in, ring_out, ring_in,
    send, recv, plane_send, plane_recv, relay_recv,
):
    me = z, y, x, c = position()
    greet(*me)
    links = Links(send, recv)
    own, f = 2 * x + y, 2 * x + c
    group, three, size, tokens = heads_in.shape
    rows = tokens // 8
    depth, cols = weight_grad.shape[1] // 8, weight_grad.shape[2]
    width = normed_ref.shape[2]
    part = width // 4
    heads = []
    for d in (1, 2, 3):
        xd, yd = flip(x, d // 2), flip(y, d % 2)
        heads.append(links.go(piece_ref.at[d], heads_in.at[own], device(z, yd, xd, c)))
    heads_in[own] = piece_ref[0]

    order = sum_order(z)

    def pair_rows(ref, d):
        return jnp.concatenate(
            [ref[lanes(block * rows, rows), :] for block in (d, 4 + d)], axis=0
        )

    def to_home(source, into):
        got = []
        for d in (1, 2, 3):
            xd, cd = flip(x, d // 2), flip(c, d % 2)
            got.append(links.go(source.at[2 * xd + cd], into.at[f], device(z, y, xd, cd)))
        into[f] = source[f]
        return got

    state = [], []

    def join(n):
        sems = plane_send.at[n], plane_recv.at[n], relay_recv.at[n]
        return weight_grad.at[n], weight_in.at[n], weight_relay.at[n], *sems

    def step(i):
        terms = right_transposed(pair_rows(rows_low, order[i]), weight_ref[...])
        return reduce_pair(links, me, state, i, terms, core_out, core_in, ring_out, ring_in)

    def weight_grads(n, ref, right):
        for k in range(2):
            for piece in range(4):
                block = 4 * (piece // 2) + 2 * flip(k, z % 2) + piece % 2
                here = pl.ds(pl.multiple_of(block * depth, depth), depth)
                left = ref[:, :, here].reshape(tokens, depth)
                weight_grad[n, here, :] = left_transposed(left, right).astype(jnp.bfloat16)
            join_go(links, me, k, *join(n))

    way = []
    results = query_out, key_out, value_out, output_out
    cut = pl.ds(pl.multiple_of((z % 2) * cols, cols), cols)

    def send_sums(n):
        for k in range(2):
            held[n, k] = join_sum(k, weight_in.at[n], plane_recv.at[n])
            way.append(column_go(links, me, k, held.at[n, k], results[n].at[:, cut]))

    weight_grads(3, low_ref, context_ref[...])

    packed[...] = jnp.zeros_like(packed)
    per_block = 4
    all_heads = BLOCK // per_block
    source, place = head_of(z, y, x, c, all_heads // 4)
    lane = lax.broadcasted_iota(jnp.int32, (1, BLOCK), 1)
    for block in range(8):
        row = jnp.zeros((1, BLOCK), jnp.float32)
        for n in range(per_block):
            hot = bucket_ref[...] == block * per_block + n
            value = lane_sum(jnp.where(hot, line_ref[...], 0.0))
            row = jnp.where(lane == n * all_heads + source * (all_heads // 4) + place, value, row)
        packed[block // 2, block % 2, 4:5, :] = row
    for made in heads:
        made.wait_recv()
    for n in range(three):
        here = slice(n * group * size, (n + 1) * group * size)
        rows_low[:, here] = heads_in[:, n].reshape(group * size, tokens).T
    step(0)
    for n in range(three):
        weight_grads(n, normed_ref, rows_low[:, n * cols : (n + 1) * cols])
    join_relay(links, me, *join(3))
    step(1)
    send_sums(3)
    join_relay(links, me, *join(0))
    join_relay(links, me, *join(1))
    step(2)
    join_relay(links, me, *join(2))
    home = to_home(layer_own, layer_ref)
    for n in range(three):
        send_sums(n)
    last = step(3)
    normed_grad = jnp.concatenate(last, axis=0)
    tokens_wide = token_ref[...].astype(jnp.float32)
    scale = rms(tokens_wide)
    unit = tokens_wide * scale
    token_grad = wide_ref[...] + norm_back(normed_grad, unit, scale, gain_ref[...])
    for i in range(4):
        token_out[i] = token_grad[:, i * part : (i + 1) * part].astype(jnp.bfloat16)
    home += to_home(token_out, home_ref)
    gain_part = jnp.sum(normed_grad * unit, axis=0, keepdims=True)
    for i in range(width // BLOCK):
        here = slice(i * BLOCK, (i + 1) * BLOCK)
        block = (i // 2) // 2, (i // 2) % 2
        packed[block[0], block[1], i % 2 : i % 2 + 1, :] = gain_part[:, here]
        packed[block[0], block[1], 2 + i % 2 : 3 + i % 2, :] = gain_two_ref[:, here]
    got = []
    for d in (1, 2, 3):
        to = device(z, y, flip(x, d // 2), flip(c, d % 2))
        got.append(links.go(packed, in_f.at[d - 1], to))
    for made in got:
        made.wait_recv()
    for made in got:
        links.done(made)
    packed[...] = packed[...] + in_f[0] + in_f[1] + in_f[2]
    made = links.go(packed.at[:, 1 - y], in_y, device(z, 1 - y, x, c))
    made.wait_recv()
    in_y[...] = in_y[...] + packed[:, y]
    got = []
    for d in (1, 2, 3):
        other = flip_pair(z, d)
        got.append(links.go(in_y.at[other], in_z.at[d - 1], device(other, y, x, c)))
    for made in got:
        made.wait_recv()
    small_ref[...] = in_y[z] + in_z[0] + in_z[1] + in_z[2]
    for made in way + home:
        made.wait_recv()
    links.finish()


def leave(pieces, normed, weight, token_rows, wide_grad, gain, low, context, layer,
          gain_two_part, line_grad, rev_buckets):
    _, _, size, tokens = pieces.shape
    rows, width = token_rows.shape
    depth, wide = weight.shape[0] // 8, weight.shape[1]
    out_wide = context.shape[1]
    cols = 2 * wide // 3
    tile = (8, BLOCK)
    return pl.pallas_call(
        exit_kernel,
        name="leave",
        out_shape=[
            *(low_array(depth, cols) for _ in range(4)),
            low_array(4, rows, width // 4),
            low_array(4, rows, width // 4),
            wide_array(*tile),
        ],
        in_specs=[IN_VMEM] * 12,
        out_specs=[IN_VMEM] * 7,
        scratch_shapes=[
            low_space(4, 3, size, tokens),
            low_space(tokens, wide),
            low_space(4, 8 * depth, out_wide),
            low_space(4, 2, 3, depth, out_wide),
            low_space(4, 2, depth, out_wide),
            low_space(4, 2, depth, out_wide),
            low_space(4, rows, width // 4),
            pltpu.VMEM((4, 2, *tile), jnp.float32),
            pltpu.VMEM((3, 4, 2, *tile), jnp.float32),
            pltpu.VMEM((4, *tile), jnp.float32),
            pltpu.VMEM((3, *tile), jnp.float32),
            *reduce_space(rows, width),
            COPIES((64,)),
            COPIES((64,)),
            COPIES((4, 2, 4, 2)),
            COPIES((4, 2, 3)),
            COPIES((4, 2)),
        ],
        compiler_params=pltpu.CompilerParams(
            collective_id=4, has_side_effects=True, vmem_limit_bytes=60 << 20
        ),
    )(pieces, normed, weight, token_rows, wide_grad, gain, low, context, layer,
      gain_two_part, line_grad, rev_buckets)


def widen_kernel(*refs):
    attn, slots, home, outs = refs[:4], refs[4:6], refs[6], refs[7:]
    z_low = (lax.axis_index("seq") // 2) % 2
    for ref, out in zip(attn, outs[:4]):
        out[...] = ref[...].astype(jnp.float32)
    size = slots[0].shape[1] // 3
    for k in range(2):
        cut = lanes((k + z_low - 2 * k * z_low) * size, size)
        for n, out in enumerate(outs[4:7]):
            out[:, cut] = slots[k][:, n * size : (n + 1) * size].astype(jnp.float32)
    outs[7][...] = home[...].astype(jnp.float32)


def widen(attn, slots, home):
    depth, cols = attn[0].shape
    size = 2 * slots[0].shape[1] // 3
    return pl.pallas_call(
        widen_kernel,
        name="widen",
        out_shape=[wide_array(depth, cols)] * 4
        + [wide_array(depth, size)] * 3
        + [wide_array(*home.shape)],
        in_specs=[IN_VMEM] * 7,
        out_specs=[IN_VMEM] * 8,
        compiler_params=pltpu.CompilerParams(vmem_limit_bytes=32 << 20),
    )(*attn, *slots, home)


def fast_shards(
    tokens_in,
    cotangent,
    gain_attn,
    query_weight,
    key_weight,
    value_weight,
    output_weight,
    bias_table,
    gain_ffn,
    gate_weight,
    up_weight,
    down_weight,
    lengths,
    buckets,
):
    seq_index, fsdp_index = lax.axis_index("seq"), lax.axis_index("fsdp")
    z, y, x, c = seq_index // 2, seq_index % 2, fsdp_index // 2, fsdp_index % 2
    z_low, z_high = z % 2, z // 2
    batch_count, slot_count, part_width = tokens_in.shape
    width = part_width * 4
    row_count = query_weight.shape[0]
    heads = query_weight.shape[1] // DH
    group_heads = heads // 2
    group_width = group_heads * DH
    hidden_width = gate_weight.shape[1] // 2
    def halves(weights):
        slots = []
        for k in range(2):
            half = k ^ z_low
            slots.append(
                jnp.concatenate(
                    [
                        lax.dynamic_slice_in_dim(w, half * (w.shape[1] // 2), w.shape[1] // 2, 1)
                        for w in weights
                    ],
                    axis=1,
                )
            )
        return slots

    small = jnp.concatenate(
        [gain_attn, gain_ffn, bias_table.reshape(-1), jnp.zeros((2 * row_count - bias_table.size,), jnp.bfloat16)]
    )
    small = small.astype(jnp.float32).reshape(8, BLOCK)
    rev_buckets = jnp.concatenate([buckets[::-1], jnp.full((1,), -1, jnp.int32)])[None, :]
    (
        token_low,
        normed_one,
        grad_own,
        pieces,
        qkv_weight,
        gain_one,
        gain_two,
        rev_line,
        slots_o,
        slots_g,
    ) = entry(
        lengths,
        tokens_in,
        cotangent,
        small,
        rev_buckets,
        (query_weight, key_weight, value_weight, output_weight, gate_weight),
    )
    pieces, *later = lax.optimization_barrier((pieces, *halves([up_weight, down_weight])))
    slots_ud = [move(later[k], spread_slot(k)) for k in range(2)]
    context_pieces, context_wide, lse, qkv_all = attend(lengths, pieces, rev_line)
    (
        layer,
        context,
        residual_low,
        residual_grad,
        gain_two_part,
        grad_pieces,
        terms_gate_up,
        terms_down,
    ) = core(context_pieces, token_low, gain_two, grad_own, slots_o, slots_g, slots_ud)

    def slot_sum(k):
        sums = [
            jnp.sum(t[k].astype(jnp.float32), axis=0).astype(jnp.bfloat16)
            for t in (terms_gate_up, terms_down)
        ]
        return jnp.concatenate(sums, axis=1)

    ffn_slots = [move(slot_sum(k), spread_slot(k)) for k in range(2)]
    qkv_grad_pieces, line_grad = attend_back(
        lengths, grad_pieces, rev_line, context_wide, lse, qkv_all
    )
    qkv_grad_pieces, *ffn_slots = lax.optimization_barrier((qkv_grad_pieces, *ffn_slots))
    *attn_sums, home, layer, small = leave(
        qkv_grad_pieces,
        normed_one,
        qkv_weight,
        token_low,
        residual_grad,
        gain_one,
        residual_low,
        context,
        layer,
        gain_two_part,
        line_grad,
        rev_buckets,
    )
    query_sum, key_sum, value_sum, output_sum, gate_sum, up_sum, down_sum, home = widen(
        attn_sums, ffn_slots, home
    )
    token_share = home.reshape(batch_count, slot_count, part_width)
    layer_out = layer.reshape(batch_count, slot_count, part_width)
    table_sum = lax.dynamic_slice_in_dim(
        small[4].reshape(-1, 4 * heads), fsdp_index * heads, heads, 1
    )
    return (
        layer_out,
        token_share,
        small[:2].reshape(-1),
        query_sum,
        key_sum,
        value_sum,
        output_sum,
        table_sum,
        small[2:4].reshape(-1),
        gate_sum,
        up_sum,
        down_sum,
    )


def solution(mesh):
    placed = (
        P(None, "seq", "fsdp"),
        P(None, "seq", "fsdp"),
        P("seq"),
        P("seq", "fsdp"),
        P("seq", "fsdp"),
        P("seq", "fsdp"),
        P("seq", "fsdp"),
        P("seq", "fsdp"),
        P("seq"),
        P("seq", "fsdp"),
        P("seq", "fsdp"),
        P("seq", "fsdp"),
        P(),
        P(),
    )
    return jax.shard_map(
        fast_shards if (mesh.shape["seq"], mesh.shape["fsdp"]) == (8, 4) else shards,
        mesh=mesh,
        in_specs=placed,
        out_specs=(
            P(None, "seq", "fsdp"),
            P(None, "seq", "fsdp"),
            P("seq"),
            P("seq", "fsdp"),
            P("seq", "fsdp"),
            P("seq", "fsdp"),
            P("seq", "fsdp"),
            P("seq", "fsdp"),
            P("seq"),
            P("seq", "fsdp"),
            P("seq", "fsdp"),
            P("seq", "fsdp"),
        ),
        check_vma=False,
    )
```

```python
from functools import partial

import jax
import jax.numpy as jnp
from jax import lax
from jax.experimental import pallas as pl
from jax.experimental.pallas import tpu as pltpu
from jax.sharding import PartitionSpec as P

DH = 64


epsilon = 1e-06
highest = lax.Precision.HIGHEST
masked_score = -1e30
root_two_over_pi = 0.7978845608028654


def plain_product(left, right):
    return jnp.dot(left, right, preferred_element_type=jnp.float32)


def right_transposed(left, right):
    return lax.dot_general(
        left, right, (((1,), (1,)), ((), ())), preferred_element_type=jnp.float32
    )


def left_transposed(left, right):
    return lax.dot_general(
        left, right, (((0,), (0,)), ((), ())), preferred_element_type=jnp.float32
    )


def normalize(rows, gain):
    row_scale = lax.rsqrt(jnp.mean(rows * rows, axis=-1, keepdims=True) + epsilon)
    unit_rows = rows * row_scale
    return (unit_rows, row_scale, (unit_rows * gain.astype(jnp.float32)).astype(jnp.bfloat16))


def norm_back(grad_normed, unit_rows, row_scale, gain):
    weighted = grad_normed * gain.astype(jnp.float32)
    return row_scale * (
        weighted - unit_rows * jnp.mean(weighted * unit_rows, axis=-1, keepdims=True)
    )


def to_heads(rows, batch_count, head_size):
    slot_count = rows.shape[0] // batch_count
    number_of_heads = rows.shape[1] // head_size
    return rows.reshape(batch_count, slot_count, number_of_heads, head_size).transpose(2, 0, 1, 3)


def from_heads(blocks):
    number_of_heads, batch_count, slot_count, head_size = blocks.shape
    return blocks.transpose(1, 2, 0, 3).reshape(
        batch_count * slot_count, number_of_heads * head_size
    )


def bias_rows(bias_line, first_query, slot_count, length):
    span = slot_count + length - 1
    segment = lax.dynamic_slice_in_dim(bias_line, length - first_query - slot_count, span)
    flat = jnp.tile(segment, slot_count)
    skewed = flat[slot_count - 1 : slot_count - 1 + slot_count * (span - 1)].reshape(
        slot_count, span - 1
    )
    return skewed[:, :length]


def bias_rows_back(block_grad, first_query, slot_count, length, line_length):
    span = slot_count + length - 1
    widened = jnp.pad(block_grad, ((0, 0), (0, span - 1 - length)))
    flat = jnp.pad(widened.reshape(-1), (slot_count - 1, 1))
    segment_grad = jnp.sum(flat.reshape(slot_count, span), axis=0)
    return lax.dynamic_update_slice_in_dim(
        jnp.zeros((line_length,), jnp.float32), segment_grad, length - first_query - slot_count, 0
    )


def full_features(block):
    gathered = lax.all_gather(block, "fsdp", axis=2, tiled=True)
    return gathered.reshape(gathered.shape[0] * gathered.shape[1], gathered.shape[2])


def feature_total(partial_rows):
    return lax.psum(partial_rows, "fsdp")


def shards(
    tokens_in,
    cotangent,
    gain_attn,
    query_weight,
    key_weight,
    value_weight,
    output_weight,
    bias_table,
    gain_ffn,
    gate_weight,
    up_weight,
    down_weight,
    lengths,
    buckets,
):
    batch_count, slot_count, part_width = tokens_in.shape
    head_size = DH
    seq_index = lax.axis_index("seq")
    fsdp_index = lax.axis_index("fsdp")
    length = slot_count * lax.axis_size("seq")
    line_length = buckets.shape[0]
    first_query = seq_index * slot_count
    positions = jnp.arange(length, dtype=jnp.int32)
    query_positions = first_query + jnp.arange(slot_count, dtype=jnp.int32)
    key_valid = positions[None, :] < lengths[:, None]
    own_valid = query_positions[None, :] < lengths[:, None]
    gain_one, query_full, key_full, value_full, output_full, table_full = (
        lax.all_gather(gain_attn, "seq", axis=0, tiled=True),
        lax.all_gather(query_weight, "seq", axis=0, tiled=True),
        lax.all_gather(key_weight, "seq", axis=0, tiled=True),
        lax.all_gather(value_weight, "seq", axis=0, tiled=True),
        lax.all_gather(output_weight, "seq", axis=0, tiled=True),
        lax.all_gather(bias_table, "seq", axis=0, tiled=True),
    )
    token_rows = full_features(tokens_in).astype(jnp.float32)
    unit_one, scale_one, normed_one = normalize(token_rows, gain_one)
    query_heads = to_heads(
        plain_product(normed_one, query_full).astype(jnp.bfloat16), batch_count, head_size
    )
    key_heads = to_heads(
        plain_product(normed_one, key_full).astype(jnp.bfloat16), batch_count, head_size
    )
    value_heads = to_heads(
        plain_product(normed_one, value_full).astype(jnp.bfloat16), batch_count, head_size
    )
    number_of_heads = query_heads.shape[0]
    flat_shape = (number_of_heads, batch_count, slot_count * head_size)
    gathered_keys, gathered_values = (
        lax.all_gather(key_heads.reshape(flat_shape), "seq", axis=2, tiled=True),
        lax.all_gather(value_heads.reshape(flat_shape), "seq", axis=2, tiled=True),
    )
    all_keys = gathered_keys.reshape(number_of_heads, batch_count, length, head_size)
    all_values = gathered_values.reshape(number_of_heads, batch_count, length, head_size)
    bucket_hot = (
        buckets[:, None] == jnp.arange(table_full.shape[0], dtype=jnp.int32)[None, :]
    ).astype(jnp.float32)
    offset_bias = lax.dot_general(
        table_full.astype(jnp.float32), bucket_hot, (((0,), (1,)), ((), ())), precision=highest
    )

    def masked_scores(query_tile_rows, key_tile_rows, bias_block):
        raw = (
            jnp.einsum(
                "jht,jxt->jhx", query_tile_rows, key_tile_rows, preferred_element_type=jnp.float32
            )
            + bias_block[None]
        )
        return jnp.where(key_valid[:, None, :], raw, masked_score)

    def attend(inputs):
        query_tile_rows, key_tile_rows, value_tile_rows, bias_line = inputs
        scores = masked_scores(
            query_tile_rows, key_tile_rows, bias_rows(bias_line, first_query, slot_count, length)
        )
        row_peak = jnp.max(scores, axis=-1, keepdims=True)
        raised = jnp.exp(scores - row_peak)
        denominator = jnp.sum(raised, axis=-1, keepdims=True)
        weights_reduced_precision = (raised / denominator).astype(jnp.bfloat16)
        context = jnp.einsum(
            "wot,wtf->wof",
            weights_reduced_precision,
            value_tile_rows,
            preferred_element_type=jnp.float32,
        ).astype(jnp.bfloat16)
        return (context, (row_peak + jnp.log(denominator))[..., 0])

    context_heads, log_totals = lax.map(attend, (query_heads, all_keys, all_values, offset_bias))
    context_rows = from_heads(context_heads)
    residual = token_rows + feature_total(right_transposed(context_rows, output_full))
    gain_two, gate_full, up_full, down_full = (
        lax.all_gather(gain_ffn, "seq", axis=0, tiled=True),
        lax.all_gather(gate_weight, "seq", axis=0, tiled=True),
        lax.all_gather(up_weight, "seq", axis=0, tiled=True),
        lax.all_gather(down_weight, "seq", axis=0, tiled=True),
    )
    unit_two, scale_two, normed_two = normalize(residual, gain_two)
    gate_pre = plain_product(normed_two, gate_full)
    up_pre = plain_product(normed_two, up_full)
    activated, gelu_back = jax.vjp(jax.nn.gelu, gate_pre)
    hidden = (activated * up_pre).astype(jnp.bfloat16)
    ffn_share = lax.psum_scatter(
        right_transposed(hidden, down_full), "fsdp", scatter_dimension=1, tiled=True
    )
    residual_share = lax.dynamic_slice_in_dim(residual, fsdp_index * part_width, part_width, 1)
    layer_out = (
        (residual_share + ffn_share)
        .astype(jnp.bfloat16)
        .reshape(batch_count, slot_count, part_width)
    )
    masked_cot = jnp.where(own_valid[:, :, None], cotangent, jnp.zeros_like(cotangent))
    grad_rows = full_features(masked_cot)
    grad_down = left_transposed(grad_rows, hidden)
    grad_hidden = plain_product(grad_rows, down_full)
    grad_gate_pre = gelu_back(grad_hidden * up_pre)[0].astype(jnp.bfloat16)
    grad_up_pre = (grad_hidden * activated).astype(jnp.bfloat16)
    grad_gate = left_transposed(normed_two, grad_gate_pre)
    grad_up = left_transposed(normed_two, grad_up_pre)
    normed_two_grad = right_transposed(grad_gate_pre, gate_full) + right_transposed(
        grad_up_pre, up_full
    )
    second_gain_piece = jnp.sum(normed_two_grad * unit_two, axis=0)
    ffn_grads = (
        lax.psum_scatter(second_gain_piece, "seq", scatter_dimension=0, tiled=True),
        lax.psum_scatter(grad_gate, "seq", scatter_dimension=0, tiled=True),
        lax.psum_scatter(grad_up, "seq", scatter_dimension=0, tiled=True),
        lax.psum_scatter(grad_down, "seq", scatter_dimension=0, tiled=True),
    )
    residual_grad = grad_rows.astype(jnp.float32) + norm_back(
        feature_total(normed_two_grad), unit_two, scale_two, gain_two
    )
    residual_low = residual_grad.astype(jnp.bfloat16)
    grad_output = left_transposed(residual_low, context_rows)
    context_grad = to_heads(
        plain_product(residual_low, output_full).astype(jnp.bfloat16), batch_count, head_size
    )

    def query_side(inputs, with_keys):
        query_tile_rows, key_tile_rows, value_tile_rows, bias_line, log_total, context_tile_rows = (
            inputs
        )
        scores = masked_scores(
            query_tile_rows, key_tile_rows, bias_rows(bias_line, first_query, slot_count, length)
        )
        probs = jnp.exp(scores - log_total[..., None])
        prob_grad = jnp.einsum(
            "jht,jxt->jhx", context_tile_rows, value_tile_rows, preferred_element_type=jnp.float32
        )
        delta = jnp.sum(probs * prob_grad, axis=-1)
        score_gradient = (probs * (prob_grad - delta[..., None])).astype(jnp.bfloat16)
        query_grad = jnp.einsum(
            "wot,wtf->wof", score_gradient, key_tile_rows, preferred_element_type=jnp.float32
        )
        bias_grad = bias_rows_back(
            jnp.sum(score_gradient.astype(jnp.float32), axis=0),
            first_query,
            slot_count,
            length,
            line_length,
        )
        key_term = jnp.einsum(
            "xic,xil->xcl", score_gradient, query_tile_rows, preferred_element_type=jnp.float32
        )
        value_term = jnp.einsum(
            "xic,xil->xcl",
            probs.astype(jnp.bfloat16),
            context_tile_rows,
            preferred_element_type=jnp.float32,
        )
        return (query_grad, bias_grad, delta, key_term, value_term)

    side_inputs = (query_heads, all_keys, all_values, offset_bias, log_totals, context_grad)
    query_grad, bias_grad, delta, key_terms, value_terms = lax.map(
        partial(query_side, with_keys=True), side_inputs
    )
    wide_shape = (number_of_heads, batch_count, length * head_size)
    key_sums, value_sums = (
        lax.psum_scatter(key_terms.reshape(wide_shape), "seq", scatter_dimension=2, tiled=True),
        lax.psum_scatter(value_terms.reshape(wide_shape), "seq", scatter_dimension=2, tiled=True),
    )
    own_shape = (number_of_heads, batch_count, slot_count, head_size)
    query_low = from_heads(query_grad.astype(jnp.bfloat16))
    key_low = from_heads(key_sums.reshape(own_shape).astype(jnp.bfloat16))
    value_low = from_heads(value_sums.reshape(own_shape).astype(jnp.bfloat16))
    grad_query = left_transposed(normed_one, query_low)
    grad_key = left_transposed(normed_one, key_low)
    grad_value = left_transposed(normed_one, value_low)
    grad_table = lax.dot_general(bucket_hot, bias_grad, (((0,), (1,)), ((), ())), precision=highest)
    normed_one_grad = (
        right_transposed(query_low, query_full)
        + right_transposed(key_low, key_full)
        + right_transposed(value_low, value_full)
    )
    gain_one_part = jnp.sum(normed_one_grad * unit_one, axis=0)
    attn_grads = (
        lax.psum_scatter(gain_one_part, "seq", scatter_dimension=0, tiled=True),
        lax.psum_scatter(grad_query, "seq", scatter_dimension=0, tiled=True),
        lax.psum_scatter(grad_key, "seq", scatter_dimension=0, tiled=True),
        lax.psum_scatter(grad_value, "seq", scatter_dimension=0, tiled=True),
        lax.psum_scatter(grad_output, "seq", scatter_dimension=0, tiled=True),
        lax.psum_scatter(grad_table, "seq", scatter_dimension=0, tiled=True),
    )
    token_grad = residual_grad + norm_back(
        feature_total(normed_one_grad), unit_one, scale_one, gain_one
    )
    token_share = lax.dynamic_slice_in_dim(
        token_grad, fsdp_index * part_width, part_width, 1
    ).reshape(batch_count, slot_count, part_width)
    gain_one_sum, gain_two_sum = lax.psum((attn_grads[0], ffn_grads[0]), "fsdp")
    return (
        layer_out,
        token_share,
        gain_one_sum,
        attn_grads[1],
        attn_grads[2],
        attn_grads[3],
        attn_grads[4],
        attn_grads[5],
        gain_two_sum,
        ffn_grads[1],
        ffn_grads[2],
        ffn_grads[3],
    )


BLOCK = 128
BOTH = ("seq", "fsdp")


def move(value, target):
    pairs = []
    for z in range(4):
        for y in range(2):
            for x in range(2):
                for c in range(2):
                    zt, yt, xt, ct = target(z, y, x, c)
                    pairs.append(((2 * z + y) * 4 + 2 * x + c, (2 * zt + yt) * 4 + 2 * xt + ct))
    return lax.ppermute(value, BOTH, pairs)


def spread_slot(k):
    return lambda z, y, x, c: (2 * c + (k ^ (z & 1)), y, x, z >> 1)


KEYS = 512
QUERIES = 512
WIDE_QUERIES = 1024
OFFSET = 1920


def skew_table(rev_ref, table):
    width = rev_ref.shape[1]
    line = jnp.broadcast_to(rev_ref[...], (8, width))
    for first in range(0, BLOCK, 8):
        table[first : first + 8, :] = pltpu.roll(
            line, (width - (BLOCK - 1) + first) % width, axis=1, stride=1, stride_axis=0
        )


def place_of(piece, part, z, y, x, c):
    c_rel, d = part // 4, part % 4
    b = jnp.bitwise_xor(x, piece // 2)
    block = (
        4 * jnp.bitwise_xor(z, d)
        + 2 * jnp.bitwise_xor(y, piece % 2)
        + jnp.bitwise_xor(c, c_rel)
    )
    return b, block


def part_of(b, block, z, y, x, c):
    piece = 2 * jnp.bitwise_xor(b, x) + jnp.bitwise_xor((block // 2) % 2, y)
    part = 4 * jnp.bitwise_xor(block % 2, c) + jnp.bitwise_xor(block // 4, z)
    return piece, part


def lanes(first, count):
    return pl.ds(pl.multiple_of(first, BLOCK), count)


def attend_kernel(sc, pieces, rev_ref, ctx_ref, ctx_wide, lse_ref, qkv, keys, table):
    z, y, x, c = position()
    for piece in range(4):
        for part in range(8):
            b, block = place_of(piece, part, z, y, x, c)
            data = pieces[piece, :, :, part * BLOCK : (part + 1) * BLOCK]
            qkv[b, :, :, lanes(block * BLOCK, BLOCK)] = data
            keys[b, lanes(block * BLOCK, BLOCK), :] = data[1].T
    skew_table(rev_ref, table)
    length = qkv.shape[-1]
    for b in range(2):
        valid = sc[b]
        full = valid // KEYS

        @pl.loop(0, length // WIDE_QUERIES)
        def _(i):
            first_query = i * WIDE_QUERIES
            query = qkv[b, 0, :, lanes(first_query, WIDE_QUERIES)]

            def tile(j, carry, masked):
                peak, total, acc = carry
                first_key = j * KEYS
                score = jnp.dot(
                    keys[b, lanes(first_key, KEYS), :], query, preferred_element_type=jnp.float32
                )
                score = score + jnp.concatenate(
                    [
                        table[:, lanes(first_query - first_key + OFFSET - t, WIDE_QUERIES)]
                        for t in range(0, KEYS, BLOCK)
                    ],
                    axis=0,
                )
                if masked:
                    position = first_key + lax.broadcasted_iota(jnp.int32, (KEYS, WIDE_QUERIES), 0)
                    score = jnp.where(position < valid, score, masked_score)
                now = jnp.maximum(peak, jnp.max(score, axis=0, keepdims=True))
                scale = jnp.exp(peak - now)
                prob = jnp.exp(score - now)
                total = total * scale + jnp.sum(prob, axis=0, keepdims=True)
                acc = acc * scale + jnp.dot(
                    qkv[b, 2, :, lanes(first_key, KEYS)],
                    prob.astype(jnp.bfloat16),
                    preferred_element_type=jnp.float32,
                )
                return now, total, acc

            carry = (
                jnp.full((1, WIDE_QUERIES), masked_score, jnp.float32),
                jnp.zeros((1, WIDE_QUERIES), jnp.float32),
                jnp.zeros((DH, WIDE_QUERIES), jnp.float32),
            )
            carry = lax.fori_loop(0, full, lambda j, s: tile(j, s, False), carry)
            peak, total, acc = lax.cond(
                valid > full * KEYS, lambda s: tile(full, s, True), lambda s: s, carry
            )
            context = acc / total
            ctx_wide[b, :, lanes(first_query, WIDE_QUERIES)] = context
            lse_ref[b, :, lanes(first_query, WIDE_QUERIES)] = peak + jnp.log(total)
            low = context.astype(jnp.bfloat16)
            for t in range(WIDE_QUERIES // BLOCK):
                piece, part = part_of(b, i * (WIDE_QUERIES // BLOCK) + t, z, y, x, c)
                ctx_ref[piece, :, lanes(part * BLOCK, BLOCK)] = low[:, t * BLOCK : (t + 1) * BLOCK]


def attend(scalars, pieces, rev_line):
    _, _, head_size, tokens = pieces.shape
    length = tokens * 2
    smem, vmem = pl.BlockSpec(memory_space=pltpu.SMEM), pl.BlockSpec(memory_space=pltpu.VMEM)
    return pl.pallas_call(
        attend_kernel,
        name="attend",
        out_shape=[
            jax.ShapeDtypeStruct((4, head_size, tokens), jnp.bfloat16),
            jax.ShapeDtypeStruct((2, head_size, length), jnp.float32),
            jax.ShapeDtypeStruct((2, 1, length), jnp.float32),
            jax.ShapeDtypeStruct((2, 3, head_size, length), jnp.bfloat16),
        ],
        in_specs=[smem] + [vmem] * 2,
        out_specs=[vmem] * 4,
        scratch_shapes=[
            pltpu.VMEM((2, length, head_size), jnp.bfloat16),
            pltpu.VMEM((BLOCK, rev_line.shape[1]), jnp.float32),
        ],
        cost_estimate=pl.CostEstimate(
            flops=46_000_000_000, bytes_accessed=4 << 20, transcendentals=0
        ),
        compiler_params=pltpu.CompilerParams(vmem_limit_bytes=48 << 20),
    )(scalars, pieces, rev_line)


def attend_back_kernel(
    sc, pieces, rev_ref, ctx_wide, lse_ref, qkv,
    out_ref, line_ref,
    queries, keys, values, grads, grads_t, delta, query_sum, key_sum, value_sum, table, table_sum,
):
    z, y, x, c = position()
    length = qkv.shape[-1]
    for piece in range(4):
        for part in range(8):
            b, block = place_of(piece, part, z, y, x, c)
            data = pieces[piece, :, part * BLOCK : (part + 1) * BLOCK]
            grads_t[b, :, lanes(block * BLOCK, BLOCK)] = data
            grads[b, lanes(block * BLOCK, BLOCK), :] = data.T
    for b in range(2):
        for first in range(0, length, BLOCK):
            here = slice(first, first + BLOCK)
            queries[b, here, :] = qkv[b, 0, :, here].T
            keys[b, here, :] = qkv[b, 1, :, here].T
            values[b, here, :] = qkv[b, 2, :, here].T
        delta[b] = jnp.sum(
            ctx_wide[b] * grads_t[b].astype(jnp.float32), axis=0, keepdims=True
        )
    skew_table(rev_ref, table)
    table_sum[...] = jnp.zeros_like(table_sum)
    query_sum[...] = jnp.zeros_like(query_sum)
    out_ref[...] = jnp.zeros_like(out_ref)
    for b in range(2):
        valid = sc[b]
        full = valid // KEYS
        count = (valid + QUERIES - 1) // QUERIES

        def key_step(j, masked):
            first_key = j * KEYS
            key, value = keys[b, lanes(first_key, KEYS), :], values[b, lanes(first_key, KEYS), :]
            key_t = qkv[b, 1, :, lanes(first_key, KEYS)]
            key_sum[...] = jnp.zeros_like(key_sum)
            value_sum[...] = jnp.zeros_like(value_sum)

            @pl.loop(0, count)
            def _(i):
                first_query = i * QUERIES
                here = lanes(first_query, QUERIES)
                score = jnp.dot(key, qkv[b, 0, :, here], preferred_element_type=jnp.float32)
                score = score + jnp.concatenate(
                    [
                        table[:, lanes(first_query - first_key + OFFSET - t, QUERIES)]
                        for t in range(0, KEYS, BLOCK)
                    ],
                    axis=0,
                )
                if masked:
                    position = first_key + lax.broadcasted_iota(jnp.int32, (KEYS, QUERIES), 0)
                    score = jnp.where(position < valid, score, masked_score)
                prob = jnp.exp(score - lse_ref[b, :, here])
                prob_grad = jnp.dot(value, grads_t[b, :, here], preferred_element_type=jnp.float32)
                score_grad = (prob * (prob_grad - delta[b, :, here])).astype(jnp.bfloat16)
                value_sum[...] += jnp.dot(
                    prob.astype(jnp.bfloat16), grads[b, here, :], preferred_element_type=jnp.float32
                )
                key_sum[...] += jnp.dot(
                    score_grad, queries[b, here, :], preferred_element_type=jnp.float32
                )
                query_sum[b, :, here] += jnp.dot(
                    key_t, score_grad, preferred_element_type=jnp.float32
                )
                for t in range(0, KEYS, BLOCK):
                    table_sum[:, lanes(first_query - first_key + OFFSET - t, QUERIES)] += score_grad[
                        t : t + BLOCK
                    ].astype(jnp.float32)

            for t in range(KEYS // BLOCK):
                piece, part = part_of(b, j * (KEYS // BLOCK) + t, z, y, x, c)
                rows = slice(t * BLOCK, (t + 1) * BLOCK)
                at = lanes(part * BLOCK, BLOCK)
                out_ref[piece, 1, :, at] = key_sum[rows, :].T.astype(jnp.bfloat16)
                out_ref[piece, 2, :, at] = value_sum[rows, :].T.astype(jnp.bfloat16)

        pl.loop(0, full)(lambda j: key_step(j, False))
        pl.when(valid > full * KEYS)(lambda: key_step(full, True))
        for block in range(length // BLOCK):
            piece, part = part_of(b, block, z, y, x, c)
            out_ref[piece, 0, :, lanes(part * BLOCK, BLOCK)] = query_sum[
                b, :, block * BLOCK : (block + 1) * BLOCK
            ].astype(jnp.bfloat16)
    width = table_sum.shape[1]
    line = jnp.zeros((8, width), jnp.float32)
    for first in range(0, BLOCK, 8):
        line = line + pltpu.roll(table_sum[first : first + 8, :], BLOCK - 8 - first, axis=1)
    ahead = 7 - lax.broadcasted_iota(jnp.int32, (8, width), 0)
    for bit in (1, 2, 4):
        line = jnp.where((ahead & bit) != 0, pltpu.roll(line, bit, axis=1), line)
    line_ref[...] = jnp.sum(line, axis=0, keepdims=True)


def attend_back(scalars, pieces, rev_line, ctx_wide, lse, qkv):
    _, head_size, tokens = pieces.shape
    length = tokens * 2
    smem, vmem = pl.BlockSpec(memory_space=pltpu.SMEM), pl.BlockSpec(memory_space=pltpu.VMEM)
    low = pltpu.VMEM((2, length, head_size), jnp.bfloat16)
    return pl.pallas_call(
        attend_back_kernel,
        name="attend_back",
        out_shape=[
            jax.ShapeDtypeStruct((4, 3, head_size, tokens), jnp.bfloat16),
            jax.ShapeDtypeStruct(rev_line.shape, jnp.float32),
        ],
        in_specs=[smem] + [vmem] * 5,
        out_specs=[vmem] * 2,
        scratch_shapes=[
            low, low, low, low,
            pltpu.VMEM((2, head_size, length), jnp.bfloat16),
            pltpu.VMEM((2, 1, length), jnp.float32),
            pltpu.VMEM((2, head_size, length), jnp.float32),
            pltpu.VMEM((KEYS, head_size), jnp.float32),
            pltpu.VMEM((KEYS, head_size), jnp.float32),
            pltpu.VMEM((BLOCK, rev_line.shape[1]), jnp.float32),
            pltpu.VMEM((BLOCK, rev_line.shape[1]), jnp.float32),
        ],
        cost_estimate=pl.CostEstimate(
            flops=46_000_000_000, bytes_accessed=4 << 20, transcendentals=0
        ),
        compiler_params=pltpu.CompilerParams(vmem_limit_bytes=48 << 20),
    )(scalars, pieces, rev_line, ctx_wide, lse, qkv)


CHUNKS = 2
MESH_ID = pl.DeviceIdType.MESH
IN_VMEM = pl.BlockSpec(memory_space=pltpu.VMEM)
IN_PLACE = pl.BlockSpec(memory_space=pl.ANY)
COPIES = pltpu.SemaphoreType.DMA


def flip(a, b):
    return a + b - 2 * a * b


def flip_pair(a, b):
    return 2 * flip(a // 2, b // 2) + flip(a % 2, b % 2)


def position():
    s, f = lax.axis_index("seq"), lax.axis_index("fsdp")
    return s // 2, s % 2, f // 2, f % 2


def device(z, y, x, c):
    return (2 * z + y, 2 * x + c)


def ring_of(z):
    high, low = z // 2, z % 2
    following = 2 * low + 1 - high
    return following, (2 * (1 - low) + high, 2 * (1 - high) + 1 - low, following)


def greet(z, y, x, c):
    peers = []
    for d in range(1, 8):
        peers.append(device(z, flip(y, d // 4), flip(x, (d // 2) % 2), flip(c, d % 2)))
        if d > 1:
            peers.append(device(flip_pair(z, d // 2), y, x, flip(c, d % 2)))
    barrier = pltpu.get_barrier_semaphore()
    for peer in peers:
        pl.semaphore_signal(barrier, inc=1, device_id=peer, device_id_type=MESH_ID)
    pl.semaphore_wait(barrier, len(peers))


def remote(source, target, send, recv, to):
    return pltpu.make_async_remote_copy(
        src_ref=source,
        dst_ref=target,
        send_sem=send,
        recv_sem=recv,
        device_id=to,
        device_id_type=MESH_ID,
    )


class Links:
    def __init__(self, send, recv):
        self.send, self.recv, self.used, self.sent = send, recv, 0, []

    def go(self, source, target, to):
        i = self.used
        self.used += 1
        made = remote(source, target, self.send.at[i], self.recv.at[i], to)
        made.start()
        self.sent.append(made)
        return made

    def go_unless(self, own, source, target, to, send=None, recv=None):
        if send is None:
            send, recv = self.send.at[self.used], self.recv.at[self.used]
            self.used += 1
        made = remote(source, target, send, recv, to)
        if own is None:
            made.start()
            self.sent.append(made)
            return made
        local = pltpu.make_async_copy(source, target, recv)
        pl.when(own)(lambda: local.start())
        pl.when(jnp.logical_not(own))(lambda: made.start())
        self.sent.append((own, made))
        return made

    def go_if(self, there, here, source, target, send, recv, to):
        made = remote(source, target, send, recv, to)
        pl.when(there)(lambda: made.start())
        if here is not None:
            local = pltpu.make_async_copy(source, target, recv)
            pl.when(here)(lambda: local.start())
        self.sent.append((jnp.logical_not(there), made))

    def done(self, made):
        made.wait_send()
        self.sent = [m for m in self.sent if m is not made]

    def finish(self):
        for made in self.sent:
            if isinstance(made, tuple):
                pl.when(jnp.logical_not(made[0]))(lambda made=made: made[1].wait_send())
            else:
                made.wait_send()


def share_start(links, rows_all, me):
    z, y, x, c = me
    following, _ = ring_of(z)
    rows = rows_all.shape[1] // CHUNKS
    ring = []
    for h in range(CHUNKS):
        here = pl.ds(h * rows, rows)
        target = rows_all.at[flip_pair(following, z), here]
        ring.append(links.go(rows_all.at[0, here], target, device(following, y, x, c)))
    core = [links.go(rows_all.at[0], rows_all.at[4], device(z, y, x, 1 - c))]
    return [ring], core


def share_step(links, rows_all, me, state, step):
    z, y, x, c = me
    following, back = ring_of(z)
    rows = rows_all.shape[1] // CHUNKS
    ring, core = state
    slot = flip_pair(z, back[step - 1])
    sent = []
    for h in range(CHUNKS):
        here = pl.ds(h * rows, rows)
        ring[-1][h].wait_recv()
        source = rows_all.at[slot, here]
        if step < 3:
            target = rows_all.at[flip_pair(following, back[step - 1]), here]
            sent.append(links.go(source, target, device(following, y, x, c)))
        core.append(links.go(source, rows_all.at[4 + slot, here], device(z, y, x, 1 - c)))
    ring.append(sent)


def share_end(state):
    for made in state[1]:
        made.wait_recv()


def sum_order(z):
    _, back = ring_of(z)
    return [flip_pair(z, b) for b in back] + [0]


def column_go(links, me, k, source, target):
    z, y, x, c = me
    own = z // 2 == c if k == 0 else None
    to = device(2 * c + flip(k, z % 2), y, x, z // 2)
    return links.go_unless(own, source, target, to)


def arrived(place, sem):
    pltpu.make_async_copy(place, place, sem).wait()


def spread_go(links, me, k, source, full, send, recv):
    z, y, x, c = me
    rows = source.shape[0]
    first = pl.multiple_of((4 * c + 2 * flip(k, z % 2) + y) * rows, rows)
    target = full.at[pl.ds(first, rows), :]
    for dy, dx in ((0, 1), (1, 0), (0, 0)):
        own = None if dy + dx else c == x
        to = device(z, flip(y, dy), flip(x, dx), x)
        links.go_unless(own, source, target, to, send.at[k, dy, dx], recv.at[k, dy, c])


def spread_relay(links, me, full, send, recv):
    z, y, x, c = me
    odd = flip(c, x)
    k, step = 1 - odd, 1 - odd
    rows = full.shape[0] // 8
    to = device(z, flip(y, odd), flip(x, 1 - odd), c)
    for r in range(2):
        first = pl.multiple_of((4 * r + 2 * flip(k, z % 2) + flip(y, step)) * rows, rows)
        here = full.at[pl.ds(first, rows), :]
        arrived(here, recv.at[k, step, r])
        made = remote(here, here, send.at[r, 1, 1], recv.at[k, 1, r], to)
        made.start()
        links.sent.append(made)


def spread_wait(me, full, recv):
    z, y, x, c = me
    odd = flip(c, x)
    here = full.at[pl.ds(0, full.shape[0] // 8), :]
    for k, step in ((1 - odd, odd), (odd, 0), (odd, 1)):
        for r in range(2):
            arrived(here, recv.at[k, step, r])


def join_go(links, me, k, grads, into, relay, send, recv, relay_recv):
    z, y, x, c = me
    odd = flip(c, x) == 1
    even = jnp.logical_not(odd)
    rows = into.shape[2]
    for r in range(2):

        def block(step):
            index = 4 * r + 2 * flip(k, z % 2) + flip(y, step)
            return grads.at[pl.ds(pl.multiple_of(index * rows, rows), rows), :]

        same, other = device(z, y, c, r), device(z, 1 - y, c, r)
        mine = jnp.logical_and(even, c == r)
        partner = jnp.logical_and(even, c != r)
        links.go_if(
            partner, mine, block(0), into.at[k, 0], send.at[k, 0, r], recv.at[k, 0], same
        )
        if k == 0:
            links.go_if(even, None, block(1), into.at[0, 1], send.at[0, 1, r], recv.at[0, 1], other)
            to = device(z, 1 - y, x, c)
        else:
            links.go_if(odd, None, block(0), into.at[1, 1], send.at[1, 1, r], recv.at[1, 1], same)
            to = device(z, y, c, c)
        links.go_if(odd, None, block(1), relay.at[r], send.at[k, 2, r], relay_recv.at[r], to)


def join_relay(links, me, grads, into, relay, send, recv, relay_recv):
    z, y, x, c = me
    odd = flip(c, x)
    k, step = 1 - odd, 1 - odd
    rows = into.shape[2]
    for r in range(2):
        arrived(relay.at[r], relay_recv.at[r])
        index = 4 * r + 2 * flip(k, z % 2) + flip(y, step)
        own = grads[pl.ds(pl.multiple_of(index * rows, rows), rows), :]
        total = relay[r].astype(jnp.float32) + own.astype(jnp.float32)
        relay[r] = total.astype(jnp.bfloat16)
        to = device(z, flip(y, step), c, r)
        made = remote(relay.at[r], into.at[k, 2], send.at[0, 3, r], recv.at[k, 2], to)
        made.start()
        links.sent.append(made)


def join_sum(k, into, recv):
    total = 0.0
    for j in range(3):
        arrived(into.at[k, j], recv.at[k, j])
        total = total + into[k, j].astype(jnp.float32)
    return total.astype(jnp.bfloat16)


def rms(rows):
    return lax.rsqrt(jnp.mean(rows * rows, axis=-1, keepdims=True) + epsilon)


def lane_sum(values):
    return jnp.sum(values, axis=-1, keepdims=True)


def head_of(z, y, x, c, heads):
    return 2 * c + z // 2, (z % 2) * (heads // 2) + 2 * x + y


def entry_kernel(
    lengths, tok_ref, cot_ref, small_ref, bucket_ref, wq_ref, wk_ref, wv_ref, wo_ref, wg_ref,
    rows_ref, normed, grads, pieces, weight, gain_one, gain_two, rev_ref, slots_o, slots_g,
    tok_in, cot_in, held, qkv, small, send, recv, plane_send, plane_recv, local,
):
    me = z, y, x, c = position()
    greet(*me)
    links = Links(send, recv)
    f, part, half = 2 * x + c, tok_in.shape[2], tok_in.shape[1]

    def gather_rows(n, ref, into):
        def source(xd, cd):
            return ref.at[xd, pl.ds(pl.multiple_of(cd * half, half), half)]

        own = pltpu.make_async_copy(source(x, c), into.at[f], local.at[n])
        own.start()
        got = []
        for d in (1, 2, 3):
            xd, cd = flip(x, d // 2), flip(c, d % 2)
            got.append(links.go(source(xd, cd), into.at[f], device(z, y, xd, cd)))
        return own, got

    tok_own, tok_got = gather_rows(0, tok_ref, tok_in)
    small[f, z, y] = small_ref[...]
    small_got = []
    for d in (1, 2, 3):
        here = small.at[f, z, y]
        small_got.append(links.go(here, here, device(flip_pair(z, d), y, x, c)))
    group_width = wq_ref.shape[1] // 2
    way = []
    for k in range(2):
        cut = pl.ds(pl.multiple_of(flip(k, z % 2) * group_width, group_width), group_width)
        for n, ref in enumerate((wq_ref, wk_ref, wv_ref)):
            target = held.at[k, :, n * group_width : (n + 1) * group_width]
            way.append(column_go(links, me, k, ref.at[:, cut], target))
    for made in small_got:
        made.wait_recv()
    here = small.at[f, :, y]
    links.go(here, here, device(z, 1 - y, x, c)).wait_recv()
    tables = []
    for d in (1, 2, 3):
        here = small.at[f]
        tables.append(links.go(here, here, device(z, y, flip(x, d // 2), flip(c, d % 2))))
    for i in range(4 * part // BLOCK):
        here = slice(i * BLOCK, (i + 1) * BLOCK)
        block = (i // 2) // 2, (i // 2) % 2
        gain_one[:, here] = small[f, block[0], block[1], i % 2 : i % 2 + 1, :]
        gain_two[:, here] = small[f, block[0], block[1], 2 + i % 2 : 3 + i % 2, :]
    tok_own.wait()
    for made in tok_got:
        made.wait_recv()
    cot_own, cot_got = gather_rows(1, cot_ref, cot_in)
    wide = [tok_in[i].astype(jnp.float32) for i in range(4)]
    mean = sum(lane_sum(w * w) for w in wide) / (4 * part)
    scale = lax.rsqrt(mean + epsilon)
    for i in range(4):
        here = slice(i * part, (i + 1) * part)
        rows_ref[:, here] = tok_in[i]
        normed[0, :, here] = (wide[i] * scale * gain_one[:, here]).astype(jnp.bfloat16)
    first = share_start(links, normed, me)
    for k in range(2):
        for made in way[3 * k : 3 * k + 3]:
            made.wait_recv()
        spread_go(links, me, k, held.at[k], weight, plane_send, plane_recv)
    share_step(links, normed, me, first, 1)
    share_step(links, normed, me, first, 2)
    later = []
    half_ffn = wg_ref.shape[1] // 2
    for k in range(2):
        side = flip(k, z % 2)
        cut = pl.ds(pl.multiple_of(side * group_width, group_width), group_width)
        later.append(column_go(links, me, k, wo_ref.at[:, cut], slots_o.at[k]))
        cut = pl.ds(pl.multiple_of(side * half_ffn, half_ffn), half_ffn)
        later.append(column_go(links, me, k, wg_ref.at[:, cut], slots_g.at[k]))
    spread_relay(links, me, weight, plane_send, plane_recv)
    for made in tables:
        made.wait_recv()
    group = qkv.shape[1]
    heads = 2 * group
    source, place = head_of(z, y, x, c, heads)
    lane = lax.broadcasted_iota(jnp.int32, (1, BLOCK), 1)
    line = jnp.zeros(bucket_ref.shape, jnp.float32)
    per_block = 4
    for n in range(8 * per_block):
        block = n // per_block
        row = small[source, block // 2, block % 2, 4:5, :]
        value = lane_sum(jnp.where(lane == (n % per_block) * heads + place, row, 0.0))
        line = jnp.where(bucket_ref[...] == n, value, line)
    rev_ref[...] = line
    spread_wait(me, weight, plane_recv)
    rows = normed.shape[1]
    sent = []

    def project(d):
        out = jnp.dot(pair_of(normed, d), weight[...], preferred_element_type=jnp.float32)
        out = out.astype(jnp.bfloat16).T
        for side, slot in enumerate((d, 4 + d)):
            here = lanes(slot * rows, rows)
            cut = out[:, side * rows : (side + 1) * rows]
            qkv[:, :, :, here] = cut.reshape(3, group, DH, rows)
            pieces[0, :, :, here] = qkv[:, 2 * x + y, :, here]
            for e in (1, 2, 3):
                xd, yd = flip(x, e // 2), flip(y, e % 2)
                source = qkv.at[:, 2 * xd + yd, :, here]
                sent.append(links.go(source, pieces.at[e, :, :, here], device(z, yd, xd, c)))

    cot_own.wait()
    for made in cot_got:
        made.wait_recv()
    slot = (4 * z + 2 * y + c) * half + lax.broadcasted_iota(jnp.int32, (half, part), 0)
    valid = slot < jnp.where(x == 0, lengths[0], lengths[1])
    for i in range(4):
        grads[:, i * part : (i + 1) * part] = jnp.where(valid, cot_in[i], jnp.zeros_like(cot_in[i]))
    order = sum_order(z)
    first[1][0].wait_recv()
    project(0)
    for step in (1, 2, 3):
        if step == 3:
            share_step(links, normed, me, first, 3)
        for made in first[1][1 + CHUNKS * (step - 1) : 1 + CHUNKS * step]:
            made.wait_recv()
        project(order[step - 1])
    for made in sent + later:
        made.wait_recv()
    links.finish()


def low_array(*shape):
    return jax.ShapeDtypeStruct(shape, jnp.bfloat16)


def wide_array(*shape):
    return jax.ShapeDtypeStruct(shape, jnp.float32)


def low_space(*shape):
    return pltpu.VMEM(shape, jnp.bfloat16)


def entry(lengths, tokens_in, cotangent, small, rev_buckets, weights):
    _, slot_count, part = tokens_in.shape
    rows, width = slot_count // 2, 4 * part
    depth, cols = weights[0].shape
    group = cols // (2 * DH)
    wide = 3 * cols // 2
    return pl.pallas_call(
        entry_kernel,
        name="entry",
        out_shape=[
            low_array(rows, width),
            low_array(8, rows, width),
            low_array(rows, width),
            low_array(4, 3, DH, 8 * rows),
            low_array(8 * depth, wide),
            wide_array(1, width),
            wide_array(1, width),
            wide_array(*rev_buckets.shape),
            low_array(2, depth, cols // 2),
            low_array(2, depth, weights[4].shape[1] // 2),
        ],
        in_specs=[pl.BlockSpec(memory_space=pltpu.SMEM)]
        + [IN_PLACE] * 2
        + [IN_VMEM] * 2
        + [IN_PLACE] * 5,
        out_specs=[IN_VMEM] * 10,
        scratch_shapes=[
            low_space(4, rows, part),
            low_space(4, rows, part),
            low_space(2, depth, wide),
            low_space(3, group, DH, 8 * rows),
            pltpu.VMEM((4, 4, 2, 8, BLOCK), jnp.float32),
            COPIES((64,)),
            COPIES((64,)),
            COPIES((2, 2, 2)),
            COPIES((2, 2, 2)),
            COPIES((2,)),
        ],
        compiler_params=pltpu.CompilerParams(
            collective_id=1, has_side_effects=True, vmem_limit_bytes=48 << 20
        ),
    )(lengths, tokens_in, cotangent, small, rev_buckets, *weights)


def gelu_pair(t):
    inner = jnp.tanh(root_two_over_pi * (t + 0.044715 * (t * t * t)))
    half = 0.5 * (1.0 + inner)
    slope = half + 0.5 * t * (1.0 - inner * inner) * root_two_over_pi * (1.0 + 0.134145 * (t * t))
    return t * half, slope


def pair_of(ref, slot):
    return jnp.concatenate([ref[slot], ref[4 + slot]], axis=0)


def pair_go(links, me, core, i, terms, core_out, core_in):
    z, y, x, c = me
    size = terms.shape[0] // 2
    core_out[i] = terms[size:].astype(jnp.bfloat16)
    core.append(links.go(core_out.at[i], core_in.at[i], device(z, y, x, 1 - c)))
    return terms[:size]


def sum_step(links, me, core, ring, i, mine, core_in, ring_out, ring_in):
    z, y, x, c = me
    following, _ = ring_of(z)
    rows = mine.shape[0] // CHUNKS
    core.wait_recv()
    sent, last = [], []
    for h in range(CHUNKS):
        cut = slice(h * rows, (h + 1) * rows)
        here = pl.ds(h * rows, rows)
        value = mine[cut] + core_in[i, here, :].astype(jnp.float32)
        if i:
            ring[-1][h].wait_recv()
            value = value + ring_in[i - 1, here, :].astype(jnp.float32)
        if i < 3:
            ring_out[i, here, :] = value.astype(jnp.bfloat16)
            target = ring_in.at[i, here]
            sent.append(links.go(ring_out.at[i, here], target, device(following, y, x, c)))
        else:
            last.append(value)
    ring.append(sent)
    return last


def reduce_pair(links, me, state, i, terms, core_out, core_in, ring_out, ring_in):
    mine = pair_go(links, me, state[0], i, terms, core_out, core_in)
    return sum_step(links, me, state[0][i], state[1], i, mine, core_in, ring_out, ring_in)


def core_kernel(
    ctx_ref, rows_ref, gain_ref, own_ref, slots_o, slots_g, slot_ud0, slot_ud1,
    layer_ref, context, low, wide_ref, part_ref, pieces, in_gu, in_d,
    residual_ref, down, hidden, out_weight, gate_up, normed, grads, pre, ctx_all, heads_out, grad_gu, grad_d,
    mine, core_out, core_in, ring_out, ring_in, ring_out2, ring_in2,
    relay_gu, relay_d, send, recv, plane_send, plane_recv, join_send, join_recv, relay_recv,
):
    me = z, y, x, c = position()
    greet(*me)
    links = Links(send, recv)
    own = 2 * x + y
    heads = []
    for d in (1, 2, 3):
        xd, yd = flip(x, d // 2), flip(y, d % 2)
        heads.append(links.go(ctx_ref.at[d], ctx_all.at[own], device(z, yd, xd, c)))
    grads[0] = own_ref[...]
    second = share_start(links, grads, me)

    ffn = down.shape[1]
    fulls = out_weight, gate_up.at[:, :ffn], gate_up.at[:, ffn:], down

    def weight_go(n):
        slots = (
            (slots_o.at[0], slots_o.at[1]),
            (slots_g.at[0], slots_g.at[1]),
            (slot_ud0.at[:, :ffn], slot_ud1.at[:, :ffn]),
            (slot_ud0.at[:, ffn:], slot_ud1.at[:, ffn:]),
        )[n]
        for k in range(2):
            spread_go(links, me, k, slots[k], fulls[n], plane_send.at[n], plane_recv.at[n])

    def weight_relay(n):
        spread_relay(links, me, fulls[n], plane_send.at[n], plane_recv.at[n])

    def weight_wait(n):
        spread_wait(me, fulls[n], plane_recv.at[n])

    weight_go(0)
    ctx_all[own] = ctx_ref[0]
    for made in heads:
        made.wait_recv()
    group, size, tokens = ctx_all.shape
    rows, width = residual_ref.shape
    depth = gate_up.shape[0] // 8
    half_tokens = tokens // 2
    context[...] = ctx_all[...].reshape(group * size, tokens).T
    weight_relay(0)
    weight_go(1)
    weight_go(2)
    weight_wait(0)
    order = sum_order(z)

    def first_row(block):
        return pl.multiple_of(block * rows, rows)

    def pair_rows(ref, d):
        return jnp.concatenate(
            [ref[pl.ds(first_row(d), rows), :], ref[pl.ds(first_row(4 + d), rows), :]], axis=0
        )

    state = [], []
    for i in range(4):
        terms = right_transposed(pair_rows(context, order[i]), out_weight[...])
        last = reduce_pair(links, me, state, i, terms, core_out, core_in, ring_out, ring_in)
        if i < 3:
            share_step(links, grads, me, second, i + 1)
        if i == 1:
            weight_go(3)
        if i == 2:
            weight_relay(1)
            weight_relay(2)
    residual = rows_ref[...].astype(jnp.float32) + jnp.concatenate(last, axis=0)
    residual_ref[...] = residual
    gain = gain_ref[...]
    normed[0] = (residual * rms(residual) * gain).astype(jnp.bfloat16)
    shared = share_start(links, normed, me)
    weight_relay(3)
    share_end(second)
    for made in state[0] + sum(state[1], []):
        links.done(made)
    ring = []

    def take_in(i):
        share_step(links, normed, me, shared, i + 1)

    def feed(i):
        d = order[i]
        for made in shared[1][:1] if i == 3 else shared[1][1 + CHUNKS * i : 1 + CHUNKS * (i + 1)]:
            made.wait_recv()
        gate_up_pre = jnp.dot(
            pair_of(normed, d), gate_up[...], preferred_element_type=jnp.float32
        )
        activated, slope = gelu_pair(gate_up_pre[:, :ffn])
        up_pre = gate_up_pre[:, ffn:]
        made = (activated * up_pre).astype(jnp.bfloat16)
        hidden[pl.ds(first_row(d), rows), :] = made[:rows]
        hidden[pl.ds(first_row(4 + d), rows), :] = made[rows:]
        if i == 0:
            weight_wait(3)
        grad_hidden = jnp.dot(pair_of(grads, d), down[...], preferred_element_type=jnp.float32)
        grad_pre = jnp.concatenate(
            [
                (grad_hidden * up_pre * slope).astype(jnp.bfloat16),
                (grad_hidden * activated).astype(jnp.bfloat16),
            ],
            axis=1,
        )
        pre[pl.ds(first_row(d), rows), :] = grad_pre[:rows]
        pre[pl.ds(first_row(4 + d), rows), :] = grad_pre[rows:]
        terms = right_transposed(grad_pre, gate_up[...])
        kept = []
        mine[i] = pair_go(links, me, kept, i, terms, core_out, core_in)
        return kept[0]

    def pass_on(i, core):
        return sum_step(links, me, core, ring, i, mine[i], core_in, ring_out2, ring_in2)

    joins = (grad_gu, in_gu, relay_gu), (grad_d, in_d, relay_d)

    def weight_grads(k):
        for n in range(4):
            block = 4 * (n // 2) + 2 * flip(k, z % 2) + n % 2
            here = pl.ds(pl.multiple_of(block * depth, depth), depth)
            left = normed[:, :, here].reshape(tokens, depth)
            grad_gu[here, :] = left_transposed(left, pre[...]).astype(jnp.bfloat16)
            left = grads[:, :, here].reshape(tokens, depth)
            grad_d[here, :] = left_transposed(left, hidden[...]).astype(jnp.bfloat16)
        for n, (grad, into, relay) in enumerate(joins):
            sems = join_send.at[n], join_recv.at[n], relay_recv.at[n]
            join_go(links, me, k, grad, into, relay, *sems)

    take_in(0)
    weight_wait(1)
    weight_wait(2)
    first = feed(0)
    pass_on(0, first)
    take_in(1)
    following = feed(1)
    take_in(2)
    final = feed(3)
    pass_on(1, following)
    third = feed(2)
    weight_grads(0)
    pass_on(2, third)
    weight_grads(1)
    last = pass_on(3, final)
    normed_grad = jnp.concatenate(last, axis=0)
    residual = residual_ref[...]
    scale = rms(residual)
    unit = residual * scale
    part_ref[...] = jnp.sum(normed_grad * unit, axis=0, keepdims=True)
    out = own_ref[...].astype(jnp.float32) + norm_back(normed_grad, unit, scale, gain)
    wide_ref[...] = out
    low[0] = out.astype(jnp.bfloat16)
    shared = share_start(links, low, me)
    sent = []

    def context_back(d):
        made = jnp.dot(pair_of(low, d), out_weight[...], preferred_element_type=jnp.float32)
        made = made.astype(jnp.bfloat16).T
        for half, slot in enumerate((d, 4 + d)):
            here = lanes(slot * rows, rows)
            cut = made[:, half * rows : (half + 1) * rows]
            heads_out[:, :, here] = cut.reshape(group, size, rows)
            pieces[0, :, here] = heads_out[own, :, here]
            for e in (1, 2, 3):
                xd, yd = flip(x, e // 2), flip(y, e % 2)
                source = heads_out.at[2 * xd + yd, :, here]
                sent.append(links.go(source, pieces.at[e, :, here], device(z, yd, xd, c)))

    shared[1][0].wait_recv()
    context_back(0)
    for made in (first, following, third, final):
        links.done(made)
    layer_core, layer_ring = [], []
    for i in range(4):
        terms = right_transposed(pair_rows(hidden, order[i]), down[...])
        mine[i] = pair_go(links, me, layer_core, i, terms, core_out, core_in)

    def layer_step(i):
        made = layer_core[i]
        return sum_step(links, me, made, layer_ring, i, mine[i], core_in, ring_out, ring_in)

    for step in (1, 2, 3):
        share_step(links, low, me, shared, step)
        if step == 2:
            layer_step(0)
            for n, (grad, into, relay) in enumerate(joins):
                sems = join_send.at[n], join_recv.at[n], relay_recv.at[n]
                join_relay(links, me, grad, into, relay, *sems)
        for made in shared[1][1 + CHUNKS * (step - 1) : 1 + CHUNKS * step]:
            made.wait_recv()
        context_back(order[step - 1])
    layer_step(1)
    layer_step(2)
    last = layer_step(3)
    layer = (residual_ref[...] + jnp.concatenate(last, axis=0)).astype(jnp.bfloat16)
    part = width // 4
    for i in range(4):
        layer_ref[i] = layer[:, i * part : (i + 1) * part]
    for made in sent:
        made.wait_recv()
    for n, (_, into, _) in enumerate(joins):
        for k in range(2):
            for j in range(3):
                arrived(into.at[k, j], join_recv.at[n, k, j])
    links.finish()


def reduce_space(rows, width):
    return [
        low_space(4, rows, width),
        low_space(4, rows, width),
        low_space(3, rows, width),
        low_space(3, rows, width),
    ]


def core(ctx_pieces, token_rows, gain, grad_own, slots_o, slots_g, slots_ud):
    _, size, tokens = ctx_pieces.shape
    rows, width = token_rows.shape
    _, depth, ffn = slots_g.shape
    group = slots_o.shape[2] // DH
    return pl.pallas_call(
        core_kernel,
        name="core",
        out_shape=[
            low_array(4, rows, width // 4),
            low_array(tokens, 4 * size),
            low_array(8, rows, width),
            wide_array(rows, width),
            wide_array(1, width),
            low_array(4, size, tokens),
            low_array(2, 3, depth, 2 * ffn),
            low_array(2, 3, depth, ffn),
        ],
        in_specs=[IN_VMEM] * 4 + [IN_PLACE] * 4,
        out_specs=[IN_VMEM] * 6 + [IN_PLACE] * 2,
        scratch_shapes=[
            pltpu.VMEM((rows, width), jnp.float32),
            low_space(8 * depth, ffn),
            low_space(tokens, ffn),
            low_space(8 * depth, group * size),
            low_space(8 * depth, 2 * ffn),
            low_space(8, rows, width),
            low_space(8, rows, width),
            low_space(tokens, 2 * ffn),
            low_space(4, size, tokens),
            low_space(group, size, tokens),
            low_space(8 * depth, 2 * ffn),
            low_space(8 * depth, ffn),
            pltpu.VMEM((4, rows, width), jnp.float32),
            *reduce_space(rows, width),
            low_space(3, rows, width),
            low_space(3, rows, width),
            low_space(2, depth, 2 * ffn),
            low_space(2, depth, ffn),
            COPIES((112,)),
            COPIES((112,)),
            COPIES((4, 2, 2, 2)),
            COPIES((4, 2, 2, 2)),
            COPIES((2, 2, 4, 2)),
            COPIES((2, 2, 3)),
            COPIES((2, 2)),
        ],
        compiler_params=pltpu.CompilerParams(
            collective_id=2, has_side_effects=True, vmem_limit_bytes=63 << 20
        ),
    )(ctx_pieces, token_rows, gain, grad_own, slots_o, slots_g, *slots_ud)


def exit_kernel(
    piece_ref, normed_ref, weight_ref, token_ref, wide_ref, gain_ref, low_ref, context_ref,
    layer_own, gain_two_ref, line_ref, bucket_ref, ffn_ref,
    query_out, key_out, value_out, output_out, home_ref, layer_ref, small_ref, ffn_out,
    heads_in, rows_low, weight_grad, weight_in, weight_relay, held, token_out,
    packed, in_f, in_y, in_z,
    core_out, core_in, ring_out, ring_in,
    send, recv, plane_send, plane_recv, relay_recv,
):
    me = z, y, x, c = position()
    greet(*me)
    links = Links(send, recv)
    own, f = 2 * x + y, 2 * x + c
    group, three, size, tokens = heads_in.shape
    rows = tokens // 8
    depth, cols = weight_grad.shape[1] // 8, weight_grad.shape[2]
    width = normed_ref.shape[2]
    part = width // 4
    heads = []
    for d in (1, 2, 3):
        xd, yd = flip(x, d // 2), flip(y, d % 2)
        heads.append(links.go(piece_ref.at[d], heads_in.at[own], device(z, yd, xd, c)))
    heads_in[own] = piece_ref[0]

    order = sum_order(z)

    def pair_rows(ref, d):
        return jnp.concatenate(
            [ref[lanes(block * rows, rows), :] for block in (d, 4 + d)], axis=0
        )

    def to_home(source, into):
        got = []
        for d in (1, 2, 3):
            xd, cd = flip(x, d // 2), flip(c, d % 2)
            got.append(links.go(source.at[2 * xd + cd], into.at[f], device(z, y, xd, cd)))
        into[f] = source[f]
        return got

    state = [], []

    def join(n):
        sems = plane_send.at[n], plane_recv.at[n], relay_recv.at[n]
        return weight_grad.at[n], weight_in.at[n], weight_relay.at[n], *sems

    def step(i):
        terms = right_transposed(pair_rows(rows_low, order[i]), weight_ref[...])
        return reduce_pair(links, me, state, i, terms, core_out, core_in, ring_out, ring_in)

    def weight_grads(n, ref, right):
        for k in range(2):
            for piece in range(4):
                block = 4 * (piece // 2) + 2 * flip(k, z % 2) + piece % 2
                here = pl.ds(pl.multiple_of(block * depth, depth), depth)
                left = ref[:, :, here].reshape(tokens, depth)
                weight_grad[n, here, :] = left_transposed(left, right).astype(jnp.bfloat16)
            join_go(links, me, k, *join(n))

    way = [column_go(links, me, 1, ffn_ref, ffn_out)]
    results = query_out, key_out, value_out, output_out
    cut = pl.ds(pl.multiple_of((z % 2) * cols, cols), cols)

    def send_sums(n):
        for k in range(2):
            held[n, k] = join_sum(k, weight_in.at[n], plane_recv.at[n])
            way.append(column_go(links, me, k, held.at[n, k], results[n].at[:, cut]))

    weight_grads(3, low_ref, context_ref[...])

    packed[...] = jnp.zeros_like(packed)
    per_block = 4
    all_heads = BLOCK // per_block
    source, place = head_of(z, y, x, c, all_heads // 4)
    lane = lax.broadcasted_iota(jnp.int32, (1, BLOCK), 1)
    for block in range(8):
        row = jnp.zeros((1, BLOCK), jnp.float32)
        for n in range(per_block):
            hot = bucket_ref[...] == block * per_block + n
            value = lane_sum(jnp.where(hot, line_ref[...], 0.0))
            row = jnp.where(lane == n * all_heads + source * (all_heads // 4) + place, value, row)
        packed[block // 2, block % 2, 4:5, :] = row
    for made in heads:
        made.wait_recv()
    for n in range(three):
        here = slice(n * group * size, (n + 1) * group * size)
        rows_low[:, here] = heads_in[:, n].reshape(group * size, tokens).T
    step(0)
    for n in range(three):
        weight_grads(n, normed_ref, rows_low[:, n * cols : (n + 1) * cols])
    join_relay(links, me, *join(3))
    step(1)
    send_sums(3)
    join_relay(links, me, *join(0))
    join_relay(links, me, *join(1))
    step(2)
    join_relay(links, me, *join(2))
    home = to_home(layer_own, layer_ref)
    for n in range(three):
        send_sums(n)
    last = step(3)
    normed_grad = jnp.concatenate(last, axis=0)
    tokens_wide = token_ref[...].astype(jnp.float32)
    scale = rms(tokens_wide)
    unit = tokens_wide * scale
    token_grad = wide_ref[...] + norm_back(normed_grad, unit, scale, gain_ref[...])
    for i in range(4):
        token_out[i] = token_grad[:, i * part : (i + 1) * part].astype(jnp.bfloat16)
    home += to_home(token_out, home_ref)
    gain_part = jnp.sum(normed_grad * unit, axis=0, keepdims=True)
    for i in range(width // BLOCK):
        here = slice(i * BLOCK, (i + 1) * BLOCK)
        block = (i // 2) // 2, (i // 2) % 2
        packed[block[0], block[1], i % 2 : i % 2 + 1, :] = gain_part[:, here]
        packed[block[0], block[1], 2 + i % 2 : 3 + i % 2, :] = gain_two_ref[:, here]
    got = []
    for d in (1, 2, 3):
        to = device(z, y, flip(x, d // 2), flip(c, d % 2))
        got.append(links.go(packed, in_f.at[d - 1], to))
    for made in got:
        made.wait_recv()
    for made in got:
        links.done(made)
    packed[...] = packed[...] + in_f[0] + in_f[1] + in_f[2]
    made = links.go(packed.at[:, 1 - y], in_y, device(z, 1 - y, x, c))
    made.wait_recv()
    in_y[...] = in_y[...] + packed[:, y]
    got = []
    for d in (1, 2, 3):
        other = flip_pair(z, d)
        got.append(links.go(in_y.at[other], in_z.at[d - 1], device(other, y, x, c)))
    for made in got:
        made.wait_recv()
    small_ref[...] = in_y[z] + in_z[0] + in_z[1] + in_z[2]
    for made in way + home:
        made.wait_recv()
    links.finish()


def leave(pieces, normed, weight, token_rows, wide_grad, gain, low, context, layer,
          gain_two_part, line_grad, rev_buckets, ffn_slot):
    _, _, size, tokens = pieces.shape
    rows, width = token_rows.shape
    depth, wide = weight.shape[0] // 8, weight.shape[1]
    out_wide = context.shape[1]
    cols = 2 * wide // 3
    tile = (8, BLOCK)
    return pl.pallas_call(
        exit_kernel,
        name="leave",
        out_shape=[
            *(low_array(depth, cols) for _ in range(4)),
            low_array(4, rows, width // 4),
            low_array(4, rows, width // 4),
            wide_array(*tile),
            low_array(*ffn_slot.shape),
        ],
        in_specs=[IN_VMEM] * 12 + [IN_PLACE],
        out_specs=[IN_VMEM] * 7 + [IN_PLACE],
        scratch_shapes=[
            low_space(4, 3, size, tokens),
            low_space(tokens, wide),
            low_space(4, 8 * depth, out_wide),
            low_space(4, 2, 3, depth, out_wide),
            low_space(4, 2, depth, out_wide),
            low_space(4, 2, depth, out_wide),
            low_space(4, rows, width // 4),
            pltpu.VMEM((4, 2, *tile), jnp.float32),
            pltpu.VMEM((3, 4, 2, *tile), jnp.float32),
            pltpu.VMEM((4, *tile), jnp.float32),
            pltpu.VMEM((3, *tile), jnp.float32),
            *reduce_space(rows, width),
            COPIES((64,)),
            COPIES((64,)),
            COPIES((4, 2, 4, 2)),
            COPIES((4, 2, 3)),
            COPIES((4, 2)),
        ],
        compiler_params=pltpu.CompilerParams(
            collective_id=4, has_side_effects=True, vmem_limit_bytes=60 << 20
        ),
    )(pieces, normed, weight, token_rows, wide_grad, gain, low, context, layer,
      gain_two_part, line_grad, rev_buckets, ffn_slot)


def widen_kernel(*refs):
    attn, slots, home, outs = refs[:4], refs[4:6], refs[6], refs[7:]
    z_low = (lax.axis_index("seq") // 2) % 2
    for ref, out in zip(attn, outs[:4]):
        out[...] = ref[...].astype(jnp.float32)
    size = slots[0].shape[1] // 3
    for k in range(2):
        cut = lanes((k + z_low - 2 * k * z_low) * size, size)
        for n, out in enumerate(outs[4:7]):
            out[:, cut] = slots[k][:, n * size : (n + 1) * size].astype(jnp.float32)
    outs[7][...] = home[...].astype(jnp.float32)


def widen(attn, slots, home):
    depth, cols = attn[0].shape
    size = 2 * slots[0].shape[1] // 3
    return pl.pallas_call(
        widen_kernel,
        name="widen",
        out_shape=[wide_array(depth, cols)] * 4
        + [wide_array(depth, size)] * 3
        + [wide_array(*home.shape)],
        in_specs=[IN_VMEM] * 7,
        out_specs=[IN_VMEM] * 8,
        compiler_params=pltpu.CompilerParams(vmem_limit_bytes=32 << 20),
    )(*attn, *slots, home)


def fast_shards(
    tokens_in,
    cotangent,
    gain_attn,
    query_weight,
    key_weight,
    value_weight,
    output_weight,
    bias_table,
    gain_ffn,
    gate_weight,
    up_weight,
    down_weight,
    lengths,
    buckets,
):
    seq_index, fsdp_index = lax.axis_index("seq"), lax.axis_index("fsdp")
    z, y, x, c = seq_index // 2, seq_index % 2, fsdp_index // 2, fsdp_index % 2
    z_low, z_high = z % 2, z // 2
    batch_count, slot_count, part_width = tokens_in.shape
    width = part_width * 4
    row_count = query_weight.shape[0]
    heads = query_weight.shape[1] // DH
    group_heads = heads // 2
    group_width = group_heads * DH
    hidden_width = gate_weight.shape[1] // 2
    def halves(weights):
        slots = []
        for k in range(2):
            half = k ^ z_low
            slots.append(
                jnp.concatenate(
                    [
                        lax.dynamic_slice_in_dim(w, half * (w.shape[1] // 2), w.shape[1] // 2, 1)
                        for w in weights
                    ],
                    axis=1,
                )
            )
        return slots

    small = jnp.concatenate(
        [gain_attn, gain_ffn, bias_table.reshape(-1), jnp.zeros((2 * row_count - bias_table.size,), jnp.bfloat16)]
    )
    small = small.astype(jnp.float32).reshape(8, BLOCK)
    rev_buckets = jnp.concatenate([buckets[::-1], jnp.full((1,), -1, jnp.int32)])[None, :]
    (
        token_low,
        normed_one,
        grad_own,
        pieces,
        qkv_weight,
        gain_one,
        gain_two,
        rev_line,
        slots_o,
        slots_g,
    ) = entry(
        lengths,
        tokens_in,
        cotangent,
        small,
        rev_buckets,
        (query_weight, key_weight, value_weight, output_weight, gate_weight),
    )
    pieces, *later = lax.optimization_barrier((pieces, *halves([up_weight, down_weight])))
    slots_ud = [move(later[k], spread_slot(k)) for k in range(2)]
    context_pieces, context_wide, lse, qkv_all = attend(lengths, pieces, rev_line)
    (
        layer,
        context,
        residual_low,
        residual_grad,
        gain_two_part,
        grad_pieces,
        terms_gate_up,
        terms_down,
    ) = core(context_pieces, token_low, gain_two, grad_own, slots_o, slots_g, slots_ud)

    def slot_sum(k):
        sums = [
            jnp.sum(t[k].astype(jnp.float32), axis=0).astype(jnp.bfloat16)
            for t in (terms_gate_up, terms_down)
        ]
        return jnp.concatenate(sums, axis=1)

    ffn_first = move(slot_sum(0), spread_slot(0))
    ffn_second = slot_sum(1)
    qkv_grad_pieces, line_grad = attend_back(
        lengths, grad_pieces, rev_line, context_wide, lse, qkv_all
    )
    qkv_grad_pieces, ffn_first = lax.optimization_barrier((qkv_grad_pieces, ffn_first))
    *attn_sums, home, layer, small, ffn_second = leave(
        qkv_grad_pieces,
        normed_one,
        qkv_weight,
        token_low,
        residual_grad,
        gain_one,
        residual_low,
        context,
        layer,
        gain_two_part,
        line_grad,
        rev_buckets,
        ffn_second,
    )
    query_sum, key_sum, value_sum, output_sum, gate_sum, up_sum, down_sum, home = widen(
        attn_sums, (ffn_first, ffn_second), home
    )
    token_share = home.reshape(batch_count, slot_count, part_width)
    layer_out = layer.reshape(batch_count, slot_count, part_width)
    table_sum = lax.dynamic_slice_in_dim(
        small[4].reshape(-1, 4 * heads), fsdp_index * heads, heads, 1
    )
    return (
        layer_out,
        token_share,
        small[:2].reshape(-1),
        query_sum,
        key_sum,
        value_sum,
        output_sum,
        table_sum,
        small[2:4].reshape(-1),
        gate_sum,
        up_sum,
        down_sum,
    )


def solution(mesh):
    placed = (
        P(None, "seq", "fsdp"),
        P(None, "seq", "fsdp"),
        P("seq"),
        P("seq", "fsdp"),
        P("seq", "fsdp"),
        P("seq", "fsdp"),
        P("seq", "fsdp"),
        P("seq", "fsdp"),
        P("seq"),
        P("seq", "fsdp"),
        P("seq", "fsdp"),
        P("seq", "fsdp"),
        P(),
        P(),
    )
    return jax.shard_map(
        fast_shards if (mesh.shape["seq"], mesh.shape["fsdp"]) == (8, 4) else shards,
        mesh=mesh,
        in_specs=placed,
        out_specs=(
            P(None, "seq", "fsdp"),
            P(None, "seq", "fsdp"),
            P("seq"),
            P("seq", "fsdp"),
            P("seq", "fsdp"),
            P("seq", "fsdp"),
            P("seq", "fsdp"),
            P("seq", "fsdp"),
            P("seq"),
            P("seq", "fsdp"),
            P("seq", "fsdp"),
            P("seq", "fsdp"),
        ),
        check_vma=False,
    )
```

```python
from functools import partial

import jax
import jax.numpy as jnp
from jax import lax
from jax.experimental import pallas as pl
from jax.experimental.pallas import tpu as pltpu
from jax.sharding import PartitionSpec as P

DH = 64


epsilon = 1e-06
highest = lax.Precision.HIGHEST
masked_score = -1e30
root_two_over_pi = 0.7978845608028654


def plain_product(left, right):
    return jnp.dot(left, right, preferred_element_type=jnp.float32)


def right_transposed(left, right):
    return lax.dot_general(
        left, right, (((1,), (1,)), ((), ())), preferred_element_type=jnp.float32
    )


def left_transposed(left, right):
    return lax.dot_general(
        left, right, (((0,), (0,)), ((), ())), preferred_element_type=jnp.float32
    )


def normalize(rows, gain):
    row_scale = lax.rsqrt(jnp.mean(rows * rows, axis=-1, keepdims=True) + epsilon)
    unit_rows = rows * row_scale
    return (unit_rows, row_scale, (unit_rows * gain.astype(jnp.float32)).astype(jnp.bfloat16))


def norm_back(grad_normed, unit_rows, row_scale, gain):
    weighted = grad_normed * gain.astype(jnp.float32)
    return row_scale * (
        weighted - unit_rows * jnp.mean(weighted * unit_rows, axis=-1, keepdims=True)
    )


def to_heads(rows, batch_count, head_size):
    slot_count = rows.shape[0] // batch_count
    number_of_heads = rows.shape[1] // head_size
    return rows.reshape(batch_count, slot_count, number_of_heads, head_size).transpose(2, 0, 1, 3)


def from_heads(blocks):
    number_of_heads, batch_count, slot_count, head_size = blocks.shape
    return blocks.transpose(1, 2, 0, 3).reshape(
        batch_count * slot_count, number_of_heads * head_size
    )


def bias_rows(bias_line, first_query, slot_count, length):
    span = slot_count + length - 1
    segment = lax.dynamic_slice_in_dim(bias_line, length - first_query - slot_count, span)
    flat = jnp.tile(segment, slot_count)
    skewed = flat[slot_count - 1 : slot_count - 1 + slot_count * (span - 1)].reshape(
        slot_count, span - 1
    )
    return skewed[:, :length]


def bias_rows_back(block_grad, first_query, slot_count, length, line_length):
    span = slot_count + length - 1
    widened = jnp.pad(block_grad, ((0, 0), (0, span - 1 - length)))
    flat = jnp.pad(widened.reshape(-1), (slot_count - 1, 1))
    segment_grad = jnp.sum(flat.reshape(slot_count, span), axis=0)
    return lax.dynamic_update_slice_in_dim(
        jnp.zeros((line_length,), jnp.float32), segment_grad, length - first_query - slot_count, 0
    )


def full_features(block):
    gathered = lax.all_gather(block, "fsdp", axis=2, tiled=True)
    return gathered.reshape(gathered.shape[0] * gathered.shape[1], gathered.shape[2])


def feature_total(partial_rows):
    return lax.psum(partial_rows, "fsdp")


def shards(
    tokens_in,
    cotangent,
    gain_attn,
    query_weight,
    key_weight,
    value_weight,
    output_weight,
    bias_table,
    gain_ffn,
    gate_weight,
    up_weight,
    down_weight,
    lengths,
    buckets,
):
    batch_count, slot_count, part_width = tokens_in.shape
    head_size = DH
    seq_index = lax.axis_index("seq")
    fsdp_index = lax.axis_index("fsdp")
    length = slot_count * lax.axis_size("seq")
    line_length = buckets.shape[0]
    first_query = seq_index * slot_count
    positions = jnp.arange(length, dtype=jnp.int32)
    query_positions = first_query + jnp.arange(slot_count, dtype=jnp.int32)
    key_valid = positions[None, :] < lengths[:, None]
    own_valid = query_positions[None, :] < lengths[:, None]
    gain_one, query_full, key_full, value_full, output_full, table_full = (
        lax.all_gather(gain_attn, "seq", axis=0, tiled=True),
        lax.all_gather(query_weight, "seq", axis=0, tiled=True),
        lax.all_gather(key_weight, "seq", axis=0, tiled=True),
        lax.all_gather(value_weight, "seq", axis=0, tiled=True),
        lax.all_gather(output_weight, "seq", axis=0, tiled=True),
        lax.all_gather(bias_table, "seq", axis=0, tiled=True),
    )
    token_rows = full_features(tokens_in).astype(jnp.float32)
    unit_one, scale_one, normed_one = normalize(token_rows, gain_one)
    query_heads = to_heads(
        plain_product(normed_one, query_full).astype(jnp.bfloat16), batch_count, head_size
    )
    key_heads = to_heads(
        plain_product(normed_one, key_full).astype(jnp.bfloat16), batch_count, head_size
    )
    value_heads = to_heads(
        plain_product(normed_one, value_full).astype(jnp.bfloat16), batch_count, head_size
    )
    number_of_heads = query_heads.shape[0]
    flat_shape = (number_of_heads, batch_count, slot_count * head_size)
    gathered_keys, gathered_values = (
        lax.all_gather(key_heads.reshape(flat_shape), "seq", axis=2, tiled=True),
        lax.all_gather(value_heads.reshape(flat_shape), "seq", axis=2, tiled=True),
    )
    all_keys = gathered_keys.reshape(number_of_heads, batch_count, length, head_size)
    all_values = gathered_values.reshape(number_of_heads, batch_count, length, head_size)
    bucket_hot = (
        buckets[:, None] == jnp.arange(table_full.shape[0], dtype=jnp.int32)[None, :]
    ).astype(jnp.float32)
    offset_bias = lax.dot_general(
        table_full.astype(jnp.float32), bucket_hot, (((0,), (1,)), ((), ())), precision=highest
    )

    def masked_scores(query_tile_rows, key_tile_rows, bias_block):
        raw = (
            jnp.einsum(
                "jht,jxt->jhx", query_tile_rows, key_tile_rows, preferred_element_type=jnp.float32
            )
            + bias_block[None]
        )
        return jnp.where(key_valid[:, None, :], raw, masked_score)

    def attend(inputs):
        query_tile_rows, key_tile_rows, value_tile_rows, bias_line = inputs
        scores = masked_scores(
            query_tile_rows, key_tile_rows, bias_rows(bias_line, first_query, slot_count, length)
        )
        row_peak = jnp.max(scores, axis=-1, keepdims=True)
        raised = jnp.exp(scores - row_peak)
        denominator = jnp.sum(raised, axis=-1, keepdims=True)
        weights_reduced_precision = (raised / denominator).astype(jnp.bfloat16)
        context = jnp.einsum(
            "wot,wtf->wof",
            weights_reduced_precision,
            value_tile_rows,
            preferred_element_type=jnp.float32,
        ).astype(jnp.bfloat16)
        return (context, (row_peak + jnp.log(denominator))[..., 0])

    context_heads, log_totals = lax.map(attend, (query_heads, all_keys, all_values, offset_bias))
    context_rows = from_heads(context_heads)
    residual = token_rows + feature_total(right_transposed(context_rows, output_full))
    gain_two, gate_full, up_full, down_full = (
        lax.all_gather(gain_ffn, "seq", axis=0, tiled=True),
        lax.all_gather(gate_weight, "seq", axis=0, tiled=True),
        lax.all_gather(up_weight, "seq", axis=0, tiled=True),
        lax.all_gather(down_weight, "seq", axis=0, tiled=True),
    )
    unit_two, scale_two, normed_two = normalize(residual, gain_two)
    gate_pre = plain_product(normed_two, gate_full)
    up_pre = plain_product(normed_two, up_full)
    activated, gelu_back = jax.vjp(jax.nn.gelu, gate_pre)
    hidden = (activated * up_pre).astype(jnp.bfloat16)
    ffn_share = lax.psum_scatter(
        right_transposed(hidden, down_full), "fsdp", scatter_dimension=1, tiled=True
    )
    residual_share = lax.dynamic_slice_in_dim(residual, fsdp_index * part_width, part_width, 1)
    layer_out = (
        (residual_share + ffn_share)
        .astype(jnp.bfloat16)
        .reshape(batch_count, slot_count, part_width)
    )
    masked_cot = jnp.where(own_valid[:, :, None], cotangent, jnp.zeros_like(cotangent))
    grad_rows = full_features(masked_cot)
    grad_down = left_transposed(grad_rows, hidden)
    grad_hidden = plain_product(grad_rows, down_full)
    grad_gate_pre = gelu_back(grad_hidden * up_pre)[0].astype(jnp.bfloat16)
    grad_up_pre = (grad_hidden * activated).astype(jnp.bfloat16)
    grad_gate = left_transposed(normed_two, grad_gate_pre)
    grad_up = left_transposed(normed_two, grad_up_pre)
    normed_two_grad = right_transposed(grad_gate_pre, gate_full) + right_transposed(
        grad_up_pre, up_full
    )
    second_gain_piece = jnp.sum(normed_two_grad * unit_two, axis=0)
    ffn_grads = (
        lax.psum_scatter(second_gain_piece, "seq", scatter_dimension=0, tiled=True),
        lax.psum_scatter(grad_gate, "seq", scatter_dimension=0, tiled=True),
        lax.psum_scatter(grad_up, "seq", scatter_dimension=0, tiled=True),
        lax.psum_scatter(grad_down, "seq", scatter_dimension=0, tiled=True),
    )
    residual_grad = grad_rows.astype(jnp.float32) + norm_back(
        feature_total(normed_two_grad), unit_two, scale_two, gain_two
    )
    residual_low = residual_grad.astype(jnp.bfloat16)
    grad_output = left_transposed(residual_low, context_rows)
    context_grad = to_heads(
        plain_product(residual_low, output_full).astype(jnp.bfloat16), batch_count, head_size
    )

    def query_side(inputs, with_keys):
        query_tile_rows, key_tile_rows, value_tile_rows, bias_line, log_total, context_tile_rows = (
            inputs
        )
        scores = masked_scores(
            query_tile_rows, key_tile_rows, bias_rows(bias_line, first_query, slot_count, length)
        )
        probs = jnp.exp(scores - log_total[..., None])
        prob_grad = jnp.einsum(
            "jht,jxt->jhx", context_tile_rows, value_tile_rows, preferred_element_type=jnp.float32
        )
        delta = jnp.sum(probs * prob_grad, axis=-1)
        score_gradient = (probs * (prob_grad - delta[..., None])).astype(jnp.bfloat16)
        query_grad = jnp.einsum(
            "wot,wtf->wof", score_gradient, key_tile_rows, preferred_element_type=jnp.float32
        )
        bias_grad = bias_rows_back(
            jnp.sum(score_gradient.astype(jnp.float32), axis=0),
            first_query,
            slot_count,
            length,
            line_length,
        )
        key_term = jnp.einsum(
            "xic,xil->xcl", score_gradient, query_tile_rows, preferred_element_type=jnp.float32
        )
        value_term = jnp.einsum(
            "xic,xil->xcl",
            probs.astype(jnp.bfloat16),
            context_tile_rows,
            preferred_element_type=jnp.float32,
        )
        return (query_grad, bias_grad, delta, key_term, value_term)

    side_inputs = (query_heads, all_keys, all_values, offset_bias, log_totals, context_grad)
    query_grad, bias_grad, delta, key_terms, value_terms = lax.map(
        partial(query_side, with_keys=True), side_inputs
    )
    wide_shape = (number_of_heads, batch_count, length * head_size)
    key_sums, value_sums = (
        lax.psum_scatter(key_terms.reshape(wide_shape), "seq", scatter_dimension=2, tiled=True),
        lax.psum_scatter(value_terms.reshape(wide_shape), "seq", scatter_dimension=2, tiled=True),
    )
    own_shape = (number_of_heads, batch_count, slot_count, head_size)
    query_low = from_heads(query_grad.astype(jnp.bfloat16))
    key_low = from_heads(key_sums.reshape(own_shape).astype(jnp.bfloat16))
    value_low = from_heads(value_sums.reshape(own_shape).astype(jnp.bfloat16))
    grad_query = left_transposed(normed_one, query_low)
    grad_key = left_transposed(normed_one, key_low)
    grad_value = left_transposed(normed_one, value_low)
    grad_table = lax.dot_general(bucket_hot, bias_grad, (((0,), (1,)), ((), ())), precision=highest)
    normed_one_grad = (
        right_transposed(query_low, query_full)
        + right_transposed(key_low, key_full)
        + right_transposed(value_low, value_full)
    )
    gain_one_part = jnp.sum(normed_one_grad * unit_one, axis=0)
    attn_grads = (
        lax.psum_scatter(gain_one_part, "seq", scatter_dimension=0, tiled=True),
        lax.psum_scatter(grad_query, "seq", scatter_dimension=0, tiled=True),
        lax.psum_scatter(grad_key, "seq", scatter_dimension=0, tiled=True),
        lax.psum_scatter(grad_value, "seq", scatter_dimension=0, tiled=True),
        lax.psum_scatter(grad_output, "seq", scatter_dimension=0, tiled=True),
        lax.psum_scatter(grad_table, "seq", scatter_dimension=0, tiled=True),
    )
    token_grad = residual_grad + norm_back(
        feature_total(normed_one_grad), unit_one, scale_one, gain_one
    )
    token_share = lax.dynamic_slice_in_dim(
        token_grad, fsdp_index * part_width, part_width, 1
    ).reshape(batch_count, slot_count, part_width)
    gain_one_sum, gain_two_sum = lax.psum((attn_grads[0], ffn_grads[0]), "fsdp")
    return (
        layer_out,
        token_share,
        gain_one_sum,
        attn_grads[1],
        attn_grads[2],
        attn_grads[3],
        attn_grads[4],
        attn_grads[5],
        gain_two_sum,
        ffn_grads[1],
        ffn_grads[2],
        ffn_grads[3],
    )


BLOCK = 128
BOTH = ("seq", "fsdp")


def move(value, target):
    pairs = []
    for z in range(4):
        for y in range(2):
            for x in range(2):
                for c in range(2):
                    zt, yt, xt, ct = target(z, y, x, c)
                    pairs.append(((2 * z + y) * 4 + 2 * x + c, (2 * zt + yt) * 4 + 2 * xt + ct))
    return lax.ppermute(value, BOTH, pairs)


def spread_slot(k):
    return lambda z, y, x, c: (2 * c + (k ^ (z & 1)), y, x, z >> 1)


KEYS = 512
QUERIES = 512
WIDE_QUERIES = 1024
OFFSET = 1920


def skew_table(rev_ref, table):
    width = rev_ref.shape[1]
    line = jnp.broadcast_to(rev_ref[...], (8, width))
    for first in range(0, BLOCK, 8):
        table[first : first + 8, :] = pltpu.roll(
            line, (width - (BLOCK - 1) + first) % width, axis=1, stride=1, stride_axis=0
        )


def place_of(piece, part, z, y, x, c):
    c_rel, d = part // 4, part % 4
    b = jnp.bitwise_xor(x, piece // 2)
    block = (
        4 * jnp.bitwise_xor(z, d)
        + 2 * jnp.bitwise_xor(y, piece % 2)
        + jnp.bitwise_xor(c, c_rel)
    )
    return b, block


def part_of(b, block, z, y, x, c):
    piece = 2 * jnp.bitwise_xor(b, x) + jnp.bitwise_xor((block // 2) % 2, y)
    part = 4 * jnp.bitwise_xor(block % 2, c) + jnp.bitwise_xor(block // 4, z)
    return piece, part


def lanes(first, count):
    return pl.ds(pl.multiple_of(first, BLOCK), count)


def attend_kernel(sc, pieces, rev_ref, ctx_ref, ctx_wide, lse_ref, qkv, keys, table):
    z, y, x, c = position()
    for piece in range(4):
        for part in range(8):
            b, block = place_of(piece, part, z, y, x, c)
            data = pieces[piece, :, :, part * BLOCK : (part + 1) * BLOCK]
            qkv[b, :, :, lanes(block * BLOCK, BLOCK)] = data
            keys[b, lanes(block * BLOCK, BLOCK), :] = data[1].T
    skew_table(rev_ref, table)
    length = qkv.shape[-1]
    for b in range(2):
        valid = sc[b]
        full = valid // KEYS

        @pl.loop(0, length // WIDE_QUERIES)
        def _(i):
            first_query = i * WIDE_QUERIES
            query = qkv[b, 0, :, lanes(first_query, WIDE_QUERIES)]

            def tile(j, carry, masked):
                peak, total, acc = carry
                first_key = j * KEYS
                score = jnp.dot(
                    keys[b, lanes(first_key, KEYS), :], query, preferred_element_type=jnp.float32
                )
                score = score + jnp.concatenate(
                    [
                        table[:, lanes(first_query - first_key + OFFSET - t, WIDE_QUERIES)]
                        for t in range(0, KEYS, BLOCK)
                    ],
                    axis=0,
                )
                if masked:
                    position = first_key + lax.broadcasted_iota(jnp.int32, (KEYS, WIDE_QUERIES), 0)
                    score = jnp.where(position < valid, score, masked_score)
                now = jnp.maximum(peak, jnp.max(score, axis=0, keepdims=True))
                scale = jnp.exp(peak - now)
                prob = jnp.exp(score - now)
                total = total * scale + jnp.sum(prob, axis=0, keepdims=True)
                acc = acc * scale + jnp.dot(
                    qkv[b, 2, :, lanes(first_key, KEYS)],
                    prob.astype(jnp.bfloat16),
                    preferred_element_type=jnp.float32,
                )
                return now, total, acc

            carry = (
                jnp.full((1, WIDE_QUERIES), masked_score, jnp.float32),
                jnp.zeros((1, WIDE_QUERIES), jnp.float32),
                jnp.zeros((DH, WIDE_QUERIES), jnp.float32),
            )
            carry = lax.fori_loop(0, full, lambda j, s: tile(j, s, False), carry)
            peak, total, acc = lax.cond(
                valid > full * KEYS, lambda s: tile(full, s, True), lambda s: s, carry
            )
            context = acc / total
            ctx_wide[b, :, lanes(first_query, WIDE_QUERIES)] = context
            lse_ref[b, :, lanes(first_query, WIDE_QUERIES)] = peak + jnp.log(total)
            low = context.astype(jnp.bfloat16)
            for t in range(WIDE_QUERIES // BLOCK):
                piece, part = part_of(b, i * (WIDE_QUERIES // BLOCK) + t, z, y, x, c)
                ctx_ref[piece, :, lanes(part * BLOCK, BLOCK)] = low[:, t * BLOCK : (t + 1) * BLOCK]


def attend(scalars, pieces, rev_line):
    _, _, head_size, tokens = pieces.shape
    length = tokens * 2
    smem, vmem = pl.BlockSpec(memory_space=pltpu.SMEM), pl.BlockSpec(memory_space=pltpu.VMEM)
    return pl.pallas_call(
        attend_kernel,
        name="attend",
        out_shape=[
            jax.ShapeDtypeStruct((4, head_size, tokens), jnp.bfloat16),
            jax.ShapeDtypeStruct((2, head_size, length), jnp.float32),
            jax.ShapeDtypeStruct((2, 1, length), jnp.float32),
            jax.ShapeDtypeStruct((2, 3, head_size, length), jnp.bfloat16),
        ],
        in_specs=[smem] + [vmem] * 2,
        out_specs=[vmem] * 4,
        scratch_shapes=[
            pltpu.VMEM((2, length, head_size), jnp.bfloat16),
            pltpu.VMEM((BLOCK, rev_line.shape[1]), jnp.float32),
        ],
        cost_estimate=pl.CostEstimate(
            flops=46_000_000_000, bytes_accessed=4 << 20, transcendentals=0
        ),
        compiler_params=pltpu.CompilerParams(vmem_limit_bytes=48 << 20),
    )(scalars, pieces, rev_line)


def attend_back_kernel(
    sc, pieces, rev_ref, ctx_wide, lse_ref, qkv,
    out_ref, line_ref,
    queries, keys, values, grads, grads_t, delta, query_sum, key_sum, value_sum, table, table_sum,
):
    z, y, x, c = position()
    length = qkv.shape[-1]
    for piece in range(4):
        for part in range(8):
            b, block = place_of(piece, part, z, y, x, c)
            data = pieces[piece, :, part * BLOCK : (part + 1) * BLOCK]
            grads_t[b, :, lanes(block * BLOCK, BLOCK)] = data
            grads[b, lanes(block * BLOCK, BLOCK), :] = data.T
    for b in range(2):
        for first in range(0, length, BLOCK):
            here = slice(first, first + BLOCK)
            queries[b, here, :] = qkv[b, 0, :, here].T
            keys[b, here, :] = qkv[b, 1, :, here].T
            values[b, here, :] = qkv[b, 2, :, here].T
        delta[b] = jnp.sum(
            ctx_wide[b] * grads_t[b].astype(jnp.float32), axis=0, keepdims=True
        )
    skew_table(rev_ref, table)
    table_sum[...] = jnp.zeros_like(table_sum)
    query_sum[...] = jnp.zeros_like(query_sum)
    out_ref[...] = jnp.zeros_like(out_ref)
    for b in range(2):
        valid = sc[b]
        full = valid // KEYS
        count = (valid + QUERIES - 1) // QUERIES

        def key_step(j, masked):
            first_key = j * KEYS
            key, value = keys[b, lanes(first_key, KEYS), :], values[b, lanes(first_key, KEYS), :]
            key_t = qkv[b, 1, :, lanes(first_key, KEYS)]
            key_sum[...] = jnp.zeros_like(key_sum)
            value_sum[...] = jnp.zeros_like(value_sum)

            @pl.loop(0, count)
            def _(i):
                first_query = i * QUERIES
                here = lanes(first_query, QUERIES)
                score = jnp.dot(key, qkv[b, 0, :, here], preferred_element_type=jnp.float32)
                score = score + jnp.concatenate(
                    [
                        table[:, lanes(first_query - first_key + OFFSET - t, QUERIES)]
                        for t in range(0, KEYS, BLOCK)
                    ],
                    axis=0,
                )
                if masked:
                    position = first_key + lax.broadcasted_iota(jnp.int32, (KEYS, QUERIES), 0)
                    score = jnp.where(position < valid, score, masked_score)
                prob = jnp.exp(score - lse_ref[b, :, here])
                prob_grad = jnp.dot(value, grads_t[b, :, here], preferred_element_type=jnp.float32)
                score_grad = (prob * (prob_grad - delta[b, :, here])).astype(jnp.bfloat16)
                value_sum[...] += jnp.dot(
                    prob.astype(jnp.bfloat16), grads[b, here, :], preferred_element_type=jnp.float32
                )
                key_sum[...] += jnp.dot(
                    score_grad, queries[b, here, :], preferred_element_type=jnp.float32
                )
                query_sum[b, :, here] += jnp.dot(
                    key_t, score_grad, preferred_element_type=jnp.float32
                )
                for t in range(0, KEYS, BLOCK):
                    table_sum[:, lanes(first_query - first_key + OFFSET - t, QUERIES)] += score_grad[
                        t : t + BLOCK
                    ].astype(jnp.float32)

            for t in range(KEYS // BLOCK):
                piece, part = part_of(b, j * (KEYS // BLOCK) + t, z, y, x, c)
                rows = slice(t * BLOCK, (t + 1) * BLOCK)
                at = lanes(part * BLOCK, BLOCK)
                out_ref[piece, 1, :, at] = key_sum[rows, :].T.astype(jnp.bfloat16)
                out_ref[piece, 2, :, at] = value_sum[rows, :].T.astype(jnp.bfloat16)

        pl.loop(0, full)(lambda j: key_step(j, False))
        pl.when(valid > full * KEYS)(lambda: key_step(full, True))
        for block in range(length // BLOCK):
            piece, part = part_of(b, block, z, y, x, c)
            out_ref[piece, 0, :, lanes(part * BLOCK, BLOCK)] = query_sum[
                b, :, block * BLOCK : (block + 1) * BLOCK
            ].astype(jnp.bfloat16)
    width = table_sum.shape[1]
    line = jnp.zeros((8, width), jnp.float32)
    for first in range(0, BLOCK, 8):
        line = line + pltpu.roll(table_sum[first : first + 8, :], BLOCK - 8 - first, axis=1)
    ahead = 7 - lax.broadcasted_iota(jnp.int32, (8, width), 0)
    for bit in (1, 2, 4):
        line = jnp.where((ahead & bit) != 0, pltpu.roll(line, bit, axis=1), line)
    line_ref[...] = jnp.sum(line, axis=0, keepdims=True)


def attend_back(scalars, pieces, rev_line, ctx_wide, lse, qkv):
    _, head_size, tokens = pieces.shape
    length = tokens * 2
    smem, vmem = pl.BlockSpec(memory_space=pltpu.SMEM), pl.BlockSpec(memory_space=pltpu.VMEM)
    low = pltpu.VMEM((2, length, head_size), jnp.bfloat16)
    return pl.pallas_call(
        attend_back_kernel,
        name="attend_back",
        out_shape=[
            jax.ShapeDtypeStruct((4, 3, head_size, tokens), jnp.bfloat16),
            jax.ShapeDtypeStruct(rev_line.shape, jnp.float32),
        ],
        in_specs=[smem] + [vmem] * 5,
        out_specs=[vmem] * 2,
        scratch_shapes=[
            low, low, low, low,
            pltpu.VMEM((2, head_size, length), jnp.bfloat16),
            pltpu.VMEM((2, 1, length), jnp.float32),
            pltpu.VMEM((2, head_size, length), jnp.float32),
            pltpu.VMEM((KEYS, head_size), jnp.float32),
            pltpu.VMEM((KEYS, head_size), jnp.float32),
            pltpu.VMEM((BLOCK, rev_line.shape[1]), jnp.float32),
            pltpu.VMEM((BLOCK, rev_line.shape[1]), jnp.float32),
        ],
        cost_estimate=pl.CostEstimate(
            flops=46_000_000_000, bytes_accessed=4 << 20, transcendentals=0
        ),
        compiler_params=pltpu.CompilerParams(vmem_limit_bytes=48 << 20),
    )(scalars, pieces, rev_line, ctx_wide, lse, qkv)


CHUNKS = 2
MESH_ID = pl.DeviceIdType.MESH
IN_VMEM = pl.BlockSpec(memory_space=pltpu.VMEM)
IN_PLACE = pl.BlockSpec(memory_space=pl.ANY)
COPIES = pltpu.SemaphoreType.DMA


def flip(a, b):
    return a + b - 2 * a * b


def flip_pair(a, b):
    return 2 * flip(a // 2, b // 2) + flip(a % 2, b % 2)


def position():
    s, f = lax.axis_index("seq"), lax.axis_index("fsdp")
    return s // 2, s % 2, f // 2, f % 2


def device(z, y, x, c):
    return (2 * z + y, 2 * x + c)


def ring_of(z):
    high, low = z // 2, z % 2
    following = 2 * low + 1 - high
    return following, (2 * (1 - low) + high, 2 * (1 - high) + 1 - low, following)


def greet(z, y, x, c):
    peers = []
    for d in range(1, 8):
        peers.append(device(z, flip(y, d // 4), flip(x, (d // 2) % 2), flip(c, d % 2)))
        if d > 1:
            peers.append(device(flip_pair(z, d // 2), y, x, flip(c, d % 2)))
    barrier = pltpu.get_barrier_semaphore()
    for peer in peers:
        pl.semaphore_signal(barrier, inc=1, device_id=peer, device_id_type=MESH_ID)
    pl.semaphore_wait(barrier, len(peers))


def remote(source, target, send, recv, to):
    return pltpu.make_async_remote_copy(
        src_ref=source,
        dst_ref=target,
        send_sem=send,
        recv_sem=recv,
        device_id=to,
        device_id_type=MESH_ID,
    )


class Links:
    def __init__(self, send, recv):
        self.send, self.recv, self.used, self.sent = send, recv, 0, []

    def go(self, source, target, to):
        i = self.used
        self.used += 1
        made = remote(source, target, self.send.at[i], self.recv.at[i], to)
        made.start()
        self.sent.append(made)
        return made

    def go_unless(self, own, source, target, to, send=None, recv=None):
        if send is None:
            send, recv = self.send.at[self.used], self.recv.at[self.used]
            self.used += 1
        made = remote(source, target, send, recv, to)
        if own is None:
            made.start()
            self.sent.append(made)
            return made
        local = pltpu.make_async_copy(source, target, recv)
        pl.when(own)(lambda: local.start())
        pl.when(jnp.logical_not(own))(lambda: made.start())
        self.sent.append((own, made))
        return made

    def go_if(self, there, here, source, target, send, recv, to):
        made = remote(source, target, send, recv, to)
        pl.when(there)(lambda: made.start())
        if here is not None:
            local = pltpu.make_async_copy(source, target, recv)
            pl.when(here)(lambda: local.start())
        self.sent.append((jnp.logical_not(there), made))

    def done(self, made):
        made.wait_send()
        self.sent = [m for m in self.sent if m is not made]

    def finish(self):
        for made in self.sent:
            if isinstance(made, tuple):
                pl.when(jnp.logical_not(made[0]))(lambda made=made: made[1].wait_send())
            else:
                made.wait_send()


def share_start(links, rows_all, me):
    z, y, x, c = me
    following, _ = ring_of(z)
    rows = rows_all.shape[1] // CHUNKS
    ring = []
    for h in range(CHUNKS):
        here = pl.ds(h * rows, rows)
        target = rows_all.at[flip_pair(following, z), here]
        ring.append(links.go(rows_all.at[0, here], target, device(following, y, x, c)))
    core = [links.go(rows_all.at[0], rows_all.at[4], device(z, y, x, 1 - c))]
    return [ring], core


def share_step(links, rows_all, me, state, step):
    z, y, x, c = me
    following, back = ring_of(z)
    rows = rows_all.shape[1] // CHUNKS
    ring, core = state
    slot = flip_pair(z, back[step - 1])
    sent = []
    for h in range(CHUNKS):
        here = pl.ds(h * rows, rows)
        ring[-1][h].wait_recv()
        source = rows_all.at[slot, here]
        if step < 3:
            target = rows_all.at[flip_pair(following, back[step - 1]), here]
            sent.append(links.go(source, target, device(following, y, x, c)))
        core.append(links.go(source, rows_all.at[4 + slot, here], device(z, y, x, 1 - c)))
    ring.append(sent)


def share_end(state):
    for made in state[1]:
        made.wait_recv()


def sum_order(z):
    _, back = ring_of(z)
    return [flip_pair(z, b) for b in back] + [0]


def column_go(links, me, k, source, target):
    z, y, x, c = me
    own = z // 2 == c if k == 0 else None
    to = device(2 * c + flip(k, z % 2), y, x, z // 2)
    return links.go_unless(own, source, target, to)


def arrived(place, sem):
    pltpu.make_async_copy(place, place, sem).wait()


def spread_go(links, me, k, source, full, send, recv):
    z, y, x, c = me
    rows = source.shape[0]
    first = pl.multiple_of((4 * c + 2 * flip(k, z % 2) + y) * rows, rows)
    target = full.at[pl.ds(first, rows), :]
    for dy, dx in ((0, 1), (1, 0), (0, 0)):
        own = None if dy + dx else c == x
        to = device(z, flip(y, dy), flip(x, dx), x)
        links.go_unless(own, source, target, to, send.at[k, dy, dx], recv.at[k, dy, c])


def spread_relay(links, me, full, send, recv):
    z, y, x, c = me
    odd = flip(c, x)
    k, step = 1 - odd, 1 - odd
    rows = full.shape[0] // 8
    to = device(z, flip(y, odd), flip(x, 1 - odd), c)
    for r in range(2):
        first = pl.multiple_of((4 * r + 2 * flip(k, z % 2) + flip(y, step)) * rows, rows)
        here = full.at[pl.ds(first, rows), :]
        arrived(here, recv.at[k, step, r])
        made = remote(here, here, send.at[r, 1, 1], recv.at[k, 1, r], to)
        made.start()
        links.sent.append(made)


def spread_wait(me, full, recv):
    z, y, x, c = me
    odd = flip(c, x)
    here = full.at[pl.ds(0, full.shape[0] // 8), :]
    for k, step in ((1 - odd, odd), (odd, 0), (odd, 1)):
        for r in range(2):
            arrived(here, recv.at[k, step, r])


def join_go(links, me, k, grads, into, relay, send, recv, relay_recv):
    z, y, x, c = me
    odd = flip(c, x) == 1
    even = jnp.logical_not(odd)
    rows = into.shape[2]
    for r in range(2):

        def block(step):
            index = 4 * r + 2 * flip(k, z % 2) + flip(y, step)
            return grads.at[pl.ds(pl.multiple_of(index * rows, rows), rows), :]

        same, other = device(z, y, c, r), device(z, 1 - y, c, r)
        mine = jnp.logical_and(even, c == r)
        partner = jnp.logical_and(even, c != r)
        links.go_if(
            partner, mine, block(0), into.at[k, 0], send.at[k, 0, r], recv.at[k, 0], same
        )
        if k == 0:
            links.go_if(even, None, block(1), into.at[0, 1], send.at[0, 1, r], recv.at[0, 1], other)
            to = device(z, 1 - y, x, c)
        else:
            links.go_if(odd, None, block(0), into.at[1, 1], send.at[1, 1, r], recv.at[1, 1], same)
            to = device(z, y, c, c)
        links.go_if(odd, None, block(1), relay.at[r], send.at[k, 2, r], relay_recv.at[r], to)


def join_relay(links, me, grads, into, relay, send, recv, relay_recv):
    z, y, x, c = me
    odd = flip(c, x)
    k, step = 1 - odd, 1 - odd
    rows = into.shape[2]
    for r in range(2):
        arrived(relay.at[r], relay_recv.at[r])
        index = 4 * r + 2 * flip(k, z % 2) + flip(y, step)
        own = grads[pl.ds(pl.multiple_of(index * rows, rows), rows), :]
        total = relay[r].astype(jnp.float32) + own.astype(jnp.float32)
        relay[r] = total.astype(jnp.bfloat16)
        to = device(z, flip(y, step), c, r)
        made = remote(relay.at[r], into.at[k, 2], send.at[0, 3, r], recv.at[k, 2], to)
        made.start()
        links.sent.append(made)


def join_sum(k, into, recv):
    total = 0.0
    for j in range(3):
        arrived(into.at[k, j], recv.at[k, j])
        total = total + into[k, j].astype(jnp.float32)
    return total.astype(jnp.bfloat16)


def rms(rows):
    return lax.rsqrt(jnp.mean(rows * rows, axis=-1, keepdims=True) + epsilon)


def lane_sum(values):
    return jnp.sum(values, axis=-1, keepdims=True)


def head_of(z, y, x, c, heads):
    return 2 * c + z // 2, (z % 2) * (heads // 2) + 2 * x + y


def entry_kernel(
    lengths, tok_ref, cot_ref, small_ref, bucket_ref, wq_ref, wk_ref, wv_ref, wo_ref, wg_ref,
    rows_ref, normed, grads, pieces, weight, gain_one, gain_two, rev_ref, slots_o, slots_g,
    tok_in, cot_in, held, qkv, small, send, recv, plane_send, plane_recv, local,
):
    me = z, y, x, c = position()
    greet(*me)
    links = Links(send, recv)
    f, part, half = 2 * x + c, tok_in.shape[2], tok_in.shape[1]

    def gather_rows(n, ref, into):
        def source(xd, cd):
            return ref.at[xd, pl.ds(pl.multiple_of(cd * half, half), half)]

        own = pltpu.make_async_copy(source(x, c), into.at[f], local.at[n])
        own.start()
        got = []
        for d in (1, 2, 3):
            xd, cd = flip(x, d // 2), flip(c, d % 2)
            got.append(links.go(source(xd, cd), into.at[f], device(z, y, xd, cd)))
        return own, got

    tok_own, tok_got = gather_rows(0, tok_ref, tok_in)
    small[f, z, y] = small_ref[...]
    small_got = []
    for d in (1, 2, 3):
        here = small.at[f, z, y]
        small_got.append(links.go(here, here, device(flip_pair(z, d), y, x, c)))
    group_width = wq_ref.shape[1] // 2
    way = []
    for k in range(2):
        cut = pl.ds(pl.multiple_of(flip(k, z % 2) * group_width, group_width), group_width)
        for n, ref in enumerate((wq_ref, wk_ref, wv_ref)):
            target = held.at[k, :, n * group_width : (n + 1) * group_width]
            way.append(column_go(links, me, k, ref.at[:, cut], target))
    for made in small_got:
        made.wait_recv()
    here = small.at[f, :, y]
    links.go(here, here, device(z, 1 - y, x, c)).wait_recv()
    tables = []
    for d in (1, 2, 3):
        here = small.at[f]
        tables.append(links.go(here, here, device(z, y, flip(x, d // 2), flip(c, d % 2))))
    for i in range(4 * part // BLOCK):
        here = slice(i * BLOCK, (i + 1) * BLOCK)
        block = (i // 2) // 2, (i // 2) % 2
        gain_one[:, here] = small[f, block[0], block[1], i % 2 : i % 2 + 1, :]
        gain_two[:, here] = small[f, block[0], block[1], 2 + i % 2 : 3 + i % 2, :]
    tok_own.wait()
    for made in tok_got:
        made.wait_recv()
    cot_own, cot_got = gather_rows(1, cot_ref, cot_in)
    wide = [tok_in[i].astype(jnp.float32) for i in range(4)]
    mean = sum(lane_sum(w * w) for w in wide) / (4 * part)
    scale = lax.rsqrt(mean + epsilon)
    for i in range(4):
        here = slice(i * part, (i + 1) * part)
        rows_ref[:, here] = tok_in[i]
        normed[0, :, here] = (wide[i] * scale * gain_one[:, here]).astype(jnp.bfloat16)
    first = share_start(links, normed, me)
    for k in range(2):
        for made in way[3 * k : 3 * k + 3]:
            made.wait_recv()
        spread_go(links, me, k, held.at[k], weight, plane_send, plane_recv)
    share_step(links, normed, me, first, 1)
    share_step(links, normed, me, first, 2)
    later = []
    half_ffn = wg_ref.shape[1] // 2
    for k in range(2):
        side = flip(k, z % 2)
        cut = pl.ds(pl.multiple_of(side * group_width, group_width), group_width)
        later.append(column_go(links, me, k, wo_ref.at[:, cut], slots_o.at[k]))
        cut = pl.ds(pl.multiple_of(side * half_ffn, half_ffn), half_ffn)
        later.append(column_go(links, me, k, wg_ref.at[:, cut], slots_g.at[k]))
    spread_relay(links, me, weight, plane_send, plane_recv)
    for made in tables:
        made.wait_recv()
    group = qkv.shape[1]
    heads = 2 * group
    source, place = head_of(z, y, x, c, heads)
    lane = lax.broadcasted_iota(jnp.int32, (1, BLOCK), 1)
    line = jnp.zeros(bucket_ref.shape, jnp.float32)
    per_block = 4
    for n in range(8 * per_block):
        block = n // per_block
        row = small[source, block // 2, block % 2, 4:5, :]
        value = lane_sum(jnp.where(lane == (n % per_block) * heads + place, row, 0.0))
        line = jnp.where(bucket_ref[...] == n, value, line)
    rev_ref[...] = line
    spread_wait(me, weight, plane_recv)
    rows = normed.shape[1]
    sent = []

    def project(d):
        out = jnp.dot(pair_of(normed, d), weight[...], preferred_element_type=jnp.float32)
        out = out.astype(jnp.bfloat16).T
        for side, slot in enumerate((d, 4 + d)):
            here = lanes(slot * rows, rows)
            cut = out[:, side * rows : (side + 1) * rows]
            qkv[:, :, :, here] = cut.reshape(3, group, DH, rows)
            pieces[0, :, :, here] = qkv[:, 2 * x + y, :, here]
            for e in (1, 2, 3):
                xd, yd = flip(x, e // 2), flip(y, e % 2)
                source = qkv.at[:, 2 * xd + yd, :, here]
                sent.append(links.go(source, pieces.at[e, :, :, here], device(z, yd, xd, c)))

    cot_own.wait()
    for made in cot_got:
        made.wait_recv()
    slot = (4 * z + 2 * y + c) * half + lax.broadcasted_iota(jnp.int32, (half, part), 0)
    valid = slot < jnp.where(x == 0, lengths[0], lengths[1])
    for i in range(4):
        grads[:, i * part : (i + 1) * part] = jnp.where(valid, cot_in[i], jnp.zeros_like(cot_in[i]))
    order = sum_order(z)
    first[1][0].wait_recv()
    project(0)
    for step in (1, 2, 3):
        if step == 3:
            share_step(links, normed, me, first, 3)
        for made in first[1][1 + CHUNKS * (step - 1) : 1 + CHUNKS * step]:
            made.wait_recv()
        project(order[step - 1])
    for made in sent + later:
        made.wait_recv()
    links.finish()


def low_array(*shape):
    return jax.ShapeDtypeStruct(shape, jnp.bfloat16)


def wide_array(*shape):
    return jax.ShapeDtypeStruct(shape, jnp.float32)


def low_space(*shape):
    return pltpu.VMEM(shape, jnp.bfloat16)


def entry(lengths, tokens_in, cotangent, small, rev_buckets, weights):
    _, slot_count, part = tokens_in.shape
    rows, width = slot_count // 2, 4 * part
    depth, cols = weights[0].shape
    group = cols // (2 * DH)
    wide = 3 * cols // 2
    return pl.pallas_call(
        entry_kernel,
        name="entry",
        out_shape=[
            low_array(rows, width),
            low_array(8, rows, width),
            low_array(rows, width),
            low_array(4, 3, DH, 8 * rows),
            low_array(8 * depth, wide),
            wide_array(1, width),
            wide_array(1, width),
            wide_array(*rev_buckets.shape),
            low_array(2, depth, cols // 2),
            low_array(2, depth, weights[4].shape[1] // 2),
        ],
        in_specs=[pl.BlockSpec(memory_space=pltpu.SMEM)]
        + [IN_PLACE] * 2
        + [IN_VMEM] * 2
        + [IN_PLACE] * 5,
        out_specs=[IN_VMEM] * 10,
        scratch_shapes=[
            low_space(4, rows, part),
            low_space(4, rows, part),
            low_space(2, depth, wide),
            low_space(3, group, DH, 8 * rows),
            pltpu.VMEM((4, 4, 2, 8, BLOCK), jnp.float32),
            COPIES((64,)),
            COPIES((64,)),
            COPIES((2, 2, 2)),
            COPIES((2, 2, 2)),
            COPIES((2,)),
        ],
        compiler_params=pltpu.CompilerParams(
            collective_id=1, has_side_effects=True, vmem_limit_bytes=48 << 20
        ),
    )(lengths, tokens_in, cotangent, small, rev_buckets, *weights)


def gelu_pair(t):
    inner = jnp.tanh(root_two_over_pi * (t + 0.044715 * (t * t * t)))
    half = 0.5 * (1.0 + inner)
    slope = half + 0.5 * t * (1.0 - inner * inner) * root_two_over_pi * (1.0 + 0.134145 * (t * t))
    return t * half, slope


def pair_of(ref, slot):
    return jnp.concatenate([ref[slot], ref[4 + slot]], axis=0)


def pair_go(links, me, core, i, terms, core_out, core_in):
    z, y, x, c = me
    size = terms.shape[0] // 2
    core_out[i] = terms[size:].astype(jnp.bfloat16)
    core.append(links.go(core_out.at[i], core_in.at[i], device(z, y, x, 1 - c)))
    return terms[:size]


def sum_step(links, me, core, ring, i, mine, core_in, ring_out, ring_in):
    z, y, x, c = me
    following, _ = ring_of(z)
    rows = mine.shape[0] // CHUNKS
    core.wait_recv()
    sent, last = [], []
    for h in range(CHUNKS):
        cut = slice(h * rows, (h + 1) * rows)
        here = pl.ds(h * rows, rows)
        value = mine[cut] + core_in[i, here, :].astype(jnp.float32)
        if i:
            ring[-1][h].wait_recv()
            value = value + ring_in[i - 1, here, :].astype(jnp.float32)
        if i < 3:
            ring_out[i, here, :] = value.astype(jnp.bfloat16)
            target = ring_in.at[i, here]
            sent.append(links.go(ring_out.at[i, here], target, device(following, y, x, c)))
        else:
            last.append(value)
    ring.append(sent)
    return last


def reduce_pair(links, me, state, i, terms, core_out, core_in, ring_out, ring_in):
    mine = pair_go(links, me, state[0], i, terms, core_out, core_in)
    return sum_step(links, me, state[0][i], state[1], i, mine, core_in, ring_out, ring_in)


def core_kernel(
    ctx_ref, rows_ref, gain_ref, own_ref, slots_o, slots_g, slot_ud0, slot_ud1,
    layer_ref, context, low, wide_ref, part_ref, pieces, in_gu, in_d,
    residual_ref, down, hidden, out_weight, gate_up, normed, grads, pre, ctx_all, heads_out, grad_gu, grad_d,
    mine, core_out, core_in, ring_out, ring_in, ring_out2, ring_in2,
    relay_gu, relay_d, send, recv, plane_send, plane_recv, join_send, join_recv, relay_recv,
):
    me = z, y, x, c = position()
    greet(*me)
    links = Links(send, recv)
    own = 2 * x + y
    heads = []
    for d in (1, 2, 3):
        xd, yd = flip(x, d // 2), flip(y, d % 2)
        heads.append(links.go(ctx_ref.at[d], ctx_all.at[own], device(z, yd, xd, c)))
    grads[0] = own_ref[...]
    second = share_start(links, grads, me)

    ffn = down.shape[1]
    fulls = out_weight, gate_up.at[:, :ffn], gate_up.at[:, ffn:], down

    def weight_go(n):
        slots = (
            (slots_o.at[0], slots_o.at[1]),
            (slots_g.at[0], slots_g.at[1]),
            (slot_ud0.at[:, :ffn], slot_ud1.at[:, :ffn]),
            (slot_ud0.at[:, ffn:], slot_ud1.at[:, ffn:]),
        )[n]
        for k in range(2):
            spread_go(links, me, k, slots[k], fulls[n], plane_send.at[n], plane_recv.at[n])

    def weight_relay(n):
        spread_relay(links, me, fulls[n], plane_send.at[n], plane_recv.at[n])

    def weight_wait(n):
        spread_wait(me, fulls[n], plane_recv.at[n])

    weight_go(0)
    ctx_all[own] = ctx_ref[0]
    for made in heads:
        made.wait_recv()
    group, size, tokens = ctx_all.shape
    rows, width = residual_ref.shape
    depth = gate_up.shape[0] // 8
    half_tokens = tokens // 2
    context[...] = ctx_all[...].reshape(group * size, tokens).T
    weight_relay(0)
    weight_go(1)
    weight_go(2)
    weight_wait(0)
    order = sum_order(z)

    def first_row(block):
        return pl.multiple_of(block * rows, rows)

    def pair_rows(ref, d):
        return jnp.concatenate(
            [ref[pl.ds(first_row(d), rows), :], ref[pl.ds(first_row(4 + d), rows), :]], axis=0
        )

    state = [], []
    for i in range(4):
        terms = right_transposed(pair_rows(context, order[i]), out_weight[...])
        last = reduce_pair(links, me, state, i, terms, core_out, core_in, ring_out, ring_in)
        if i < 3:
            share_step(links, grads, me, second, i + 1)
        if i == 1:
            weight_go(3)
        if i == 2:
            weight_relay(1)
            weight_relay(2)
    residual = rows_ref[...].astype(jnp.float32) + jnp.concatenate(last, axis=0)
    residual_ref[...] = residual
    gain = gain_ref[...]
    normed[0] = (residual * rms(residual) * gain).astype(jnp.bfloat16)
    shared = share_start(links, normed, me)
    weight_relay(3)
    share_end(second)
    for made in state[0] + sum(state[1], []):
        links.done(made)
    ring = []

    def take_in(i):
        share_step(links, normed, me, shared, i + 1)

    def feed(i):
        d = order[i]
        for made in shared[1][:1] if i == 3 else shared[1][1 + CHUNKS * i : 1 + CHUNKS * (i + 1)]:
            made.wait_recv()
        gate_up_pre = jnp.dot(
            pair_of(normed, d), gate_up[...], preferred_element_type=jnp.float32
        )
        activated, slope = gelu_pair(gate_up_pre[:, :ffn])
        up_pre = gate_up_pre[:, ffn:]
        made = (activated * up_pre).astype(jnp.bfloat16)
        hidden[pl.ds(first_row(d), rows), :] = made[:rows]
        hidden[pl.ds(first_row(4 + d), rows), :] = made[rows:]
        if i == 0:
            weight_wait(3)
        grad_hidden = jnp.dot(pair_of(grads, d), down[...], preferred_element_type=jnp.float32)
        grad_pre = jnp.concatenate(
            [
                (grad_hidden * up_pre * slope).astype(jnp.bfloat16),
                (grad_hidden * activated).astype(jnp.bfloat16),
            ],
            axis=1,
        )
        pre[pl.ds(first_row(d), rows), :] = grad_pre[:rows]
        pre[pl.ds(first_row(4 + d), rows), :] = grad_pre[rows:]
        terms = right_transposed(grad_pre, gate_up[...])
        kept = []
        mine[i] = pair_go(links, me, kept, i, terms, core_out, core_in)
        return kept[0]

    def pass_on(i, core):
        return sum_step(links, me, core, ring, i, mine[i], core_in, ring_out2, ring_in2)

    joins = (grad_gu, in_gu, relay_gu), (grad_d, in_d, relay_d)

    def weight_grads(k):
        for n in range(4):
            block = 4 * (n // 2) + 2 * flip(k, z % 2) + n % 2
            here = pl.ds(pl.multiple_of(block * depth, depth), depth)
            left = normed[:, :, here].reshape(tokens, depth)
            grad_gu[here, :] = left_transposed(left, pre[...]).astype(jnp.bfloat16)
            left = grads[:, :, here].reshape(tokens, depth)
            grad_d[here, :] = left_transposed(left, hidden[...]).astype(jnp.bfloat16)
        for n, (grad, into, relay) in enumerate(joins):
            sems = join_send.at[n], join_recv.at[n], relay_recv.at[n]
            join_go(links, me, k, grad, into, relay, *sems)

    take_in(0)
    weight_wait(1)
    weight_wait(2)
    first = feed(0)
    pass_on(0, first)
    take_in(1)
    following = feed(1)
    take_in(2)
    final = feed(3)
    pass_on(1, following)
    third = feed(2)
    weight_grads(0)
    pass_on(2, third)
    weight_grads(1)
    last = pass_on(3, final)
    normed_grad = jnp.concatenate(last, axis=0)
    residual = residual_ref[...]
    scale = rms(residual)
    unit = residual * scale
    part_ref[...] = jnp.sum(normed_grad * unit, axis=0, keepdims=True)
    out = own_ref[...].astype(jnp.float32) + norm_back(normed_grad, unit, scale, gain)
    wide_ref[...] = out
    low[0] = out.astype(jnp.bfloat16)
    shared = share_start(links, low, me)
    sent = []

    def context_back(d):
        made = jnp.dot(pair_of(low, d), out_weight[...], preferred_element_type=jnp.float32)
        made = made.astype(jnp.bfloat16).T
        for half, slot in enumerate((d, 4 + d)):
            here = lanes(slot * rows, rows)
            cut = made[:, half * rows : (half + 1) * rows]
            heads_out[:, :, here] = cut.reshape(group, size, rows)
            pieces[0, :, here] = heads_out[own, :, here]
            for e in (1, 2, 3):
                xd, yd = flip(x, e // 2), flip(y, e % 2)
                source = heads_out.at[2 * xd + yd, :, here]
                sent.append(links.go(source, pieces.at[e, :, here], device(z, yd, xd, c)))

    shared[1][0].wait_recv()
    context_back(0)
    for made in (first, following, third, final):
        links.done(made)
    layer_core, layer_ring = [], []
    for i in range(4):
        terms = right_transposed(pair_rows(hidden, order[i]), down[...])
        mine[i] = pair_go(links, me, layer_core, i, terms, core_out, core_in)

    def layer_step(i):
        made = layer_core[i]
        return sum_step(links, me, made, layer_ring, i, mine[i], core_in, ring_out, ring_in)

    for step in (1, 2, 3):
        share_step(links, low, me, shared, step)
        if step == 2:
            layer_step(0)
            for n, (grad, into, relay) in enumerate(joins):
                sems = join_send.at[n], join_recv.at[n], relay_recv.at[n]
                join_relay(links, me, grad, into, relay, *sems)
        for made in shared[1][1 + CHUNKS * (step - 1) : 1 + CHUNKS * step]:
            made.wait_recv()
        context_back(order[step - 1])
    layer_step(1)
    layer_step(2)
    last = layer_step(3)
    layer = (residual_ref[...] + jnp.concatenate(last, axis=0)).astype(jnp.bfloat16)
    part = width // 4
    for i in range(4):
        layer_ref[i] = layer[:, i * part : (i + 1) * part]
    for made in sent:
        made.wait_recv()
    for n, (_, into, _) in enumerate(joins):
        for k in range(2):
            for j in range(3):
                arrived(into.at[k, j], join_recv.at[n, k, j])
    links.finish()


def reduce_space(rows, width):
    return [
        low_space(4, rows, width),
        low_space(4, rows, width),
        low_space(3, rows, width),
        low_space(3, rows, width),
    ]


def core(ctx_pieces, token_rows, gain, grad_own, slots_o, slots_g, slots_ud):
    _, size, tokens = ctx_pieces.shape
    rows, width = token_rows.shape
    _, depth, ffn = slots_g.shape
    group = slots_o.shape[2] // DH
    return pl.pallas_call(
        core_kernel,
        name="core",
        out_shape=[
            low_array(4, rows, width // 4),
            low_array(tokens, 4 * size),
            low_array(8, rows, width),
            wide_array(rows, width),
            wide_array(1, width),
            low_array(4, size, tokens),
            low_array(2, 3, depth, 2 * ffn),
            low_array(2, 3, depth, ffn),
        ],
        in_specs=[IN_VMEM] * 4 + [IN_PLACE] * 4,
        out_specs=[IN_VMEM] * 6 + [IN_PLACE] * 2,
        scratch_shapes=[
            pltpu.VMEM((rows, width), jnp.float32),
            low_space(8 * depth, ffn),
            low_space(tokens, ffn),
            low_space(8 * depth, group * size),
            low_space(8 * depth, 2 * ffn),
            low_space(8, rows, width),
            low_space(8, rows, width),
            low_space(tokens, 2 * ffn),
            low_space(4, size, tokens),
            low_space(group, size, tokens),
            low_space(8 * depth, 2 * ffn),
            low_space(8 * depth, ffn),
            pltpu.VMEM((4, rows, width), jnp.float32),
            *reduce_space(rows, width),
            low_space(3, rows, width),
            low_space(3, rows, width),
            low_space(2, depth, 2 * ffn),
            low_space(2, depth, ffn),
            COPIES((112,)),
            COPIES((112,)),
            COPIES((4, 2, 2, 2)),
            COPIES((4, 2, 2, 2)),
            COPIES((2, 2, 4, 2)),
            COPIES((2, 2, 3)),
            COPIES((2, 2)),
        ],
        compiler_params=pltpu.CompilerParams(
            collective_id=2, has_side_effects=True, vmem_limit_bytes=63 << 20
        ),
    )(ctx_pieces, token_rows, gain, grad_own, slots_o, slots_g, *slots_ud)


def exit_kernel(
    piece_ref, normed_ref, weight_ref, token_ref, wide_ref, gain_ref, low_ref, context_ref,
    layer_own, gain_two_ref, line_ref, bucket_ref, ffn_ref,
    query_out, key_out, value_out, output_out, home_ref, layer_ref, small_ref, ffn_out,
    heads_in, rows_low, weight_grad, weight_in, weight_relay, held, token_out,
    packed, in_f, in_y, in_z,
    core_out, core_in, ring_out, ring_in,
    send, recv, plane_send, plane_recv, relay_recv,
):
    me = z, y, x, c = position()
    greet(*me)
    links = Links(send, recv)
    own, f = 2 * x + y, 2 * x + c
    group, three, size, tokens = heads_in.shape
    rows = tokens // 8
    depth, cols = weight_grad.shape[1] // 8, weight_grad.shape[2]
    width = normed_ref.shape[2]
    part = width // 4
    heads = []
    for d in (1, 2, 3):
        xd, yd = flip(x, d // 2), flip(y, d % 2)
        heads.append(links.go(piece_ref.at[d], heads_in.at[own], device(z, yd, xd, c)))
    heads_in[own] = piece_ref[0]

    order = sum_order(z)

    def pair_rows(ref, d):
        return jnp.concatenate(
            [ref[lanes(block * rows, rows), :] for block in (d, 4 + d)], axis=0
        )

    def to_home(source, into):
        got = []
        for d in (1, 2, 3):
            xd, cd = flip(x, d // 2), flip(c, d % 2)
            got.append(links.go(source.at[2 * xd + cd], into.at[f], device(z, y, xd, cd)))
        into[f] = source[f]
        return got

    state = [], []

    def join(n):
        sems = plane_send.at[n], plane_recv.at[n], relay_recv.at[n]
        return weight_grad.at[n], weight_in.at[n], weight_relay.at[n], *sems

    def step(i):
        terms = right_transposed(pair_rows(rows_low, order[i]), weight_ref[...])
        return reduce_pair(links, me, state, i, terms, core_out, core_in, ring_out, ring_in)

    def weight_grads(n, ref, right):
        for k in range(2):
            for piece in range(4):
                block = 4 * (piece // 2) + 2 * flip(k, z % 2) + piece % 2
                here = pl.ds(pl.multiple_of(block * depth, depth), depth)
                left = ref[:, :, here].reshape(tokens, depth)
                weight_grad[n, here, :] = left_transposed(left, right).astype(jnp.bfloat16)
            join_go(links, me, k, *join(n))

    way = [column_go(links, me, 1, ffn_ref, ffn_out)]
    results = query_out, key_out, value_out, output_out
    cut = pl.ds(pl.multiple_of((z % 2) * cols, cols), cols)

    def send_sums(n):
        for k in range(2):
            held[n, k] = join_sum(k, weight_in.at[n], plane_recv.at[n])
            way.append(column_go(links, me, k, held.at[n, k], results[n].at[:, cut]))

    weight_grads(3, low_ref, context_ref[...])

    packed[...] = jnp.zeros_like(packed)
    per_block = 4
    all_heads = BLOCK // per_block
    source, place = head_of(z, y, x, c, all_heads // 4)
    lane = lax.broadcasted_iota(jnp.int32, (1, BLOCK), 1)
    for block in range(8):
        row = jnp.zeros((1, BLOCK), jnp.float32)
        for n in range(per_block):
            hot = bucket_ref[...] == block * per_block + n
            value = lane_sum(jnp.where(hot, line_ref[...], 0.0))
            row = jnp.where(lane == n * all_heads + source * (all_heads // 4) + place, value, row)
        packed[block // 2, block % 2, 4:5, :] = row
    for made in heads:
        made.wait_recv()
    for n in range(three):
        here = slice(n * group * size, (n + 1) * group * size)
        rows_low[:, here] = heads_in[:, n].reshape(group * size, tokens).T
    step(0)
    for n in range(three):
        weight_grads(n, normed_ref, rows_low[:, n * cols : (n + 1) * cols])
    join_relay(links, me, *join(3))
    step(1)
    send_sums(3)
    join_relay(links, me, *join(0))
    join_relay(links, me, *join(1))
    step(2)
    join_relay(links, me, *join(2))
    home = to_home(layer_own, layer_ref)
    for n in range(three):
        send_sums(n)
    last = step(3)
    normed_grad = jnp.concatenate(last, axis=0)
    tokens_wide = token_ref[...].astype(jnp.float32)
    scale = rms(tokens_wide)
    unit = tokens_wide * scale
    token_grad = wide_ref[...] + norm_back(normed_grad, unit, scale, gain_ref[...])
    for i in range(4):
        token_out[i] = token_grad[:, i * part : (i + 1) * part].astype(jnp.bfloat16)
    home += to_home(token_out, home_ref)
    gain_part = jnp.sum(normed_grad * unit, axis=0, keepdims=True)
    for i in range(width // BLOCK):
        here = slice(i * BLOCK, (i + 1) * BLOCK)
        block = (i // 2) // 2, (i // 2) % 2
        packed[block[0], block[1], i % 2 : i % 2 + 1, :] = gain_part[:, here]
        packed[block[0], block[1], 2 + i % 2 : 3 + i % 2, :] = gain_two_ref[:, here]
    got = []
    for d in (1, 2, 3):
        to = device(z, y, flip(x, d // 2), flip(c, d % 2))
        got.append(links.go(packed, in_f.at[d - 1], to))
    for made in got:
        made.wait_recv()
    for made in got:
        links.done(made)
    packed[...] = packed[...] + in_f[0] + in_f[1] + in_f[2]
    made = links.go(packed.at[:, 1 - y], in_y, device(z, 1 - y, x, c))
    made.wait_recv()
    in_y[...] = in_y[...] + packed[:, y]
    got = []
    for d in (1, 2, 3):
        other = flip_pair(z, d)
        got.append(links.go(in_y.at[other], in_z.at[d - 1], device(other, y, x, c)))
    for made in got:
        made.wait_recv()
    small_ref[...] = in_y[z] + in_z[0] + in_z[1] + in_z[2]
    for made in way + home:
        made.wait_recv()
    links.finish()


def leave(pieces, normed, weight, token_rows, wide_grad, gain, low, context, layer,
          gain_two_part, line_grad, rev_buckets, ffn_slot):
    _, _, size, tokens = pieces.shape
    rows, width = token_rows.shape
    depth, wide = weight.shape[0] // 8, weight.shape[1]
    out_wide = context.shape[1]
    cols = 2 * wide // 3
    tile = (8, BLOCK)
    return pl.pallas_call(
        exit_kernel,
        name="leave",
        out_shape=[
            *(low_array(depth, cols) for _ in range(4)),
            low_array(4, rows, width // 4),
            low_array(4, rows, width // 4),
            wide_array(*tile),
            low_array(*ffn_slot.shape),
        ],
        in_specs=[IN_VMEM] * 12 + [IN_PLACE],
        out_specs=[IN_VMEM] * 7 + [IN_PLACE],
        scratch_shapes=[
            low_space(4, 3, size, tokens),
            low_space(tokens, wide),
            low_space(4, 8 * depth, out_wide),
            low_space(4, 2, 3, depth, out_wide),
            low_space(4, 2, depth, out_wide),
            low_space(4, 2, depth, out_wide),
            low_space(4, rows, width // 4),
            pltpu.VMEM((4, 2, *tile), jnp.float32),
            pltpu.VMEM((3, 4, 2, *tile), jnp.float32),
            pltpu.VMEM((4, *tile), jnp.float32),
            pltpu.VMEM((3, *tile), jnp.float32),
            *reduce_space(rows, width),
            COPIES((64,)),
            COPIES((64,)),
            COPIES((4, 2, 4, 2)),
            COPIES((4, 2, 3)),
            COPIES((4, 2)),
        ],
        compiler_params=pltpu.CompilerParams(
            collective_id=4, has_side_effects=True, vmem_limit_bytes=60 << 20
        ),
    )(pieces, normed, weight, token_rows, wide_grad, gain, low, context, layer,
      gain_two_part, line_grad, rev_buckets, ffn_slot)


def widen_kernel(*refs):
    sources, outs, spaces, sem = refs[:7], refs[7:15], refs[15:22], refs[22]
    copies = [
        pltpu.make_async_copy(source, space, sem.at[n])
        for n, (source, space) in enumerate(zip(sources, spaces))
    ]
    for copy in copies:
        copy.start()
    for copy in copies:
        copy.wait()
    attn, slots, home = spaces[:4], spaces[4:6], spaces[6]
    z_low = (lax.axis_index("seq") // 2) % 2
    for ref, out in zip(attn, outs[:4]):
        out[...] = ref[...].astype(jnp.float32)
    size = slots[0].shape[1] // 3
    for k in range(2):
        cut = lanes((k + z_low - 2 * k * z_low) * size, size)
        for n, out in enumerate(outs[4:7]):
            out[:, cut] = slots[k][:, n * size : (n + 1) * size].astype(jnp.float32)
    outs[7][...] = home[...].astype(jnp.float32)


def widen(attn, slots, home):
    depth, cols = attn[0].shape
    size = 2 * slots[0].shape[1] // 3
    return pl.pallas_call(
        widen_kernel,
        name="widen",
        out_shape=[wide_array(depth, cols)] * 4
        + [wide_array(depth, size)] * 3
        + [wide_array(*home.shape)],
        in_specs=[IN_PLACE] * 7,
        out_specs=[IN_VMEM] * 8,
        scratch_shapes=[low_space(*a.shape) for a in (*attn, *slots, home)] + [COPIES((7,))],
        compiler_params=pltpu.CompilerParams(vmem_limit_bytes=60 << 20),
    )(*attn, *slots, home)


def fast_shards(
    tokens_in,
    cotangent,
    gain_attn,
    query_weight,
    key_weight,
    value_weight,
    output_weight,
    bias_table,
    gain_ffn,
    gate_weight,
    up_weight,
    down_weight,
    lengths,
    buckets,
):
    seq_index, fsdp_index = lax.axis_index("seq"), lax.axis_index("fsdp")
    z, y, x, c = seq_index // 2, seq_index % 2, fsdp_index // 2, fsdp_index % 2
    z_low, z_high = z % 2, z // 2
    batch_count, slot_count, part_width = tokens_in.shape
    width = part_width * 4
    row_count = query_weight.shape[0]
    heads = query_weight.shape[1] // DH
    group_heads = heads // 2
    group_width = group_heads * DH
    hidden_width = gate_weight.shape[1] // 2
    def halves(weights):
        slots = []
        for k in range(2):
            half = k ^ z_low
            slots.append(
                jnp.concatenate(
                    [
                        lax.dynamic_slice_in_dim(w, half * (w.shape[1] // 2), w.shape[1] // 2, 1)
                        for w in weights
                    ],
                    axis=1,
                )
            )
        return slots

    small = jnp.concatenate(
        [gain_attn, gain_ffn, bias_table.reshape(-1), jnp.zeros((2 * row_count - bias_table.size,), jnp.bfloat16)]
    )
    small = small.astype(jnp.float32).reshape(8, BLOCK)
    rev_buckets = jnp.concatenate([buckets[::-1], jnp.full((1,), -1, jnp.int32)])[None, :]
    (
        token_low,
        normed_one,
        grad_own,
        pieces,
        qkv_weight,
        gain_one,
        gain_two,
        rev_line,
        slots_o,
        slots_g,
    ) = entry(
        lengths,
        tokens_in,
        cotangent,
        small,
        rev_buckets,
        (query_weight, key_weight, value_weight, output_weight, gate_weight),
    )
    pieces, *later = lax.optimization_barrier((pieces, *halves([up_weight, down_weight])))
    slots_ud = [move(later[k], spread_slot(k)) for k in range(2)]
    context_pieces, context_wide, lse, qkv_all = attend(lengths, pieces, rev_line)
    (
        layer,
        context,
        residual_low,
        residual_grad,
        gain_two_part,
        grad_pieces,
        terms_gate_up,
        terms_down,
    ) = core(context_pieces, token_low, gain_two, grad_own, slots_o, slots_g, slots_ud)

    def slot_sum(k):
        sums = [
            jnp.sum(t[k].astype(jnp.float32), axis=0).astype(jnp.bfloat16)
            for t in (terms_gate_up, terms_down)
        ]
        return jnp.concatenate(sums, axis=1)

    ffn_first = move(slot_sum(0), spread_slot(0))
    ffn_second = slot_sum(1)
    qkv_grad_pieces, line_grad = attend_back(
        lengths, grad_pieces, rev_line, context_wide, lse, qkv_all
    )
    qkv_grad_pieces, ffn_first = lax.optimization_barrier((qkv_grad_pieces, ffn_first))
    *attn_sums, home, layer, small, ffn_second = leave(
        qkv_grad_pieces,
        normed_one,
        qkv_weight,
        token_low,
        residual_grad,
        gain_one,
        residual_low,
        context,
        layer,
        gain_two_part,
        line_grad,
        rev_buckets,
        ffn_second,
    )
    query_sum, key_sum, value_sum, output_sum, gate_sum, up_sum, down_sum, home = widen(
        attn_sums, (ffn_first, ffn_second), home
    )
    token_share = home.reshape(batch_count, slot_count, part_width)
    layer_out = layer.reshape(batch_count, slot_count, part_width)
    table_sum = lax.dynamic_slice_in_dim(
        small[4].reshape(-1, 4 * heads), fsdp_index * heads, heads, 1
    )
    return (
        layer_out,
        token_share,
        small[:2].reshape(-1),
        query_sum,
        key_sum,
        value_sum,
        output_sum,
        table_sum,
        small[2:4].reshape(-1),
        gate_sum,
        up_sum,
        down_sum,
    )


def solution(mesh):
    placed = (
        P(None, "seq", "fsdp"),
        P(None, "seq", "fsdp"),
        P("seq"),
        P("seq", "fsdp"),
        P("seq", "fsdp"),
        P("seq", "fsdp"),
        P("seq", "fsdp"),
        P("seq", "fsdp"),
        P("seq"),
        P("seq", "fsdp"),
        P("seq", "fsdp"),
        P("seq", "fsdp"),
        P(),
        P(),
    )
    return jax.shard_map(
        fast_shards if (mesh.shape["seq"], mesh.shape["fsdp"]) == (8, 4) else shards,
        mesh=mesh,
        in_specs=placed,
        out_specs=(
            P(None, "seq", "fsdp"),
            P(None, "seq", "fsdp"),
            P("seq"),
            P("seq", "fsdp"),
            P("seq", "fsdp"),
            P("seq", "fsdp"),
            P("seq", "fsdp"),
            P("seq", "fsdp"),
            P("seq"),
            P("seq", "fsdp"),
            P("seq", "fsdp"),
            P("seq", "fsdp"),
        ),
        check_vma=False,
    )
```

```python
from functools import partial

import jax
import jax.numpy as jnp
from jax import lax
from jax.experimental import pallas as pl
from jax.experimental.pallas import tpu as pltpu
from jax.sharding import PartitionSpec as P

DH = 64


epsilon = 1e-06
highest = lax.Precision.HIGHEST
masked_score = -1e30
root_two_over_pi = 0.7978845608028654


def plain_product(left, right):
    return jnp.dot(left, right, preferred_element_type=jnp.float32)


def right_transposed(left, right):
    return lax.dot_general(
        left, right, (((1,), (1,)), ((), ())), preferred_element_type=jnp.float32
    )


def left_transposed(left, right):
    return lax.dot_general(
        left, right, (((0,), (0,)), ((), ())), preferred_element_type=jnp.float32
    )


def normalize(rows, gain):
    row_scale = lax.rsqrt(jnp.mean(rows * rows, axis=-1, keepdims=True) + epsilon)
    unit_rows = rows * row_scale
    return (unit_rows, row_scale, (unit_rows * gain.astype(jnp.float32)).astype(jnp.bfloat16))


def norm_back(grad_normed, unit_rows, row_scale, gain):
    weighted = grad_normed * gain.astype(jnp.float32)
    return row_scale * (
        weighted - unit_rows * jnp.mean(weighted * unit_rows, axis=-1, keepdims=True)
    )


def to_heads(rows, batch_count, head_size):
    slot_count = rows.shape[0] // batch_count
    number_of_heads = rows.shape[1] // head_size
    return rows.reshape(batch_count, slot_count, number_of_heads, head_size).transpose(2, 0, 1, 3)


def from_heads(blocks):
    number_of_heads, batch_count, slot_count, head_size = blocks.shape
    return blocks.transpose(1, 2, 0, 3).reshape(
        batch_count * slot_count, number_of_heads * head_size
    )


def bias_rows(bias_line, first_query, slot_count, length):
    span = slot_count + length - 1
    segment = lax.dynamic_slice_in_dim(bias_line, length - first_query - slot_count, span)
    flat = jnp.tile(segment, slot_count)
    skewed = flat[slot_count - 1 : slot_count - 1 + slot_count * (span - 1)].reshape(
        slot_count, span - 1
    )
    return skewed[:, :length]


def bias_rows_back(block_grad, first_query, slot_count, length, line_length):
    span = slot_count + length - 1
    widened = jnp.pad(block_grad, ((0, 0), (0, span - 1 - length)))
    flat = jnp.pad(widened.reshape(-1), (slot_count - 1, 1))
    segment_grad = jnp.sum(flat.reshape(slot_count, span), axis=0)
    return lax.dynamic_update_slice_in_dim(
        jnp.zeros((line_length,), jnp.float32), segment_grad, length - first_query - slot_count, 0
    )


def full_features(block):
    gathered = lax.all_gather(block, "fsdp", axis=2, tiled=True)
    return gathered.reshape(gathered.shape[0] * gathered.shape[1], gathered.shape[2])


def feature_total(partial_rows):
    return lax.psum(partial_rows, "fsdp")


def shards(
    tokens_in,
    cotangent,
    gain_attn,
    query_weight,
    key_weight,
    value_weight,
    output_weight,
    bias_table,
    gain_ffn,
    gate_weight,
    up_weight,
    down_weight,
    lengths,
    buckets,
):
    batch_count, slot_count, part_width = tokens_in.shape
    head_size = DH
    seq_index = lax.axis_index("seq")
    fsdp_index = lax.axis_index("fsdp")
    length = slot_count * lax.axis_size("seq")
    line_length = buckets.shape[0]
    first_query = seq_index * slot_count
    positions = jnp.arange(length, dtype=jnp.int32)
    query_positions = first_query + jnp.arange(slot_count, dtype=jnp.int32)
    key_valid = positions[None, :] < lengths[:, None]
    own_valid = query_positions[None, :] < lengths[:, None]
    gain_one, query_full, key_full, value_full, output_full, table_full = (
        lax.all_gather(gain_attn, "seq", axis=0, tiled=True),
        lax.all_gather(query_weight, "seq", axis=0, tiled=True),
        lax.all_gather(key_weight, "seq", axis=0, tiled=True),
        lax.all_gather(value_weight, "seq", axis=0, tiled=True),
        lax.all_gather(output_weight, "seq", axis=0, tiled=True),
        lax.all_gather(bias_table, "seq", axis=0, tiled=True),
    )
    token_rows = full_features(tokens_in).astype(jnp.float32)
    unit_one, scale_one, normed_one = normalize(token_rows, gain_one)
    query_heads = to_heads(
        plain_product(normed_one, query_full).astype(jnp.bfloat16), batch_count, head_size
    )
    key_heads = to_heads(
        plain_product(normed_one, key_full).astype(jnp.bfloat16), batch_count, head_size
    )
    value_heads = to_heads(
        plain_product(normed_one, value_full).astype(jnp.bfloat16), batch_count, head_size
    )
    number_of_heads = query_heads.shape[0]
    flat_shape = (number_of_heads, batch_count, slot_count * head_size)
    gathered_keys, gathered_values = (
        lax.all_gather(key_heads.reshape(flat_shape), "seq", axis=2, tiled=True),
        lax.all_gather(value_heads.reshape(flat_shape), "seq", axis=2, tiled=True),
    )
    all_keys = gathered_keys.reshape(number_of_heads, batch_count, length, head_size)
    all_values = gathered_values.reshape(number_of_heads, batch_count, length, head_size)
    bucket_hot = (
        buckets[:, None] == jnp.arange(table_full.shape[0], dtype=jnp.int32)[None, :]
    ).astype(jnp.float32)
    offset_bias = lax.dot_general(
        table_full.astype(jnp.float32), bucket_hot, (((0,), (1,)), ((), ())), precision=highest
    )

    def masked_scores(query_tile_rows, key_tile_rows, bias_block):
        raw = (
            jnp.einsum(
                "jht,jxt->jhx", query_tile_rows, key_tile_rows, preferred_element_type=jnp.float32
            )
            + bias_block[None]
        )
        return jnp.where(key_valid[:, None, :], raw, masked_score)

    def attend(inputs):
        query_tile_rows, key_tile_rows, value_tile_rows, bias_line = inputs
        scores = masked_scores(
            query_tile_rows, key_tile_rows, bias_rows(bias_line, first_query, slot_count, length)
        )
        row_peak = jnp.max(scores, axis=-1, keepdims=True)
        raised = jnp.exp(scores - row_peak)
        denominator = jnp.sum(raised, axis=-1, keepdims=True)
        weights_reduced_precision = (raised / denominator).astype(jnp.bfloat16)
        context = jnp.einsum(
            "wot,wtf->wof",
            weights_reduced_precision,
            value_tile_rows,
            preferred_element_type=jnp.float32,
        ).astype(jnp.bfloat16)
        return (context, (row_peak + jnp.log(denominator))[..., 0])

    context_heads, log_totals = lax.map(attend, (query_heads, all_keys, all_values, offset_bias))
    context_rows = from_heads(context_heads)
    residual = token_rows + feature_total(right_transposed(context_rows, output_full))
    gain_two, gate_full, up_full, down_full = (
        lax.all_gather(gain_ffn, "seq", axis=0, tiled=True),
        lax.all_gather(gate_weight, "seq", axis=0, tiled=True),
        lax.all_gather(up_weight, "seq", axis=0, tiled=True),
        lax.all_gather(down_weight, "seq", axis=0, tiled=True),
    )
    unit_two, scale_two, normed_two = normalize(residual, gain_two)
    gate_pre = plain_product(normed_two, gate_full)
    up_pre = plain_product(normed_two, up_full)
    activated, gelu_back = jax.vjp(jax.nn.gelu, gate_pre)
    hidden = (activated * up_pre).astype(jnp.bfloat16)
    ffn_share = lax.psum_scatter(
        right_transposed(hidden, down_full), "fsdp", scatter_dimension=1, tiled=True
    )
    residual_share = lax.dynamic_slice_in_dim(residual, fsdp_index * part_width, part_width, 1)
    layer_out = (
        (residual_share + ffn_share)
        .astype(jnp.bfloat16)
        .reshape(batch_count, slot_count, part_width)
    )
    masked_cot = jnp.where(own_valid[:, :, None], cotangent, jnp.zeros_like(cotangent))
    grad_rows = full_features(masked_cot)
    grad_down = left_transposed(grad_rows, hidden)
    grad_hidden = plain_product(grad_rows, down_full)
    grad_gate_pre = gelu_back(grad_hidden * up_pre)[0].astype(jnp.bfloat16)
    grad_up_pre = (grad_hidden * activated).astype(jnp.bfloat16)
    grad_gate = left_transposed(normed_two, grad_gate_pre)
    grad_up = left_transposed(normed_two, grad_up_pre)
    normed_two_grad = right_transposed(grad_gate_pre, gate_full) + right_transposed(
        grad_up_pre, up_full
    )
    second_gain_piece = jnp.sum(normed_two_grad * unit_two, axis=0)
    ffn_grads = (
        lax.psum_scatter(second_gain_piece, "seq", scatter_dimension=0, tiled=True),
        lax.psum_scatter(grad_gate, "seq", scatter_dimension=0, tiled=True),
        lax.psum_scatter(grad_up, "seq", scatter_dimension=0, tiled=True),
        lax.psum_scatter(grad_down, "seq", scatter_dimension=0, tiled=True),
    )
    residual_grad = grad_rows.astype(jnp.float32) + norm_back(
        feature_total(normed_two_grad), unit_two, scale_two, gain_two
    )
    residual_low = residual_grad.astype(jnp.bfloat16)
    grad_output = left_transposed(residual_low, context_rows)
    context_grad = to_heads(
        plain_product(residual_low, output_full).astype(jnp.bfloat16), batch_count, head_size
    )

    def query_side(inputs, with_keys):
        query_tile_rows, key_tile_rows, value_tile_rows, bias_line, log_total, context_tile_rows = (
            inputs
        )
        scores = masked_scores(
            query_tile_rows, key_tile_rows, bias_rows(bias_line, first_query, slot_count, length)
        )
        probs = jnp.exp(scores - log_total[..., None])
        prob_grad = jnp.einsum(
            "jht,jxt->jhx", context_tile_rows, value_tile_rows, preferred_element_type=jnp.float32
        )
        delta = jnp.sum(probs * prob_grad, axis=-1)
        score_gradient = (probs * (prob_grad - delta[..., None])).astype(jnp.bfloat16)
        query_grad = jnp.einsum(
            "wot,wtf->wof", score_gradient, key_tile_rows, preferred_element_type=jnp.float32
        )
        bias_grad = bias_rows_back(
            jnp.sum(score_gradient.astype(jnp.float32), axis=0),
            first_query,
            slot_count,
            length,
            line_length,
        )
        key_term = jnp.einsum(
            "xic,xil->xcl", score_gradient, query_tile_rows, preferred_element_type=jnp.float32
        )
        value_term = jnp.einsum(
            "xic,xil->xcl",
            probs.astype(jnp.bfloat16),
            context_tile_rows,
            preferred_element_type=jnp.float32,
        )
        return (query_grad, bias_grad, delta, key_term, value_term)

    side_inputs = (query_heads, all_keys, all_values, offset_bias, log_totals, context_grad)
    query_grad, bias_grad, delta, key_terms, value_terms = lax.map(
        partial(query_side, with_keys=True), side_inputs
    )
    wide_shape = (number_of_heads, batch_count, length * head_size)
    key_sums, value_sums = (
        lax.psum_scatter(key_terms.reshape(wide_shape), "seq", scatter_dimension=2, tiled=True),
        lax.psum_scatter(value_terms.reshape(wide_shape), "seq", scatter_dimension=2, tiled=True),
    )
    own_shape = (number_of_heads, batch_count, slot_count, head_size)
    query_low = from_heads(query_grad.astype(jnp.bfloat16))
    key_low = from_heads(key_sums.reshape(own_shape).astype(jnp.bfloat16))
    value_low = from_heads(value_sums.reshape(own_shape).astype(jnp.bfloat16))
    grad_query = left_transposed(normed_one, query_low)
    grad_key = left_transposed(normed_one, key_low)
    grad_value = left_transposed(normed_one, value_low)
    grad_table = lax.dot_general(bucket_hot, bias_grad, (((0,), (1,)), ((), ())), precision=highest)
    normed_one_grad = (
        right_transposed(query_low, query_full)
        + right_transposed(key_low, key_full)
        + right_transposed(value_low, value_full)
    )
    gain_one_part = jnp.sum(normed_one_grad * unit_one, axis=0)
    attn_grads = (
        lax.psum_scatter(gain_one_part, "seq", scatter_dimension=0, tiled=True),
        lax.psum_scatter(grad_query, "seq", scatter_dimension=0, tiled=True),
        lax.psum_scatter(grad_key, "seq", scatter_dimension=0, tiled=True),
        lax.psum_scatter(grad_value, "seq", scatter_dimension=0, tiled=True),
        lax.psum_scatter(grad_output, "seq", scatter_dimension=0, tiled=True),
        lax.psum_scatter(grad_table, "seq", scatter_dimension=0, tiled=True),
    )
    token_grad = residual_grad + norm_back(
        feature_total(normed_one_grad), unit_one, scale_one, gain_one
    )
    token_share = lax.dynamic_slice_in_dim(
        token_grad, fsdp_index * part_width, part_width, 1
    ).reshape(batch_count, slot_count, part_width)
    gain_one_sum, gain_two_sum = lax.psum((attn_grads[0], ffn_grads[0]), "fsdp")
    return (
        layer_out,
        token_share,
        gain_one_sum,
        attn_grads[1],
        attn_grads[2],
        attn_grads[3],
        attn_grads[4],
        attn_grads[5],
        gain_two_sum,
        ffn_grads[1],
        ffn_grads[2],
        ffn_grads[3],
    )


BLOCK = 128
BOTH = ("seq", "fsdp")


def move(value, target):
    pairs = []
    for z in range(4):
        for y in range(2):
            for x in range(2):
                for c in range(2):
                    zt, yt, xt, ct = target(z, y, x, c)
                    pairs.append(((2 * z + y) * 4 + 2 * x + c, (2 * zt + yt) * 4 + 2 * xt + ct))
    return lax.ppermute(value, BOTH, pairs)


def spread_slot(k):
    return lambda z, y, x, c: (2 * c + (k ^ (z & 1)), y, x, z >> 1)


KEYS = 512
QUERIES = 512
WIDE_QUERIES = 1024
OFFSET = 1920


def skew_table(rev_ref, table):
    width = rev_ref.shape[1]
    line = jnp.broadcast_to(rev_ref[...], (8, width))
    for first in range(0, BLOCK, 8):
        table[first : first + 8, :] = pltpu.roll(
            line, (width - (BLOCK - 1) + first) % width, axis=1, stride=1, stride_axis=0
        )


def place_of(piece, part, z, y, x, c):
    c_rel, d = part // 4, part % 4
    b = jnp.bitwise_xor(x, piece // 2)
    block = (
        4 * jnp.bitwise_xor(z, d)
        + 2 * jnp.bitwise_xor(y, piece % 2)
        + jnp.bitwise_xor(c, c_rel)
    )
    return b, block


def part_of(b, block, z, y, x, c):
    piece = 2 * jnp.bitwise_xor(b, x) + jnp.bitwise_xor((block // 2) % 2, y)
    part = 4 * jnp.bitwise_xor(block % 2, c) + jnp.bitwise_xor(block // 4, z)
    return piece, part


def lanes(first, count):
    return pl.ds(pl.multiple_of(first, BLOCK), count)


def attend_kernel(sc, pieces, rev_ref, ctx_ref, ctx_wide, lse_ref, qkv, keys, table):
    z, y, x, c = position()
    for piece in range(4):
        for part in range(8):
            b, block = place_of(piece, part, z, y, x, c)
            data = pieces[piece, :, :, part * BLOCK : (part + 1) * BLOCK]
            qkv[b, :, :, lanes(block * BLOCK, BLOCK)] = data
            keys[b, lanes(block * BLOCK, BLOCK), :] = data[1].T
    skew_table(rev_ref, table)
    length = qkv.shape[-1]
    for b in range(2):
        valid = sc[b]
        full = valid // KEYS

        @pl.loop(0, length // WIDE_QUERIES)
        def _(i):
            first_query = i * WIDE_QUERIES
            query = qkv[b, 0, :, lanes(first_query, WIDE_QUERIES)]

            def tile(j, carry, masked):
                peak, total, acc = carry
                first_key = j * KEYS
                score = jnp.dot(
                    keys[b, lanes(first_key, KEYS), :], query, preferred_element_type=jnp.float32
                )
                score = score + jnp.concatenate(
                    [
                        table[:, lanes(first_query - first_key + OFFSET - t, WIDE_QUERIES)]
                        for t in range(0, KEYS, BLOCK)
                    ],
                    axis=0,
                )
                if masked:
                    position = first_key + lax.broadcasted_iota(jnp.int32, (KEYS, WIDE_QUERIES), 0)
                    score = jnp.where(position < valid, score, masked_score)
                now = jnp.maximum(peak, jnp.max(score, axis=0, keepdims=True))
                scale = jnp.exp(peak - now)
                prob = jnp.exp(score - now)
                total = total * scale + jnp.sum(prob, axis=0, keepdims=True)
                acc = acc * scale + jnp.dot(
                    qkv[b, 2, :, lanes(first_key, KEYS)],
                    prob.astype(jnp.bfloat16),
                    preferred_element_type=jnp.float32,
                )
                return now, total, acc

            carry = (
                jnp.full((1, WIDE_QUERIES), masked_score, jnp.float32),
                jnp.zeros((1, WIDE_QUERIES), jnp.float32),
                jnp.zeros((DH, WIDE_QUERIES), jnp.float32),
            )
            carry = lax.fori_loop(0, full, lambda j, s: tile(j, s, False), carry)
            peak, total, acc = lax.cond(
                valid > full * KEYS, lambda s: tile(full, s, True), lambda s: s, carry
            )
            context = acc / total
            ctx_wide[b, :, lanes(first_query, WIDE_QUERIES)] = context
            lse_ref[b, :, lanes(first_query, WIDE_QUERIES)] = peak + jnp.log(total)
            low = context.astype(jnp.bfloat16)
            for t in range(WIDE_QUERIES // BLOCK):
                piece, part = part_of(b, i * (WIDE_QUERIES // BLOCK) + t, z, y, x, c)
                ctx_ref[piece, :, lanes(part * BLOCK, BLOCK)] = low[:, t * BLOCK : (t + 1) * BLOCK]


def attend(scalars, pieces, rev_line):
    _, _, head_size, tokens = pieces.shape
    length = tokens * 2
    smem, vmem = pl.BlockSpec(memory_space=pltpu.SMEM), pl.BlockSpec(memory_space=pltpu.VMEM)
    return pl.pallas_call(
        attend_kernel,
        name="attend",
        out_shape=[
            jax.ShapeDtypeStruct((4, head_size, tokens), jnp.bfloat16),
            jax.ShapeDtypeStruct((2, head_size, length), jnp.float32),
            jax.ShapeDtypeStruct((2, 1, length), jnp.float32),
            jax.ShapeDtypeStruct((2, 3, head_size, length), jnp.bfloat16),
        ],
        in_specs=[smem] + [vmem] * 2,
        out_specs=[vmem] * 4,
        scratch_shapes=[
            pltpu.VMEM((2, length, head_size), jnp.bfloat16),
            pltpu.VMEM((BLOCK, rev_line.shape[1]), jnp.float32),
        ],
        cost_estimate=pl.CostEstimate(
            flops=46_000_000_000, bytes_accessed=4 << 20, transcendentals=0
        ),
        compiler_params=pltpu.CompilerParams(vmem_limit_bytes=48 << 20),
    )(scalars, pieces, rev_line)


def attend_back_kernel(
    sc, pieces, rev_ref, ctx_wide, lse_ref, qkv,
    out_ref, line_ref,
    queries, keys, values, grads, grads_t, delta, query_sum, key_sum, value_sum, table, table_sum,
):
    z, y, x, c = position()
    length = qkv.shape[-1]
    for piece in range(4):
        for part in range(8):
            b, block = place_of(piece, part, z, y, x, c)
            data = pieces[piece, :, part * BLOCK : (part + 1) * BLOCK]
            grads_t[b, :, lanes(block * BLOCK, BLOCK)] = data
            grads[b, lanes(block * BLOCK, BLOCK), :] = data.T
    for b in range(2):
        for first in range(0, length, BLOCK):
            here = slice(first, first + BLOCK)
            queries[b, here, :] = qkv[b, 0, :, here].T
            keys[b, here, :] = qkv[b, 1, :, here].T
            values[b, here, :] = qkv[b, 2, :, here].T
        delta[b] = jnp.sum(
            ctx_wide[b] * grads_t[b].astype(jnp.float32), axis=0, keepdims=True
        )
    skew_table(rev_ref, table)
    table_sum[...] = jnp.zeros_like(table_sum)
    query_sum[...] = jnp.zeros_like(query_sum)
    out_ref[...] = jnp.zeros_like(out_ref)
    for b in range(2):
        valid = sc[b]
        full = valid // KEYS
        count = (valid + QUERIES - 1) // QUERIES

        def key_step(j, masked):
            first_key = j * KEYS
            key, value = keys[b, lanes(first_key, KEYS), :], values[b, lanes(first_key, KEYS), :]
            key_t = qkv[b, 1, :, lanes(first_key, KEYS)]
            key_sum[...] = jnp.zeros_like(key_sum)
            value_sum[...] = jnp.zeros_like(value_sum)

            @pl.loop(0, count)
            def _(i):
                first_query = i * QUERIES
                here = lanes(first_query, QUERIES)
                score = jnp.dot(key, qkv[b, 0, :, here], preferred_element_type=jnp.float32)
                score = score + jnp.concatenate(
                    [
                        table[:, lanes(first_query - first_key + OFFSET - t, QUERIES)]
                        for t in range(0, KEYS, BLOCK)
                    ],
                    axis=0,
                )
                if masked:
                    position = first_key + lax.broadcasted_iota(jnp.int32, (KEYS, QUERIES), 0)
                    score = jnp.where(position < valid, score, masked_score)
                prob = jnp.exp(score - lse_ref[b, :, here])
                prob_grad = jnp.dot(value, grads_t[b, :, here], preferred_element_type=jnp.float32)
                score_grad = (prob * (prob_grad - delta[b, :, here])).astype(jnp.bfloat16)
                value_sum[...] += jnp.dot(
                    prob.astype(jnp.bfloat16), grads[b, here, :], preferred_element_type=jnp.float32
                )
                key_sum[...] += jnp.dot(
                    score_grad, queries[b, here, :], preferred_element_type=jnp.float32
                )
                query_sum[b, :, here] += jnp.dot(
                    key_t, score_grad, preferred_element_type=jnp.float32
                )
                for t in range(0, KEYS, BLOCK):
                    table_sum[:, lanes(first_query - first_key + OFFSET - t, QUERIES)] += score_grad[
                        t : t + BLOCK
                    ].astype(jnp.float32)

            for t in range(KEYS // BLOCK):
                piece, part = part_of(b, j * (KEYS // BLOCK) + t, z, y, x, c)
                rows = slice(t * BLOCK, (t + 1) * BLOCK)
                at = lanes(part * BLOCK, BLOCK)
                out_ref[piece, 1, :, at] = key_sum[rows, :].T.astype(jnp.bfloat16)
                out_ref[piece, 2, :, at] = value_sum[rows, :].T.astype(jnp.bfloat16)

        pl.loop(0, full)(lambda j: key_step(j, False))
        pl.when(valid > full * KEYS)(lambda: key_step(full, True))
        for block in range(length // BLOCK):
            piece, part = part_of(b, block, z, y, x, c)
            out_ref[piece, 0, :, lanes(part * BLOCK, BLOCK)] = query_sum[
                b, :, block * BLOCK : (block + 1) * BLOCK
            ].astype(jnp.bfloat16)
    width = table_sum.shape[1]
    line = jnp.zeros((8, width), jnp.float32)
    for first in range(0, BLOCK, 8):
        line = line + pltpu.roll(table_sum[first : first + 8, :], BLOCK - 8 - first, axis=1)
    ahead = 7 - lax.broadcasted_iota(jnp.int32, (8, width), 0)
    for bit in (1, 2, 4):
        line = jnp.where((ahead & bit) != 0, pltpu.roll(line, bit, axis=1), line)
    line_ref[...] = jnp.sum(line, axis=0, keepdims=True)


def attend_back(scalars, pieces, rev_line, ctx_wide, lse, qkv):
    _, head_size, tokens = pieces.shape
    length = tokens * 2
    smem, vmem = pl.BlockSpec(memory_space=pltpu.SMEM), pl.BlockSpec(memory_space=pltpu.VMEM)
    low = pltpu.VMEM((2, length, head_size), jnp.bfloat16)
    return pl.pallas_call(
        attend_back_kernel,
        name="attend_back",
        out_shape=[
            jax.ShapeDtypeStruct((4, 3, head_size, tokens), jnp.bfloat16),
            jax.ShapeDtypeStruct(rev_line.shape, jnp.float32),
        ],
        in_specs=[smem] + [vmem] * 5,
        out_specs=[vmem] * 2,
        scratch_shapes=[
            low, low, low, low,
            pltpu.VMEM((2, head_size, length), jnp.bfloat16),
            pltpu.VMEM((2, 1, length), jnp.float32),
            pltpu.VMEM((2, head_size, length), jnp.float32),
            pltpu.VMEM((KEYS, head_size), jnp.float32),
            pltpu.VMEM((KEYS, head_size), jnp.float32),
            pltpu.VMEM((BLOCK, rev_line.shape[1]), jnp.float32),
            pltpu.VMEM((BLOCK, rev_line.shape[1]), jnp.float32),
        ],
        cost_estimate=pl.CostEstimate(
            flops=46_000_000_000, bytes_accessed=4 << 20, transcendentals=0
        ),
        compiler_params=pltpu.CompilerParams(vmem_limit_bytes=48 << 20),
    )(scalars, pieces, rev_line, ctx_wide, lse, qkv)


CHUNKS = 4
MESH_ID = pl.DeviceIdType.MESH
IN_VMEM = pl.BlockSpec(memory_space=pltpu.VMEM)
IN_PLACE = pl.BlockSpec(memory_space=pl.ANY)
COPIES = pltpu.SemaphoreType.DMA


def flip(a, b):
    return a + b - 2 * a * b


def flip_pair(a, b):
    return 2 * flip(a // 2, b // 2) + flip(a % 2, b % 2)


def position():
    s, f = lax.axis_index("seq"), lax.axis_index("fsdp")
    return s // 2, s % 2, f // 2, f % 2


def device(z, y, x, c):
    return (2 * z + y, 2 * x + c)


def ring_of(z):
    high, low = z // 2, z % 2
    following = 2 * low + 1 - high
    return following, (2 * (1 - low) + high, 2 * (1 - high) + 1 - low, following)


def greet(z, y, x, c):
    peers = []
    for d in range(1, 8):
        peers.append(device(z, flip(y, d // 4), flip(x, (d // 2) % 2), flip(c, d % 2)))
        if d > 1:
            peers.append(device(flip_pair(z, d // 2), y, x, flip(c, d % 2)))
    barrier = pltpu.get_barrier_semaphore()
    for peer in peers:
        pl.semaphore_signal(barrier, inc=1, device_id=peer, device_id_type=MESH_ID)
    pl.semaphore_wait(barrier, len(peers))


def remote(source, target, send, recv, to):
    return pltpu.make_async_remote_copy(
        src_ref=source,
        dst_ref=target,
        send_sem=send,
        recv_sem=recv,
        device_id=to,
        device_id_type=MESH_ID,
    )


class Links:
    def __init__(self, send, recv):
        self.send, self.recv, self.used, self.sent = send, recv, 0, []

    def go(self, source, target, to):
        i = self.used
        self.used += 1
        made = remote(source, target, self.send.at[i], self.recv.at[i], to)
        made.start()
        self.sent.append(made)
        return made

    def go_unless(self, own, source, target, to, send=None, recv=None):
        if send is None:
            send, recv = self.send.at[self.used], self.recv.at[self.used]
            self.used += 1
        made = remote(source, target, send, recv, to)
        if own is None:
            made.start()
            self.sent.append(made)
            return made
        local = pltpu.make_async_copy(source, target, recv)
        pl.when(own)(lambda: local.start())
        pl.when(jnp.logical_not(own))(lambda: made.start())
        self.sent.append((own, made))
        return made

    def go_if(self, there, here, source, target, send, recv, to):
        made = remote(source, target, send, recv, to)
        pl.when(there)(lambda: made.start())
        if here is not None:
            local = pltpu.make_async_copy(source, target, recv)
            pl.when(here)(lambda: local.start())
        self.sent.append((jnp.logical_not(there), made))

    def done(self, made):
        made.wait_send()
        self.sent = [m for m in self.sent if m is not made]

    def finish(self):
        for made in self.sent:
            if isinstance(made, tuple):
                pl.when(jnp.logical_not(made[0]))(lambda made=made: made[1].wait_send())
            else:
                made.wait_send()


def share_start(links, rows_all, me):
    z, y, x, c = me
    following, _ = ring_of(z)
    rows = rows_all.shape[1] // CHUNKS
    ring = []
    for h in range(CHUNKS):
        here = pl.ds(h * rows, rows)
        target = rows_all.at[flip_pair(following, z), here]
        ring.append(links.go(rows_all.at[0, here], target, device(following, y, x, c)))
    core = [links.go(rows_all.at[0], rows_all.at[4], device(z, y, x, 1 - c))]
    return [ring], core


def share_step(links, rows_all, me, state, step):
    z, y, x, c = me
    following, back = ring_of(z)
    rows = rows_all.shape[1] // CHUNKS
    ring, core = state
    slot = flip_pair(z, back[step - 1])
    sent = []
    for h in range(CHUNKS):
        here = pl.ds(h * rows, rows)
        ring[-1][h].wait_recv()
        source = rows_all.at[slot, here]
        if step < 3:
            target = rows_all.at[flip_pair(following, back[step - 1]), here]
            sent.append(links.go(source, target, device(following, y, x, c)))
        core.append(links.go(source, rows_all.at[4 + slot, here], device(z, y, x, 1 - c)))
    ring.append(sent)


def share_end(state):
    for made in state[1]:
        made.wait_recv()


def sum_order(z):
    _, back = ring_of(z)
    return [flip_pair(z, b) for b in back] + [0]


def column_go(links, me, k, source, target):
    z, y, x, c = me
    own = z // 2 == c if k == 0 else None
    to = device(2 * c + flip(k, z % 2), y, x, z // 2)
    return links.go_unless(own, source, target, to)


def arrived(place, sem):
    pltpu.make_async_copy(place, place, sem).wait()


def spread_go(links, me, k, source, full, send, recv):
    z, y, x, c = me
    rows = source.shape[0]
    first = pl.multiple_of((4 * c + 2 * flip(k, z % 2) + y) * rows, rows)
    target = full.at[pl.ds(first, rows), :]
    for dy, dx in ((0, 1), (1, 0), (0, 0)):
        own = None if dy + dx else c == x
        to = device(z, flip(y, dy), flip(x, dx), x)
        links.go_unless(own, source, target, to, send.at[k, dy, dx], recv.at[k, dy, c])


def spread_relay(links, me, full, send, recv):
    z, y, x, c = me
    odd = flip(c, x)
    k, step = 1 - odd, 1 - odd
    rows = full.shape[0] // 8
    to = device(z, flip(y, odd), flip(x, 1 - odd), c)
    for r in range(2):
        first = pl.multiple_of((4 * r + 2 * flip(k, z % 2) + flip(y, step)) * rows, rows)
        here = full.at[pl.ds(first, rows), :]
        arrived(here, recv.at[k, step, r])
        made = remote(here, here, send.at[r, 1, 1], recv.at[k, 1, r], to)
        made.start()
        links.sent.append(made)


def spread_wait(me, full, recv):
    z, y, x, c = me
    odd = flip(c, x)
    here = full.at[pl.ds(0, full.shape[0] // 8), :]
    for k, step in ((1 - odd, odd), (odd, 0), (odd, 1)):
        for r in range(2):
            arrived(here, recv.at[k, step, r])


def join_go(links, me, k, grads, into, relay, send, recv, relay_recv):
    z, y, x, c = me
    odd = flip(c, x) == 1
    even = jnp.logical_not(odd)
    rows = into.shape[2]
    for r in range(2):

        def block(step):
            index = 4 * r + 2 * flip(k, z % 2) + flip(y, step)
            return grads.at[pl.ds(pl.multiple_of(index * rows, rows), rows), :]

        same, other = device(z, y, c, r), device(z, 1 - y, c, r)
        mine = jnp.logical_and(even, c == r)
        partner = jnp.logical_and(even, c != r)
        links.go_if(
            partner, mine, block(0), into.at[k, 0], send.at[k, 0, r], recv.at[k, 0], same
        )
        if k == 0:
            links.go_if(even, None, block(1), into.at[0, 1], send.at[0, 1, r], recv.at[0, 1], other)
            to = device(z, 1 - y, x, c)
        else:
            links.go_if(odd, None, block(0), into.at[1, 1], send.at[1, 1, r], recv.at[1, 1], same)
            to = device(z, y, c, c)
        links.go_if(odd, None, block(1), relay.at[r], send.at[k, 2, r], relay_recv.at[r], to)


def join_relay(links, me, grads, into, relay, send, recv, relay_recv):
    z, y, x, c = me
    odd = flip(c, x)
    k, step = 1 - odd, 1 - odd
    rows = into.shape[2]
    for r in range(2):
        arrived(relay.at[r], relay_recv.at[r])
        index = 4 * r + 2 * flip(k, z % 2) + flip(y, step)
        own = grads[pl.ds(pl.multiple_of(index * rows, rows), rows), :]
        total = relay[r].astype(jnp.float32) + own.astype(jnp.float32)
        relay[r] = total.astype(jnp.bfloat16)
        to = device(z, flip(y, step), c, r)
        made = remote(relay.at[r], into.at[k, 2], send.at[0, 3, r], recv.at[k, 2], to)
        made.start()
        links.sent.append(made)


def join_sum(k, into, recv):
    total = 0.0
    for j in range(3):
        arrived(into.at[k, j], recv.at[k, j])
        total = total + into[k, j].astype(jnp.float32)
    return total.astype(jnp.bfloat16)


def rms(rows):
    return lax.rsqrt(jnp.mean(rows * rows, axis=-1, keepdims=True) + epsilon)


def lane_sum(values):
    return jnp.sum(values, axis=-1, keepdims=True)


def head_of(z, y, x, c, heads):
    return 2 * c + z // 2, (z % 2) * (heads // 2) + 2 * x + y


def entry_kernel(
    lengths, tok_ref, cot_ref, small_ref, bucket_ref, wq_ref, wk_ref, wv_ref, wo_ref, wg_ref,
    rows_ref, normed, grads, pieces, weight, gain_one, gain_two, rev_ref, slots_o, slots_g,
    tok_in, cot_in, held, qkv, small, send, recv, plane_send, plane_recv, local,
):
    me = z, y, x, c = position()
    greet(*me)
    links = Links(send, recv)
    f, part, half = 2 * x + c, tok_in.shape[2], tok_in.shape[1]

    def gather_rows(n, ref, into):
        def source(xd, cd):
            return ref.at[xd, pl.ds(pl.multiple_of(cd * half, half), half)]

        own = pltpu.make_async_copy(source(x, c), into.at[f], local.at[n])
        own.start()
        got = []
        for d in (1, 2, 3):
            xd, cd = flip(x, d // 2), flip(c, d % 2)
            got.append(links.go(source(xd, cd), into.at[f], device(z, y, xd, cd)))
        return own, got

    tok_own, tok_got = gather_rows(0, tok_ref, tok_in)
    small[f, z, y] = small_ref[...]
    small_got = []
    for d in (1, 2, 3):
        here = small.at[f, z, y]
        small_got.append(links.go(here, here, device(flip_pair(z, d), y, x, c)))
    group_width = wq_ref.shape[1] // 2
    way = []
    for k in range(2):
        cut = pl.ds(pl.multiple_of(flip(k, z % 2) * group_width, group_width), group_width)
        for n, ref in enumerate((wq_ref, wk_ref, wv_ref)):
            target = held.at[k, :, n * group_width : (n + 1) * group_width]
            way.append(column_go(links, me, k, ref.at[:, cut], target))
    for made in small_got:
        made.wait_recv()
    here = small.at[f, :, y]
    links.go(here, here, device(z, 1 - y, x, c)).wait_recv()
    tables = []
    for d in (1, 2, 3):
        here = small.at[f]
        tables.append(links.go(here, here, device(z, y, flip(x, d // 2), flip(c, d % 2))))
    for i in range(4 * part // BLOCK):
        here = slice(i * BLOCK, (i + 1) * BLOCK)
        block = (i // 2) // 2, (i // 2) % 2
        gain_one[:, here] = small[f, block[0], block[1], i % 2 : i % 2 + 1, :]
        gain_two[:, here] = small[f, block[0], block[1], 2 + i % 2 : 3 + i % 2, :]
    tok_own.wait()
    for made in tok_got:
        made.wait_recv()
    cot_own, cot_got = gather_rows(1, cot_ref, cot_in)
    wide = [tok_in[i].astype(jnp.float32) for i in range(4)]
    mean = sum(lane_sum(w * w) for w in wide) / (4 * part)
    scale = lax.rsqrt(mean + epsilon)
    for i in range(4):
        here = slice(i * part, (i + 1) * part)
        rows_ref[:, here] = tok_in[i]
        normed[0, :, here] = (wide[i] * scale * gain_one[:, here]).astype(jnp.bfloat16)
    first = share_start(links, normed, me)
    for k in range(2):
        for made in way[3 * k : 3 * k + 3]:
            made.wait_recv()
        spread_go(links, me, k, held.at[k], weight, plane_send, plane_recv)
    share_step(links, normed, me, first, 1)
    share_step(links, normed, me, first, 2)
    later = []
    half_ffn = wg_ref.shape[1] // 2
    for k in range(2):
        side = flip(k, z % 2)
        cut = pl.ds(pl.multiple_of(side * group_width, group_width), group_width)
        later.append(column_go(links, me, k, wo_ref.at[:, cut], slots_o.at[k]))
        cut = pl.ds(pl.multiple_of(side * half_ffn, half_ffn), half_ffn)
        later.append(column_go(links, me, k, wg_ref.at[:, cut], slots_g.at[k]))
    spread_relay(links, me, weight, plane_send, plane_recv)
    for made in tables:
        made.wait_recv()
    group = qkv.shape[1]
    heads = 2 * group
    source, place = head_of(z, y, x, c, heads)
    lane = lax.broadcasted_iota(jnp.int32, (1, BLOCK), 1)
    line = jnp.zeros(bucket_ref.shape, jnp.float32)
    per_block = 4
    for n in range(8 * per_block):
        block = n // per_block
        row = small[source, block // 2, block % 2, 4:5, :]
        value = lane_sum(jnp.where(lane == (n % per_block) * heads + place, row, 0.0))
        line = jnp.where(bucket_ref[...] == n, value, line)
    rev_ref[...] = line
    spread_wait(me, weight, plane_recv)
    rows = normed.shape[1]
    sent = []

    def project(d):
        out = jnp.dot(pair_of(normed, d), weight[...], preferred_element_type=jnp.float32)
        out = out.astype(jnp.bfloat16).T
        for side, slot in enumerate((d, 4 + d)):
            here = lanes(slot * rows, rows)
            cut = out[:, side * rows : (side + 1) * rows]
            qkv[:, :, :, here] = cut.reshape(3, group, DH, rows)
            pieces[0, :, :, here] = qkv[:, 2 * x + y, :, here]
            for e in (1, 2, 3):
                xd, yd = flip(x, e // 2), flip(y, e % 2)
                source = qkv.at[:, 2 * xd + yd, :, here]
                sent.append(links.go(source, pieces.at[e, :, :, here], device(z, yd, xd, c)))

    cot_own.wait()
    for made in cot_got:
        made.wait_recv()
    slot = (4 * z + 2 * y + c) * half + lax.broadcasted_iota(jnp.int32, (half, part), 0)
    valid = slot < jnp.where(x == 0, lengths[0], lengths[1])
    for i in range(4):
        grads[:, i * part : (i + 1) * part] = jnp.where(valid, cot_in[i], jnp.zeros_like(cot_in[i]))
    order = sum_order(z)
    first[1][0].wait_recv()
    project(0)
    for step in (1, 2, 3):
        if step == 3:
            share_step(links, normed, me, first, 3)
        for made in first[1][1 + CHUNKS * (step - 1) : 1 + CHUNKS * step]:
            made.wait_recv()
        project(order[step - 1])
    for made in sent + later:
        made.wait_recv()
    links.finish()


def low_array(*shape):
    return jax.ShapeDtypeStruct(shape, jnp.bfloat16)


def wide_array(*shape):
    return jax.ShapeDtypeStruct(shape, jnp.float32)


def low_space(*shape):
    return pltpu.VMEM(shape, jnp.bfloat16)


def entry(lengths, tokens_in, cotangent, small, rev_buckets, weights):
    _, slot_count, part = tokens_in.shape
    rows, width = slot_count // 2, 4 * part
    depth, cols = weights[0].shape
    group = cols // (2 * DH)
    wide = 3 * cols // 2
    return pl.pallas_call(
        entry_kernel,
        name="entry",
        out_shape=[
            low_array(rows, width),
            low_array(8, rows, width),
            low_array(rows, width),
            low_array(4, 3, DH, 8 * rows),
            low_array(8 * depth, wide),
            wide_array(1, width),
            wide_array(1, width),
            wide_array(*rev_buckets.shape),
            low_array(2, depth, cols // 2),
            low_array(2, depth, weights[4].shape[1] // 2),
        ],
        in_specs=[pl.BlockSpec(memory_space=pltpu.SMEM)]
        + [IN_PLACE] * 2
        + [IN_VMEM] * 2
        + [IN_PLACE] * 5,
        out_specs=[IN_VMEM] * 10,
        scratch_shapes=[
            low_space(4, rows, part),
            low_space(4, rows, part),
            low_space(2, depth, wide),
            low_space(3, group, DH, 8 * rows),
            pltpu.VMEM((4, 4, 2, 8, BLOCK), jnp.float32),
            COPIES((96,)),
            COPIES((96,)),
            COPIES((2, 2, 2)),
            COPIES((2, 2, 2)),
            COPIES((2,)),
        ],
        compiler_params=pltpu.CompilerParams(
            collective_id=1, has_side_effects=True, vmem_limit_bytes=48 << 20
        ),
    )(lengths, tokens_in, cotangent, small, rev_buckets, *weights)


def gelu_pair(t):
    inner = jnp.tanh(root_two_over_pi * (t + 0.044715 * (t * t * t)))
    half = 0.5 * (1.0 + inner)
    slope = half + 0.5 * t * (1.0 - inner * inner) * root_two_over_pi * (1.0 + 0.134145 * (t * t))
    return t * half, slope


def pair_of(ref, slot):
    return jnp.concatenate([ref[slot], ref[4 + slot]], axis=0)


def pair_go(links, me, core, i, terms, core_out, core_in):
    z, y, x, c = me
    size = terms.shape[0] // 2
    core_out[i] = terms[size:].astype(jnp.bfloat16)
    core.append(links.go(core_out.at[i], core_in.at[i], device(z, y, x, 1 - c)))
    return terms[:size]


def sum_step(links, me, core, ring, i, mine, core_in, ring_out, ring_in):
    z, y, x, c = me
    following, _ = ring_of(z)
    rows = mine.shape[0] // CHUNKS
    core.wait_recv()
    sent, last = [], []
    for h in range(CHUNKS):
        cut = slice(h * rows, (h + 1) * rows)
        here = pl.ds(h * rows, rows)
        value = mine[cut] + core_in[i, here, :].astype(jnp.float32)
        if i:
            ring[-1][h].wait_recv()
            value = value + ring_in[i - 1, here, :].astype(jnp.float32)
        if i < 3:
            ring_out[i, here, :] = value.astype(jnp.bfloat16)
            target = ring_in.at[i, here]
            sent.append(links.go(ring_out.at[i, here], target, device(following, y, x, c)))
        else:
            last.append(value)
    ring.append(sent)
    return last


def reduce_pair(links, me, state, i, terms, core_out, core_in, ring_out, ring_in):
    mine = pair_go(links, me, state[0], i, terms, core_out, core_in)
    return sum_step(links, me, state[0][i], state[1], i, mine, core_in, ring_out, ring_in)


def core_kernel(
    ctx_ref, rows_ref, gain_ref, own_ref, slots_o, slots_g, slot_ud0, slot_ud1,
    layer_ref, context, low, wide_ref, part_ref, pieces, in_gu, in_d,
    residual_ref, down, hidden, out_weight, gate_up, normed, grads, pre, ctx_all, heads_out, grad_gu, grad_d,
    mine, core_out, core_in, ring_out, ring_in, ring_out2, ring_in2,
    relay_gu, relay_d, send, recv, plane_send, plane_recv, join_send, join_recv, relay_recv,
):
    me = z, y, x, c = position()
    greet(*me)
    links = Links(send, recv)
    own = 2 * x + y
    heads = []
    for d in (1, 2, 3):
        xd, yd = flip(x, d // 2), flip(y, d % 2)
        heads.append(links.go(ctx_ref.at[d], ctx_all.at[own], device(z, yd, xd, c)))
    grads[0] = own_ref[...]
    second = share_start(links, grads, me)

    ffn = down.shape[1]
    fulls = out_weight, gate_up.at[:, :ffn], gate_up.at[:, ffn:], down

    def weight_go(n):
        slots = (
            (slots_o.at[0], slots_o.at[1]),
            (slots_g.at[0], slots_g.at[1]),
            (slot_ud0.at[:, :ffn], slot_ud1.at[:, :ffn]),
            (slot_ud0.at[:, ffn:], slot_ud1.at[:, ffn:]),
        )[n]
        for k in range(2):
            spread_go(links, me, k, slots[k], fulls[n], plane_send.at[n], plane_recv.at[n])

    def weight_relay(n):
        spread_relay(links, me, fulls[n], plane_send.at[n], plane_recv.at[n])

    def weight_wait(n):
        spread_wait(me, fulls[n], plane_recv.at[n])

    weight_go(0)
    ctx_all[own] = ctx_ref[0]
    for made in heads:
        made.wait_recv()
    group, size, tokens = ctx_all.shape
    rows, width = residual_ref.shape
    depth = gate_up.shape[0] // 8
    half_tokens = tokens // 2
    context[...] = ctx_all[...].reshape(group * size, tokens).T
    weight_relay(0)
    weight_go(1)
    weight_go(2)
    weight_wait(0)
    order = sum_order(z)

    def first_row(block):
        return pl.multiple_of(block * rows, rows)

    def pair_rows(ref, d):
        return jnp.concatenate(
            [ref[pl.ds(first_row(d), rows), :], ref[pl.ds(first_row(4 + d), rows), :]], axis=0
        )

    state = [], []
    for i in range(4):
        terms = right_transposed(pair_rows(context, order[i]), out_weight[...])
        last = reduce_pair(links, me, state, i, terms, core_out, core_in, ring_out, ring_in)
        if i < 3:
            share_step(links, grads, me, second, i + 1)
        if i == 1:
            weight_go(3)
        if i == 2:
            weight_relay(1)
            weight_relay(2)
    residual = rows_ref[...].astype(jnp.float32) + jnp.concatenate(last, axis=0)
    residual_ref[...] = residual
    gain = gain_ref[...]
    normed[0] = (residual * rms(residual) * gain).astype(jnp.bfloat16)
    shared = share_start(links, normed, me)
    weight_relay(3)
    share_end(second)
    for made in state[0] + sum(state[1], []):
        links.done(made)
    ring = []

    def take_in(i):
        share_step(links, normed, me, shared, i + 1)

    def feed(i):
        d = order[i]
        for made in shared[1][:1] if i == 3 else shared[1][1 + CHUNKS * i : 1 + CHUNKS * (i + 1)]:
            made.wait_recv()
        gate_up_pre = jnp.dot(
            pair_of(normed, d), gate_up[...], preferred_element_type=jnp.float32
        )
        activated, slope = gelu_pair(gate_up_pre[:, :ffn])
        up_pre = gate_up_pre[:, ffn:]
        made = (activated * up_pre).astype(jnp.bfloat16)
        hidden[pl.ds(first_row(d), rows), :] = made[:rows]
        hidden[pl.ds(first_row(4 + d), rows), :] = made[rows:]
        if i == 0:
            weight_wait(3)
        grad_hidden = jnp.dot(pair_of(grads, d), down[...], preferred_element_type=jnp.float32)
        grad_pre = jnp.concatenate(
            [
                (grad_hidden * up_pre * slope).astype(jnp.bfloat16),
                (grad_hidden * activated).astype(jnp.bfloat16),
            ],
            axis=1,
        )
        pre[pl.ds(first_row(d), rows), :] = grad_pre[:rows]
        pre[pl.ds(first_row(4 + d), rows), :] = grad_pre[rows:]
        terms = right_transposed(grad_pre, gate_up[...])
        kept = []
        mine[i] = pair_go(links, me, kept, i, terms, core_out, core_in)
        return kept[0]

    def pass_on(i, core):
        return sum_step(links, me, core, ring, i, mine[i], core_in, ring_out2, ring_in2)

    joins = (grad_gu, in_gu, relay_gu), (grad_d, in_d, relay_d)

    def weight_grads(k):
        for n in range(4):
            block = 4 * (n // 2) + 2 * flip(k, z % 2) + n % 2
            here = pl.ds(pl.multiple_of(block * depth, depth), depth)
            left = normed[:, :, here].reshape(tokens, depth)
            grad_gu[here, :] = left_transposed(left, pre[...]).astype(jnp.bfloat16)
            left = grads[:, :, here].reshape(tokens, depth)
            grad_d[here, :] = left_transposed(left, hidden[...]).astype(jnp.bfloat16)
        for n, (grad, into, relay) in enumerate(joins):
            sems = join_send.at[n], join_recv.at[n], relay_recv.at[n]
            join_go(links, me, k, grad, into, relay, *sems)

    take_in(0)
    weight_wait(1)
    weight_wait(2)
    first = feed(0)
    pass_on(0, first)
    take_in(1)
    following = feed(1)
    take_in(2)
    final = feed(3)
    pass_on(1, following)
    third = feed(2)
    weight_grads(0)
    pass_on(2, third)
    weight_grads(1)
    last = pass_on(3, final)
    normed_grad = jnp.concatenate(last, axis=0)
    residual = residual_ref[...]
    scale = rms(residual)
    unit = residual * scale
    part_ref[...] = jnp.sum(normed_grad * unit, axis=0, keepdims=True)
    out = own_ref[...].astype(jnp.float32) + norm_back(normed_grad, unit, scale, gain)
    wide_ref[...] = out
    low[0] = out.astype(jnp.bfloat16)
    shared = share_start(links, low, me)
    sent = []

    def context_back(d):
        made = jnp.dot(pair_of(low, d), out_weight[...], preferred_element_type=jnp.float32)
        made = made.astype(jnp.bfloat16).T
        for half, slot in enumerate((d, 4 + d)):
            here = lanes(slot * rows, rows)
            cut = made[:, half * rows : (half + 1) * rows]
            heads_out[:, :, here] = cut.reshape(group, size, rows)
            pieces[0, :, here] = heads_out[own, :, here]
            for e in (1, 2, 3):
                xd, yd = flip(x, e // 2), flip(y, e % 2)
                source = heads_out.at[2 * xd + yd, :, here]
                sent.append(links.go(source, pieces.at[e, :, here], device(z, yd, xd, c)))

    shared[1][0].wait_recv()
    context_back(0)
    for made in (first, following, third, final):
        links.done(made)
    layer_core, layer_ring = [], []
    for i in range(4):
        terms = right_transposed(pair_rows(hidden, order[i]), down[...])
        mine[i] = pair_go(links, me, layer_core, i, terms, core_out, core_in)

    def layer_step(i):
        made = layer_core[i]
        return sum_step(links, me, made, layer_ring, i, mine[i], core_in, ring_out, ring_in)

    for step in (1, 2, 3):
        share_step(links, low, me, shared, step)
        if step == 2:
            layer_step(0)
            for n, (grad, into, relay) in enumerate(joins):
                sems = join_send.at[n], join_recv.at[n], relay_recv.at[n]
                join_relay(links, me, grad, into, relay, *sems)
        for made in shared[1][1 + CHUNKS * (step - 1) : 1 + CHUNKS * step]:
            made.wait_recv()
        context_back(order[step - 1])
    layer_step(1)
    layer_step(2)
    last = layer_step(3)
    layer = (residual_ref[...] + jnp.concatenate(last, axis=0)).astype(jnp.bfloat16)
    part = width // 4
    for i in range(4):
        layer_ref[i] = layer[:, i * part : (i + 1) * part]
    for made in sent:
        made.wait_recv()
    for n, (_, into, _) in enumerate(joins):
        for k in range(2):
            for j in range(3):
                arrived(into.at[k, j], join_recv.at[n, k, j])
    links.finish()


def reduce_space(rows, width):
    return [
        low_space(4, rows, width),
        low_space(4, rows, width),
        low_space(3, rows, width),
        low_space(3, rows, width),
    ]


def core(ctx_pieces, token_rows, gain, grad_own, slots_o, slots_g, slots_ud):
    _, size, tokens = ctx_pieces.shape
    rows, width = token_rows.shape
    _, depth, ffn = slots_g.shape
    group = slots_o.shape[2] // DH
    return pl.pallas_call(
        core_kernel,
        name="core",
        out_shape=[
            low_array(4, rows, width // 4),
            low_array(tokens, 4 * size),
            low_array(8, rows, width),
            wide_array(rows, width),
            wide_array(1, width),
            low_array(4, size, tokens),
            low_array(2, 3, depth, 2 * ffn),
            low_array(2, 3, depth, ffn),
        ],
        in_specs=[IN_VMEM] * 4 + [IN_PLACE] * 4,
        out_specs=[IN_VMEM] * 6 + [IN_PLACE] * 2,
        scratch_shapes=[
            pltpu.VMEM((rows, width), jnp.float32),
            low_space(8 * depth, ffn),
            low_space(tokens, ffn),
            low_space(8 * depth, group * size),
            low_space(8 * depth, 2 * ffn),
            low_space(8, rows, width),
            low_space(8, rows, width),
            low_space(tokens, 2 * ffn),
            low_space(4, size, tokens),
            low_space(group, size, tokens),
            low_space(8 * depth, 2 * ffn),
            low_space(8 * depth, ffn),
            pltpu.VMEM((4, rows, width), jnp.float32),
            *reduce_space(rows, width),
            low_space(3, rows, width),
            low_space(3, rows, width),
            low_space(2, depth, 2 * ffn),
            low_space(2, depth, ffn),
            COPIES((176,)),
            COPIES((176,)),
            COPIES((4, 2, 2, 2)),
            COPIES((4, 2, 2, 2)),
            COPIES((2, 2, 4, 2)),
            COPIES((2, 2, 3)),
            COPIES((2, 2)),
        ],
        compiler_params=pltpu.CompilerParams(
            collective_id=2, has_side_effects=True, vmem_limit_bytes=63 << 20
        ),
    )(ctx_pieces, token_rows, gain, grad_own, slots_o, slots_g, *slots_ud)


def exit_kernel(
    piece_ref, normed_ref, weight_ref, token_ref, wide_ref, gain_ref, low_ref, context_ref,
    layer_own, gain_two_ref, line_ref, bucket_ref, ffn_ref,
    query_out, key_out, value_out, output_out, home_ref, layer_ref, small_ref, ffn_out,
    heads_in, rows_low, weight_grad, weight_in, weight_relay, held, token_out,
    packed, in_f, in_y, in_z,
    core_out, core_in, ring_out, ring_in,
    send, recv, plane_send, plane_recv, relay_recv,
):
    me = z, y, x, c = position()
    greet(*me)
    links = Links(send, recv)
    own, f = 2 * x + y, 2 * x + c
    group, three, size, tokens = heads_in.shape
    rows = tokens // 8
    depth, cols = weight_grad.shape[1] // 8, weight_grad.shape[2]
    width = normed_ref.shape[2]
    part = width // 4
    heads = []
    for d in (1, 2, 3):
        xd, yd = flip(x, d // 2), flip(y, d % 2)
        heads.append(links.go(piece_ref.at[d], heads_in.at[own], device(z, yd, xd, c)))
    heads_in[own] = piece_ref[0]

    order = sum_order(z)

    def pair_rows(ref, d):
        return jnp.concatenate(
            [ref[lanes(block * rows, rows), :] for block in (d, 4 + d)], axis=0
        )

    def to_home(source, into):
        got = []
        for d in (1, 2, 3):
            xd, cd = flip(x, d // 2), flip(c, d % 2)
            got.append(links.go(source.at[2 * xd + cd], into.at[f], device(z, y, xd, cd)))
        into[f] = source[f]
        return got

    state = [], []

    def join(n):
        sems = plane_send.at[n], plane_recv.at[n], relay_recv.at[n]
        return weight_grad.at[n], weight_in.at[n], weight_relay.at[n], *sems

    def step(i):
        terms = right_transposed(pair_rows(rows_low, order[i]), weight_ref[...])
        return reduce_pair(links, me, state, i, terms, core_out, core_in, ring_out, ring_in)

    def weight_grads(n, ref, right):
        for k in range(2):
            for piece in range(4):
                block = 4 * (piece // 2) + 2 * flip(k, z % 2) + piece % 2
                here = pl.ds(pl.multiple_of(block * depth, depth), depth)
                left = ref[:, :, here].reshape(tokens, depth)
                weight_grad[n, here, :] = left_transposed(left, right).astype(jnp.bfloat16)
            join_go(links, me, k, *join(n))

    way = [column_go(links, me, 1, ffn_ref, ffn_out)]
    results = query_out, key_out, value_out, output_out
    cut = pl.ds(pl.multiple_of((z % 2) * cols, cols), cols)

    def send_sums(n):
        for k in range(2):
            held[n, k] = join_sum(k, weight_in.at[n], plane_recv.at[n])
            way.append(column_go(links, me, k, held.at[n, k], results[n].at[:, cut]))

    weight_grads(3, low_ref, context_ref[...])

    packed[...] = jnp.zeros_like(packed)
    per_block = 4
    all_heads = BLOCK // per_block
    source, place = head_of(z, y, x, c, all_heads // 4)
    lane = lax.broadcasted_iota(jnp.int32, (1, BLOCK), 1)
    for block in range(8):
        row = jnp.zeros((1, BLOCK), jnp.float32)
        for n in range(per_block):
            hot = bucket_ref[...] == block * per_block + n
            value = lane_sum(jnp.where(hot, line_ref[...], 0.0))
            row = jnp.where(lane == n * all_heads + source * (all_heads // 4) + place, value, row)
        packed[block // 2, block % 2, 4:5, :] = row
    for made in heads:
        made.wait_recv()
    for n in range(three):
        here = slice(n * group * size, (n + 1) * group * size)
        rows_low[:, here] = heads_in[:, n].reshape(group * size, tokens).T
    step(0)
    for n in range(three):
        weight_grads(n, normed_ref, rows_low[:, n * cols : (n + 1) * cols])
    join_relay(links, me, *join(3))
    step(1)
    send_sums(3)
    join_relay(links, me, *join(0))
    join_relay(links, me, *join(1))
    step(2)
    join_relay(links, me, *join(2))
    home = to_home(layer_own, layer_ref)
    for n in range(three):
        send_sums(n)
    last = step(3)
    normed_grad = jnp.concatenate(last, axis=0)
    tokens_wide = token_ref[...].astype(jnp.float32)
    scale = rms(tokens_wide)
    unit = tokens_wide * scale
    token_grad = wide_ref[...] + norm_back(normed_grad, unit, scale, gain_ref[...])
    for i in range(4):
        token_out[i] = token_grad[:, i * part : (i + 1) * part].astype(jnp.bfloat16)
    home += to_home(token_out, home_ref)
    gain_part = jnp.sum(normed_grad * unit, axis=0, keepdims=True)
    for i in range(width // BLOCK):
        here = slice(i * BLOCK, (i + 1) * BLOCK)
        block = (i // 2) // 2, (i // 2) % 2
        packed[block[0], block[1], i % 2 : i % 2 + 1, :] = gain_part[:, here]
        packed[block[0], block[1], 2 + i % 2 : 3 + i % 2, :] = gain_two_ref[:, here]
    got = []
    for d in (1, 2, 3):
        to = device(z, y, flip(x, d // 2), flip(c, d % 2))
        got.append(links.go(packed, in_f.at[d - 1], to))
    for made in got:
        made.wait_recv()
    for made in got:
        links.done(made)
    packed[...] = packed[...] + in_f[0] + in_f[1] + in_f[2]
    made = links.go(packed.at[:, 1 - y], in_y, device(z, 1 - y, x, c))
    made.wait_recv()
    in_y[...] = in_y[...] + packed[:, y]
    got = []
    for d in (1, 2, 3):
        other = flip_pair(z, d)
        got.append(links.go(in_y.at[other], in_z.at[d - 1], device(other, y, x, c)))
    for made in got:
        made.wait_recv()
    small_ref[...] = in_y[z] + in_z[0] + in_z[1] + in_z[2]
    for made in way + home:
        made.wait_recv()
    links.finish()


def leave(pieces, normed, weight, token_rows, wide_grad, gain, low, context, layer,
          gain_two_part, line_grad, rev_buckets, ffn_slot):
    _, _, size, tokens = pieces.shape
    rows, width = token_rows.shape
    depth, wide = weight.shape[0] // 8, weight.shape[1]
    out_wide = context.shape[1]
    cols = 2 * wide // 3
    tile = (8, BLOCK)
    return pl.pallas_call(
        exit_kernel,
        name="leave",
        out_shape=[
            *(low_array(depth, cols) for _ in range(4)),
            low_array(4, rows, width // 4),
            low_array(4, rows, width // 4),
            wide_array(*tile),
            low_array(*ffn_slot.shape),
        ],
        in_specs=[IN_VMEM] * 12 + [IN_PLACE],
        out_specs=[IN_VMEM] * 7 + [IN_PLACE],
        scratch_shapes=[
            low_space(4, 3, size, tokens),
            low_space(tokens, wide),
            low_space(4, 8 * depth, out_wide),
            low_space(4, 2, 3, depth, out_wide),
            low_space(4, 2, depth, out_wide),
            low_space(4, 2, depth, out_wide),
            low_space(4, rows, width // 4),
            pltpu.VMEM((4, 2, *tile), jnp.float32),
            pltpu.VMEM((3, 4, 2, *tile), jnp.float32),
            pltpu.VMEM((4, *tile), jnp.float32),
            pltpu.VMEM((3, *tile), jnp.float32),
            *reduce_space(rows, width),
            COPIES((96,)),
            COPIES((96,)),
            COPIES((4, 2, 4, 2)),
            COPIES((4, 2, 3)),
            COPIES((4, 2)),
        ],
        compiler_params=pltpu.CompilerParams(
            collective_id=4, has_side_effects=True, vmem_limit_bytes=60 << 20
        ),
    )(pieces, normed, weight, token_rows, wide_grad, gain, low, context, layer,
      gain_two_part, line_grad, rev_buckets, ffn_slot)


def widen_kernel(*refs):
    sources, outs, spaces, sem = refs[:7], refs[7:15], refs[15:22], refs[22]
    copies = [
        pltpu.make_async_copy(source, space, sem.at[n])
        for n, (source, space) in enumerate(zip(sources, spaces))
    ]
    for copy in copies:
        copy.start()
    for copy in copies:
        copy.wait()
    attn, slots, home = spaces[:4], spaces[4:6], spaces[6]
    z_low = (lax.axis_index("seq") // 2) % 2
    for ref, out in zip(attn, outs[:4]):
        out[...] = ref[...].astype(jnp.float32)
    size = slots[0].shape[1] // 3
    for k in range(2):
        cut = lanes((k + z_low - 2 * k * z_low) * size, size)
        for n, out in enumerate(outs[4:7]):
            out[:, cut] = slots[k][:, n * size : (n + 1) * size].astype(jnp.float32)
    outs[7][...] = home[...].astype(jnp.float32)


def widen(attn, slots, home):
    depth, cols = attn[0].shape
    size = 2 * slots[0].shape[1] // 3
    return pl.pallas_call(
        widen_kernel,
        name="widen",
        out_shape=[wide_array(depth, cols)] * 4
        + [wide_array(depth, size)] * 3
        + [wide_array(*home.shape)],
        in_specs=[IN_PLACE] * 7,
        out_specs=[IN_VMEM] * 8,
        scratch_shapes=[low_space(*a.shape) for a in (*attn, *slots, home)] + [COPIES((7,))],
        compiler_params=pltpu.CompilerParams(vmem_limit_bytes=60 << 20),
    )(*attn, *slots, home)


def fast_shards(
    tokens_in,
    cotangent,
    gain_attn,
    query_weight,
    key_weight,
    value_weight,
    output_weight,
    bias_table,
    gain_ffn,
    gate_weight,
    up_weight,
    down_weight,
    lengths,
    buckets,
):
    seq_index, fsdp_index = lax.axis_index("seq"), lax.axis_index("fsdp")
    z, y, x, c = seq_index // 2, seq_index % 2, fsdp_index // 2, fsdp_index % 2
    z_low, z_high = z % 2, z // 2
    batch_count, slot_count, part_width = tokens_in.shape
    width = part_width * 4
    row_count = query_weight.shape[0]
    heads = query_weight.shape[1] // DH
    group_heads = heads // 2
    group_width = group_heads * DH
    hidden_width = gate_weight.shape[1] // 2
    def halves(weights):
        slots = []
        for k in range(2):
            half = k ^ z_low
            slots.append(
                jnp.concatenate(
                    [
                        lax.dynamic_slice_in_dim(w, half * (w.shape[1] // 2), w.shape[1] // 2, 1)
                        for w in weights
                    ],
                    axis=1,
                )
            )
        return slots

    small = jnp.concatenate(
        [gain_attn, gain_ffn, bias_table.reshape(-1), jnp.zeros((2 * row_count - bias_table.size,), jnp.bfloat16)]
    )
    small = small.astype(jnp.float32).reshape(8, BLOCK)
    rev_buckets = jnp.concatenate([buckets[::-1], jnp.full((1,), -1, jnp.int32)])[None, :]
    (
        token_low,
        normed_one,
        grad_own,
        pieces,
        qkv_weight,
        gain_one,
        gain_two,
        rev_line,
        slots_o,
        slots_g,
    ) = entry(
        lengths,
        tokens_in,
        cotangent,
        small,
        rev_buckets,
        (query_weight, key_weight, value_weight, output_weight, gate_weight),
    )
    pieces, *later = lax.optimization_barrier((pieces, *halves([up_weight, down_weight])))
    slots_ud = [move(later[k], spread_slot(k)) for k in range(2)]
    context_pieces, context_wide, lse, qkv_all = attend(lengths, pieces, rev_line)
    (
        layer,
        context,
        residual_low,
        residual_grad,
        gain_two_part,
        grad_pieces,
        terms_gate_up,
        terms_down,
    ) = core(context_pieces, token_low, gain_two, grad_own, slots_o, slots_g, slots_ud)

    def slot_sum(k):
        sums = [
            jnp.sum(t[k].astype(jnp.float32), axis=0).astype(jnp.bfloat16)
            for t in (terms_gate_up, terms_down)
        ]
        return jnp.concatenate(sums, axis=1)

    ffn_first = move(slot_sum(0), spread_slot(0))
    ffn_second = slot_sum(1)
    qkv_grad_pieces, line_grad = attend_back(
        lengths, grad_pieces, rev_line, context_wide, lse, qkv_all
    )
    qkv_grad_pieces, ffn_first = lax.optimization_barrier((qkv_grad_pieces, ffn_first))
    *attn_sums, home, layer, small, ffn_second = leave(
        qkv_grad_pieces,
        normed_one,
        qkv_weight,
        token_low,
        residual_grad,
        gain_one,
        residual_low,
        context,
        layer,
        gain_two_part,
        line_grad,
        rev_buckets,
        ffn_second,
    )
    query_sum, key_sum, value_sum, output_sum, gate_sum, up_sum, down_sum, home = widen(
        attn_sums, (ffn_first, ffn_second), home
    )
    token_share = home.reshape(batch_count, slot_count, part_width)
    layer_out = layer.reshape(batch_count, slot_count, part_width)
    table_sum = lax.dynamic_slice_in_dim(
        small[4].reshape(-1, 4 * heads), fsdp_index * heads, heads, 1
    )
    return (
        layer_out,
        token_share,
        small[:2].reshape(-1),
        query_sum,
        key_sum,
        value_sum,
        output_sum,
        table_sum,
        small[2:4].reshape(-1),
        gate_sum,
        up_sum,
        down_sum,
    )


def solution(mesh):
    placed = (
        P(None, "seq", "fsdp"),
        P(None, "seq", "fsdp"),
        P("seq"),
        P("seq", "fsdp"),
        P("seq", "fsdp"),
        P("seq", "fsdp"),
        P("seq", "fsdp"),
        P("seq", "fsdp"),
        P("seq"),
        P("seq", "fsdp"),
        P("seq", "fsdp"),
        P("seq", "fsdp"),
        P(),
        P(),
    )
    return jax.shard_map(
        fast_shards if (mesh.shape["seq"], mesh.shape["fsdp"]) == (8, 4) else shards,
        mesh=mesh,
        in_specs=placed,
        out_specs=(
            P(None, "seq", "fsdp"),
            P(None, "seq", "fsdp"),
            P("seq"),
            P("seq", "fsdp"),
            P("seq", "fsdp"),
            P("seq", "fsdp"),
            P("seq", "fsdp"),
            P("seq", "fsdp"),
            P("seq"),
            P("seq", "fsdp"),
            P("seq", "fsdp"),
            P("seq", "fsdp"),
        ),
        check_vma=False,
    )
```
